32 devices in a mesh: tile: 8 (over z, x), layer: 4 (over y, core).
Axes of the slice: x: 2, y: 2, z: 4, core: 2. Of those that a mesh axis runs over, the one named last changes fastest.
Arguments:
- head_start: float32 [8, 512, 512], P('layer', 'tile'), may hold values from -2 to 0.5
- soil_class: int32 [8, 512, 512], P('layer', 'tile'), may hold values from 0 to 11
- land_mask: int32 [512, 512], P('tile'), may hold values 0 or 1
- ks_table: float32 [12], replicated, may hold values from 0.2 to 5
- alpha_table: float32 [12], replicated, may hold values from 0.5 to 2
- store_table: float32 [12], replicated, may hold values from 0.5 to 2
- section: float32 [128, 128], P('tile'), may hold values from -6 to 6
- cross_owner: int32 [8, 256], P('tile'), may hold values from 0 to 7, as said below
- cross_local: int32 [8, 256], P('tile'), may hold values from 0 to 15
- node_cell: int32 [8, 256, 128], P('tile'), may hold values from -1 to 32767, as said below
- bed_cond: float32 [8, 256, 128], P('tile'), may hold values from 0.5 to 4
Outputs:
- head: float32 [8, 512, 512], P('layer', 'tile')
- inflow: float32 [128, 128], P('tile', 'layer')
The draws below stay inside these ranges and needn't reach their ends.
Inputs may be any that keep to these rules, and one draw needn't show every extreme that they name: `cross_owner`: no strip's row names one owner in more than 32 slots, and in every row some owner is named in exactly 32 slots. `node_cell`: -1 marks a node outside the strip; other values index the strip's top-layer cells row-major over 64 x 512. In each strip the slots with nodes come first, the rest are padding with every node -1.
All inputs are finite; a program needn't handle non-finite values. No bound on the sum of `land_mask` on one device may be relied on, other than what follows from the above.
Results may differ from the reference program's by a relative error of at most 0.00002.
Values sent between devices are 32-bit elements; how exact they have to be, the bound alone decides.
No kernel may reach another device: no remote copies, remote signals or barrier semaphores. Data moves between devices by JAX's collectives and lax.ppermute only.
A program may use at most 64 MiB of HBM per device.

```python
import math
import jax
import jax.numpy as jnp

CX = 64
NY = 512
NCLASS = 12
NODES = 128
RPT = 16
CSLOT = 256
ITERS = 2
SWEEPS = 3
TILES = 8
NX = 512
NZ = 8
REACHES = 128


def draw_cross_owner(key, part):
    rounds = (CSLOT + TILES - 1) // TILES
    keys = jax.random.split(key, TILES * rounds)
    perms = jax.vmap(lambda single: jax.random.permutation(single, TILES))(keys)
    return perms.reshape(TILES, rounds * TILES)[:, :CSLOT].astype(jnp.int32)


def draw_node_cell(key, part):
    key_live, key_start, key_length, key_cell = jax.random.split(jax.random.fold_in(key, 17), 4)
    live_slots = jax.random.randint(key_live, (TILES, 1), CSLOT // 2, CSLOT + 1)
    slot_order = jnp.arange(CSLOT, dtype=jnp.int32)[None, :]
    slot_live = slot_order < live_slots
    length = jax.random.randint(key_length, (TILES, CSLOT, 1), NODES // 2, NODES + 1)
    start = jax.random.randint(key_start, (TILES, CSLOT, 1), 0, NODES - length + 1)
    node_order = jnp.arange(NODES, dtype=jnp.int32)[None, None, :]
    inside = (node_order >= start) & (node_order < start + length) & slot_live[:, :, None]
    chosen = jax.random.randint(key_cell, (TILES, CSLOT, NODES), 0, CX * NY)
    return jnp.where(inside, chosen, -1).astype(jnp.int32)


def set_ends(array, key, low, largest):
    spot = [jax.random.randint(jax.random.fold_in(key, axis), (), 0, length) for axis, length in enumerate(array.shape)]
    main_axis = array.shape.index(max(array.shape))
    next_to = spot[:main_axis] + [(spot[main_axis] + 1) % array.shape[main_axis]] + spot[main_axis + 1:]
    return array.at[tuple(spot)].set(low).at[tuple(next_to)].set(largest)


def block_scale(stream_key, extent, pieces, smallest, largest):
    loudness = 1.0
    for position, shards_of in pieces:
        draws = jax.random.uniform(jax.random.fold_in(jax.random.fold_in(stream_key, 6), position), (shards_of,), jnp.float32, smallest / len(pieces), largest / len(pieces))
        loudness = loudness * jnp.repeat(jnp.exp(draws), extent[position] // shards_of).reshape((-1,) + (1,) * (len(extent) - 1 - position))
    return loudness


def noise(key, dims, scale, limit, cuts=(), kind=jnp.bfloat16):
    drawn = scale * jax.random.normal(key, dims, jnp.float32)
    if cuts:
        drawn = drawn * block_scale(key, dims, cuts, -0.22, 0.18)
    return jnp.clip(drawn, -limit, limit).astype(kind)


def setup_inputs(seed: int = 0) -> dict:
    streams_of = jax.random.split(jax.random.key(seed), 12)
    return {
        "head_start": jnp.clip(-2.0 + 2.5 * jax.random.uniform(streams_of[0], (NZ, NX, NY), jnp.float32) ** block_scale(streams_of[0], (NZ, NX, NY), ((0, 4), (1, 8)), -0.2, 0.2), -2.0, 0.5),
        "soil_class": set_ends(jax.random.randint(streams_of[1], (NZ, NX, NY), 0, NCLASS), jax.random.fold_in(streams_of[1], 1), 0, NCLASS - 1).astype(jnp.int32),
        "land_mask": set_ends((jax.random.randint(streams_of[2], (NX, NY), 0, 8) < 7).astype(jnp.int32), jax.random.fold_in(streams_of[2], 1), 0, 1),
        "ks_table": jnp.clip(jnp.exp(jax.random.uniform(streams_of[3], (NCLASS,), jnp.float32, math.log(0.2), math.log(5.0))), 0.2, 5.0),
        "alpha_table": jnp.clip(jax.random.uniform(streams_of[4], (NCLASS,), jnp.float32, 0.5, 2.0), 0.5, 2.0),
        "store_table": jnp.clip(jax.random.uniform(streams_of[5], (NCLASS,), jnp.float32, 0.5, 2.0), 0.5, 2.0),
        "section": noise(streams_of[6], (REACHES, NODES), 1.0, 6.0, ((0, 8),), jnp.float32),
        "cross_owner": draw_cross_owner(jax.random.fold_in(streams_of[11], 71), 0),
        "cross_local": set_ends(jax.random.randint(streams_of[8], (TILES, CSLOT), 0, RPT), jax.random.fold_in(streams_of[8], 1), 0, RPT - 1).astype(jnp.int32),
        "node_cell": draw_node_cell(jax.random.fold_in(streams_of[11], 71), 0),
        "bed_cond": jnp.clip(jnp.exp(math.log(4.0) - 2.0794415 * jax.random.uniform(streams_of[10], (TILES, CSLOT, NODES), jnp.float32) ** block_scale(streams_of[10], (TILES, CSLOT, NODES), ((0, 8),), -0.2, 0.2)), 0.5, 4.0),
    }


LATERAL = 1.0
VERTICAL = 2.0
GRAVITY = 1.0
NEIGHBOURS = ((0, -1, VERTICAL), (0, 1, VERTICAL), (1, -1, LATERAL), (1, 1, LATERAL), (2, -1, LATERAL), (2, 1, LATERAL))


def beside(padded, axis_id, step):
    spans = [slice(1, -1), slice(1, -1), slice(1, -1)]
    spans[axis_id] = slice(1 + step, padded.shape[axis_id] - 1 + step)
    return padded[tuple(spans)]


def neighbor_weights(cond_pad, open_pad):
    centre = cond_pad[1:-1, 1:-1, 1:-1]
    centre_open = open_pad[1:-1, 1:-1, 1:-1]
    result = []
    for axis_id, step, factor in NEIGHBOURS:
        far = beside(cond_pad, axis_id, step)
        far_open = beside(open_pad, axis_id, step)
        result.append(factor * 2.0 * centre_open * far_open / (centre + far))
    return result


def relax(head_pad, weights, store, head_old, riv_diag, riv_rhs):
    total = store * head_old
    diagonal_sum = store
    for weight, (axis_id, step, factor) in zip(weights, NEIGHBOURS):
        total = total + weight * beside(head_pad, axis_id, step)
        diagonal_sum = diagonal_sum + weight
    total = total + GRAVITY * (weights[0] - weights[1]) + riv_rhs
    return total / (diagonal_sum + riv_diag)


def reference(head_start, soil_class, land_mask, ks_table, alpha_table, store_table, section, cross_owner, cross_local, node_cell, bed_cond):
    ks = ks_table[soil_class]
    alpha = alpha_table[soil_class]
    store = store_table[soil_class]
    landf = land_mask.astype(jnp.float32)[None]
    reach_row = cross_owner * RPT + cross_local
    slot_section = section[reach_row]
    tile_ids = jnp.arange(TILES, dtype=jnp.int32)[:, None, None]
    in_tile = node_cell >= 0
    safe_cell = jnp.where(in_tile, node_cell, 0)
    grid_row = tile_ids * CX + safe_cell // NY
    flat_index = jnp.where(in_tile, grid_row * NY + safe_cell % NY, NX * NY)
    bed_terms = jnp.where(in_tile, bed_cond, 0.0)
    diag_top = jnp.zeros((NX * NY,), jnp.float32).at[flat_index.reshape(-1)].add(bed_terms.reshape(-1), mode="drop")
    rhs_top = jnp.zeros((NX * NY,), jnp.float32).at[flat_index.reshape(-1)].add((bed_terms * slot_section).reshape(-1), mode="drop")
    riv_diag = jnp.zeros((NZ, NX, NY), jnp.float32).at[0].set(diag_top.reshape(NX, NY))
    riv_rhs = jnp.zeros((NZ, NX, NY), jnp.float32).at[0].set(rhs_top.reshape(NX, NY))
    head = head_start
    for picard in range(ITERS):
        conduct = ks * jnp.exp(alpha * jnp.minimum(head, 0.0))
        cond_pad = jnp.pad(conduct, 1)
        open_pad = jnp.pad(conduct * landf, 1)
        weights = neighbor_weights(cond_pad, open_pad)
        for sweep in range(SWEEPS):
            head = relax(jnp.pad(head, 1), weights, store, head_start, riv_diag, riv_rhs)
    top_flat = head[0].reshape(-1)
    node_head = top_flat[jnp.where(in_tile, flat_index, 0)]
    slot_in = jnp.where(in_tile, bed_cond * (node_head - slot_section), 0.0)
    inflow = jnp.zeros((REACHES, NODES), jnp.float32).at[reach_row.reshape(-1)].add(slot_in.reshape(-1, NODES))
    return head, inflow
```

```python
import functools

import jax
import jax.numpy as jnp
from jax import lax
from jax.experimental import pallas as pl
from jax.experimental.pallas import tpu as pltpu
from jax.sharding import PartitionSpec as P

ITERS = 2
SWEEPS = 3

LATERAL = 1.0
VERTICAL = 2.0
GRAVITY = 1.0

PAD = 8
HALO = ITERS * SWEEPS
LANES = 128
VMEM_LIMIT = 48 * 1024 * 1024
FLAT = ("tile", "layer")

in_vmem = pl.BlockSpec(memory_space=pltpu.VMEM)
in_smem = pl.BlockSpec(memory_space=pltpu.SMEM)


def bf16_pieces(value, count):
    pieces = []
    for _ in range(count):
        piece = value.astype(jnp.bfloat16)
        pieces.append(piece)
        value = value - piece.astype(jnp.float32)
    return pieces


def one_hot(row, size, on):
    index = lax.broadcasted_iota(jnp.int32, (16, LANES), 0)
    zero = jnp.zeros((16, LANES), jnp.bfloat16)
    tiles = []
    for start in range(0, size, 16):
        here = (index + start).astype(jnp.float32).astype(jnp.bfloat16)
        tiles.append(jnp.where(row == here, on, zero))
    return jnp.concatenate(tiles, axis=0)


def row_copies(ref, slot):
    return jnp.broadcast_to(ref[pl.ds(slot, 1), :], (16, LANES)).astype(jnp.bfloat16)


def split_cells(cells, first_row, breadth):
    local = cells - first_row * breadth
    block = jnp.where(cells < 0, -1, local >> 7)
    return block.astype(jnp.float32), (local & (LANES - 1)).astype(jnp.float32)


def scatter_into(out_ref, value, cells, first_row, breadth, blocks, block_sc, lane_sc, high_sc, low_sc):
    block, lane = split_cells(cells, first_row, breadth)
    block_sc[...] = block
    lane_sc[...] = lane
    high, low = bf16_pieces(value, 2)
    high_sc[...] = high.astype(jnp.float32)
    low_sc[...] = low.astype(jnp.float32)
    slots = value.shape[0]
    group = 8
    one = jnp.ones((16, LANES), jnp.bfloat16)

    def step(number, total):
        left, right = [], []
        for place in range(group):
            slot = number * group + place
            lanes = row_copies(lane_sc, slot)
            left.append(one_hot(row_copies(block_sc, slot), blocks, one))
            right.append(
                jnp.concatenate(
                    [
                        one_hot(lanes, LANES, row_copies(high_sc, slot)),
                        one_hot(lanes, LANES, row_copies(low_sc, slot)),
                    ],
                    axis=0,
                )
            )
        return total + lax.dot_general(
            jnp.concatenate(left, axis=1),
            jnp.concatenate(right, axis=1),
            (((1,), (1,)), ((), ())),
            preferred_element_type=jnp.float32,
        )

    total = lax.fori_loop(0, slots // group, step, jnp.zeros((blocks, 2 * LANES), jnp.float32))
    out_ref[...] = total[:, :LANES] + total[:, LANES:]


def diag_kernel(breadth, blocks, place_ref, cells_ref, bed_ref, diag_ref, *scratch):
    first_row = place_ref[0] - HALO
    scatter_into(diag_ref, bed_ref[...], cells_ref[...], first_row, breadth, blocks, *scratch)


def rhs_kernel(
    breadth, blocks, place_ref, cells_ref, bed_ref, section_ref, row_ref, rhs_ref, slot_section_ref, *scratch
):
    first_row = place_ref[0] - HALO
    rows = section_ref.shape[0]
    slots = row_ref.shape[1]
    index = lax.broadcasted_iota(jnp.int32, (rows, slots), 0)
    pick = jnp.where(index == row_ref[...], 1.0, 0.0).astype(jnp.bfloat16)
    picked = jnp.zeros(slot_section_ref.shape, jnp.float32)
    for piece in bf16_pieces(section_ref[...], 3):
        picked = picked + lax.dot_general(
            pick, piece, (((0,), (0,)), ((), ())), preferred_element_type=jnp.float32
        )
    slot_section_ref[...] = picked
    scatter_into(
        rhs_ref, bed_ref[...] * picked, cells_ref[...], first_row, breadth, blocks, *scratch
    )


def flow_kernel(
    place_ref, ks_ref, alpha_ref, store_ref, block_ref, land_ref, halo_ref, land_halo_ref,
    diag_ref, rhs_ref, riv_halo_ref, head_ref,
    soil_sc, first_sc, ks_sc, alpha_sc, diag_sc, rhs_sc, wx_sc, wy_sc, wz_sc, base_sc, inv_sc,
    ping_sc, pong_sc, land_sc, dtop_sc, rtop_sc,
):
    sources, _, held, window, breadth = block_ref.shape
    layers = sources * held
    span = window - 2 * PAD
    low, high = PAD - HALO, PAD + span
    is_first = place_ref[1] == 1
    is_last = place_ref[2] == 1
    per_row = breadth // LANES

    def put_rows(ref, layer, row, value):
        for part in range(per_row):
            spot = pl.ds(row * layers + layer, value.shape[0], stride=layers)
            ref[part, spot, :] = value[:, part * LANES:(part + 1) * LANES]

    for source in range(sources):
        for held_layer in range(held):
            layer = source * held + held_layer
            put_rows(first_sc, layer, 0, block_ref[source, 0, held_layer])
            put_rows(soil_sc, layer, 0, block_ref[source, 1, held_layer])
    land_sc[...] = land_ref[...]
    dtop_sc[...] = diag_ref[...]
    rtop_sc[...] = rhs_ref[...]
    side = riv_halo_ref.shape[1]
    for chosen, row, block in ((is_first, low, 0), (is_last, high, diag_ref.shape[0] - side)):
        @pl.when(chosen)
        def _(row=row, block=block):
            for layer in range(layers):
                put_rows(first_sc, layer, row, halo_ref[layer])
                put_rows(soil_sc, layer, row, halo_ref[layers + layer])
            land_sc[pl.ds(row, HALO), :] = land_halo_ref[...]
            dtop_sc[pl.ds(block, side), :] = riv_halo_ref[0]
            rtop_sc[pl.ds(block, side), :] = riv_halo_ref[1]

    def get(ref, row):
        spot = pl.ds(pl.multiple_of(row * layers, layers), layers)
        return jnp.concatenate([ref[part, spot, :] for part in range(per_row)], axis=1)

    def put(ref, row, value):
        spot = pl.ds(pl.multiple_of(row * layers, layers), layers)
        for part in range(per_row):
            ref[part, spot, :] = value[:, part * LANES:(part + 1) * LANES]

    level = lax.broadcasted_iota(jnp.int32, (layers, breadth), 0)
    column = lax.broadcasted_iota(jnp.int32, (layers, breadth), 1)
    top = level == 0
    not_bottom = level < layers - 1
    not_last = column < breadth - 1

    def riv_row(ref, row):
        first = (row - low) * per_row
        parts = [
            jnp.broadcast_to(ref[pl.ds(first + part, 1), :], (layers, LANES)) for part in range(per_row)
        ]
        return jnp.where(top, jnp.concatenate(parts, axis=1), 0.0)

    def prepare(row, _):
        soil = get(soil_sc, row)
        ks = jnp.full(soil.shape, ks_ref[0])
        alpha = jnp.full(soil.shape, alpha_ref[0])
        store = jnp.full(soil.shape, store_ref[0])
        for kind in range(1, ks_ref.shape[0]):
            hit = soil == float(kind)
            ks = jnp.where(hit, ks_ref[kind], ks)
            alpha = jnp.where(hit, alpha_ref[kind], alpha)
            store = jnp.where(hit, store_ref[kind], store)
        put(ks_sc, row, ks)
        put(alpha_sc, row, alpha)
        put(diag_sc, row, store + riv_row(dtop_sc, row))
        put(rhs_sc, row, store * get(first_sc, row) + riv_row(rtop_sc, row))
        return 0

    lax.fori_loop(low, window - low, prepare, 0)

    def east(field):
        return pltpu.roll(field, breadth - 1, 1)

    def west(field):
        return pltpu.roll(field, 1, 1)

    def below(field):
        return pltpu.roll(field, layers - 1, 0)

    def above(field):
        return pltpu.roll(field, 1, 0)

    def make_weights(now_sc, first, last):
        def conduct(row):
            cond = get(ks_sc, row) * jnp.exp(get(alpha_sc, row) * jnp.minimum(get(now_sc, row), 0.0))
            return cond, cond * land_sc[pl.ds(row, 1), :]

        def face(factor, cond, opened, far, far_open):
            return factor * 2.0 * opened * far_open / (cond + far)

        def step(row, carried):
            cond, opened, wx_before = carried
            far, far_open = conduct(row + 1)
            wx = face(LATERAL, cond, opened, far, far_open)
            wy = jnp.where(not_last, face(LATERAL, cond, opened, east(cond), east(opened)), 0.0)
            wz = jnp.where(not_bottom, face(VERTICAL, cond, opened, below(cond), below(opened)), 0.0)
            wz_above = above(wz)
            total = get(diag_sc, row) + wx_before + wx + wy + west(wy) + wz + wz_above
            inverse = 1.0 / total
            put(wx_sc, row, wx)
            put(wy_sc, row, wy)
            put(wz_sc, row, wz)
            put(inv_sc, row, inverse)
            put(base_sc, row, get(rhs_sc, row) + GRAVITY * (wz_above - wz))
            return far, far_open, wx

        cond, opened = conduct(first)
        far, far_open = conduct(first + 1)
        wx = face(LATERAL, cond, opened, far, far_open)
        put(wx_sc, first, wx)
        lax.fori_loop(first + 1, last, step, (far, far_open, wx))

    def sweep(now_sc, later_sc, first, last):
        def step(row, carried):
            before, here, wx_before = carried
            after = get(now_sc, row + 1)
            wx = get(wx_sc, row)
            wy = get(wy_sc, row)
            wz = get(wz_sc, row)
            total = get(base_sc, row) + wx_before * before + wx * after
            total = total + wy * east(here) + west(wy * here)
            total = total + wz * below(here) + above(wz * here)
            put(later_sc, row, total * get(inv_sc, row))
            return here, after, wx

        lax.fori_loop(
            first, last, step, (get(now_sc, first - 1), get(now_sc, first), get(wx_sc, first - 1))
        )

    now_sc, spare = first_sc, [ping_sc, pong_sc]
    first, last = low, window - low
    for picard in range(ITERS):
        make_weights(now_sc, first, last - 1)
        for _ in range(SWEEPS):
            first, last = first + 1, last - 1
            later_sc = spare[0]
            sweep(now_sc, later_sc, first, last)
            spare = [spare[1], later_sc]
            now_sc = later_sc
    for layer in range(layers):
        for part in range(per_row):
            spot = pl.ds(PAD * layers + layer, span, stride=layers)
            head_ref[layer, :, pl.ds(part * LANES, LANES)] = now_sc[part, spot, :]


def inflow_kernel(
    place_ref, top_ref, cells_ref, bed_ref, slot_section_ref, row_ref, out_ref,
    block_sc, lane_sc, head_sc, turned_sc,
):
    span, breadth = top_ref.shape
    per_row = breadth // LANES
    blocks = span * per_row
    cells = cells_ref[...]
    block, lane = split_cells(cells, place_ref[0], breadth)
    block_sc[...] = block
    lane_sc[...] = lane
    for part in range(per_row):
        turned_sc[pl.ds(part, span, stride=per_row), :] = top_ref[:, part * LANES:(part + 1) * LANES]
    pieces = bf16_pieces(turned_sc[...].T, 3)
    table = jnp.concatenate(pieces, axis=1)
    slots = cells.shape[0]
    group = 8
    one = jnp.ones((16, LANES), jnp.bfloat16)
    index = lax.broadcasted_iota(jnp.int32, (LANES, LANES), 0).astype(jnp.float32)

    def step(number, _):
        hots = []
        for place in range(group):
            hot = one_hot(row_copies(block_sc, number * group + place), blocks, one)
            hots.append(jnp.concatenate([hot] * len(pieces), axis=0))
        found = lax.dot_general(
            table, jnp.concatenate(hots, axis=1), (((1,), (0,)), ((), ())),
            preferred_element_type=jnp.float32,
        )
        for place in range(group):
            slot = number * group + place
            lanes = jnp.broadcast_to(lane_sc[pl.ds(slot, 1), :], (LANES, LANES))
            mine = jnp.where(index == lanes, found[:, place * LANES:(place + 1) * LANES], 0.0)
            head_sc[pl.ds(slot, 1), :] = jnp.sum(mine, axis=0, keepdims=True)
        return 0

    lax.fori_loop(0, slots // group, step, 0)
    block = block_sc[...]
    inside = (block >= 0.0) & (block < float(blocks))
    slot_in = jnp.where(inside, bed_ref[...] * (head_sc[...] - slot_section_ref[...]), 0.0)
    rows = out_ref.shape[0]
    index = lax.broadcasted_iota(jnp.int32, (rows, slots), 0)
    put = jnp.where(index == row_ref[...], 1.0, 0.0).astype(jnp.bfloat16)
    total = jnp.zeros(out_ref.shape, jnp.float32)
    for piece in bf16_pieces(slot_in, 3):
        total = total + lax.dot_general(
            put, piece, (((1,), (0,)), ((), ())), preferred_element_type=jnp.float32
        )
    out_ref[...] = total


def call(kernel, out_shape, in_specs, scratch, flops, moved):
    single = not isinstance(out_shape, (tuple, list))
    return pl.pallas_call(
        kernel,
        out_shape=out_shape,
        in_specs=in_specs,
        out_specs=in_vmem if single else tuple(in_vmem for _ in out_shape),
        scratch_shapes=scratch,
        compiler_params=pltpu.CompilerParams(vmem_limit_bytes=VMEM_LIMIT),
        cost_estimate=pl.CostEstimate(flops=flops, bytes_accessed=moved, transcendentals=0),
    )


def on_device(
    head_start,
    soil_class,
    land_mask,
    ks_table,
    alpha_table,
    store_table,
    section,
    cross_owner,
    cross_local,
    node_cell,
    bed_cond,
):
    held, across, breadth = head_start.shape
    reach_rows, node_count = section.shape
    tiles = lax.axis_size("tile")
    groups = lax.axis_size("layer")
    layers = held * groups
    span = across // groups
    window = span + 2 * PAD
    per_row = breadth // LANES
    blocks = (span + 2 * HALO) * per_row
    part = lax.axis_index("layer")
    is_first = part == 0
    is_last = part == groups - 1
    place = jnp.stack([part * span, is_first.astype(jnp.int32), is_last.astype(jnp.int32)]).astype(jnp.int32)
    swap = []
    for tile in range(tiles - 1):
        end, start = tile * groups + groups - 1, (tile + 1) * groups
        swap += [(end, start), (start, end)]

    cells = node_cell[0]
    bed = bed_cond[0]
    slots = cells.shape[0]
    reach = cross_owner * reach_rows + cross_local

    both = jnp.stack([head_start, soil_class.astype(jnp.float32)])
    both = jnp.pad(both, ((0, 0), (0, 0), (PAD, PAD), (0, 0)))
    windows = jnp.stack([both[:, :, p * span:p * span + window] for p in range(groups)])
    block = lax.all_to_all(windows, "layer", 0, 0)

    spread = jnp.broadcast_to(section[None], (tiles, reach_rows, node_count))
    whole_section = lax.all_to_all(spread, "tile", 0, 0).reshape(tiles * reach_rows, node_count)

    node_scratch = [pltpu.VMEM((slots, LANES), jnp.float32) for _ in range(4)]
    riv_shape = jax.ShapeDtypeStruct((blocks, LANES), jnp.float32)
    flops = 2 * blocks * 2 * LANES * slots * LANES
    node_bytes = slots * LANES * 4
    diag = call(
        functools.partial(diag_kernel, breadth, blocks), riv_shape, [in_smem, in_vmem, in_vmem],
        node_scratch, flops, 2 * node_bytes,
    )(place, cells, bed)
    rhs, slot_section = call(
        functools.partial(rhs_kernel, breadth, blocks),
        (riv_shape, jax.ShapeDtypeStruct((slots, node_count), jnp.float32)),
        [in_smem] + [in_vmem] * 4, node_scratch, flops, 4 * node_bytes,
    )(place, cells, bed, whole_section, reach)

    land = jnp.pad(land_mask.astype(jnp.float32), ((PAD, PAD), (0, 0)))
    land = lax.dynamic_slice_in_dim(land, part * span, window, 0)

    send_row = jnp.where(is_first, PAD, PAD + span - HALO)
    edge = lax.dynamic_slice_in_dim(block, send_row, HALO, 3)
    edge = jnp.moveaxis(edge, 1, 0).reshape(2 * layers, HALO, breadth)
    edge = jnp.concatenate([edge, lax.dynamic_slice_in_dim(land, send_row, HALO, 0)[None]])
    halo = lax.ppermute(edge, FLAT, swap)
    side = HALO * per_row
    riv = jnp.stack([diag, rhs])
    riv_edge = jnp.where(is_first, riv[:, side:2 * side], riv[:, blocks - 2 * side:blocks - side])
    riv_halo = lax.ppermute(riv_edge, FLAT, swap)

    field = pltpu.VMEM((per_row, window * layers, LANES), jnp.float32)
    out = call(
        flow_kernel, jax.ShapeDtypeStruct((layers, span, breadth), jnp.float32),
        [in_smem] * 4 + [in_vmem] * 7,
        [field] * 13
        + [pltpu.VMEM((window, breadth), jnp.float32)]
        + [pltpu.VMEM((blocks, LANES), jnp.float32)] * 2,
        100 * layers * window * breadth, 8 * layers * window * breadth,
    )(
        place, ks_table, alpha_table, store_table, block, land, halo[:2 * layers], halo[2 * layers],
        diag, rhs, riv_halo,
    )
    back = lax.all_to_all(out.reshape(groups, held, span, breadth), "layer", 0, 0)
    head = jnp.moveaxis(back, 0, 1).reshape(held, across, breadth)

    partial = call(
        inflow_kernel, jax.ShapeDtypeStruct((tiles * reach_rows, node_count), jnp.float32),
        [in_smem] + [in_vmem] * 5,
        [pltpu.VMEM((slots, LANES), jnp.float32)] * 3 + [pltpu.VMEM((span * per_row, LANES), jnp.float32)],
        flops, 4 * node_bytes,
    )(place, out[0], cells, bed, slot_section, reach)
    quarter = node_count // groups
    terms = partial.reshape(tiles, reach_rows, groups, quarter)
    terms = jnp.moveaxis(terms, 2, 1).reshape(tiles * groups, reach_rows, quarter)
    inflow = jnp.sum(lax.all_to_all(terms, FLAT, 0, 0), axis=0)
    return head, inflow


def solution(mesh):
    placed = (
        P("layer", "tile", None),
        P("layer", "tile", None),
        P("tile", None),
        P(),
        P(),
        P(),
        P("tile", None),
        P("tile", None),
        P("tile", None),
        P("tile", None, None),
        P("tile", None, None),
    )
    return jax.shard_map(
        on_device,
        mesh=mesh,
        in_specs=placed,
        out_specs=(P("layer", "tile", None), P("tile", "layer")),
        check_vma=False,
    )
```

```python
import functools

import jax
import jax.numpy as jnp
from jax import lax
from jax.experimental import pallas as pl
from jax.experimental.pallas import tpu as pltpu
from jax.sharding import PartitionSpec as P

ITERS = 2
SWEEPS = 3

LATERAL = 1.0
VERTICAL = 2.0
GRAVITY = 1.0

PAD = 8
HALO = ITERS * SWEEPS
LANES = 128
VMEM_LIMIT = 48 * 1024 * 1024
FLAT = ("tile", "layer")

in_vmem = pl.BlockSpec(memory_space=pltpu.VMEM)
in_smem = pl.BlockSpec(memory_space=pltpu.SMEM)


def bf16_pieces(value, count):
    pieces = []
    for _ in range(count):
        piece = value.astype(jnp.bfloat16)
        pieces.append(piece)
        value = value - piece.astype(jnp.float32)
    return pieces


def one_hot(row, size, on):
    index = lax.broadcasted_iota(jnp.int32, (16, LANES), 0)
    zero = jnp.zeros((16, LANES), jnp.bfloat16)
    tiles = []
    for start in range(0, size, 16):
        here = (index + start).astype(jnp.float32).astype(jnp.bfloat16)
        tiles.append(jnp.where(row == here, on, zero))
    return jnp.concatenate(tiles, axis=0)


def row_copies(ref, slot):
    return jnp.broadcast_to(ref[pl.ds(slot, 1), :], (16, LANES)).astype(jnp.bfloat16)


def split_cells(cells, first_row, breadth, width):
    local = cells - first_row * breadth
    shift = width.bit_length() - 1
    block = jnp.where(cells < 0, -1, local >> shift)
    return block.astype(jnp.float32), (local & (width - 1)).astype(jnp.float32)


def river_kernel(
    breadth, place_ref, cells_ref, bed_ref, section_ref, row_ref, diag_ref, rhs_ref, slot_section_ref,
    spot_sc, dhigh_sc, dlow_sc, rhigh_sc, rlow_sc, turned_sc, sum_sc,
):
    rows = section_ref.shape[0]
    slots = row_ref.shape[1]
    index = lax.broadcasted_iota(jnp.int32, (rows, slots), 0)
    pick = jnp.where(index == row_ref[...], 1.0, 0.0).astype(jnp.bfloat16)
    picked = jnp.zeros(slot_section_ref.shape, jnp.float32)
    for piece in bf16_pieces(section_ref[...], 3):
        picked = picked + lax.dot_general(
            pick, piece, (((0,), (0,)), ((), ())), preferred_element_type=jnp.float32
        )
    slot_section_ref[...] = picked

    half = LANES // 2
    block, spot = split_cells(cells_ref[...], place_ref[0] - HALO, breadth, half)
    spot_sc[...] = spot
    bed = bed_ref[...]
    for value, high_sc, low_sc in ((bed, dhigh_sc, dlow_sc), (bed * picked, rhigh_sc, rlow_sc)):
        high, low = bf16_pieces(value, 2)
        high_sc[...] = high.astype(jnp.float32)
        low_sc[...] = low.astype(jnp.float32)
    blocks = 2 * diag_ref.shape[0]
    group = 32
    tiles = slots // LANES
    for part in range(tiles):
        turned_sc[part] = block[part * LANES:(part + 1) * LANES, :].T
    names = lax.broadcasted_iota(jnp.int32, (LANES, LANES), 1)
    names = [(names + start).astype(jnp.float32).astype(jnp.bfloat16) for start in range(0, blocks, LANES)]
    one = jnp.ones((LANES, LANES), jnp.bfloat16)
    zero = jnp.zeros((LANES, LANES), jnp.bfloat16)

    def step(number, total):
        first = number * group
        columns = turned_sc[first // LANES]
        columns = pltpu.roll(columns, lax.rem(LANES - lax.rem(first, LANES), LANES), 1)
        left, right = [], []
        for place in range(group):
            slot = first + place
            spots = row_copies(spot_sc, slot)
            left.append(
                jnp.concatenate(
                    [one_hot(spots, half, row_copies(ref, slot)) for ref in (dhigh_sc, dlow_sc, rhigh_sc, rlow_sc)],
                    axis=0,
                )
            )
            column = jnp.broadcast_to(columns[:, place:place + 1], (LANES, LANES)).astype(jnp.bfloat16)
            right.append(jnp.concatenate([jnp.where(column == name, one, zero) for name in names], axis=1))
        return total + lax.dot_general(
            jnp.concatenate(left, axis=1),
            jnp.concatenate(right, axis=0),
            (((1,), (0,)), ((), ())),
            preferred_element_type=jnp.float32,
        )

    total = lax.fori_loop(0, slots // group, step, jnp.zeros((4 * half, len(names) * LANES), jnp.float32))
    both = jnp.concatenate([total[:half] + total[half:2 * half], total[2 * half:3 * half] + total[3 * half:]], axis=0)
    for part in range(len(names)):
        sum_sc[pl.ds(part * LANES, LANES), :] = both[:, part * LANES:(part + 1) * LANES].T
    low_half = lax.broadcasted_iota(jnp.int32, diag_ref.shape, 1) < half
    even = sum_sc[pl.ds(0, blocks // 2, stride=2), :]
    odd = sum_sc[pl.ds(1, blocks // 2, stride=2), :]
    diag_ref[...] = jnp.where(low_half, even, pltpu.roll(odd, half, 1))
    rhs_ref[...] = jnp.where(low_half, pltpu.roll(even, half, 1), odd)


def prepare_kernel(place_ref, head_ref, soil_ref, section_ref, land_ref, *out_refs):
    window_refs, spread_ref, land_out_ref = out_refs[:-2], out_refs[-2], out_refs[-1]
    groups = len(window_refs)
    _, held, window, _ = window_refs[0].shape
    across = head_ref.shape[1]
    span = across // groups

    def span_of(target):
        return jnp.where(place_ref[3] == 1, groups - 1 - target, target)

    def pieces(number):
        for start in range(0, window, PAD):
            row = jnp.clip(number * span - PAD + start, 0, across - PAD)
            yield pl.ds(start, PAD), pl.ds(pl.multiple_of(row, PAD), PAD)

    for step, out_ref in enumerate(window_refs):
        for to, spot in pieces(span_of(place_ref[4] ^ step)):
            for layer in range(held):
                out_ref[0, layer, to, :] = head_ref[layer, spot, :]
                out_ref[1, layer, to, :] = soil_ref[layer, spot, :].astype(jnp.float32)
    for to, spot in pieces(span_of(place_ref[4])):
        land_out_ref[to, :] = land_ref[spot, :].astype(jnp.float32)
    section = section_ref[...]
    for tile in range(spread_ref.shape[0]):
        spread_ref[tile] = section


def flow_kernel(
    groups, place_ref, ks_ref, alpha_ref, store_ref, land_ref, halo_ref, diag_ref, rhs_ref, *refs,
):
    block_refs, head_refs = refs[:groups], refs[groups:2 * groups]
    (
        soil_sc, first_sc, ks_sc, alpha_sc, diag_sc, rhs_sc, wx_sc, wy_sc, wz_sc, base_sc, inv_sc,
        ping_sc, pong_sc, land_sc, dtop_sc, rtop_sc,
    ) = refs[2 * groups:]
    _, held, window, breadth = block_refs[0].shape
    layers = groups * held
    span = window - 2 * PAD
    low, high = PAD - HALO, PAD + span
    is_first = place_ref[1] == 1
    is_last = place_ref[2] == 1
    per_row = breadth // LANES

    def put_rows(ref, layer, row, value):
        for part in range(per_row):
            spot = pl.ds(row * layers + layer, value.shape[0], stride=layers)
            ref[part, spot, :] = value[:, part * LANES:(part + 1) * LANES]

    for step, block_ref in enumerate(block_refs):
        for held_layer in range(held):
            layer = (place_ref[4] ^ step) * held + held_layer
            put_rows(first_sc, layer, 0, block_ref[0, held_layer])
            put_rows(soil_sc, layer, 0, block_ref[1, held_layer])
    land_sc[...] = land_ref[...]
    dtop_sc[...] = diag_ref[...]
    rtop_sc[...] = rhs_ref[...]
    for chosen, row in ((is_first, low), (is_last, high)):
        @pl.when(chosen)
        def _(row=row):
            for entry in range(layers):
                layer = (place_ref[4] ^ (entry // held)) * held + entry % held
                put_rows(first_sc, layer, row, halo_ref[entry])
                put_rows(soil_sc, layer, row, halo_ref[layers + entry])
            land_sc[pl.ds(row, HALO), :] = halo_ref[2 * layers]
            for part in range(per_row):
                spot = pl.ds((row - low) * per_row + part, HALO, stride=per_row)
                lanes = pl.ds(part * LANES, LANES)
                dtop_sc[spot, :] = halo_ref[2 * layers + 1, :, lanes]
                rtop_sc[spot, :] = halo_ref[2 * layers + 2, :, lanes]

    def get(ref, row):
        spot = pl.ds(row * layers, layers)
        return jnp.concatenate([ref[part, spot, :] for part in range(per_row)], axis=1)

    def put(ref, row, value):
        spot = pl.ds(row * layers, layers)
        for part in range(per_row):
            ref[part, spot, :] = value[:, part * LANES:(part + 1) * LANES]

    level = lax.broadcasted_iota(jnp.int32, (layers, breadth), 0)
    column = lax.broadcasted_iota(jnp.int32, (layers, breadth), 1)
    top = level == 0
    not_bottom = level < layers - 1
    not_last = column < breadth - 1

    def riv_row(ref, row):
        first = (row - low) * per_row
        parts = [
            jnp.broadcast_to(ref[pl.ds(first + part, 1), :], (layers, LANES)) for part in range(per_row)
        ]
        return jnp.where(top, jnp.concatenate(parts, axis=1), 0.0)

    lane = lax.broadcasted_iota(jnp.int32, (layers, LANES), 1)

    def lane_table(ref):
        table = jnp.zeros((layers, LANES), jnp.float32)
        for kind in range(ref.shape[0]):
            table = jnp.where(lane == kind, ref[kind], table)
        return table

    tables = [lane_table(ref) for ref in (ks_ref, alpha_ref, store_ref)]

    def lookup(soil):
        found = []
        for table in tables:
            parts = [
                jnp.take_along_axis(
                    table, soil[:, part * LANES:(part + 1) * LANES], axis=1, mode="promise_in_bounds"
                )
                for part in range(per_row)
            ]
            found.append(jnp.concatenate(parts, axis=1))
        return found

    for row in range(low, window - low):
        ks, alpha, store = lookup(get(soil_sc, row).astype(jnp.int32))
        put(ks_sc, row, ks)
        put(alpha_sc, row, alpha)
        put(diag_sc, row, store + riv_row(dtop_sc, row))
        put(rhs_sc, row, store * get(first_sc, row) + riv_row(rtop_sc, row))

    def east(field):
        return pltpu.roll(field, breadth - 1, 1)

    def west(field):
        return pltpu.roll(field, 1, 1)

    def below(field):
        return pltpu.roll(field, layers - 1, 0)

    def above(field):
        return pltpu.roll(field, 1, 0)

    def make_weights(now_sc, first, last):
        def conduct(row):
            cond = get(ks_sc, row) * jnp.exp(get(alpha_sc, row) * jnp.minimum(get(now_sc, row), 0.0))
            return cond, cond * land_sc[pl.ds(row, 1), :]

        def face(factor, cond, opened, far, far_open):
            return factor * 2.0 * opened * far_open / (cond + far)

        def step(row, carried):
            cond, opened, wx_before = carried
            far, far_open = conduct(row + 1)
            wx = face(LATERAL, cond, opened, far, far_open)
            wy = jnp.where(not_last, face(LATERAL, cond, opened, east(cond), east(opened)), 0.0)
            wz = jnp.where(not_bottom, face(VERTICAL, cond, opened, below(cond), below(opened)), 0.0)
            wz_above = above(wz)
            total = get(diag_sc, row) + wx_before + wx + wy + west(wy) + wz + wz_above
            inverse = 1.0 / total
            put(wx_sc, row, wx)
            put(wy_sc, row, wy)
            put(wz_sc, row, wz)
            put(inv_sc, row, inverse)
            put(base_sc, row, get(rhs_sc, row) + GRAVITY * (wz_above - wz))
            return far, far_open, wx

        cond, opened = conduct(first)
        far, far_open = conduct(first + 1)
        wx = face(LATERAL, cond, opened, far, far_open)
        put(wx_sc, first, wx)
        carried = far, far_open, wx
        for row in range(first + 1, last):
            carried = step(row, carried)

    def sweep(now_sc, later_sc, first, last):
        def step(row, carried):
            before, here, wx_before = carried
            after = get(now_sc, row + 1)
            wx = get(wx_sc, row)
            wy = get(wy_sc, row)
            wz = get(wz_sc, row)
            total = get(base_sc, row) + wx_before * before + wx * after
            total = total + wy * east(here) + west(wy * here)
            total = total + wz * below(here) + above(wz * here)
            put(later_sc, row, total * get(inv_sc, row))
            return here, after, wx

        carried = get(now_sc, first - 1), get(now_sc, first), get(wx_sc, first - 1)
        for row in range(first, last):
            carried = step(row, carried)

    now_sc, spare = first_sc, [ping_sc, pong_sc]
    first, last = low, window - low
    for picard in range(ITERS):
        make_weights(now_sc, first, last - 1)
        for _ in range(SWEEPS):
            first, last = first + 1, last - 1
            later_sc = spare[0]
            sweep(now_sc, later_sc, first, last)
            spare = [spare[1], later_sc]
            now_sc = later_sc
    for part in range(per_row):
        lanes = pl.ds(part * LANES, LANES)
        top_rows = now_sc[part, pl.ds(PAD * layers, span, stride=layers), :]
        for step, head_ref in enumerate(head_refs):
            for held_layer in range(held):
                layer = (place_ref[4] ^ step) * held + held_layer
                head_ref[held_layer, :, lanes] = now_sc[part, pl.ds(PAD * layers + layer, span, stride=layers), :]
            head_ref[held, :, lanes] = top_rows


def inflow_kernel(
    groups, place_ref, cells_ref, bed_ref, slot_section_ref, row_ref, *refs,
):
    back_refs = refs[:groups]
    head_ref, out_ref, block_sc, lane_sc, found_sc, turned_sc = refs[groups:]
    _, span, breadth = back_refs[0].shape
    held, across, _ = head_ref.shape
    per_row = breadth // LANES
    blocks = across * per_row
    slots = cells_ref.shape[0]
    quarter = LANES // groups
    packed = slots // groups
    flip = place_ref[3]
    for step, back_ref in enumerate(back_refs):
        source = place_ref[4] ^ step
        number = jnp.where(flip == 1, groups - 1 - source, source)
        rows = pl.ds(pl.multiple_of(number * span, span), span)
        for layer in range(held):
            head_ref[layer, rows, :] = back_ref[layer]
        for part in range(per_row):
            spot = pl.ds(number * span * per_row + part, span, stride=per_row)
            turned_sc[spot, :] = back_ref[held, :, part * LANES:(part + 1) * LANES]

    own = lax.broadcasted_iota(jnp.int32, (packed, LANES), 1) // quarter

    def pack(ref):
        result = None
        for number in range(groups):
            shift = lax.rem((number + groups - place_ref[4]) * quarter, LANES)
            moved = pltpu.roll(ref[pl.ds(number * packed, packed), :], shift, 1)
            result = moved if result is None else jnp.where(own == number, moved, result)
        return result

    cells = pack(cells_ref)
    block, lane = split_cells(cells, 0, breadth, LANES)
    block_sc[...] = block
    lane_sc[...] = lane
    pieces = bf16_pieces(turned_sc[...].T, 2)
    group = 32
    one = jnp.ones((16, LANES), jnp.bfloat16)
    index = lax.broadcasted_iota(jnp.int32, (LANES, LANES), 0).astype(jnp.float32)

    def step(number, _):
        hots = jnp.concatenate(
            [one_hot(row_copies(block_sc, number * group + place), blocks, one) for place in range(group)], axis=1
        )
        found = jnp.zeros((LANES, group * LANES), jnp.float32)
        for piece in pieces:
            found = found + lax.dot_general(
                piece, hots, (((1,), (0,)), ((), ())), preferred_element_type=jnp.float32
            )
        for place in range(group):
            row = number * group + place
            lanes = jnp.broadcast_to(lane_sc[pl.ds(row, 1), :], (LANES, LANES))
            mine = jnp.where(index == lanes, found[:, place * LANES:(place + 1) * LANES], 0.0)
            found_sc[pl.ds(row, 1), :] = jnp.sum(mine, axis=0, keepdims=True)
        return 0

    lax.fori_loop(0, packed // group, step, 0)
    slot_in = jnp.where(cells >= 0, pack(bed_ref) * (found_sc[...] - pack(slot_section_ref)), 0.0)
    spread = jnp.concatenate(
        [slot_in if number == 0 else pltpu.roll(slot_in, LANES - number * quarter, 1) for number in range(groups)],
        axis=0,
    )
    rows = out_ref.shape[0]
    index = lax.broadcasted_iota(jnp.int32, (rows, slots), 0)
    put = jnp.where(index == row_ref[...], 1.0, 0.0).astype(jnp.bfloat16)
    total = jnp.zeros((rows, LANES), jnp.float32)
    for piece in bf16_pieces(spread, 3):
        total = total + lax.dot_general(
            put, piece, (((1,), (0,)), ((), ())), preferred_element_type=jnp.float32
        )
    out_ref[...] = total


def call(kernel, out_shape, in_specs, scratch, flops, moved):
    single = not isinstance(out_shape, (tuple, list))
    return pl.pallas_call(
        kernel,
        out_shape=out_shape,
        in_specs=in_specs,
        out_specs=in_vmem if single else tuple(in_vmem for _ in out_shape),
        scratch_shapes=scratch,
        compiler_params=pltpu.CompilerParams(vmem_limit_bytes=VMEM_LIMIT),
        cost_estimate=pl.CostEstimate(flops=flops, bytes_accessed=moved, transcendentals=0),
    )


def on_device(
    head_start,
    soil_class,
    land_mask,
    ks_table,
    alpha_table,
    store_table,
    section,
    cross_owner,
    cross_local,
    node_cell,
    bed_cond,
):
    held, across, breadth = head_start.shape
    reach_rows, node_count = section.shape
    tiles = lax.axis_size("tile")
    groups = lax.axis_size("layer")
    layers = held * groups
    span = across // groups
    window = span + 2 * PAD
    per_row = breadth // LANES
    blocks = (span + 2 * HALO) * per_row
    tile = lax.axis_index("tile")
    layer = lax.axis_index("layer")
    flip = lax.rem(tile, 2) == 1
    number = jnp.where(flip, groups - 1 - layer, layer)
    is_first = number == 0
    is_last = number == groups - 1
    place = jnp.stack([number * span, is_first, is_last, flip, layer]).astype(jnp.int32)
    swap = []
    for upper in range(tiles - 1):
        index = groups - 1 if upper % 2 == 0 else 0
        one, two = upper * groups + index, (upper + 1) * groups + index
        swap += [(one, two), (two, one)]

    cells = node_cell[0]
    bed = bed_cond[0]
    slots = cells.shape[0]
    reach = cross_owner * reach_rows + cross_local

    def exchange(parts):
        received = [parts[0]]
        for step in range(1, groups):
            received.append(lax.ppermute(parts[step], "layer", [(i, i ^ step) for i in range(groups)]))
        return received

    field_bytes = held * across * breadth * 4
    window_shape = jax.ShapeDtypeStruct((2, held, window, breadth), jnp.float32)
    *windows, spread, land = call(
        prepare_kernel,
        (window_shape,) * groups
        + (
            jax.ShapeDtypeStruct((tiles, reach_rows, node_count), jnp.float32),
            jax.ShapeDtypeStruct((window, breadth), jnp.float32),
        ),
        [in_smem] + [in_vmem] * 4, [], 0, 8 * field_bytes,
    )(place, head_start, soil_class, section, land_mask)
    whole_section = lax.all_to_all(spread, "tile", 0, 0).reshape(tiles * reach_rows, node_count)
    received = exchange(windows)

    node_scratch = pltpu.VMEM((slots, LANES), jnp.float32)
    riv_shape = jax.ShapeDtypeStruct((blocks, LANES), jnp.float32)
    node_bytes = slots * LANES * 4
    diag, rhs, slot_section = call(
        functools.partial(river_kernel, breadth),
        (riv_shape, riv_shape, jax.ShapeDtypeStruct((slots, node_count), jnp.float32)),
        [in_smem] + [in_vmem] * 4,
        [node_scratch] * 5
        + [pltpu.VMEM((slots // LANES, LANES, LANES), jnp.float32)]
        + [pltpu.VMEM((-(-2 * blocks // LANES) * LANES, LANES), jnp.float32)],
        2 * blocks * 4 * LANES * slots * LANES, 4 * node_bytes,
    )(place, cells, bed, whole_section, reach)

    send_row = jnp.where(is_first, PAD, PAD + span - HALO)
    edges = [lax.dynamic_slice_in_dim(block, send_row, HALO, 2) for block in received]
    edge = jnp.stack(edges, axis=1).reshape(2 * layers, HALO, breadth)
    edge = jnp.concatenate([edge, lax.dynamic_slice_in_dim(land, send_row, HALO, 0)[None]])
    side = HALO * per_row
    riv = jnp.stack([diag, rhs])
    riv_edge = jnp.where(is_first, riv[:, side:2 * side], riv[:, blocks - 2 * side:blocks - side])
    edge = jnp.concatenate([edge, riv_edge.reshape(2, HALO, breadth)])
    halo = lax.ppermute(edge, FLAT, swap)

    field = pltpu.VMEM((per_row, window * layers, LANES), jnp.float32)
    out_shape = jax.ShapeDtypeStruct((held + 1, span, breadth), jnp.float32)
    out = call(
        functools.partial(flow_kernel, groups), (out_shape,) * groups,
        [in_smem] * 4 + [in_vmem] * (4 + groups),
        [field] * 13
        + [pltpu.VMEM((window, breadth), jnp.float32)]
        + [pltpu.VMEM((blocks, LANES), jnp.float32)] * 2,
        100 * layers * window * breadth, 8 * layers * window * breadth,
    )(place, ks_table, alpha_table, store_table, land, halo, diag, rhs, *received)
    back = exchange(out)

    packed = pltpu.VMEM((slots // groups, LANES), jnp.float32)
    head, partial = call(
        functools.partial(inflow_kernel, groups),
        (
            jax.ShapeDtypeStruct(head_start.shape, jnp.float32),
            jax.ShapeDtypeStruct((tiles * reach_rows, node_count), jnp.float32),
        ),
        [in_smem] + [in_vmem] * (4 + groups),
        [packed] * 3 + [pltpu.VMEM((across * per_row, LANES), jnp.float32)],
        4 * across * breadth * slots * node_count // groups, 8 * node_bytes,
    )(place, cells, bed, slot_section, reach, *back)
    terms = lax.all_to_all(partial.reshape(tiles, reach_rows, node_count), "tile", 0, 0)
    return head, jnp.sum(terms, axis=0)[:, :node_count // groups]


def solution(mesh):
    placed = (
        P("layer", "tile", None),
        P("layer", "tile", None),
        P("tile", None),
        P(),
        P(),
        P(),
        P("tile", None),
        P("tile", None),
        P("tile", None),
        P("tile", None, None),
        P("tile", None, None),
    )
    return jax.shard_map(
        on_device,
        mesh=mesh,
        in_specs=placed,
        out_specs=(P("layer", "tile", None), P("tile", "layer")),
        check_vma=False,
    )
```

```python
import functools

import jax
import jax.numpy as jnp
from jax import lax
from jax.experimental import pallas as pl
from jax.experimental.pallas import tpu as pltpu
from jax.sharding import PartitionSpec as P

ITERS = 2
SWEEPS = 3

LATERAL = 1.0
VERTICAL = 2.0
GRAVITY = 1.0

HALO = ITERS * SWEEPS
BLOCK = 32
LANES = 128
VMEM_LIMIT = 48 * 1024 * 1024
FLAT = ("tile", "layer")

in_vmem = pl.BlockSpec(memory_space=pltpu.VMEM)
in_smem = pl.BlockSpec(memory_space=pltpu.SMEM)


def bf16_pieces(value, count):
    pieces = []
    for _ in range(count):
        piece = value.astype(jnp.bfloat16)
        pieces.append(piece)
        value = value - piece.astype(jnp.float32)
    return pieces


def reciprocal(value):
    guess = pl.reciprocal(value, approx=True)
    return guess * (2.0 - value * guess)


def one_hot(row, size, on):
    index = lax.broadcasted_iota(jnp.int32, (16, LANES), 0)
    zero = jnp.zeros((16, LANES), jnp.bfloat16)
    tiles = []
    for start in range(0, size, 16):
        here = (index + start).astype(jnp.float32).astype(jnp.bfloat16)
        tiles.append(jnp.where(row == here, on, zero))
    return jnp.concatenate(tiles, axis=0)


def row_copies(ref, slot):
    return jnp.broadcast_to(ref[pl.ds(slot, 1), :], (16, LANES)).astype(jnp.bfloat16)


def split_cells(cells, first_row, breadth, width):
    local = cells - first_row * breadth
    shift = width.bit_length() - 1
    block = jnp.where(cells < 0, -1, local >> shift)
    return block.astype(jnp.float32), (local & (width - 1)).astype(jnp.float32)


def river_kernel(
    breadth, place_ref, cells_ref, bed_ref, section_ref, row_ref, diag_ref, rhs_ref, slot_section_ref,
    spot_sc, dhigh_sc, dlow_sc, rhigh_sc, rlow_sc, turned_sc, sum_sc,
):
    rows = section_ref.shape[0]
    slots = row_ref.shape[1]
    index = lax.broadcasted_iota(jnp.int32, (rows, slots), 0)
    pick = jnp.where(index == row_ref[...], 1.0, 0.0).astype(jnp.bfloat16)
    picked = jnp.zeros(slot_section_ref.shape, jnp.float32)
    for piece in bf16_pieces(section_ref[...], 3):
        picked = picked + lax.dot_general(
            pick, piece, (((0,), (0,)), ((), ())), preferred_element_type=jnp.float32
        )
    slot_section_ref[...] = picked

    block, spot = split_cells(cells_ref[...], place_ref[0], breadth, BLOCK)
    spot_sc[...] = spot
    bed = bed_ref[...]
    for value, high_sc, low_sc in ((bed, dhigh_sc, dlow_sc), (bed * picked, rhigh_sc, rlow_sc)):
        high, low = bf16_pieces(value, 2)
        high_sc[...] = high.astype(jnp.float32)
        low_sc[...] = low.astype(jnp.float32)
    share = LANES // BLOCK
    blocks = share * diag_ref.shape[0]
    group = 32
    tiles = slots // LANES
    for part in range(tiles):
        turned_sc[part] = block[part * LANES:(part + 1) * LANES, :].T
    names = lax.broadcasted_iota(jnp.int32, (LANES, LANES), 1)
    names = [(names + start).astype(jnp.float32).astype(jnp.bfloat16) for start in range(0, blocks, LANES)]
    one = jnp.ones((LANES, LANES), jnp.bfloat16)
    zero = jnp.zeros((LANES, LANES), jnp.bfloat16)

    def step(number, total):
        first = number * group
        columns = turned_sc[first // LANES]
        columns = pltpu.roll(columns, lax.rem(LANES - lax.rem(first, LANES), LANES), 1)
        left, right = [], []
        for place in range(group):
            slot = first + place
            spots = row_copies(spot_sc, slot)
            left.append(
                jnp.concatenate(
                    [one_hot(spots, BLOCK, row_copies(ref, slot)) for ref in (dhigh_sc, dlow_sc, rhigh_sc, rlow_sc)],
                    axis=0,
                )
            )
            column = jnp.broadcast_to(columns[:, place:place + 1], (LANES, LANES)).astype(jnp.bfloat16)
            right.append(jnp.concatenate([jnp.where(column == name, one, zero) for name in names], axis=1))
        return total + lax.dot_general(
            jnp.concatenate(left, axis=1),
            jnp.concatenate(right, axis=0),
            (((1,), (0,)), ((), ())),
            preferred_element_type=jnp.float32,
        )

    total = lax.fori_loop(0, slots // group, step, jnp.zeros((4 * BLOCK, blocks), jnp.float32))
    lane = lax.broadcasted_iota(jnp.int32, diag_ref.shape, 1) // BLOCK
    for number, ref in ((0, diag_ref), (2, rhs_ref)):
        first = number * BLOCK
        both = total[first:first + BLOCK] + total[first + BLOCK:first + 2 * BLOCK]
        both = jnp.concatenate([both] * share, axis=0)
        for part in range(blocks // LANES):
            sum_sc[pl.ds(part * LANES, LANES), :] = both[:, part * LANES:(part + 1) * LANES].T
        result = sum_sc[pl.ds(0, blocks // share, stride=share), :]
        for part in range(1, share):
            result = jnp.where(lane == part, sum_sc[pl.ds(part, blocks // share, stride=share), :], result)
        ref[...] = result


def prepare_kernel(groups, place_ref, head_hbm, soil_hbm, section_hbm, land_hbm, *refs):
    block_refs, spread_ref, land_out_ref = refs[:groups], refs[groups], refs[groups + 1]
    head_ref, soil_ref, section_ref, land_ref, sems = refs[groups + 2:]
    held, across, _ = head_ref.shape
    span = across // groups
    pairs = [(section_hbm, section_ref), (land_hbm, land_ref)]
    for layer in range(held):
        pairs += [(head_hbm.at[layer], head_ref.at[layer]), (soil_hbm.at[layer], soil_ref.at[layer])]
    copies = [pltpu.make_async_copy(here, there, sems.at[k]) for k, (here, there) in enumerate(pairs)]
    for copy in copies:
        copy.start()

    def rows_of(target):
        number = jnp.where(place_ref[1] == 1, groups - 1 - target, target)
        return pl.ds(pl.multiple_of(number * span, span), span)

    copies[0].wait()
    section = section_ref[...]
    for tile in range(spread_ref.shape[0]):
        spread_ref[tile] = section
    copies[1].wait()
    land_out_ref[...] = land_ref[rows_of(place_ref[2]), :].astype(jnp.float32)
    for layer in range(held):
        copies[2 + 2 * layer].wait()
        copies[3 + 2 * layer].wait()
        for step, out_ref in enumerate(block_refs):
            rows = rows_of(place_ref[2] ^ step)
            out_ref[0, layer] = head_ref[layer, rows, :]
            out_ref[1, layer] = soil_ref[layer, rows, :].astype(jnp.float32)


def flow_kernel(
    groups, place_ref, ks_ref, alpha_ref, store_ref, land_ref, near_ref, far_ref, diag_ref, rhs_ref, *refs,
):
    block_refs, head_refs = refs[:groups], refs[groups:2 * groups]
    (
        soil_sc, first_sc, ks_sc, alpha_sc, diag_sc, rhs_sc, wx_sc, wy_sc, wz_sc, base_sc, inv_sc,
        ping_sc, pong_sc, land_sc, dtop_sc, rtop_sc,
    ) = refs[2 * groups:]
    _, held, span, breadth = block_refs[0].shape
    layers = groups * held
    window = span + 2 * HALO
    per_row = breadth // LANES
    side = HALO * per_row

    def put_rows(ref, layer, row, value):
        for part in range(per_row):
            spot = pl.ds(row * layers + layer, value.shape[0], stride=layers)
            ref[part, spot, :] = value[:, part * LANES:(part + 1) * LANES]

    for step, block_ref in enumerate(block_refs):
        for held_layer in range(held):
            layer = (place_ref[2] ^ step) * held + held_layer
            put_rows(first_sc, layer, HALO, block_ref[0, held_layer])
            put_rows(soil_sc, layer, HALO, block_ref[1, held_layer])
    land_sc[pl.ds(HALO, span), :] = land_ref[...]
    dtop_sc[pl.ds(side, span * per_row), :] = diag_ref[...]
    rtop_sc[pl.ds(side, span * per_row), :] = rhs_ref[...]

    def put_halo(ref, partner, row):
        def entry(number):
            return ref[pl.ds(number * HALO, HALO), :]

        for number in range(layers):
            layer = (partner ^ (number // held)) * held + number % held
            put_rows(first_sc, layer, row, entry(number))
            put_rows(soil_sc, layer, row, entry(layers + number))
        land_sc[pl.ds(row, HALO), :] = entry(2 * layers)
        for number, top_sc in ((2 * layers + 1, dtop_sc), (2 * layers + 2, rtop_sc)):
            value = entry(number)
            for part in range(per_row):
                spot = pl.ds(row * per_row + part, HALO, stride=per_row)
                top_sc[spot, :] = value[:, part * LANES:(part + 1) * LANES]

    for odd, above_ref, below_ref in ((0, far_ref, near_ref), (1, near_ref, far_ref)):
        @pl.when(place_ref[3] == odd)
        def _(above_ref=above_ref, below_ref=below_ref):
            for ref, row in ((above_ref, 0), (below_ref, HALO + span)):
                put_halo(ref, place_ref[4] if ref is near_ref else place_ref[5], row)

    def get(ref, row):
        spot = pl.ds(row * layers, layers)
        return jnp.concatenate([ref[part, spot, :] for part in range(per_row)], axis=1)

    def put(ref, row, value):
        spot = pl.ds(row * layers, layers)
        for part in range(per_row):
            ref[part, spot, :] = value[:, part * LANES:(part + 1) * LANES]

    level = lax.broadcasted_iota(jnp.int32, (layers, breadth), 0)
    column = lax.broadcasted_iota(jnp.int32, (layers, breadth), 1)
    top = level == 0
    not_bottom = level < layers - 1
    not_last = column < breadth - 1

    def riv_row(ref, row):
        first = row * per_row
        parts = [
            jnp.broadcast_to(ref[pl.ds(first + part, 1), :], (layers, LANES)) for part in range(per_row)
        ]
        return jnp.where(top, jnp.concatenate(parts, axis=1), 0.0)

    lane = lax.broadcasted_iota(jnp.int32, (layers, LANES), 1)

    def lane_table(ref):
        table = jnp.zeros((layers, LANES), jnp.float32)
        for kind in range(ref.shape[0]):
            table = jnp.where(lane == kind, ref[kind], table)
        return table

    tables = [lane_table(ref) for ref in (ks_ref, alpha_ref, store_ref)]

    def lookup(soil):
        found = []
        for table in tables:
            parts = [
                jnp.take_along_axis(
                    table, soil[:, part * LANES:(part + 1) * LANES], axis=1, mode="promise_in_bounds"
                )
                for part in range(per_row)
            ]
            found.append(jnp.concatenate(parts, axis=1))
        return found

    for row in range(window):
        ks, alpha, store = lookup(get(soil_sc, row).astype(jnp.int32))
        put(ks_sc, row, ks)
        put(alpha_sc, row, alpha)
        put(diag_sc, row, store + riv_row(dtop_sc, row))
        put(rhs_sc, row, store * get(first_sc, row) + riv_row(rtop_sc, row))

    def east(field):
        return pltpu.roll(field, breadth - 1, 1)

    def west(field):
        return pltpu.roll(field, 1, 1)

    def below(field):
        return pltpu.roll(field, layers - 1, 0)

    def above(field):
        return pltpu.roll(field, 1, 0)

    def make_weights(now_sc, first, last):
        def conduct(row):
            cond = get(ks_sc, row) * jnp.exp(get(alpha_sc, row) * jnp.minimum(get(now_sc, row), 0.0))
            return cond, cond * land_sc[pl.ds(row, 1), :]

        def face(factor, cond, opened, far, far_open):
            return factor * 2.0 * opened * far_open * reciprocal(cond + far)

        def step(row, carried):
            cond, opened, wx_before = carried
            far, far_open = conduct(row + 1)
            wx = face(LATERAL, cond, opened, far, far_open)
            wy = jnp.where(not_last, face(LATERAL, cond, opened, east(cond), east(opened)), 0.0)
            wz = jnp.where(not_bottom, face(VERTICAL, cond, opened, below(cond), below(opened)), 0.0)
            wz_above = above(wz)
            total = get(diag_sc, row) + wx_before + wx + wy + west(wy) + wz + wz_above
            inverse = reciprocal(total)
            put(wx_sc, row, wx)
            put(wy_sc, row, wy)
            put(wz_sc, row, wz)
            put(inv_sc, row, inverse)
            put(base_sc, row, get(rhs_sc, row) + GRAVITY * (wz_above - wz))
            return far, far_open, wx

        cond, opened = conduct(first)
        far, far_open = conduct(first + 1)
        wx = face(LATERAL, cond, opened, far, far_open)
        put(wx_sc, first, wx)
        carried = far, far_open, wx
        for row in range(first + 1, last):
            carried = step(row, carried)

    def sweep(now_sc, later_sc, first, last):
        def step(row, carried):
            before, here, wx_before = carried
            after = get(now_sc, row + 1)
            wx = get(wx_sc, row)
            wy = get(wy_sc, row)
            wz = get(wz_sc, row)
            total = get(base_sc, row) + wx_before * before + wx * after
            total = total + wy * east(here) + west(wy * here)
            total = total + wz * below(here) + above(wz * here)
            put(later_sc, row, total * get(inv_sc, row))
            return here, after, wx

        carried = get(now_sc, first - 1), get(now_sc, first), get(wx_sc, first - 1)
        for row in range(first, last):
            carried = step(row, carried)

    now_sc, spare = first_sc, [ping_sc, pong_sc]
    first, last = 0, window
    for picard in range(ITERS):
        make_weights(now_sc, first, last - 1)
        for _ in range(SWEEPS):
            first, last = first + 1, last - 1
            later_sc = spare[0]
            sweep(now_sc, later_sc, first, last)
            spare = [spare[1], later_sc]
            now_sc = later_sc
    for part in range(per_row):
        lanes = pl.ds(part * LANES, LANES)
        top_rows = now_sc[part, pl.ds(HALO * layers, span, stride=layers), :]
        for step, head_ref in enumerate(head_refs):
            for held_layer in range(held):
                layer = (place_ref[2] ^ step) * held + held_layer
                head_ref[held_layer, :, lanes] = now_sc[part, pl.ds(HALO * layers + layer, span, stride=layers), :]
            head_ref[held, :, lanes] = top_rows


def inflow_kernel(
    groups, place_ref, cells_ref, bed_ref, slot_section_ref, row_ref, *refs,
):
    back_refs = refs[:groups]
    head_ref, out_ref, block_sc, lane_sc, found_sc, turned_sc = refs[groups:]
    _, span, breadth = back_refs[0].shape
    held, across, _ = head_ref.shape
    per_row = breadth // LANES
    blocks = across * per_row
    slots = cells_ref.shape[0]
    quarter = LANES // groups
    packed = slots // groups
    flip = place_ref[1]
    for step, back_ref in enumerate(back_refs):
        source = place_ref[2] ^ step
        number = jnp.where(flip == 1, groups - 1 - source, source)
        rows = pl.ds(pl.multiple_of(number * span, span), span)
        for layer in range(held):
            head_ref[layer, rows, :] = back_ref[layer]
        for part in range(per_row):
            spot = pl.ds(number * span * per_row + part, span, stride=per_row)
            turned_sc[spot, :] = back_ref[held, :, part * LANES:(part + 1) * LANES]

    own = lax.broadcasted_iota(jnp.int32, (packed, LANES), 1) // quarter

    def pack(ref):
        result = None
        for number in range(groups):
            shift = lax.rem((number + groups - place_ref[2]) * quarter, LANES)
            moved = pltpu.roll(ref[pl.ds(number * packed, packed), :], shift, 1)
            result = moved if result is None else jnp.where(own == number, moved, result)
        return result

    cells = pack(cells_ref)
    block, lane = split_cells(cells, 0, breadth, LANES)
    block_sc[...] = block
    lane_sc[...] = lane
    pieces = bf16_pieces(turned_sc[...].T, 2)
    group = 32
    one = jnp.ones((16, LANES), jnp.bfloat16)
    index = lax.broadcasted_iota(jnp.int32, (LANES, LANES), 0).astype(jnp.float32)

    def step(number, _):
        hots = jnp.concatenate(
            [one_hot(row_copies(block_sc, number * group + place), blocks, one) for place in range(group)], axis=1
        )
        found = jnp.zeros((LANES, group * LANES), jnp.float32)
        for piece in pieces:
            found = found + lax.dot_general(
                piece, hots, (((1,), (0,)), ((), ())), preferred_element_type=jnp.float32
            )
        for place in range(group):
            row = number * group + place
            lanes = jnp.broadcast_to(lane_sc[pl.ds(row, 1), :], (LANES, LANES))
            mine = jnp.where(index == lanes, found[:, place * LANES:(place + 1) * LANES], 0.0)
            found_sc[pl.ds(row, 1), :] = jnp.sum(mine, axis=0, keepdims=True)
        return 0

    lax.fori_loop(0, packed // group, step, 0)
    slot_in = jnp.where(cells >= 0, pack(bed_ref) * (found_sc[...] - pack(slot_section_ref)), 0.0)
    spread = jnp.concatenate(
        [slot_in if number == 0 else pltpu.roll(slot_in, LANES - number * quarter, 1) for number in range(groups)],
        axis=0,
    )
    rows = out_ref.shape[0]
    index = lax.broadcasted_iota(jnp.int32, (rows, slots), 0)
    put = jnp.where(index == row_ref[...], 1.0, 0.0).astype(jnp.bfloat16)
    total = jnp.zeros((rows, LANES), jnp.float32)
    for piece in bf16_pieces(spread, 3):
        total = total + lax.dot_general(
            put, piece, (((1,), (0,)), ((), ())), preferred_element_type=jnp.float32
        )
    out_ref[...] = total


def call(kernel, out_shape, in_specs, scratch, flops, moved):
    single = not isinstance(out_shape, (tuple, list))
    return pl.pallas_call(
        kernel,
        out_shape=out_shape,
        in_specs=in_specs,
        out_specs=in_vmem if single else tuple(in_vmem for _ in out_shape),
        scratch_shapes=scratch,
        compiler_params=pltpu.CompilerParams(vmem_limit_bytes=VMEM_LIMIT),
        cost_estimate=pl.CostEstimate(flops=flops, bytes_accessed=moved, transcendentals=0),
    )


def on_device(
    head_start,
    soil_class,
    land_mask,
    ks_table,
    alpha_table,
    store_table,
    section,
    cross_owner,
    cross_local,
    node_cell,
    bed_cond,
):
    held, across, breadth = head_start.shape
    reach_rows, node_count = section.shape
    tiles = lax.axis_size("tile")
    groups = lax.axis_size("layer")
    layers = held * groups
    span = across // groups
    per_row = breadth // LANES
    blocks = span * per_row
    tile = lax.axis_index("tile")
    layer = lax.axis_index("layer")
    flip = lax.rem(tile, 2)
    number = jnp.where(flip == 1, groups - 1 - layer, layer)
    odd = lax.rem(number, 2)
    end = (number == 0) | (number == groups - 1)
    far_partner = jnp.where(end, layer, layer ^ (groups - 1))
    place = jnp.stack([number * span, flip, layer, odd, layer ^ 1, far_partner]).astype(jnp.int32)
    near = [(i, i ^ 1) for i in range(groups)]
    far = []
    for upper in range(tiles):
        far += [(upper * groups + i, upper * groups + (i ^ (groups - 1))) for i in range(1, groups - 1)]
        if upper + 1 < tiles:
            index = groups - 1 if upper % 2 == 0 else 0
            one, two = upper * groups + index, (upper + 1) * groups + index
            far += [(one, two), (two, one)]

    cells = node_cell[0]
    bed = bed_cond[0]
    slots = cells.shape[0]
    reach = cross_owner * reach_rows + cross_local

    def exchange(parts):
        received = [parts[0]]
        for step in range(1, groups):
            received.append(lax.ppermute(parts[step], "layer", [(i, i ^ step) for i in range(groups)]))
        return received

    field_bytes = held * across * breadth * 4
    *own_blocks, spread, land = call(
        functools.partial(prepare_kernel, groups),
        (jax.ShapeDtypeStruct((2, held, span, breadth), jnp.float32),) * groups
        + (
            jax.ShapeDtypeStruct((tiles, reach_rows, node_count), jnp.float32),
            jax.ShapeDtypeStruct((span, breadth), jnp.float32),
        ),
        [in_smem] + [pl.BlockSpec(memory_space=pl.ANY)] * 4,
        [
            pltpu.VMEM(head_start.shape, jnp.float32),
            pltpu.VMEM(soil_class.shape, jnp.int32),
            pltpu.VMEM(section.shape, jnp.float32),
            pltpu.VMEM(land_mask.shape, jnp.int32),
            pltpu.SemaphoreType.DMA((2 + 2 * held,)),
        ],
        0, 4 * field_bytes,
    )(place, head_start, soil_class, section, land_mask)
    whole_section = lax.all_to_all(spread, "tile", 0, 0).reshape(tiles * reach_rows, node_count)
    received = exchange(own_blocks)

    node_scratch = pltpu.VMEM((slots, LANES), jnp.float32)
    riv_shape = jax.ShapeDtypeStruct((blocks, LANES), jnp.float32)
    node_bytes = slots * LANES * 4
    diag, rhs, slot_section = call(
        functools.partial(river_kernel, breadth),
        (riv_shape, riv_shape, jax.ShapeDtypeStruct((slots, node_count), jnp.float32)),
        [in_smem] + [in_vmem] * 4,
        [node_scratch] * 5
        + [pltpu.VMEM((slots // LANES, LANES, LANES), jnp.float32)]
        + [pltpu.VMEM((span * breadth // BLOCK, LANES), jnp.float32)],
        8 * span * breadth * slots * LANES, 4 * node_bytes,
    )(place, cells, bed, whole_section, reach)

    def edge(bottom):
        row = jnp.where(bottom, span - HALO, 0)
        grid = [lax.dynamic_slice_in_dim(block, row, HALO, 2) for block in received]
        river = [jnp.where(bottom, term[blocks - side:], term[:side]) for term in (diag, rhs)]
        return jnp.concatenate(
            [
                jnp.stack(grid, axis=1).reshape(2 * layers * HALO, breadth),
                lax.dynamic_slice_in_dim(land, row, HALO, 0),
                jnp.concatenate(river).reshape(2 * HALO, breadth),
            ]
        )

    side = HALO * per_row
    near_halo = lax.ppermute(edge(odd == 0), "layer", near)
    far_halo = lax.ppermute(edge(odd == 1), FLAT, far)

    window = span + 2 * HALO
    field = pltpu.VMEM((per_row, window * layers, LANES), jnp.float32)
    out_shape = jax.ShapeDtypeStruct((held + 1, span, breadth), jnp.float32)
    out = call(
        functools.partial(flow_kernel, groups), (out_shape,) * groups,
        [in_smem] * 4 + [in_vmem] * (5 + groups),
        [field] * 13
        + [pltpu.VMEM((window, breadth), jnp.float32)]
        + [pltpu.VMEM((window * per_row, LANES), jnp.float32)] * 2,
        100 * layers * window * breadth, 8 * layers * window * breadth,
    )(place, ks_table, alpha_table, store_table, land, near_halo, far_halo, diag, rhs, *received)
    back = exchange(out)

    packed = pltpu.VMEM((slots // groups, LANES), jnp.float32)
    head, partial = call(
        functools.partial(inflow_kernel, groups),
        (
            jax.ShapeDtypeStruct(head_start.shape, jnp.float32),
            jax.ShapeDtypeStruct((tiles * reach_rows, node_count), jnp.float32),
        ),
        [in_smem] + [in_vmem] * (4 + groups),
        [packed] * 3 + [pltpu.VMEM((across * per_row, LANES), jnp.float32)],
        4 * across * breadth * slots * node_count // groups, 8 * node_bytes,
    )(place, cells, bed, slot_section, reach, *back)
    terms = lax.all_to_all(partial.reshape(tiles, reach_rows, node_count), "tile", 0, 0)
    return head, jnp.sum(terms, axis=0)[:, :node_count // groups]


def solution(mesh):
    placed = (
        P("layer", "tile", None),
        P("layer", "tile", None),
        P("tile", None),
        P(),
        P(),
        P(),
        P("tile", None),
        P("tile", None),
        P("tile", None),
        P("tile", None, None),
        P("tile", None, None),
    )
    return jax.shard_map(
        on_device,
        mesh=mesh,
        in_specs=placed,
        out_specs=(P("layer", "tile", None), P("tile", "layer")),
        check_vma=False,
    )
```

```python
import functools

import jax
import jax.numpy as jnp
from jax import lax
from jax.experimental import pallas as pl
from jax.experimental.pallas import tpu as pltpu
from jax.sharding import PartitionSpec as P

ITERS = 2
SWEEPS = 3

LATERAL = 1.0
VERTICAL = 2.0
GRAVITY = 1.0

HALO = ITERS * SWEEPS
BLOCK = 32
LANES = 128
VMEM_LIMIT = 48 * 1024 * 1024
FLAT = ("tile", "layer")

in_vmem = pl.BlockSpec(memory_space=pltpu.VMEM)
in_hbm = pl.BlockSpec(memory_space=pltpu.HBM)
in_smem = pl.BlockSpec(memory_space=pltpu.SMEM)


def bf16_pieces(value, count):
    pieces = []
    for _ in range(count):
        piece = value.astype(jnp.bfloat16)
        pieces.append(piece)
        value = value - piece.astype(jnp.float32)
    return pieces


def reciprocal(value):
    guess = pl.reciprocal(value, approx=True)
    return guess * (2.0 - value * guess)


def one_hot(row, size, on):
    index = lax.broadcasted_iota(jnp.int32, (16, LANES), 0)
    zero = jnp.zeros((16, LANES), jnp.bfloat16)
    tiles = []
    for start in range(0, size, 16):
        here = (index + start).astype(jnp.float32).astype(jnp.bfloat16)
        tiles.append(jnp.where(row == here, on, zero))
    return jnp.concatenate(tiles, axis=0)


def row_copies(ref, slot):
    return jnp.broadcast_to(ref[pl.ds(slot, 1), :], (16, LANES)).astype(jnp.bfloat16)


def split_cells(cells, first_row, breadth, width):
    local = cells - first_row * breadth
    shift = width.bit_length() - 1
    block = jnp.where(cells < 0, -1, local >> shift)
    return block.astype(jnp.float32), (local & (width - 1)).astype(jnp.float32)


def river_kernel(
    breadth, place_ref, cells_ref, bed_ref, section_ref, row_ref, diag_ref, rhs_ref, slot_section_ref,
    block_sc, spot_sc, dhigh_sc, dlow_sc, rhigh_sc, rlow_sc, sum_sc,
):
    rows = section_ref.shape[0]
    slots = row_ref.shape[1]
    index = lax.broadcasted_iota(jnp.int32, (rows, slots), 0)
    pick = jnp.where(index == row_ref[...], 1.0, 0.0).astype(jnp.bfloat16)
    picked = jnp.zeros(slot_section_ref.shape, jnp.float32)
    for piece in bf16_pieces(section_ref[...], 3):
        picked = picked + lax.dot_general(
            pick, piece, (((0,), (0,)), ((), ())), preferred_element_type=jnp.float32
        )
    slot_section_ref[...] = picked

    block, spot = split_cells(cells_ref[...], place_ref[0], breadth, BLOCK)
    block_sc[...] = block
    spot_sc[...] = spot
    bed = bed_ref[...]
    for value, high_sc, low_sc in ((bed, dhigh_sc, dlow_sc), (bed * picked, rhigh_sc, rlow_sc)):
        high, low = bf16_pieces(value, 2)
        high_sc[...] = high.astype(jnp.float32)
        low_sc[...] = low.astype(jnp.float32)
    share = LANES // BLOCK
    blocks = share * diag_ref.shape[0]
    group = 32
    one = jnp.ones((16, LANES), jnp.bfloat16)

    def step(number, total):
        left, right = [], []
        for place in range(group):
            slot = number * group + place
            spots = row_copies(spot_sc, slot)
            left.append(one_hot(row_copies(block_sc, slot), blocks, one))
            right.append(
                jnp.concatenate(
                    [one_hot(spots, BLOCK, row_copies(ref, slot)) for ref in (dhigh_sc, dlow_sc, rhigh_sc, rlow_sc)],
                    axis=0,
                )
            )
        return total + lax.dot_general(
            jnp.concatenate(left, axis=1),
            jnp.concatenate(right, axis=1),
            (((1,), (1,)), ((), ())),
            preferred_element_type=jnp.float32,
        )

    total = lax.fori_loop(0, slots // group, step, jnp.zeros((blocks, 4 * BLOCK), jnp.float32))
    sum_sc[...] = total + pltpu.roll(total, LANES - BLOCK, 1)
    lane = lax.broadcasted_iota(jnp.int32, diag_ref.shape, 1) // BLOCK
    parts = [sum_sc[pl.ds(part, blocks // share, stride=share), :] for part in range(share)]
    for ref, first in ((diag_ref, 0), (rhs_ref, 2)):
        result = None
        for part in range(share):
            shift = (part - first) * BLOCK % LANES
            moved = pltpu.roll(parts[part], shift, 1) if shift else parts[part]
            result = moved if result is None else jnp.where(lane == part, moved, result)
        ref[...] = result


def prepare_kernel(groups, place_ref, head_hbm, soil_hbm, section_hbm, land_hbm, *refs):
    block_refs, spread_ref, land_out_ref = refs[:groups], refs[groups], refs[groups + 1]
    head_ref, soil_ref, section_ref, land_ref, sems = refs[groups + 2:]
    held, across, _ = head_ref.shape
    span = across // groups
    pairs = [(section_hbm, section_ref), (land_hbm, land_ref)]
    for layer in range(held):
        pairs += [(head_hbm.at[layer], head_ref.at[layer]), (soil_hbm.at[layer], soil_ref.at[layer])]
    copies = [pltpu.make_async_copy(here, there, sems.at[k]) for k, (here, there) in enumerate(pairs)]
    for copy in copies:
        copy.start()

    def rows_of(target):
        number = jnp.where(place_ref[1] == 1, groups - 1 - target, target)
        return pl.ds(pl.multiple_of(number * span, span), span)

    copies[0].wait()
    section = section_ref[...]
    for tile in range(spread_ref.shape[0]):
        spread_ref[tile] = section
    copies[1].wait()
    land_out_ref[...] = land_ref[rows_of(place_ref[2]), :].astype(jnp.float32)
    for layer in range(held):
        copies[2 + 2 * layer].wait()
        copies[3 + 2 * layer].wait()
        for step, out_ref in enumerate(block_refs):
            rows = rows_of(place_ref[2] ^ step)
            out_ref[0, layer] = head_ref[layer, rows, :]
            out_ref[1, layer] = soil_ref[layer, rows, :].astype(jnp.float32)


class Rows:
    def __init__(self, layers, breadth):
        self.layers, self.breadth, self.per_row = layers, breadth, breadth // LANES

    def get(self, ref, row):
        spot = pl.ds(row * self.layers, self.layers)
        return jnp.concatenate([ref[part, spot, :] for part in range(self.per_row)], axis=1)

    def put(self, ref, row, value):
        spot = pl.ds(row * self.layers, self.layers)
        for part in range(self.per_row):
            ref[part, spot, :] = value[:, part * LANES:(part + 1) * LANES]

    def put_layer(self, ref, layer, row, value):
        for part in range(self.per_row):
            spot = pl.ds(row * self.layers + layer, value.shape[0], stride=self.layers)
            ref[part, spot, :] = value[:, part * LANES:(part + 1) * LANES]

    def east(self, field):
        return pltpu.roll(field, self.breadth - 1, 1)

    def west(self, field):
        return pltpu.roll(field, 1, 1)

    def below(self, field):
        return pltpu.roll(field, self.layers - 1, 0)

    def above(self, field):
        return pltpu.roll(field, 1, 0)


def face_weights(rows, refs, first, last, diag_of, base_of, finish):
    now_ref, ks_ref, alpha_ref, land_ref, wx_ref, wy_ref, wz_ref = refs
    level = lax.broadcasted_iota(jnp.int32, (rows.layers, rows.breadth), 0)
    column = lax.broadcasted_iota(jnp.int32, (rows.layers, rows.breadth), 1)
    not_bottom = level < rows.layers - 1
    not_last = column < rows.breadth - 1

    def conduct(row):
        cond = rows.get(ks_ref, row) * jnp.exp(rows.get(alpha_ref, row) * jnp.minimum(rows.get(now_ref, row), 0.0))
        return cond, cond * land_ref[pl.ds(row, 1), :]

    def face(factor, cond, opened, far, far_open):
        return factor * 2.0 * opened * far_open * reciprocal(cond + far)

    cond, opened = conduct(first)
    far, far_open = conduct(first + 1)
    wx = face(LATERAL, cond, opened, far, far_open)
    rows.put(wx_ref, first, wx)
    for row in range(first + 1, last):
        cond, opened, wx_before = far, far_open, wx
        far, far_open = conduct(row + 1)
        wx = face(LATERAL, cond, opened, far, far_open)
        wy = face(LATERAL, cond, opened, rows.east(cond), rows.east(opened))
        wz = face(VERTICAL, cond, opened, rows.below(cond), rows.below(opened))
        wy = jnp.where(not_last, wy, 0.0)
        wz = jnp.where(not_bottom, wz, 0.0)
        wz_above = rows.above(wz)
        rows.put(wx_ref, row, wx)
        rows.put(wy_ref, row, wy)
        rows.put(wz_ref, row, wz)
        diagonal = diag_of(row) + wx_before + wx + wy + rows.west(wy) + wz + wz_above
        finish(row, diagonal, base_of(row) + GRAVITY * (wz_above - wz))


def stage_kernel(groups, place_ref, ks_ref, alpha_ref, store_ref, land_ref, near_ref, far_ref, after_ref, *refs):
    block_refs = refs[:groups]
    (
        first_out, ks_out, alpha_out, store_out, land_out, wx_out, wy_out, wz_out, diag_out, base_out, soil_sc,
    ) = refs[groups:]
    _, held, span, breadth = block_refs[0].shape
    layers = groups * held
    window = span + 2 * HALO
    rows = Rows(layers, breadth)

    for step, block_ref in enumerate(block_refs):
        for held_layer in range(held):
            layer = (place_ref[2] ^ step) * held + held_layer
            rows.put_layer(first_out, layer, HALO, block_ref[0, held_layer])
            rows.put_layer(soil_sc, layer, HALO, block_ref[1, held_layer])
    land_out[pl.ds(HALO, span), :] = land_ref[...]

    def put_halo(ref, partner, row):
        def entry(number):
            return ref[pl.ds(number * HALO, HALO), :]

        for number in range(layers):
            layer = (partner ^ (number // held)) * held + number % held
            rows.put_layer(first_out, layer, row, entry(number))
            rows.put_layer(soil_sc, layer, row, entry(layers + number))
        land_out[pl.ds(row, HALO), :] = entry(2 * layers)

    for odd, above_ref, below_ref in ((0, far_ref, near_ref), (1, near_ref, far_ref)):
        @pl.when(place_ref[3] == odd)
        def _(above_ref=above_ref, below_ref=below_ref):
            for ref, row in ((above_ref, 0), (below_ref, HALO + span)):
                put_halo(ref, place_ref[4] if ref is near_ref else place_ref[5], row)

    lane = lax.broadcasted_iota(jnp.int32, (layers, LANES), 1)

    def lane_table(ref):
        table = jnp.zeros((layers, LANES), jnp.float32)
        for kind in range(ref.shape[0]):
            table = jnp.where(lane == kind, ref[kind], table)
        return table

    tables = [lane_table(ref) for ref in (ks_ref, alpha_ref, store_ref)]
    for row in range(window):
        soil = rows.get(soil_sc, row).astype(jnp.int32)
        for table, out in zip(tables, (ks_out, alpha_out, store_out)):
            parts = [
                jnp.take_along_axis(
                    table, soil[:, part * LANES:(part + 1) * LANES], axis=1, mode="promise_in_bounds"
                )
                for part in range(rows.per_row)
            ]
            rows.put(out, row, jnp.concatenate(parts, axis=1))

    def finish(row, diagonal, base):
        rows.put(diag_out, row, diagonal)
        rows.put(base_out, row, base)

    face_weights(
        rows, (first_out, ks_out, alpha_out, land_out, wx_out, wy_out, wz_out), 0, window - 1,
        lambda row: rows.get(store_out, row),
        lambda row: rows.get(store_out, row) * rows.get(first_out, row),
        finish,
    )


def flow_kernel(groups, place_ref, near_ref, far_ref, diag_ref, rhs_ref, *refs):
    first_ref, ks_ref, alpha_ref, store_ref, land_ref, wx_ref, wy_ref, wz_ref, partial_ref, gravity_ref = refs[:10]
    head_refs = refs[10:10 + groups]
    wx_sc, wy_sc, wz_sc, base_sc, inv_sc, ping_sc, pong_sc, dtop_sc, rtop_sc = refs[10 + groups:]
    held, span, breadth = head_refs[0].shape
    held -= 1
    layers = groups * held
    window = span + 2 * HALO
    rows = Rows(layers, breadth)
    side = HALO * rows.per_row
    inner = span * rows.per_row

    is_odd = place_ref[3] == 1
    for number, (own_ref, top_sc) in enumerate(((diag_ref, dtop_sc), (rhs_ref, rtop_sc))):
        spot = pl.ds(number * side, side)
        near, far = near_ref[spot, :], far_ref[spot, :]
        top_sc[pl.ds(0, side), :] = jnp.where(is_odd, near, far)
        top_sc[pl.ds(side, inner), :] = own_ref[...]
        top_sc[pl.ds(side + inner, side), :] = jnp.where(is_odd, far, near)

    top = lax.broadcasted_iota(jnp.int32, (layers, breadth), 0) == 0

    def riv_row(ref, row):
        parts = [
            jnp.broadcast_to(ref[pl.ds(row * rows.per_row + part, 1), :], (layers, LANES))
            for part in range(rows.per_row)
        ]
        return jnp.where(top, jnp.concatenate(parts, axis=1), 0.0)

    def finish(row, diagonal, base):
        rows.put(inv_sc, row, reciprocal(diagonal + riv_row(dtop_sc, row)))
        rows.put(base_sc, row, base + riv_row(rtop_sc, row))

    def sweep(now_ref, later_ref, weights, first, last):
        before, here = rows.get(now_ref, first - 1), rows.get(now_ref, first)
        wx_before = rows.get(weights[0], first - 1)
        for row in range(first, last):
            after = rows.get(now_ref, row + 1)
            wx, wy, wz = [rows.get(ref, row) for ref in weights]
            total = rows.get(base_sc, row) + wx_before * before + wx * after
            total = total + wy * rows.east(here) + rows.west(wy * here)
            total = total + wz * rows.below(here) + rows.above(wz * here)
            rows.put(later_ref, row, total * rows.get(inv_sc, row))
            before, here, wx_before = here, after, wx

    now_ref, spare = first_ref, [ping_sc, pong_sc]
    first, last = 0, window
    for picard in range(ITERS):
        if picard == 0:
            weights = wx_ref, wy_ref, wz_ref
            for row in range(first + 1, last - 1):
                finish(row, rows.get(partial_ref, row), rows.get(gravity_ref, row))
        else:
            weights = wx_sc, wy_sc, wz_sc
            face_weights(
                rows, (now_ref, ks_ref, alpha_ref, land_ref, *weights), first, last - 1,
                lambda row: rows.get(store_ref, row),
                lambda row: rows.get(store_ref, row) * rows.get(first_ref, row),
                finish,
            )
        for _ in range(SWEEPS):
            first, last = first + 1, last - 1
            later_ref = spare[0]
            sweep(now_ref, later_ref, weights, first, last)
            spare = [spare[1], later_ref]
            now_ref = later_ref
    for part in range(rows.per_row):
        lanes = pl.ds(part * LANES, LANES)
        top_rows = now_ref[part, pl.ds(HALO * layers, span, stride=layers), :]
        for step, head_ref in enumerate(head_refs):
            for held_layer in range(held):
                layer = (place_ref[2] ^ step) * held + held_layer
                head_ref[held_layer, :, lanes] = now_ref[part, pl.ds(HALO * layers + layer, span, stride=layers), :]
            head_ref[held, :, lanes] = top_rows


def inflow_kernel(
    groups, place_ref, cells_ref, bed_ref, slot_section_ref, row_ref, *refs,
):
    back_refs = refs[:groups]
    head_ref, out_ref, block_sc, lane_sc, found_sc, turned_sc = refs[groups:]
    _, span, breadth = back_refs[0].shape
    held, across, _ = head_ref.shape
    per_row = breadth // LANES
    blocks = across * per_row
    slots = cells_ref.shape[0]
    quarter = LANES // groups
    packed = slots // groups
    flip = place_ref[1]
    for step, back_ref in enumerate(back_refs):
        source = place_ref[2] ^ step
        number = jnp.where(flip == 1, groups - 1 - source, source)
        rows = pl.ds(pl.multiple_of(number * span, span), span)
        for layer in range(held):
            head_ref[layer, rows, :] = back_ref[layer]
        for part in range(per_row):
            spot = pl.ds(number * span * per_row + part, span, stride=per_row)
            turned_sc[spot, :] = back_ref[held, :, part * LANES:(part + 1) * LANES]

    own = lax.broadcasted_iota(jnp.int32, (packed, LANES), 1) // quarter

    def pack(ref):
        result = None
        for number in range(groups):
            shift = lax.rem((number + groups - place_ref[2]) * quarter, LANES)
            moved = pltpu.roll(ref[pl.ds(number * packed, packed), :], shift, 1)
            result = moved if result is None else jnp.where(own == number, moved, result)
        return result

    cells = pack(cells_ref)
    block, lane = split_cells(cells, 0, breadth, LANES)
    block_sc[...] = block
    lane_sc[...] = lane
    pieces = bf16_pieces(turned_sc[...].T, 2)
    group = 32
    one = jnp.ones((16, LANES), jnp.bfloat16)
    index = lax.broadcasted_iota(jnp.int32, (LANES, LANES), 0).astype(jnp.float32)

    def step(number, _):
        hots = jnp.concatenate(
            [one_hot(row_copies(block_sc, number * group + place), blocks, one) for place in range(group)], axis=1
        )
        found = jnp.zeros((LANES, group * LANES), jnp.float32)
        for piece in pieces:
            found = found + lax.dot_general(
                piece, hots, (((1,), (0,)), ((), ())), preferred_element_type=jnp.float32
            )
        for place in range(group):
            row = number * group + place
            lanes = jnp.broadcast_to(lane_sc[pl.ds(row, 1), :], (LANES, LANES))
            mine = jnp.where(index == lanes, found[:, place * LANES:(place + 1) * LANES], 0.0)
            found_sc[pl.ds(row, 1), :] = jnp.sum(mine, axis=0, keepdims=True)
        return 0

    lax.fori_loop(0, packed // group, step, 0)
    slot_in = jnp.where(cells >= 0, pack(bed_ref) * (found_sc[...] - pack(slot_section_ref)), 0.0)
    spread = jnp.concatenate(
        [slot_in if number == 0 else pltpu.roll(slot_in, LANES - number * quarter, 1) for number in range(groups)],
        axis=0,
    )
    rows = out_ref.shape[0]
    index = lax.broadcasted_iota(jnp.int32, (rows, slots), 0)
    put = jnp.where(index == row_ref[...], 1.0, 0.0).astype(jnp.bfloat16)
    total = jnp.zeros((rows, LANES), jnp.float32)
    for piece in bf16_pieces(spread, 3):
        total = total + lax.dot_general(
            put, piece, (((1,), (0,)), ((), ())), preferred_element_type=jnp.float32
        )
    out_ref[...] = total


def call(kernel, out_shape, in_specs, scratch, flops, moved):
    single = not isinstance(out_shape, (tuple, list))
    return pl.pallas_call(
        kernel,
        out_shape=out_shape,
        in_specs=in_specs,
        out_specs=in_vmem if single else tuple(in_vmem for _ in out_shape),
        scratch_shapes=scratch,
        compiler_params=pltpu.CompilerParams(vmem_limit_bytes=VMEM_LIMIT),
        cost_estimate=pl.CostEstimate(flops=flops, bytes_accessed=moved, transcendentals=0),
    )


def on_device(
    head_start,
    soil_class,
    land_mask,
    ks_table,
    alpha_table,
    store_table,
    section,
    cross_owner,
    cross_local,
    node_cell,
    bed_cond,
):
    held, across, breadth = head_start.shape
    reach_rows, node_count = section.shape
    tiles = lax.axis_size("tile")
    groups = lax.axis_size("layer")
    layers = held * groups
    span = across // groups
    per_row = breadth // LANES
    blocks = span * per_row
    tile = lax.axis_index("tile")
    layer = lax.axis_index("layer")
    flip = lax.rem(tile, 2)
    number = jnp.where(flip == 1, groups - 1 - layer, layer)
    odd = lax.rem(number, 2)
    end = (number == 0) | (number == groups - 1)
    far_partner = jnp.where(end, layer, layer ^ (groups - 1))
    place = jnp.stack([number * span, flip, layer, odd, layer ^ 1, far_partner]).astype(jnp.int32)
    near = [(i, i ^ 1) for i in range(groups)]
    far = []
    for upper in range(tiles):
        far += [(upper * groups + i, upper * groups + (i ^ (groups - 1))) for i in range(1, groups - 1)]
        if upper + 1 < tiles:
            index = groups - 1 if upper % 2 == 0 else 0
            one, two = upper * groups + index, (upper + 1) * groups + index
            far += [(one, two), (two, one)]

    cells = node_cell[0]
    bed = bed_cond[0]
    slots = cells.shape[0]
    reach = cross_owner * reach_rows + cross_local

    def exchange(parts):
        received = [parts[0]]
        for step in range(1, groups):
            received.append(lax.ppermute(parts[step], "layer", [(i, i ^ step) for i in range(groups)]))
        return received

    field_bytes = held * across * breadth * 4
    *own_blocks, spread, land = call(
        functools.partial(prepare_kernel, groups),
        (jax.ShapeDtypeStruct((2, held, span, breadth), jnp.float32),) * groups
        + (
            jax.ShapeDtypeStruct((tiles, reach_rows, node_count), jnp.float32),
            jax.ShapeDtypeStruct((span, breadth), jnp.float32),
        ),
        [in_smem] + [in_hbm] * 4,
        [
            pltpu.VMEM(head_start.shape, jnp.float32),
            pltpu.VMEM(soil_class.shape, jnp.int32),
            pltpu.VMEM(section.shape, jnp.float32),
            pltpu.VMEM(land_mask.shape, jnp.int32),
            pltpu.SemaphoreType.DMA((2 + 2 * held,)),
        ],
        0, 4 * field_bytes,
    )(place, head_start, soil_class, section, land_mask)
    whole_section = lax.all_to_all(spread, "tile", 0, 0).reshape(tiles * reach_rows, node_count)
    received = exchange(own_blocks)

    node_scratch = pltpu.VMEM((slots, LANES), jnp.float32)
    riv_shape = jax.ShapeDtypeStruct((blocks, LANES), jnp.float32)
    node_bytes = slots * LANES * 4
    diag, rhs, slot_section = call(
        functools.partial(river_kernel, breadth),
        (riv_shape, riv_shape, jax.ShapeDtypeStruct((slots, node_count), jnp.float32)),
        [in_smem] + [in_vmem] * 4,
        [node_scratch] * 6
        + [pltpu.VMEM((span * breadth // BLOCK, LANES), jnp.float32)],
        8 * span * breadth * slots * LANES, 4 * node_bytes,
    )(place, cells, bed, whole_section, reach)

    side = HALO * per_row

    def grid_edge(bottom):
        row = jnp.where(bottom, span - HALO, 0)
        grid = [lax.dynamic_slice_in_dim(block, row, HALO, 2) for block in received]
        grid = jnp.stack(grid, axis=1).reshape(2 * layers * HALO, breadth)
        return jnp.concatenate([grid, lax.dynamic_slice_in_dim(land, row, HALO, 0)])

    def river_edge(bottom):
        return jnp.concatenate([jnp.where(bottom, term[blocks - side:], term[:side]) for term in (diag, rhs)])

    near_grid = lax.ppermute(grid_edge(odd == 0), "layer", near)
    far_grid = lax.ppermute(grid_edge(odd == 1), FLAT, far)
    near_river = lax.ppermute(river_edge(odd == 0), "layer", near)
    far_river = lax.ppermute(river_edge(odd == 1), FLAT, far)

    window = span + 2 * HALO
    cells_held = layers * window * breadth
    field_shape = jax.ShapeDtypeStruct((per_row, window * layers, LANES), jnp.float32)
    field = pltpu.VMEM(field_shape.shape, jnp.float32)
    staged = call(
        functools.partial(stage_kernel, groups),
        (field_shape,) * 4 + (jax.ShapeDtypeStruct((window, breadth), jnp.float32),) + (field_shape,) * 5,
        [in_smem] * 4 + [in_vmem] * (4 + groups), [field], 60 * cells_held, 40 * cells_held,
    )(place, ks_table, alpha_table, store_table, land, near_grid, far_grid, diag, *received)
    out_shape = jax.ShapeDtypeStruct((held + 1, span, breadth), jnp.float32)
    out = call(
        functools.partial(flow_kernel, groups), (out_shape,) * groups,
        [in_smem] + [in_vmem] * (4 + len(staged)),
        [field] * 7 + [pltpu.VMEM((window * per_row, LANES), jnp.float32)] * 2,
        100 * cells_held, 40 * cells_held,
    )(place, near_river, far_river, diag, rhs, *staged)
    back = exchange(out)

    packed = pltpu.VMEM((slots // groups, LANES), jnp.float32)
    head, partial = call(
        functools.partial(inflow_kernel, groups),
        (
            jax.ShapeDtypeStruct(head_start.shape, jnp.float32),
            jax.ShapeDtypeStruct((tiles * reach_rows, node_count), jnp.float32),
        ),
        [in_smem] + [in_vmem] * (4 + groups),
        [packed] * 3 + [pltpu.VMEM((across * per_row, LANES), jnp.float32)],
        4 * across * breadth * slots * node_count // groups, 8 * node_bytes,
    )(place, cells, bed, slot_section, reach, *back)
    terms = lax.all_to_all(partial.reshape(tiles, reach_rows, node_count), "tile", 0, 0)
    return head, jnp.sum(terms, axis=0)[:, :node_count // groups]


def solution(mesh):
    placed = (
        P("layer", "tile", None),
        P("layer", "tile", None),
        P("tile", None),
        P(),
        P(),
        P(),
        P("tile", None),
        P("tile", None),
        P("tile", None),
        P("tile", None, None),
        P("tile", None, None),
    )
    return jax.shard_map(
        on_device,
        mesh=mesh,
        in_specs=placed,
        out_specs=(P("layer", "tile", None), P("tile", "layer")),
        check_vma=False,
    )
```

```python
import functools

import jax
import jax.numpy as jnp
from jax import lax
from jax.experimental import pallas as pl
from jax.experimental.pallas import tpu as pltpu
from jax.sharding import PartitionSpec as P

ITERS = 2
SWEEPS = 3

LATERAL = 1.0
VERTICAL = 2.0
GRAVITY = 1.0

HALO = ITERS * SWEEPS
BLOCK = 64
LANES = 128
VMEM_LIMIT = 32 * 1024 * 1024
VMEM_MOST = 60 * 1024 * 1024
FLAT = ("tile", "layer")

in_vmem = pl.BlockSpec(memory_space=pltpu.VMEM)
in_hbm = pl.BlockSpec(memory_space=pltpu.HBM)
in_smem = pl.BlockSpec(memory_space=pltpu.SMEM)


def bf16_pieces(value, count):
    pieces = []
    for _ in range(count):
        piece = value.astype(jnp.bfloat16)
        pieces.append(piece)
        value = value - piece.astype(jnp.float32)
    return pieces


def reciprocal(value):
    guess = pl.reciprocal(value, approx=True)
    return guess * (2.0 - value * guess)


def one_hot(row, size, on):
    index = lax.broadcasted_iota(jnp.int32, (16, LANES), 0)
    zero = jnp.zeros((16, LANES), jnp.bfloat16)
    tiles = []
    for start in range(0, size, 16):
        here = (index + start).astype(jnp.float32).astype(jnp.bfloat16)
        tiles.append(jnp.where(row == here, on, zero))
    return jnp.concatenate(tiles, axis=0)


def row_copies(ref, slot):
    return jnp.broadcast_to(ref[pl.ds(slot, 1), :], (16, LANES)).astype(jnp.bfloat16)


def split_cells(cells, first_row, breadth, width):
    local = cells - first_row * breadth
    shift = width.bit_length() - 1
    block = jnp.where(cells < 0, -1, local >> shift)
    return block.astype(jnp.float32), (local & (width - 1)).astype(jnp.float32)


def river_kernel(
    breadth, place_ref, cells_ref, bed_ref, section_ref, row_ref, diag_ref, rhs_ref, slot_section_ref,
    block_sc, spot_sc, dhigh_sc, dlow_sc, rhigh_sc, rlow_sc, sum_sc,
):
    rows = section_ref.shape[0]
    slots = row_ref.shape[1]
    index = lax.broadcasted_iota(jnp.int32, (rows, slots), 0)
    pick = jnp.where(index == row_ref[...], 1.0, 0.0).astype(jnp.bfloat16)
    picked = jnp.zeros(slot_section_ref.shape, jnp.float32)
    for piece in bf16_pieces(section_ref[...], 3):
        picked = picked + lax.dot_general(
            pick, piece, (((0,), (0,)), ((), ())), preferred_element_type=jnp.float32
        )
    slot_section_ref[...] = picked

    block, spot = split_cells(cells_ref[...], place_ref[0], breadth, BLOCK)
    block_sc[...] = block
    spot_sc[...] = spot
    bed = bed_ref[...]
    for value, high_sc, low_sc in ((bed, dhigh_sc, dlow_sc), (bed * picked, rhigh_sc, rlow_sc)):
        high, low = bf16_pieces(value, 2)
        high_sc[...] = high.astype(jnp.float32)
        low_sc[...] = low.astype(jnp.float32)
    share = LANES // BLOCK
    blocks = share * diag_ref.shape[0]
    group = 32
    one = jnp.ones((16, LANES), jnp.bfloat16)

    def step(number, total):
        for pair in range(0, group, 2):
            left, right = [], []
            for slot in (number * group + pair, number * group + pair + 1):
                spots = row_copies(spot_sc, slot)
                left.append(one_hot(row_copies(block_sc, slot), blocks, one))
                right.append(
                    jnp.concatenate(
                        [one_hot(spots, BLOCK, row_copies(ref, slot)) for ref in (dhigh_sc, dlow_sc, rhigh_sc, rlow_sc)],
                        axis=0,
                    )
                )
            total = total + lax.dot_general(
                jnp.concatenate(left, axis=1),
                jnp.concatenate(right, axis=1),
                (((1,), (1,)), ((), ())),
                preferred_element_type=jnp.float32,
            )
        return total

    total = lax.fori_loop(0, slots // group, step, jnp.zeros((blocks, 4 * BLOCK), jnp.float32))
    low_half = lax.broadcasted_iota(jnp.int32, diag_ref.shape, 1) < BLOCK
    for number, ref in ((0, diag_ref), (1, rhs_ref)):
        part = total[:, number * LANES:(number + 1) * LANES]
        sum_sc[...] = part + pltpu.roll(part, BLOCK, 1)
        ref[...] = jnp.where(
            low_half, sum_sc[pl.ds(0, blocks // share, stride=share), :], sum_sc[pl.ds(1, blocks // share, stride=share), :]
        )


def prepare_kernel(groups, place_ref, head_hbm, soil_hbm, section_hbm, land_hbm, *refs):
    block_refs, spread_ref, land_out_ref = refs[:groups], refs[groups], refs[groups + 1]
    head_ref, soil_ref, section_ref, land_ref, sems = refs[groups + 2:]
    held, across, _ = head_ref.shape
    span = across // groups
    pairs = [(section_hbm, section_ref), (land_hbm, land_ref)]
    for layer in range(held):
        pairs += [(head_hbm.at[layer], head_ref.at[layer]), (soil_hbm.at[layer], soil_ref.at[layer])]
    copies = [pltpu.make_async_copy(here, there, sems.at[k]) for k, (here, there) in enumerate(pairs)]
    for copy in copies:
        copy.start()

    def rows_of(target):
        number = jnp.where(place_ref[1] == 1, groups - 1 - target, target)
        return pl.ds(pl.multiple_of(number * span, span), span)

    copies[0].wait()
    section = section_ref[...]
    for tile in range(spread_ref.shape[0]):
        spread_ref[tile] = section
    copies[1].wait()
    land_out_ref[...] = land_ref[rows_of(place_ref[2]), :].astype(jnp.float32)
    for layer in range(held):
        copies[2 + 2 * layer].wait()
        copies[3 + 2 * layer].wait()
        for step, out_ref in enumerate(block_refs):
            rows = rows_of(place_ref[2] ^ step)
            out_ref[0, layer] = head_ref[layer, rows, :]
            out_ref[1, layer] = soil_ref[layer, rows, :].astype(jnp.float32)


class Rows:
    def __init__(self, layers, breadth):
        self.layers, self.breadth, self.per_row = layers, breadth, breadth // LANES

    def get(self, ref, row):
        spot = pl.ds(row * self.layers, self.layers)
        return jnp.concatenate([ref[part, spot, :] for part in range(self.per_row)], axis=1)

    def put(self, ref, row, value):
        spot = pl.ds(row * self.layers, self.layers)
        for part in range(self.per_row):
            ref[part, spot, :] = value[:, part * LANES:(part + 1) * LANES]

    def put_layer(self, ref, layer, row, value):
        for part in range(self.per_row):
            spot = pl.ds(row * self.layers + layer, value.shape[0], stride=self.layers)
            ref[part, spot, :] = value[:, part * LANES:(part + 1) * LANES]

    def east(self, field):
        return pltpu.roll(field, self.breadth - 1, 1)

    def west(self, field):
        return pltpu.roll(field, 1, 1)

    def below(self, field):
        return pltpu.roll(field, self.layers - 1, 0)

    def above(self, field):
        return pltpu.roll(field, 1, 0)


class Joined:
    def __init__(self, rows, own, full, first, last):
        self.rows, self.own, self.full, self.first, self.last = rows, own, full, first, last

    def get(self, row):
        if self.first <= row < self.last:
            return self.rows.get(self.own, row - self.first)
        return self.rows.get(self.full, row)

    def put(self, row, value):
        self.rows.put(self.full, row, value)


class Faces:
    def __init__(self, rows):
        self.rows = rows
        level = lax.broadcasted_iota(jnp.int32, (rows.layers, rows.breadth), 0)
        column = lax.broadcasted_iota(jnp.int32, (rows.layers, rows.breadth), 1)
        self.not_bottom = level < rows.layers - 1
        self.not_last = column < rows.breadth - 1

    def conduct(self, ks, alpha, head, land):
        cond = ks * jnp.exp(alpha * jnp.minimum(head, 0.0))
        return cond, cond * land

    def face(self, factor, here, there):
        return factor * 2.0 * here[1] * there[1] * reciprocal(here[0] + there[0])

    def between_rows(self, here, there):
        return self.face(LATERAL, here, there)

    def in_row(self, here):
        rows = self.rows
        cond, opened = here
        wy = self.face(LATERAL, here, (rows.east(cond), rows.east(opened)))
        wz = self.face(VERTICAL, here, (rows.below(cond), rows.below(opened)))
        wy = jnp.where(self.not_last, wy, 0.0)
        wz = jnp.where(self.not_bottom, wz, 0.0)
        wz_above = rows.above(wz)
        return wy, wz, wy + rows.west(wy) + wz + wz_above, GRAVITY * (wz_above - wz)


def lane_tables(refs, layers):
    lane = lax.broadcasted_iota(jnp.int32, (layers, LANES), 1)
    tables = []
    for ref in refs:
        table = jnp.zeros((layers, LANES), jnp.float32)
        for kind in range(ref.shape[0]):
            table = jnp.where(lane == kind, ref[kind], table)
        tables.append(table)
    return tables


def look_up(rows, table, soil):
    parts = [
        jnp.take_along_axis(table, soil[:, part * LANES:(part + 1) * LANES], axis=1, mode="promise_in_bounds")
        for part in range(rows.per_row)
    ]
    return jnp.concatenate(parts, axis=1)


def stage_kernel(groups, place_ref, ks_ref, alpha_ref, store_ref, land_ref, *refs):
    block_refs = refs[:groups]
    first_out, ks_out, alpha_out, store_out, wx_out, wy_out, wz_out, diag_out, base_out, soil_sc = refs[groups:]
    _, held, span, breadth = block_refs[0].shape
    layers = groups * held
    rows = Rows(layers, breadth)
    faces = Faces(rows)

    for step, block_ref in enumerate(block_refs):
        for held_layer in range(held):
            layer = (place_ref[2] ^ step) * held + held_layer
            rows.put_layer(first_out, layer, 0, block_ref[0, held_layer])
            rows.put_layer(soil_sc, layer, 0, block_ref[1, held_layer])
    tables = lane_tables((ks_ref, alpha_ref, store_ref), layers)
    before = None
    for row in range(span):
        soil = rows.get(soil_sc, row).astype(jnp.int32)
        ks, alpha, store = [look_up(rows, table, soil) for table in tables]
        first = rows.get(first_out, row)
        here = faces.conduct(ks, alpha, first, land_ref[pl.ds(row, 1), :])
        wy, wz, diagonal, gravity = faces.in_row(here)
        for ref, value in (
            (ks_out, ks), (alpha_out, alpha), (store_out, store), (wy_out, wy), (wz_out, wz),
            (diag_out, store + diagonal), (base_out, store * first + gravity),
        ):
            rows.put(ref, row, value)
        if row > 0:
            rows.put(wx_out, row - 1, faces.between_rows(before, here))
        before = here


def flow_kernel(
    groups, place_ref, kst_ref, alphat_ref, storet_ref, land_ref, near_ref, far_ref, diag_ref, rhs_ref, *refs,
):
    first_ref, ks_ref, alpha_ref, store_ref, wx_ref, wy_ref, wz_ref, partial_ref, gravity_ref = refs[:9]
    head_refs, top_ref = refs[9:9 + groups], refs[9 + groups]
    (
        first_sc, soil_sc, ks_sc, alpha_sc, store_sc, wx_sc, wy_sc, wz_sc, base_sc, inv_sc, ping_sc, pong_sc,
        land_sc, dtop_sc, rtop_sc,
    ) = refs[10 + groups:]
    held, span, breadth = head_refs[0].shape
    layers = groups * held
    window = span + 2 * HALO
    last_own = HALO + span
    rows = Rows(layers, breadth)
    faces = Faces(rows)
    side = HALO * rows.per_row

    land_sc[pl.ds(HALO, span), :] = land_ref[...]
    dtop_sc[pl.ds(side, span * rows.per_row), :] = diag_ref[...]
    rtop_sc[pl.ds(side, span * rows.per_row), :] = rhs_ref[...]

    def put_halo(ref, partner, row):
        def entry(number):
            return ref[pl.ds(number * HALO, HALO), :]

        for number in range(layers):
            layer = (partner ^ (number // held)) * held + number % held
            rows.put_layer(first_sc, layer, row, entry(number))
            rows.put_layer(soil_sc, layer, row, entry(layers + number))
        land_sc[pl.ds(row, HALO), :] = entry(2 * layers)
        for number, top_sc in ((2 * layers + 1, dtop_sc), (2 * layers + 2, rtop_sc)):
            value = entry(number)
            for part in range(rows.per_row):
                spot = pl.ds(row * rows.per_row + part, HALO, stride=rows.per_row)
                top_sc[spot, :] = value[:, part * LANES:(part + 1) * LANES]

    for odd, above_ref, below_ref in ((0, far_ref, near_ref), (1, near_ref, far_ref)):
        @pl.when(place_ref[3] == odd)
        def _(above_ref=above_ref, below_ref=below_ref):
            for ref, row in ((above_ref, 0), (below_ref, last_own)):
                put_halo(ref, place_ref[4] if ref is near_ref else place_ref[5], row)

    tables = lane_tables((kst_ref, alphat_ref, storet_ref), layers)
    for row in [*range(HALO), *range(last_own, window)]:
        soil = rows.get(soil_sc, row).astype(jnp.int32)
        for table, ref in zip(tables, (ks_sc, alpha_sc, store_sc)):
            rows.put(ref, row, look_up(rows, table, soil))

    def joined(own, full, last=last_own):
        return Joined(rows, own, full, HALO, last)

    first, ks, alpha, store = [
        joined(own, full)
        for own, full in ((first_ref, first_sc), (ks_ref, ks_sc), (alpha_ref, alpha_sc), (store_ref, store_sc))
    ]
    top = lax.broadcasted_iota(jnp.int32, (layers, breadth), 0) == 0

    def riv_row(ref, row):
        parts = [
            jnp.broadcast_to(ref[pl.ds(row * rows.per_row + part, 1), :], (layers, LANES))
            for part in range(rows.per_row)
        ]
        return jnp.where(top, jnp.concatenate(parts, axis=1), 0.0)

    def finish(row, diagonal, base):
        rows.put(inv_sc, row, reciprocal(diagonal + riv_row(dtop_sc, row)))
        rows.put(base_sc, row, base + riv_row(rtop_sc, row))

    def conduct(now, row):
        return faces.conduct(ks.get(row), alpha.get(row), now.get(row), land_sc[pl.ds(row, 1), :])

    def sweep(now, later_ref, weights, begin, stop):
        wx_of, wy_of, wz_of = weights
        before, here, wx_before = now.get(begin - 1), now.get(begin), wx_of.get(begin - 1)
        for row in range(begin, stop):
            after = now.get(row + 1)
            wx, wy, wz = wx_of.get(row), wy_of.get(row), wz_of.get(row)
            total = rows.get(base_sc, row) + wx_before * before + wx * after
            total = total + wy * rows.east(here) + rows.west(wy * here)
            total = total + wz * rows.below(here) + rows.above(wz * here)
            rows.put(later_ref, row, total * rows.get(inv_sc, row))
            before, here, wx_before = here, after, wx

    now, spare = first, [ping_sc, pong_sc]
    begin, stop = 0, window
    for picard in range(ITERS):
        early = picard == 0
        wx_of = joined(wx_ref, wx_sc, last_own - 1 if early else HALO)
        wy_of, wz_of = [joined(own, full, last_own if early else HALO) for own, full in ((wy_ref, wy_sc), (wz_ref, wz_sc))]
        before, wx_before = None, None
        for row in range(begin, stop):
            staged = early and HALO <= row < last_own
            here = conduct(now, row) if not staged or row in (HALO, last_own - 1) else None
            if row > begin:
                if early and HALO <= row - 1 < last_own - 1:
                    wx = wx_of.get(row - 1)
                else:
                    wx = faces.between_rows(before, here)
                    wx_of.put(row - 1, wx)
                if row - 1 > begin:
                    diagonal, base = pending
                    finish(row - 1, diagonal + wx_before + wx, base)
                wx_before = wx
            if staged:
                pending = rows.get(partial_ref, row - HALO), rows.get(gravity_ref, row - HALO)
            elif begin < row < stop - 1:
                wy, wz, diagonal, gravity = faces.in_row(here)
                wy_of.put(row, wy)
                wz_of.put(row, wz)
                pending = store.get(row) + diagonal, store.get(row) * first.get(row) + gravity
            before = here
        for _ in range(SWEEPS):
            begin, stop = begin + 1, stop - 1
            later_ref = spare[0]
            sweep(now, later_ref, (wx_of, wy_of, wz_of), begin, stop)
            spare = [spare[1], later_ref]
            now = joined(None, later_ref, HALO)
    for part in range(rows.per_row):
        lanes = pl.ds(part * LANES, LANES)
        top_ref[:, lanes] = later_ref[part, pl.ds(HALO * layers, span, stride=layers), :]
        for step, head_ref in enumerate(head_refs):
            for held_layer in range(held):
                layer = (place_ref[2] ^ step) * held + held_layer
                head_ref[held_layer, :, lanes] = later_ref[part, pl.ds(HALO * layers + layer, span, stride=layers), :]


def inflow_kernel(groups, place_ref, cells_ref, bed_ref, slot_section_ref, row_ref, *refs):
    top_refs = refs[:groups]
    out_ref, block_sc, lane_sc, found_sc, turned_sc = refs[groups:]
    span, breadth = top_refs[0].shape
    per_row = breadth // LANES
    blocks = groups * span * per_row
    slots = cells_ref.shape[0]
    quarter = LANES // groups
    packed = slots // groups
    for step, top_ref in enumerate(top_refs):
        source = place_ref[2] ^ step
        number = jnp.where(place_ref[1] == 1, groups - 1 - source, source)
        for part in range(per_row):
            spot = pl.ds(number * span * per_row + part, span, stride=per_row)
            turned_sc[spot, :] = top_ref[:, part * LANES:(part + 1) * LANES]

    own = lax.broadcasted_iota(jnp.int32, (packed, LANES), 1) // quarter

    def pack(ref):
        result = None
        for number in range(groups):
            shift = lax.rem((number + groups - place_ref[2]) * quarter, LANES)
            moved = pltpu.roll(ref[pl.ds(number * packed, packed), :], shift, 1)
            result = moved if result is None else jnp.where(own == number, moved, result)
        return result

    cells = pack(cells_ref)
    block, lane = split_cells(cells, 0, breadth, LANES)
    block_sc[...] = block
    lane_sc[...] = lane
    table = jnp.concatenate(bf16_pieces(turned_sc[...].T, 2), axis=1)
    group = 32
    one = jnp.ones((16, LANES), jnp.bfloat16)
    index = lax.broadcasted_iota(jnp.int32, (LANES, LANES), 0).astype(jnp.float32)

    def step(number, _):
        for pair in range(0, group, 2):
            places = (number * group + pair, number * group + pair + 1)
            hots = jnp.concatenate([one_hot(row_copies(block_sc, row), blocks, one) for row in places], axis=1)
            found = lax.dot_general(
                table, jnp.concatenate([hots, hots], axis=0), (((1,), (0,)), ((), ())),
                preferred_element_type=jnp.float32,
            )
            for place, row in enumerate(places):
                lanes = jnp.broadcast_to(lane_sc[pl.ds(row, 1), :], (LANES, LANES))
                mine = jnp.where(index == lanes, found[:, place * LANES:(place + 1) * LANES], 0.0)
                found_sc[pl.ds(row, 1), :] = jnp.sum(mine, axis=0, keepdims=True)
        return 0

    lax.fori_loop(0, packed // group, step, 0)
    slot_in = jnp.where(cells >= 0, pack(bed_ref) * (found_sc[...] - pack(slot_section_ref)), 0.0)
    spread = jnp.concatenate(
        [slot_in if number == 0 else pltpu.roll(slot_in, LANES - number * quarter, 1) for number in range(groups)],
        axis=0,
    )
    rows = out_ref.shape[0]
    index = lax.broadcasted_iota(jnp.int32, (rows, slots), 0)
    put = jnp.where(index == row_ref[...], 1.0, 0.0).astype(jnp.bfloat16)
    total = jnp.zeros((rows, LANES), jnp.float32)
    for piece in bf16_pieces(spread, 3):
        total = total + lax.dot_general(
            put, piece, (((1,), (0,)), ((), ())), preferred_element_type=jnp.float32
        )
    out_ref[...] = total


def result_kernel(groups, place_ref, terms_ref, *refs):
    back_refs = refs[:groups]
    head_ref, inflow_ref = refs[groups:]
    held, span, _ = back_refs[0].shape
    for step, back_ref in enumerate(back_refs):
        source = place_ref[2] ^ step
        number = jnp.where(place_ref[1] == 1, groups - 1 - source, source)
        for layer in range(held):
            head_ref[layer, pl.ds(pl.multiple_of(number * span, span), span), :] = back_ref[layer]
    total = terms_ref[0]
    for tile in range(1, terms_ref.shape[0]):
        total = total + terms_ref[tile]
    inflow_ref[...] = total[:, :inflow_ref.shape[1]]


def call(kernel, out_shape, in_specs, scratch, flops, moved, vmem=VMEM_LIMIT):
    single = not isinstance(out_shape, (tuple, list))
    return pl.pallas_call(
        kernel,
        out_shape=out_shape,
        in_specs=in_specs,
        out_specs=in_vmem if single else tuple(in_vmem for _ in out_shape),
        scratch_shapes=scratch,
        compiler_params=pltpu.CompilerParams(vmem_limit_bytes=vmem),
        cost_estimate=pl.CostEstimate(flops=flops, bytes_accessed=moved, transcendentals=0),
    )


def on_device(
    head_start,
    soil_class,
    land_mask,
    ks_table,
    alpha_table,
    store_table,
    section,
    cross_owner,
    cross_local,
    node_cell,
    bed_cond,
):
    held, across, breadth = head_start.shape
    reach_rows, node_count = section.shape
    tiles = lax.axis_size("tile")
    groups = lax.axis_size("layer")
    layers = held * groups
    span = across // groups
    per_row = breadth // LANES
    blocks = span * per_row
    tile = lax.axis_index("tile")
    layer = lax.axis_index("layer")
    flip = lax.rem(tile, 2)
    number = jnp.where(flip == 1, groups - 1 - layer, layer)
    odd = lax.rem(number, 2)
    end = (number == 0) | (number == groups - 1)
    far_partner = jnp.where(end, layer, layer ^ (groups - 1))
    place = jnp.stack([number * span, flip, layer, odd, layer ^ 1, far_partner]).astype(jnp.int32)
    near = [(i, i ^ 1) for i in range(groups)]
    far = []
    for upper in range(tiles):
        far += [(upper * groups + i, upper * groups + (i ^ (groups - 1))) for i in range(1, groups - 1)]
        if upper + 1 < tiles:
            index = groups - 1 if upper % 2 == 0 else 0
            one, two = upper * groups + index, (upper + 1) * groups + index
            far += [(one, two), (two, one)]

    cells = node_cell[0]
    bed = bed_cond[0]
    slots = cells.shape[0]
    reach = cross_owner * reach_rows + cross_local

    def exchange(parts):
        received = [parts[0]]
        for step in range(1, groups):
            received.append(lax.ppermute(parts[step], "layer", [(i, i ^ step) for i in range(groups)]))
        return received

    field_bytes = held * across * breadth * 4
    *own_blocks, spread, land = call(
        functools.partial(prepare_kernel, groups),
        (jax.ShapeDtypeStruct((2, held, span, breadth), jnp.float32),) * groups
        + (
            jax.ShapeDtypeStruct((tiles, reach_rows, node_count), jnp.float32),
            jax.ShapeDtypeStruct((span, breadth), jnp.float32),
        ),
        [in_smem] + [in_hbm] * 4,
        [
            pltpu.VMEM(head_start.shape, jnp.float32),
            pltpu.VMEM(soil_class.shape, jnp.int32),
            pltpu.VMEM(section.shape, jnp.float32),
            pltpu.VMEM(land_mask.shape, jnp.int32),
            pltpu.SemaphoreType.DMA((2 + 2 * held,)),
        ],
        0, 4 * field_bytes, VMEM_MOST,
    )(place, head_start, soil_class, section, land_mask)
    whole_section = lax.all_to_all(spread, "tile", 0, 0).reshape(tiles * reach_rows, node_count)
    received = exchange(own_blocks)

    node_scratch = pltpu.VMEM((slots, LANES), jnp.float32)
    riv_shape = jax.ShapeDtypeStruct((blocks, LANES), jnp.float32)
    node_bytes = slots * LANES * 4
    diag, rhs, slot_section = call(
        functools.partial(river_kernel, breadth),
        (riv_shape, riv_shape, jax.ShapeDtypeStruct((slots, node_count), jnp.float32)),
        [in_smem] + [in_vmem] * 4,
        [node_scratch] * 6
        + [pltpu.VMEM((span * breadth // BLOCK, LANES), jnp.float32)],
        8 * span * breadth * slots * LANES, 4 * node_bytes,
    )(place, cells, bed, whole_section, reach)

    side = HALO * per_row

    def edge(bottom):
        row = jnp.where(bottom, span - HALO, 0)
        grid = [lax.dynamic_slice_in_dim(block, row, HALO, 2) for block in received]
        river = [jnp.where(bottom, term[blocks - side:], term[:side]) for term in (diag, rhs)]
        return jnp.concatenate(
            [
                jnp.stack(grid, axis=1).reshape(2 * layers * HALO, breadth),
                lax.dynamic_slice_in_dim(land, row, HALO, 0),
                jnp.concatenate(river).reshape(2 * HALO, breadth),
            ]
        )

    near_halo = lax.ppermute(edge(odd == 0), "layer", near)
    far_halo = lax.ppermute(edge(odd == 1), FLAT, far)

    window = span + 2 * HALO
    cells_held = layers * span * breadth
    own_field = jax.ShapeDtypeStruct((per_row, span * layers, LANES), jnp.float32)
    field = pltpu.VMEM((per_row, window * layers, LANES), jnp.float32)
    staged = call(
        functools.partial(stage_kernel, groups), (own_field,) * 9,
        [in_smem] * 4 + [in_vmem] * (1 + groups), [pltpu.VMEM(own_field.shape, jnp.float32)],
        60 * cells_held, 40 * cells_held,
    )(place, ks_table, alpha_table, store_table, land, *received)
    head_shape = jax.ShapeDtypeStruct((held, span, breadth), jnp.float32)
    *heads, top = call(
        functools.partial(flow_kernel, groups),
        (head_shape,) * groups + (jax.ShapeDtypeStruct((span, breadth), jnp.float32),),
        [in_smem] * 4 + [in_vmem] * (5 + len(staged)),
        [field] * 12
        + [pltpu.VMEM((window, breadth), jnp.float32)]
        + [pltpu.VMEM((window * per_row, LANES), jnp.float32)] * 2,
        200 * cells_held, 60 * cells_held,
    )(place, ks_table, alpha_table, store_table, land, near_halo, far_halo, diag, rhs, *staged)
    tops = exchange([top] * groups)
    backs = exchange(heads)

    packed = pltpu.VMEM((slots // groups, LANES), jnp.float32)
    partial = call(
        functools.partial(inflow_kernel, groups),
        jax.ShapeDtypeStruct((tiles * reach_rows, node_count), jnp.float32),
        [in_smem] + [in_vmem] * (4 + groups),
        [packed] * 3 + [pltpu.VMEM((across * per_row, LANES), jnp.float32)],
        4 * across * breadth * slots * node_count // groups, 8 * node_bytes,
    )(place, cells, bed, slot_section, reach, *tops)
    terms = lax.all_to_all(partial.reshape(tiles, reach_rows, node_count), "tile", 0, 0)
    return call(
        functools.partial(result_kernel, groups),
        (
            jax.ShapeDtypeStruct(head_start.shape, jnp.float32),
            jax.ShapeDtypeStruct((reach_rows, node_count // groups), jnp.float32),
        ),
        [in_smem] + [in_vmem] * (1 + groups), [], 0, 2 * field_bytes,
    )(place, terms, *backs)


def solution(mesh):
    placed = (
        P("layer", "tile", None),
        P("layer", "tile", None),
        P("tile", None),
        P(),
        P(),
        P(),
        P("tile", None),
        P("tile", None),
        P("tile", None),
        P("tile", None, None),
        P("tile", None, None),
    )
    return jax.shard_map(
        on_device,
        mesh=mesh,
        in_specs=placed,
        out_specs=(P("layer", "tile", None), P("tile", "layer")),
        check_vma=False,
    )
```

```python
import functools

import jax
import jax.numpy as jnp
from jax import lax
from jax.experimental import pallas as pl
from jax.experimental.pallas import tpu as pltpu
from jax.sharding import PartitionSpec as P

ITERS = 2
SWEEPS = 3

LATERAL = 1.0
VERTICAL = 2.0
GRAVITY = 1.0

HALO = ITERS * SWEEPS
BLOCK = 64
LANES = 128
VMEM_LIMIT = 32 * 1024 * 1024
VMEM_MOST = 60 * 1024 * 1024
FLAT = ("tile", "layer")

in_vmem = pl.BlockSpec(memory_space=pltpu.VMEM)
in_hbm = pl.BlockSpec(memory_space=pltpu.HBM)
in_smem = pl.BlockSpec(memory_space=pltpu.SMEM)


def bf16_pieces(value, count):
    pieces = []
    for _ in range(count):
        piece = value.astype(jnp.bfloat16)
        pieces.append(piece)
        value = value - piece.astype(jnp.float32)
    return pieces


def reciprocal(value):
    guess = pl.reciprocal(value, approx=True)
    return guess * (2.0 - value * guess)


def names_of(size):
    index = lax.broadcasted_iota(jnp.int32, (16, LANES), 0)
    return [(index + start).astype(jnp.float32).astype(jnp.bfloat16) for start in range(0, size, 16)]


def one_hot(row, names):
    one = jnp.ones((16, LANES), jnp.bfloat16)
    zero = jnp.zeros((16, LANES), jnp.bfloat16)
    return [jnp.maximum(one - jnp.abs(row - name), zero) for name in names]


def row_copies(ref, first, place):
    rows = ref[pl.ds(pl.multiple_of(first + place // 8 * 8, 8), 8), :]
    return jnp.broadcast_to(rows[place % 8:place % 8 + 1, :], (16, LANES)).astype(jnp.bfloat16)


def position():
    tile, layer = lax.axis_index("tile"), lax.axis_index("layer")
    groups = lax.axis_size("layer")
    flip = lax.rem(tile, 2)
    return layer, flip, jnp.where(flip == 1, groups - 1 - layer, layer)


def span_at(flip, groups, layer):
    return jnp.where(flip == 1, groups - 1 - layer, layer)


def split_cells(cells, first_row, breadth, width):
    local = cells - first_row * breadth
    shift = width.bit_length() - 1
    block = jnp.where(cells < 0, -1, local >> shift)
    return block.astype(jnp.float32), (local & (width - 1)).astype(jnp.float32)


def river_kernel(
    breadth, reach_rows, cells_ref, bed_ref, section_ref, owner_ref, local_ref, land_ref, *refs,
):
    groups = lax.axis_size("layer")
    block_refs = refs[:groups]
    (
        diag_ref, rhs_ref, slot_section_ref, near_ref, far_ref,
        block_sc, spot_sc, dhigh_sc, dlow_sc, rhigh_sc, rlow_sc, sum_sc,
    ) = refs[groups:]
    layer, flip, number = position()
    span = land_ref.shape[0]
    rows = section_ref.shape[0]
    slots = owner_ref.shape[1]
    index = lax.broadcasted_iota(jnp.int32, (rows, slots), 0)
    reach = owner_ref[...] * reach_rows + local_ref[...]
    pick = jnp.where(index == reach, 1.0, 0.0).astype(jnp.bfloat16)
    picked = jnp.zeros(slot_section_ref.shape, jnp.float32)
    for piece in bf16_pieces(section_ref[...], 3):
        picked = picked + lax.dot_general(
            pick, piece, (((0,), (0,)), ((), ())), preferred_element_type=jnp.float32
        )
    slot_section_ref[...] = picked

    block, spot = split_cells(cells_ref[...], number * span, breadth, BLOCK)
    block_sc[...] = block
    spot_sc[...] = spot
    bed = bed_ref[...]
    for value, high_sc, low_sc in ((bed, dhigh_sc, dlow_sc), (bed * picked, rhigh_sc, rlow_sc)):
        high, low = bf16_pieces(value, 2)
        high_sc[...] = high.astype(jnp.float32)
        low_sc[...] = low.astype(jnp.float32)
    share = LANES // BLOCK
    blocks = share * diag_ref.shape[0]
    group = 32
    block_names, spot_names = names_of(blocks), names_of(BLOCK)

    def step(count, total):
        first = count * group
        for pair in range(0, group, 2):
            left, right = [], []
            for place in (pair, pair + 1):
                left.append(jnp.concatenate(one_hot(row_copies(block_sc, first, place), block_names), axis=0))
                hot = one_hot(row_copies(spot_sc, first, place), spot_names)
                values = [row_copies(ref, first, place) for ref in (dhigh_sc, dlow_sc, rhigh_sc, rlow_sc)]
                right.append(jnp.concatenate([tile * value for value in values for tile in hot], axis=0))
            total = total + lax.dot_general(
                jnp.concatenate(left, axis=1),
                jnp.concatenate(right, axis=1),
                (((1,), (1,)), ((), ())),
                preferred_element_type=jnp.float32,
            )
        return total

    total = lax.fori_loop(0, slots // group, step, jnp.zeros((blocks, 4 * BLOCK), jnp.float32))
    low_half = lax.broadcasted_iota(jnp.int32, diag_ref.shape, 1) < BLOCK
    for count, ref in ((0, diag_ref), (1, rhs_ref)):
        part = total[:, count * LANES:(count + 1) * LANES]
        sum_sc[...] = part + pltpu.roll(part, BLOCK, 1)
        ref[...] = jnp.where(
            low_half, sum_sc[pl.ds(0, blocks // share, stride=share), :], sum_sc[pl.ds(1, blocks // share, stride=share), :]
        )

    odd = lax.rem(number, 2) == 1
    per_row = breadth // LANES

    def put_edges(entry, top, bottom, lanes=slice(None)):
        near_ref[pl.ds(entry * HALO, HALO), lanes] = jnp.where(odd, top, bottom)
        far_ref[pl.ds(entry * HALO, HALO), lanes] = jnp.where(odd, bottom, top)

    entry = 0
    for kind in range(2):
        for block_ref in block_refs:
            for held_layer in range(block_ref.shape[1]):
                field = block_ref[kind, held_layer]
                put_edges(entry, field[:HALO], field[span - HALO:])
                entry += 1
    put_edges(entry, land_ref[:HALO, :], land_ref[span - HALO:, :])
    for ref in (diag_ref, rhs_ref):
        entry += 1
        for part in range(per_row):
            top = ref[pl.ds(part, HALO, stride=per_row), :]
            bottom = ref[pl.ds((span - HALO) * per_row + part, HALO, stride=per_row), :]
            put_edges(entry, top, bottom, slice(part * LANES, (part + 1) * LANES))


def spread_kernel(section_hbm, spread_ref, section_ref, sem):
    copy = pltpu.make_async_copy(section_hbm, section_ref, sem)
    copy.start()
    copy.wait()
    for tile in range(spread_ref.shape[0]):
        spread_ref[tile] = section_ref[...]


def prepare_kernel(head_hbm, soil_hbm, land_hbm, *refs):
    groups = lax.axis_size("layer")
    block_refs, land_out_ref = refs[:groups], refs[groups]
    head_ref, soil_ref, land_ref, sems = refs[groups + 1:]
    held, across, _ = head_ref.shape
    span = across // groups
    pairs = [(land_hbm, land_ref)]
    for layer in range(held):
        pairs += [(head_hbm.at[layer], head_ref.at[layer]), (soil_hbm.at[layer], soil_ref.at[layer])]
    copies = [pltpu.make_async_copy(here, there, sems.at[k]) for k, (here, there) in enumerate(pairs)]
    for copy in copies:
        copy.start()
    own, flip, _ = position()

    def rows_of(target):
        return pl.ds(pl.multiple_of(span_at(flip, groups, target) * span, span), span)

    copies[0].wait()
    land_out_ref[...] = land_ref[rows_of(own), :].astype(jnp.float32)
    for layer in range(held):
        copies[1 + 2 * layer].wait()
        copies[2 + 2 * layer].wait()
        for step, out_ref in enumerate(block_refs):
            rows = rows_of(own ^ step)
            out_ref[0, layer] = head_ref[layer, rows, :]
            out_ref[1, layer] = soil_ref[layer, rows, :].astype(jnp.float32)


class Rows:
    def __init__(self, layers, breadth):
        self.layers, self.breadth, self.per_row = layers, breadth, breadth // LANES

    def get(self, ref, row):
        spot = pl.ds(row * self.layers, self.layers)
        return jnp.concatenate([ref[part, spot, :] for part in range(self.per_row)], axis=1)

    def put(self, ref, row, value):
        spot = pl.ds(row * self.layers, self.layers)
        for part in range(self.per_row):
            ref[part, spot, :] = value[:, part * LANES:(part + 1) * LANES]

    def put_layer(self, ref, layer, row, value):
        for part in range(self.per_row):
            spot = pl.ds(row * self.layers + layer, value.shape[0], stride=self.layers)
            ref[part, spot, :] = value[:, part * LANES:(part + 1) * LANES]

    def east(self, field):
        return pltpu.roll(field, self.breadth - 1, 1)

    def west(self, field):
        return pltpu.roll(field, 1, 1)

    def below(self, field):
        return pltpu.roll(field, self.layers - 1, 0)

    def above(self, field):
        return pltpu.roll(field, 1, 0)


class Joined:
    def __init__(self, rows, own, full, first, last):
        self.rows, self.own, self.full, self.first, self.last = rows, own, full, first, last

    def get(self, row):
        if self.first <= row < self.last:
            return self.rows.get(self.own, row - self.first)
        return self.rows.get(self.full, row)

    def put(self, row, value):
        self.rows.put(self.full, row, value)


class Faces:
    def __init__(self, rows):
        self.rows = rows
        level = lax.broadcasted_iota(jnp.int32, (rows.layers, rows.breadth), 0)
        column = lax.broadcasted_iota(jnp.int32, (rows.layers, rows.breadth), 1)
        self.not_bottom = level < rows.layers - 1
        self.not_last = column < rows.breadth - 1

    def conduct(self, ks, alpha, head, land):
        cond = ks * jnp.exp(alpha * jnp.minimum(head, 0.0))
        return cond, cond * land

    def face(self, factor, here, there):
        return factor * 2.0 * here[1] * there[1] * reciprocal(here[0] + there[0])

    def between_rows(self, here, there):
        return self.face(LATERAL, here, there)

    def in_row(self, here):
        rows = self.rows
        cond, opened = here
        wy = self.face(LATERAL, here, (rows.east(cond), rows.east(opened)))
        wz = self.face(VERTICAL, here, (rows.below(cond), rows.below(opened)))
        wy = jnp.where(self.not_last, wy, 0.0)
        wz = jnp.where(self.not_bottom, wz, 0.0)
        wz_above = rows.above(wz)
        return wy, wz, wy + rows.west(wy) + wz + wz_above, GRAVITY * (wz_above - wz)


def lane_tables(refs, layers):
    lane = lax.broadcasted_iota(jnp.int32, (layers, LANES), 1)
    tables = []
    for ref in refs:
        table = jnp.zeros((layers, LANES), jnp.float32)
        for kind in range(ref.shape[0]):
            table = jnp.where(lane == kind, ref[kind], table)
        tables.append(table)
    return tables


def look_up(rows, table, soil):
    parts = [
        jnp.take_along_axis(table, soil[:, part * LANES:(part + 1) * LANES], axis=1, mode="promise_in_bounds")
        for part in range(rows.per_row)
    ]
    return jnp.concatenate(parts, axis=1)


def stage_kernel(ks_ref, alpha_ref, store_ref, land_ref, *refs):
    groups = lax.axis_size("layer")
    own, _, _ = position()
    block_refs = refs[:groups]
    first_out, ks_out, alpha_out, store_out, wx_out, wy_out, wz_out, diag_out, base_out, soil_sc = refs[groups:]
    _, held, span, breadth = block_refs[0].shape
    layers = groups * held
    rows = Rows(layers, breadth)
    faces = Faces(rows)

    for step, block_ref in enumerate(block_refs):
        for held_layer in range(held):
            layer = (own ^ step) * held + held_layer
            rows.put_layer(first_out, layer, 0, block_ref[0, held_layer])
            rows.put_layer(soil_sc, layer, 0, block_ref[1, held_layer])
    tables = lane_tables((ks_ref, alpha_ref, store_ref), layers)
    before = None
    for row in range(span):
        soil = rows.get(soil_sc, row).astype(jnp.int32)
        ks, alpha, store = [look_up(rows, table, soil) for table in tables]
        first = rows.get(first_out, row)
        here = faces.conduct(ks, alpha, first, land_ref[pl.ds(row, 1), :])
        wy, wz, diagonal, gravity = faces.in_row(here)
        for ref, value in (
            (ks_out, ks), (alpha_out, alpha), (store_out, store), (wy_out, wy), (wz_out, wz),
            (diag_out, store + diagonal), (base_out, store * first + gravity),
        ):
            rows.put(ref, row, value)
        if row > 0:
            rows.put(wx_out, row - 1, faces.between_rows(before, here))
        before = here


def flow_kernel(kst_ref, alphat_ref, storet_ref, land_ref, near_ref, far_ref, diag_ref, rhs_ref, *refs):
    groups = lax.axis_size("layer")
    own, _, number = position()
    end = (number == 0) | (number == groups - 1)
    far_partner = jnp.where(end, own, own ^ (groups - 1))
    first_ref, ks_ref, alpha_ref, store_ref, wx_ref, wy_ref, wz_ref, partial_ref, gravity_ref = refs[:9]
    head_refs, top_ref = refs[9:9 + groups], refs[9 + groups]
    (
        first_sc, soil_sc, ks_sc, alpha_sc, store_sc, wx_sc, wy_sc, wz_sc, base_sc, inv_sc, ping_sc, pong_sc,
        land_sc, dtop_sc, rtop_sc,
    ) = refs[10 + groups:]
    held, span, breadth = head_refs[0].shape
    layers = groups * held
    window = span + 2 * HALO
    last_own = HALO + span
    rows = Rows(layers, breadth)
    faces = Faces(rows)
    side = HALO * rows.per_row

    land_sc[pl.ds(HALO, span), :] = land_ref[...]
    dtop_sc[pl.ds(side, span * rows.per_row), :] = diag_ref[...]
    rtop_sc[pl.ds(side, span * rows.per_row), :] = rhs_ref[...]

    def put_halo(ref, partner, row):
        def entry(number):
            return ref[pl.ds(number * HALO, HALO), :]

        for count in range(layers):
            layer = (partner ^ (count // held)) * held + count % held
            rows.put_layer(first_sc, layer, row, entry(count))
            rows.put_layer(soil_sc, layer, row, entry(layers + count))
        land_sc[pl.ds(row, HALO), :] = entry(2 * layers)
        for count, top_sc in ((2 * layers + 1, dtop_sc), (2 * layers + 2, rtop_sc)):
            value = entry(count)
            for part in range(rows.per_row):
                spot = pl.ds(row * rows.per_row + part, HALO, stride=rows.per_row)
                top_sc[spot, :] = value[:, part * LANES:(part + 1) * LANES]

    for odd, above_ref, below_ref in ((0, far_ref, near_ref), (1, near_ref, far_ref)):
        @pl.when(lax.rem(number, 2) == odd)
        def _(above_ref=above_ref, below_ref=below_ref):
            for ref, row in ((above_ref, 0), (below_ref, last_own)):
                put_halo(ref, own ^ 1 if ref is near_ref else far_partner, row)

    tables = lane_tables((kst_ref, alphat_ref, storet_ref), layers)
    for row in [*range(HALO), *range(last_own, window)]:
        soil = rows.get(soil_sc, row).astype(jnp.int32)
        for table, ref in zip(tables, (ks_sc, alpha_sc, store_sc)):
            rows.put(ref, row, look_up(rows, table, soil))

    def joined(own, full, last=last_own):
        return Joined(rows, own, full, HALO, last)

    first, ks, alpha, store = [
        joined(own, full)
        for own, full in ((first_ref, first_sc), (ks_ref, ks_sc), (alpha_ref, alpha_sc), (store_ref, store_sc))
    ]
    top = lax.broadcasted_iota(jnp.int32, (layers, breadth), 0) == 0

    def riv_row(ref, row):
        parts = [
            jnp.broadcast_to(ref[pl.ds(row * rows.per_row + part, 1), :], (layers, LANES))
            for part in range(rows.per_row)
        ]
        return jnp.where(top, jnp.concatenate(parts, axis=1), 0.0)

    def finish(row, diagonal, base):
        rows.put(inv_sc, row, reciprocal(diagonal + riv_row(dtop_sc, row)))
        rows.put(base_sc, row, base + riv_row(rtop_sc, row))

    def conduct(now, row):
        return faces.conduct(ks.get(row), alpha.get(row), now.get(row), land_sc[pl.ds(row, 1), :])

    def sweep(now, later_ref, weights, begin, stop):
        wx_of, wy_of, wz_of = weights
        before, here, wx_before = now.get(begin - 1), now.get(begin), wx_of.get(begin - 1)
        for row in range(begin, stop):
            after = now.get(row + 1)
            wx, wy, wz = wx_of.get(row), wy_of.get(row), wz_of.get(row)
            total = rows.get(base_sc, row) + wx_before * before + wx * after
            total = total + wy * rows.east(here) + rows.west(wy * here)
            total = total + wz * rows.below(here) + rows.above(wz * here)
            rows.put(later_ref, row, total * rows.get(inv_sc, row))
            before, here, wx_before = here, after, wx

    now, spare = first, [ping_sc, pong_sc]
    begin, stop = 0, window
    for picard in range(ITERS):
        early = picard == 0
        wx_of = joined(wx_ref, wx_sc, last_own - 1 if early else HALO)
        wy_of, wz_of = [joined(own, full, last_own if early else HALO) for own, full in ((wy_ref, wy_sc), (wz_ref, wz_sc))]
        before, wx_before = None, None
        for row in range(begin, stop):
            staged = early and HALO <= row < last_own
            here = conduct(now, row) if not staged or row in (HALO, last_own - 1) else None
            if row > begin:
                if early and HALO <= row - 1 < last_own - 1:
                    wx = wx_of.get(row - 1)
                else:
                    wx = faces.between_rows(before, here)
                    wx_of.put(row - 1, wx)
                if row - 1 > begin:
                    diagonal, base = pending
                    finish(row - 1, diagonal + wx_before + wx, base)
                wx_before = wx
            if staged:
                pending = rows.get(partial_ref, row - HALO), rows.get(gravity_ref, row - HALO)
            elif begin < row < stop - 1:
                wy, wz, diagonal, gravity = faces.in_row(here)
                wy_of.put(row, wy)
                wz_of.put(row, wz)
                pending = store.get(row) + diagonal, store.get(row) * first.get(row) + gravity
            before = here
        for _ in range(SWEEPS):
            begin, stop = begin + 1, stop - 1
            later_ref = spare[0]
            sweep(now, later_ref, (wx_of, wy_of, wz_of), begin, stop)
            spare = [spare[1], later_ref]
            now = joined(None, later_ref, HALO)
    for part in range(rows.per_row):
        lanes = pl.ds(part * LANES, LANES)
        top_ref[:, lanes] = later_ref[part, pl.ds(HALO * layers, span, stride=layers), :]
        for step, head_ref in enumerate(head_refs):
            for held_layer in range(held):
                layer = (own ^ step) * held + held_layer
                head_ref[held_layer, :, lanes] = later_ref[part, pl.ds(HALO * layers + layer, span, stride=layers), :]


def inflow_kernel(reach_rows, cells_ref, bed_ref, slot_section_ref, owner_ref, local_ref, *refs):
    groups = lax.axis_size("layer")
    own_layer, flip, _ = position()
    top_refs = refs[:groups]
    out_ref, block_sc, lane_sc, found_sc, turned_sc = refs[groups:]
    span, breadth = top_refs[0].shape
    per_row = breadth // LANES
    blocks = groups * span * per_row
    slots = cells_ref.shape[0]
    quarter = LANES // groups
    packed = slots // groups
    for step, top_ref in enumerate(top_refs):
        number = span_at(flip, groups, own_layer ^ step)
        for part in range(per_row):
            spot = pl.ds(number * span * per_row + part, span, stride=per_row)
            turned_sc[spot, :] = top_ref[:, part * LANES:(part + 1) * LANES]

    own = lax.broadcasted_iota(jnp.int32, (packed, LANES), 1) // quarter

    def pack(ref):
        result = None
        for number in range(groups):
            shift = lax.rem((number + groups - own_layer) * quarter, LANES)
            moved = pltpu.roll(ref[pl.ds(number * packed, packed), :], shift, 1)
            result = moved if result is None else jnp.where(own == number, moved, result)
        return result

    cells = pack(cells_ref)
    block, lane = split_cells(cells, 0, breadth, LANES)
    block_sc[...] = block
    lane_sc[...] = lane
    table = jnp.concatenate(bf16_pieces(turned_sc[...].T, 2), axis=1)
    group = 32
    names = names_of(blocks)
    index = lax.broadcasted_iota(jnp.int32, (8, LANES), 0).astype(jnp.float32)

    def step(count, _):
        first = pl.multiple_of(count * group, group)
        for pair in range(0, group, 2):
            hots = jnp.concatenate(
                [
                    jnp.concatenate(one_hot(row_copies(block_sc, first, place), names), axis=0)
                    for place in (pair, pair + 1)
                ],
                axis=1,
            )
            found = lax.dot_general(
                table, jnp.concatenate([hots, hots], axis=0), (((1,), (0,)), ((), ())),
                preferred_element_type=jnp.float32,
            )
            for place in (pair, pair + 1):
                rows = lane_sc[pl.ds(first + place // 8 * 8, 8), :]
                lanes = jnp.broadcast_to(rows[place % 8:place % 8 + 1, :], (8, LANES))
                mine = found[:, (place - pair) * LANES:(place - pair + 1) * LANES]
                total = jnp.zeros((8, LANES), jnp.float32)
                for start in range(0, LANES, 8):
                    total = total + jnp.where(lanes == index + float(start), mine[start:start + 8], 0.0)
                found_sc[pl.ds(first + place, 1), :] = jnp.sum(total, axis=0, keepdims=True)
        return 0

    lax.fori_loop(0, packed // group, step, 0)
    slot_in = jnp.where(cells >= 0, pack(bed_ref) * (found_sc[...] - pack(slot_section_ref)), 0.0)
    spread = jnp.concatenate(
        [slot_in if number == 0 else pltpu.roll(slot_in, LANES - number * quarter, 1) for number in range(groups)],
        axis=0,
    )
    rows = out_ref.shape[0]
    index = lax.broadcasted_iota(jnp.int32, (rows, slots), 0)
    reach = owner_ref[...] * reach_rows + local_ref[...]
    put = jnp.where(index == reach, 1.0, 0.0).astype(jnp.bfloat16)
    total = jnp.zeros((rows, LANES), jnp.float32)
    for piece in bf16_pieces(spread, 3):
        total = total + lax.dot_general(
            put, piece, (((1,), (0,)), ((), ())), preferred_element_type=jnp.float32
        )
    out_ref[...] = total


def result_kernel(terms_ref, *refs):
    groups = lax.axis_size("layer")
    back_refs = refs[:groups]
    head_hbm, inflow_ref, sems = refs[groups:]
    _, span, _ = back_refs[0].shape
    own, flip, _ = position()
    copies = []
    for step, back_ref in enumerate(back_refs):
        rows = pl.ds(pl.multiple_of(span_at(flip, groups, own ^ step) * span, span), span)
        copies.append(pltpu.make_async_copy(back_ref, head_hbm.at[:, rows, :], sems.at[step]))
        copies[-1].start()
    total = terms_ref[0]
    for tile in range(1, terms_ref.shape[0]):
        total = total + terms_ref[tile]
    inflow_ref[...] = total[:, :inflow_ref.shape[1]]
    for copy in copies:
        copy.wait()


def call(kernel, out_shape, in_specs, scratch, flops, moved, vmem=VMEM_LIMIT, out_specs=None):
    single = not isinstance(out_shape, (tuple, list))
    return pl.pallas_call(
        kernel,
        out_shape=out_shape,
        in_specs=in_specs,
        out_specs=out_specs or (in_vmem if single else tuple(in_vmem for _ in out_shape)),
        scratch_shapes=scratch,
        compiler_params=pltpu.CompilerParams(vmem_limit_bytes=vmem),
        cost_estimate=pl.CostEstimate(flops=flops, bytes_accessed=moved, transcendentals=0),
    )


def on_device(
    head_start,
    soil_class,
    land_mask,
    ks_table,
    alpha_table,
    store_table,
    section,
    cross_owner,
    cross_local,
    node_cell,
    bed_cond,
):
    held, across, breadth = head_start.shape
    reach_rows, node_count = section.shape
    tiles = lax.axis_size("tile")
    groups = lax.axis_size("layer")
    layers = held * groups
    span = across // groups
    per_row = breadth // LANES
    blocks = span * per_row
    near = [(i, i ^ 1) for i in range(groups)]
    far = []
    for upper in range(tiles):
        far += [(upper * groups + i, upper * groups + (i ^ (groups - 1))) for i in range(1, groups - 1)]
        if upper + 1 < tiles:
            index = groups - 1 if upper % 2 == 0 else 0
            one, two = upper * groups + index, (upper + 1) * groups + index
            far += [(one, two), (two, one)]

    cells = node_cell[0]
    bed = bed_cond[0]
    slots = cells.shape[0]

    def exchange(parts):
        received = [parts[0]]
        for step in range(1, groups):
            received.append(lax.ppermute(parts[step], "layer", [(i, i ^ step) for i in range(groups)]))
        return received

    field_bytes = held * across * breadth * 4
    spread = call(
        spread_kernel, jax.ShapeDtypeStruct((tiles, reach_rows, node_count), jnp.float32), [in_hbm],
        [pltpu.VMEM(section.shape, jnp.float32), pltpu.SemaphoreType.DMA(())], 0, 0, VMEM_MOST,
    )(section)
    *own_blocks, land = call(
        prepare_kernel,
        (jax.ShapeDtypeStruct((2, held, span, breadth), jnp.float32),) * groups
        + (jax.ShapeDtypeStruct((span, breadth), jnp.float32),),
        [in_hbm] * 3,
        [
            pltpu.VMEM(head_start.shape, jnp.float32),
            pltpu.VMEM(soil_class.shape, jnp.int32),
            pltpu.VMEM(land_mask.shape, jnp.int32),
            pltpu.SemaphoreType.DMA((1 + 2 * held,)),
        ],
        0, 4 * field_bytes, VMEM_MOST,
    )(head_start, soil_class, land_mask)
    whole_section = lax.all_to_all(spread, "tile", 0, 0).reshape(tiles * reach_rows, node_count)
    received = exchange(own_blocks)

    node_scratch = pltpu.VMEM((slots, LANES), jnp.float32)
    riv_shape = jax.ShapeDtypeStruct((blocks, LANES), jnp.float32)
    node_bytes = slots * LANES * 4
    edges = jax.ShapeDtypeStruct(((2 * layers + 3) * HALO, breadth), jnp.float32)
    diag, rhs, slot_section, near_edge, far_edge = call(
        functools.partial(river_kernel, breadth, reach_rows),
        (riv_shape, riv_shape, jax.ShapeDtypeStruct((slots, node_count), jnp.float32), edges, edges),
        [in_vmem] * (6 + groups),
        [node_scratch] * 6 + [pltpu.VMEM((span * breadth // BLOCK, LANES), jnp.float32)],
        8 * span * breadth * slots * LANES, 4 * node_bytes,
    )(cells, bed, whole_section, cross_owner, cross_local, land, *received)
    near_halo = lax.ppermute(near_edge, "layer", near)
    far_halo = lax.ppermute(far_edge, FLAT, far)

    window = span + 2 * HALO
    cells_held = layers * span * breadth
    own_field = jax.ShapeDtypeStruct((per_row, span * layers, LANES), jnp.float32)
    field = pltpu.VMEM((per_row, window * layers, LANES), jnp.float32)
    staged = call(
        stage_kernel, (own_field,) * 9,
        [in_smem] * 3 + [in_vmem] * (1 + groups), [pltpu.VMEM(own_field.shape, jnp.float32)],
        60 * cells_held, 40 * cells_held,
    )(ks_table, alpha_table, store_table, land, *received)
    head_shape = jax.ShapeDtypeStruct((held, span, breadth), jnp.float32)
    *heads, top = call(
        flow_kernel,
        (head_shape,) * groups + (jax.ShapeDtypeStruct((span, breadth), jnp.float32),),
        [in_smem] * 3 + [in_vmem] * (5 + len(staged)),
        [field] * 12
        + [pltpu.VMEM((window, breadth), jnp.float32)]
        + [pltpu.VMEM((window * per_row, LANES), jnp.float32)] * 2,
        200 * cells_held, 60 * cells_held,
    )(ks_table, alpha_table, store_table, land, near_halo, far_halo, diag, rhs, *staged)
    tops = exchange([top] * groups)
    backs = exchange(heads)

    packed = pltpu.VMEM((slots // groups, LANES), jnp.float32)
    partial = call(
        functools.partial(inflow_kernel, reach_rows),
        jax.ShapeDtypeStruct((tiles * reach_rows, node_count), jnp.float32),
        [in_vmem] * (5 + groups),
        [packed] * 3 + [pltpu.VMEM((across * per_row, LANES), jnp.float32)],
        4 * across * breadth * slots * node_count // groups, 8 * node_bytes,
    )(cells, bed, slot_section, cross_owner, cross_local, *tops)
    terms = lax.all_to_all(partial.reshape(tiles, reach_rows, node_count), "tile", 0, 0)
    return call(
        result_kernel,
        (
            jax.ShapeDtypeStruct(head_start.shape, jnp.float32),
            jax.ShapeDtypeStruct((reach_rows, node_count // groups), jnp.float32),
        ),
        [in_vmem] * (1 + groups), [pltpu.SemaphoreType.DMA((groups,))], 0, 2 * field_bytes,
        out_specs=(in_hbm, in_vmem),
    )(terms, *backs)


def solution(mesh):
    placed = (
        P("layer", "tile", None),
        P("layer", "tile", None),
        P("tile", None),
        P(),
        P(),
        P(),
        P("tile", None),
        P("tile", None),
        P("tile", None),
        P("tile", None, None),
        P("tile", None, None),
    )
    return jax.shard_map(
        on_device,
        mesh=mesh,
        in_specs=placed,
        out_specs=(P("layer", "tile", None), P("tile", "layer")),
        check_vma=False,
    )
```

```python
import functools

import jax
import jax.numpy as jnp
from jax import lax
from jax.experimental import pallas as pl
from jax.experimental.pallas import tpu as pltpu
from jax.sharding import PartitionSpec as P

ITERS = 2
SWEEPS = 3

LATERAL = 1.0
VERTICAL = 2.0
GRAVITY = 1.0

HALO = ITERS * SWEEPS
BLOCK = 64
LANES = 128
VMEM_LIMIT = 32 * 1024 * 1024
VMEM_MOST = 60 * 1024 * 1024
FLAT = ("tile", "layer")

in_vmem = pl.BlockSpec(memory_space=pltpu.VMEM)
in_hbm = pl.BlockSpec(memory_space=pltpu.HBM)
in_smem = pl.BlockSpec(memory_space=pltpu.SMEM)


def bf16_pieces(value, count):
    pieces = []
    for _ in range(count):
        piece = value.astype(jnp.bfloat16)
        pieces.append(piece)
        value = value - piece.astype(jnp.float32)
    return pieces


def reciprocal(value):
    guess = pl.reciprocal(value, approx=True)
    return guess * (2.0 - value * guess)


def names_of(size):
    index = lax.broadcasted_iota(jnp.int32, (16, LANES), 0)
    return [(index + start).astype(jnp.float32).astype(jnp.bfloat16) for start in range(0, size, 16)]


def one_hot(row, names):
    one = jnp.ones((16, LANES), jnp.bfloat16)
    zero = jnp.zeros((16, LANES), jnp.bfloat16)
    return [jnp.maximum(one - jnp.abs(row - name), zero) for name in names]


def row_copies(ref, first, place):
    rows = ref[pl.ds(pl.multiple_of(first + place // 8 * 8, 8), 8), :]
    return jnp.broadcast_to(rows[place % 8:place % 8 + 1, :], (16, LANES)).astype(jnp.bfloat16)


def position():
    tile, layer = lax.axis_index("tile"), lax.axis_index("layer")
    groups = lax.axis_size("layer")
    flip = lax.rem(tile, 2)
    return layer, flip, jnp.where(flip == 1, groups - 1 - layer, layer)


def span_at(flip, groups, layer):
    return jnp.where(flip == 1, groups - 1 - layer, layer)


def split_cells(cells, first_row, breadth, width):
    local = cells - first_row * breadth
    shift = width.bit_length() - 1
    block = jnp.where(cells < 0, -1, local >> shift)
    return block.astype(jnp.float32), (local & (width - 1)).astype(jnp.float32)


def river_kernel(
    breadth, span, reach_rows, cells_ref, bed_ref, section_ref, owner_ref, local_ref,
    diag_ref, rhs_ref, slot_section_ref, block_sc, spot_sc, dhigh_sc, dlow_sc, rhigh_sc, rlow_sc, sum_sc,
):
    _, _, number = position()
    rows = section_ref.shape[0]
    slots = owner_ref.shape[1]
    index = lax.broadcasted_iota(jnp.int32, (rows, slots), 0)
    reach = owner_ref[...] * reach_rows + local_ref[...]
    pick = jnp.where(index == reach, 1.0, 0.0).astype(jnp.bfloat16)
    picked = jnp.zeros(slot_section_ref.shape, jnp.float32)
    for piece in bf16_pieces(section_ref[...], 3):
        picked = picked + lax.dot_general(
            pick, piece, (((0,), (0,)), ((), ())), preferred_element_type=jnp.float32
        )
    slot_section_ref[...] = picked

    block, spot = split_cells(cells_ref[...], number * span, breadth, BLOCK)
    block_sc[...] = block
    spot_sc[...] = spot
    bed = bed_ref[...]
    for value, high_sc, low_sc in ((bed, dhigh_sc, dlow_sc), (bed * picked, rhigh_sc, rlow_sc)):
        high, low = bf16_pieces(value, 2)
        high_sc[...] = high.astype(jnp.float32)
        low_sc[...] = low.astype(jnp.float32)
    share = LANES // BLOCK
    blocks = share * diag_ref.shape[0]
    group = 32
    block_names, spot_names = names_of(blocks), names_of(BLOCK)

    def matmul(first, places):
        left, right = [], []
        for place in places:
            left.append(jnp.concatenate(one_hot(row_copies(block_sc, first, place), block_names), axis=0))
            hot = one_hot(row_copies(spot_sc, first, place), spot_names)
            values = [row_copies(ref, first, place) for ref in (dhigh_sc, dlow_sc, rhigh_sc, rlow_sc)]
            right.append(jnp.concatenate([tile * value for value in values for tile in hot], axis=0))
        return lax.dot_general(
            jnp.concatenate(left, axis=1),
            jnp.concatenate(right, axis=1),
            (((1,), (1,)), ((), ())),
            preferred_element_type=jnp.float32,
        )

    def step(count, total):
        first = count * group
        half = group // 2
        return total + (matmul(first, range(half)) + matmul(first, range(half, group)))

    total = lax.fori_loop(0, slots // group, step, jnp.zeros((blocks, 4 * BLOCK), jnp.float32))
    low_half = lax.broadcasted_iota(jnp.int32, diag_ref.shape, 1) < BLOCK
    for count, ref in ((0, diag_ref), (1, rhs_ref)):
        part = total[:, count * LANES:(count + 1) * LANES]
        sum_sc[...] = part + pltpu.roll(part, BLOCK, 1)
        ref[...] = jnp.where(
            low_half, sum_sc[pl.ds(0, blocks // share, stride=share), :], sum_sc[pl.ds(1, blocks // share, stride=share), :]
        )


def edge_kernel(land_ref, diag_ref, rhs_ref, *refs):
    block_refs, (near_ref, far_ref) = refs[:-2], refs[-2:]
    _, held, span, breadth = block_refs[0].shape
    _, _, number = position()
    odd = lax.rem(number, 2) == 1
    per_row = breadth // LANES

    def put_edges(entry, top, bottom, lanes=slice(None)):
        near_ref[pl.ds(entry * HALO, HALO), lanes] = jnp.where(odd, top, bottom)
        far_ref[pl.ds(entry * HALO, HALO), lanes] = jnp.where(odd, bottom, top)

    entry = 0
    for kind in range(2):
        for block_ref in block_refs:
            for held_layer in range(held):
                put_edges(entry, block_ref[kind, held_layer, :HALO, :], block_ref[kind, held_layer, span - HALO:, :])
                entry += 1
    put_edges(entry, land_ref[:HALO, :], land_ref[span - HALO:, :])
    for ref in (diag_ref, rhs_ref):
        entry += 1
        for part in range(per_row):
            top = ref[pl.ds(part, HALO, stride=per_row), :]
            bottom = ref[pl.ds((span - HALO) * per_row + part, HALO, stride=per_row), :]
            put_edges(entry, top, bottom, slice(part * LANES, (part + 1) * LANES))


def spread_kernel(section_hbm, spread_ref, section_ref, sem):
    copy = pltpu.make_async_copy(section_hbm, section_ref, sem)
    copy.start()
    copy.wait()
    for tile in range(spread_ref.shape[0]):
        spread_ref[tile] = section_ref[...]


def prepare_kernel(head_hbm, soil_hbm, land_hbm, after_hbm, *refs):
    del after_hbm
    groups = lax.axis_size("layer")
    block_refs, land_out_ref = refs[:groups], refs[groups]
    head_ref, soil_ref, land_ref, sems = refs[groups + 1:]
    held, across, _ = head_ref.shape
    span = across // groups
    pairs = [(land_hbm, land_ref)]
    for layer in range(held):
        pairs += [(head_hbm.at[layer], head_ref.at[layer]), (soil_hbm.at[layer], soil_ref.at[layer])]
    copies = [pltpu.make_async_copy(here, there, sems.at[k]) for k, (here, there) in enumerate(pairs)]
    for copy in copies:
        copy.start()
    own, flip, _ = position()

    def rows_of(target):
        return pl.ds(pl.multiple_of(span_at(flip, groups, target) * span, span), span)

    copies[0].wait()
    land_out_ref[...] = land_ref[rows_of(own), :].astype(jnp.float32)
    for layer in range(held):
        copies[1 + 2 * layer].wait()
        copies[2 + 2 * layer].wait()
        for step, out_ref in enumerate(block_refs):
            rows = rows_of(own ^ step)
            out_ref[0, layer] = head_ref[layer, rows, :]
            out_ref[1, layer] = soil_ref[layer, rows, :].astype(jnp.float32)


class Rows:
    def __init__(self, layers, breadth):
        self.layers, self.breadth, self.per_row = layers, breadth, breadth // LANES

    def get(self, ref, row):
        spot = pl.ds(row * self.layers, self.layers)
        return jnp.concatenate([ref[part, spot, :] for part in range(self.per_row)], axis=1)

    def put(self, ref, row, value):
        spot = pl.ds(row * self.layers, self.layers)
        for part in range(self.per_row):
            ref[part, spot, :] = value[:, part * LANES:(part + 1) * LANES]

    def put_layer(self, ref, layer, row, value):
        for part in range(self.per_row):
            spot = pl.ds(row * self.layers + layer, value.shape[0], stride=self.layers)
            ref[part, spot, :] = value[:, part * LANES:(part + 1) * LANES]

    def east(self, field):
        return pltpu.roll(field, self.breadth - 1, 1)

    def west(self, field):
        return pltpu.roll(field, 1, 1)

    def below(self, field):
        return pltpu.roll(field, self.layers - 1, 0)

    def above(self, field):
        return pltpu.roll(field, 1, 0)


class Joined:
    def __init__(self, rows, own, full, first, last):
        self.rows, self.own, self.full, self.first, self.last = rows, own, full, first, last

    def get(self, row):
        if self.first <= row < self.last:
            return self.rows.get(self.own, row - self.first)
        return self.rows.get(self.full, row)

    def put(self, row, value):
        self.rows.put(self.full, row, value)


class Faces:
    def __init__(self, rows):
        self.rows = rows
        level = lax.broadcasted_iota(jnp.int32, (rows.layers, rows.breadth), 0)
        column = lax.broadcasted_iota(jnp.int32, (rows.layers, rows.breadth), 1)
        self.not_bottom = level < rows.layers - 1
        self.not_last = column < rows.breadth - 1

    def conduct(self, ks, alpha, head, land):
        cond = ks * jnp.exp(alpha * jnp.minimum(head, 0.0))
        return cond, cond * land

    def face(self, factor, here, there):
        return factor * 2.0 * here[1] * there[1] * reciprocal(here[0] + there[0])

    def between_rows(self, here, there):
        return self.face(LATERAL, here, there)

    def in_row(self, here):
        rows = self.rows
        cond, opened = here
        wy = self.face(LATERAL, here, (rows.east(cond), rows.east(opened)))
        wz = self.face(VERTICAL, here, (rows.below(cond), rows.below(opened)))
        wy = jnp.where(self.not_last, wy, 0.0)
        wz = jnp.where(self.not_bottom, wz, 0.0)
        wz_above = rows.above(wz)
        return wy, wz, wy + rows.west(wy) + wz + wz_above, GRAVITY * (wz_above - wz)


def lane_tables(refs, layers):
    lane = lax.broadcasted_iota(jnp.int32, (layers, LANES), 1)
    tables = []
    for ref in refs:
        table = jnp.zeros((layers, LANES), jnp.float32)
        for kind in range(ref.shape[0]):
            table = jnp.where(lane == kind, ref[kind], table)
        tables.append(table)
    return tables


def look_up(rows, table, soil):
    parts = [
        jnp.take_along_axis(table, soil[:, part * LANES:(part + 1) * LANES], axis=1, mode="promise_in_bounds")
        for part in range(rows.per_row)
    ]
    return jnp.concatenate(parts, axis=1)


def stage_kernel(ks_ref, alpha_ref, store_ref, land_ref, *refs):
    groups = lax.axis_size("layer")
    own, _, _ = position()
    block_refs = refs[:groups]
    first_out, ks_out, alpha_out, store_out, wx_out, wy_out, wz_out, diag_out, base_out, soil_sc = refs[groups:]
    _, held, span, breadth = block_refs[0].shape
    layers = groups * held
    rows = Rows(layers, breadth)
    faces = Faces(rows)

    for step, block_ref in enumerate(block_refs):
        for held_layer in range(held):
            layer = (own ^ step) * held + held_layer
            rows.put_layer(first_out, layer, 0, block_ref[0, held_layer])
            rows.put_layer(soil_sc, layer, 0, block_ref[1, held_layer])
    tables = lane_tables((ks_ref, alpha_ref, store_ref), layers)
    before = None
    for row in range(span):
        soil = rows.get(soil_sc, row).astype(jnp.int32)
        ks, alpha, store = [look_up(rows, table, soil) for table in tables]
        first = rows.get(first_out, row)
        here = faces.conduct(ks, alpha, first, land_ref[pl.ds(row, 1), :])
        wy, wz, diagonal, gravity = faces.in_row(here)
        for ref, value in (
            (ks_out, ks), (alpha_out, alpha), (store_out, store), (wy_out, wy), (wz_out, wz),
            (diag_out, store + diagonal), (base_out, store * first + gravity),
        ):
            rows.put(ref, row, value)
        if row > 0:
            rows.put(wx_out, row - 1, faces.between_rows(before, here))
        before = here


def flow_kernel(kst_ref, alphat_ref, storet_ref, land_ref, near_ref, far_ref, diag_ref, rhs_ref, *refs):
    groups = lax.axis_size("layer")
    own, _, number = position()
    end = (number == 0) | (number == groups - 1)
    far_partner = jnp.where(end, own, own ^ (groups - 1))
    first_ref, ks_ref, alpha_ref, store_ref, wx_ref, wy_ref, wz_ref, partial_ref, gravity_ref = refs[:9]
    head_refs, top_ref = refs[9:9 + groups], refs[9 + groups]
    (
        first_sc, soil_sc, ks_sc, alpha_sc, store_sc, wx_sc, wy_sc, wz_sc, base_sc, inv_sc, ping_sc, pong_sc,
        land_sc, dtop_sc, rtop_sc,
    ) = refs[10 + groups:]
    held, span, breadth = head_refs[0].shape
    layers = groups * held
    window = span + 2 * HALO
    last_own = HALO + span
    rows = Rows(layers, breadth)
    faces = Faces(rows)
    side = HALO * rows.per_row

    land_sc[pl.ds(HALO, span), :] = land_ref[...]
    dtop_sc[pl.ds(side, span * rows.per_row), :] = diag_ref[...]
    rtop_sc[pl.ds(side, span * rows.per_row), :] = rhs_ref[...]

    def put_halo(ref, partner, row):
        def entry(number):
            return ref[pl.ds(number * HALO, HALO), :]

        for count in range(layers):
            layer = (partner ^ (count // held)) * held + count % held
            rows.put_layer(first_sc, layer, row, entry(count))
            rows.put_layer(soil_sc, layer, row, entry(layers + count))
        land_sc[pl.ds(row, HALO), :] = entry(2 * layers)
        for count, top_sc in ((2 * layers + 1, dtop_sc), (2 * layers + 2, rtop_sc)):
            value = entry(count)
            for part in range(rows.per_row):
                spot = pl.ds(row * rows.per_row + part, HALO, stride=rows.per_row)
                top_sc[spot, :] = value[:, part * LANES:(part + 1) * LANES]

    for odd, above_ref, below_ref in ((0, far_ref, near_ref), (1, near_ref, far_ref)):
        @pl.when(lax.rem(number, 2) == odd)
        def _(above_ref=above_ref, below_ref=below_ref):
            for ref, row in ((above_ref, 0), (below_ref, last_own)):
                put_halo(ref, own ^ 1 if ref is near_ref else far_partner, row)

    tables = lane_tables((kst_ref, alphat_ref, storet_ref), layers)
    for row in [*range(HALO), *range(last_own, window)]:
        soil = rows.get(soil_sc, row).astype(jnp.int32)
        for table, ref in zip(tables, (ks_sc, alpha_sc, store_sc)):
            rows.put(ref, row, look_up(rows, table, soil))

    def joined(own, full, last=last_own):
        return Joined(rows, own, full, HALO, last)

    first, ks, alpha, store = [
        joined(own, full)
        for own, full in ((first_ref, first_sc), (ks_ref, ks_sc), (alpha_ref, alpha_sc), (store_ref, store_sc))
    ]
    top = lax.broadcasted_iota(jnp.int32, (layers, breadth), 0) == 0

    def riv_row(ref, row):
        parts = [
            jnp.broadcast_to(ref[pl.ds(row * rows.per_row + part, 1), :], (layers, LANES))
            for part in range(rows.per_row)
        ]
        return jnp.where(top, jnp.concatenate(parts, axis=1), 0.0)

    def finish(row, diagonal, base):
        rows.put(inv_sc, row, reciprocal(diagonal + riv_row(dtop_sc, row)))
        rows.put(base_sc, row, base + riv_row(rtop_sc, row))

    def conduct(now, row):
        return faces.conduct(ks.get(row), alpha.get(row), now.get(row), land_sc[pl.ds(row, 1), :])

    def sweep(now, later_ref, weights, begin, stop):
        wx_of, wy_of, wz_of = weights
        before, here, wx_before = now.get(begin - 1), now.get(begin), wx_of.get(begin - 1)
        for row in range(begin, stop):
            after = now.get(row + 1)
            wx, wy, wz = wx_of.get(row), wy_of.get(row), wz_of.get(row)
            total = rows.get(base_sc, row) + wx_before * before + wx * after
            total = total + wy * rows.east(here) + rows.west(wy * here)
            total = total + wz * rows.below(here) + rows.above(wz * here)
            rows.put(later_ref, row, total * rows.get(inv_sc, row))
            before, here, wx_before = here, after, wx

    now, spare = first, [ping_sc, pong_sc]
    begin, stop = 0, window
    for picard in range(ITERS):
        early = picard == 0
        wx_of = joined(wx_ref, wx_sc, last_own - 1 if early else HALO)
        wy_of, wz_of = [joined(own, full, last_own if early else HALO) for own, full in ((wy_ref, wy_sc), (wz_ref, wz_sc))]
        before, wx_before = None, None
        for row in range(begin, stop):
            staged = early and HALO <= row < last_own
            here = conduct(now, row) if not staged or row in (HALO, last_own - 1) else None
            if row > begin:
                if early and HALO <= row - 1 < last_own - 1:
                    wx = wx_of.get(row - 1)
                else:
                    wx = faces.between_rows(before, here)
                    wx_of.put(row - 1, wx)
                if row - 1 > begin:
                    diagonal, base = pending
                    finish(row - 1, diagonal + wx_before + wx, base)
                wx_before = wx
            if staged:
                pending = rows.get(partial_ref, row - HALO), rows.get(gravity_ref, row - HALO)
            elif begin < row < stop - 1:
                wy, wz, diagonal, gravity = faces.in_row(here)
                wy_of.put(row, wy)
                wz_of.put(row, wz)
                pending = store.get(row) + diagonal, store.get(row) * first.get(row) + gravity
            before = here
        for _ in range(SWEEPS):
            begin, stop = begin + 1, stop - 1
            later_ref = spare[0]
            sweep(now, later_ref, (wx_of, wy_of, wz_of), begin, stop)
            spare = [spare[1], later_ref]
            now = joined(None, later_ref, HALO)
    for part in range(rows.per_row):
        lanes = pl.ds(part * LANES, LANES)
        top_ref[:, lanes] = later_ref[part, pl.ds(HALO * layers, span, stride=layers), :]
        for step, head_ref in enumerate(head_refs):
            for held_layer in range(held):
                layer = (own ^ step) * held + held_layer
                head_ref[held_layer, :, lanes] = later_ref[part, pl.ds(HALO * layers + layer, span, stride=layers), :]


def inflow_kernel(reach_rows, cells_ref, bed_ref, slot_section_ref, owner_ref, local_ref, *refs):
    groups = lax.axis_size("layer")
    own_layer, flip, _ = position()
    top_refs = refs[:groups]
    out_ref, block_sc, lane_sc, found_sc, turned_sc = refs[groups:]
    span, breadth = top_refs[0].shape
    per_row = breadth // LANES
    blocks = groups * span * per_row
    slots = cells_ref.shape[0]
    quarter = LANES // groups
    packed = slots // groups
    for step, top_ref in enumerate(top_refs):
        number = span_at(flip, groups, own_layer ^ step)
        for part in range(per_row):
            spot = pl.ds(number * span * per_row + part, span, stride=per_row)
            turned_sc[spot, :] = top_ref[:, part * LANES:(part + 1) * LANES]

    own = lax.broadcasted_iota(jnp.int32, (packed, LANES), 1) // quarter

    def pack(ref):
        result = None
        for number in range(groups):
            shift = lax.rem((number + groups - own_layer) * quarter, LANES)
            moved = pltpu.roll(ref[pl.ds(number * packed, packed), :], shift, 1)
            result = moved if result is None else jnp.where(own == number, moved, result)
        return result

    cells = pack(cells_ref)
    block, lane = split_cells(cells, 0, breadth, LANES)
    block_sc[...] = block
    lane_sc[...] = lane
    table = jnp.concatenate(bf16_pieces(turned_sc[...].T, 2), axis=1)
    group = 32
    names = names_of(blocks)
    index = lax.broadcasted_iota(jnp.int32, (8, LANES), 0).astype(jnp.float32)

    def step(count, _):
        first = pl.multiple_of(count * group, group)
        for pair in range(0, group, 2):
            hots = jnp.concatenate(
                [
                    jnp.concatenate(one_hot(row_copies(block_sc, first, place), names), axis=0)
                    for place in (pair, pair + 1)
                ],
                axis=1,
            )
            found = lax.dot_general(
                table, jnp.concatenate([hots, hots], axis=0), (((1,), (0,)), ((), ())),
                preferred_element_type=jnp.float32,
            )
            for place in (pair, pair + 1):
                rows = lane_sc[pl.ds(first + place // 8 * 8, 8), :]
                lanes = jnp.broadcast_to(rows[place % 8:place % 8 + 1, :], (8, LANES))
                mine = found[:, (place - pair) * LANES:(place - pair + 1) * LANES]
                total = jnp.zeros((8, LANES), jnp.float32)
                for start in range(0, LANES, 8):
                    total = total + jnp.where(lanes == index + float(start), mine[start:start + 8], 0.0)
                found_sc[pl.ds(first + place, 1), :] = jnp.sum(total, axis=0, keepdims=True)
        return 0

    lax.fori_loop(0, packed // group, step, 0)
    slot_in = jnp.where(cells >= 0, pack(bed_ref) * (found_sc[...] - pack(slot_section_ref)), 0.0)
    spread = jnp.concatenate(
        [slot_in if number == 0 else pltpu.roll(slot_in, LANES - number * quarter, 1) for number in range(groups)],
        axis=0,
    )
    rows = out_ref.shape[0]
    index = lax.broadcasted_iota(jnp.int32, (rows, slots), 0)
    reach = owner_ref[...] * reach_rows + local_ref[...]
    put = jnp.where(index == reach, 1.0, 0.0).astype(jnp.bfloat16)
    total = jnp.zeros((rows, LANES), jnp.float32)
    for piece in bf16_pieces(spread, 3):
        total = total + lax.dot_general(
            put, piece, (((1,), (0,)), ((), ())), preferred_element_type=jnp.float32
        )
    out_ref[...] = total


def head_kernel(*refs):
    groups = lax.axis_size("layer")
    back_refs, (head_hbm, sems) = refs[:groups], refs[groups:]
    _, span, _ = back_refs[0].shape
    own, flip, _ = position()
    copies = []
    for step, back_ref in enumerate(back_refs):
        rows = pl.ds(pl.multiple_of(span_at(flip, groups, own ^ step) * span, span), span)
        copies.append(pltpu.make_async_copy(back_ref, head_hbm.at[:, rows, :], sems.at[step]))
        copies[-1].start()
    for copy in copies:
        copy.wait()


def call(kernel, out_shape, in_specs, scratch, flops, moved, vmem=VMEM_LIMIT, out_specs=None):
    single = not isinstance(out_shape, (tuple, list))
    return pl.pallas_call(
        kernel,
        out_shape=out_shape,
        in_specs=in_specs,
        out_specs=out_specs or (in_vmem if single else tuple(in_vmem for _ in out_shape)),
        scratch_shapes=scratch,
        compiler_params=pltpu.CompilerParams(vmem_limit_bytes=vmem),
        cost_estimate=pl.CostEstimate(flops=flops, bytes_accessed=moved, transcendentals=0),
    )


def on_device(
    head_start,
    soil_class,
    land_mask,
    ks_table,
    alpha_table,
    store_table,
    section,
    cross_owner,
    cross_local,
    node_cell,
    bed_cond,
):
    held, across, breadth = head_start.shape
    reach_rows, node_count = section.shape
    tiles = lax.axis_size("tile")
    groups = lax.axis_size("layer")
    layers = held * groups
    span = across // groups
    per_row = breadth // LANES
    blocks = span * per_row
    near = [(i, i ^ 1) for i in range(groups)]
    far = []
    for upper in range(tiles):
        far += [(upper * groups + i, upper * groups + (i ^ (groups - 1))) for i in range(1, groups - 1)]
        if upper + 1 < tiles:
            index = groups - 1 if upper % 2 == 0 else 0
            one, two = upper * groups + index, (upper + 1) * groups + index
            far += [(one, two), (two, one)]

    cells = node_cell[0]
    bed = bed_cond[0]
    slots = cells.shape[0]

    def exchange(parts):
        received = [parts[0]]
        for step in range(1, groups):
            received.append(lax.ppermute(parts[step], "layer", [(i, i ^ step) for i in range(groups)]))
        return received

    field_bytes = held * across * breadth * 4
    spread = call(
        spread_kernel, jax.ShapeDtypeStruct((tiles, reach_rows, node_count), jnp.float32), [in_hbm],
        [pltpu.VMEM(section.shape, jnp.float32), pltpu.SemaphoreType.DMA(())], 0, 0, VMEM_MOST,
    )(section)
    whole_section = lax.all_to_all(spread, "tile", 0, 0).reshape(tiles * reach_rows, node_count)
    *own_blocks, land = call(
        prepare_kernel,
        (jax.ShapeDtypeStruct((2, held, span, breadth), jnp.float32),) * groups
        + (jax.ShapeDtypeStruct((span, breadth), jnp.float32),),
        [in_hbm] * 4,
        [
            pltpu.VMEM(head_start.shape, jnp.float32),
            pltpu.VMEM(soil_class.shape, jnp.int32),
            pltpu.VMEM(land_mask.shape, jnp.int32),
            pltpu.SemaphoreType.DMA((1 + 2 * held,)),
        ],
        0, 4 * field_bytes, VMEM_MOST,
    )(head_start, soil_class, land_mask, whole_section)
    received = exchange(own_blocks)

    node_scratch = pltpu.VMEM((slots, LANES), jnp.float32)
    riv_shape = jax.ShapeDtypeStruct((blocks, LANES), jnp.float32)
    node_bytes = slots * LANES * 4
    diag, rhs, slot_section = call(
        functools.partial(river_kernel, breadth, span, reach_rows),
        (riv_shape, riv_shape, jax.ShapeDtypeStruct((slots, node_count), jnp.float32)),
        [in_vmem] * 5,
        [node_scratch] * 6 + [pltpu.VMEM((span * breadth // BLOCK, LANES), jnp.float32)],
        8 * span * breadth * slots * LANES, 4 * node_bytes,
    )(cells, bed, whole_section, cross_owner, cross_local)
    edges = jax.ShapeDtypeStruct(((2 * layers + 3) * HALO, breadth), jnp.float32)
    near_edge, far_edge = call(
        edge_kernel, (edges, edges), [in_vmem] * (3 + groups), [], 0, 8 * layers * HALO * breadth * 4,
    )(land, diag, rhs, *received)
    near_halo = lax.ppermute(near_edge, "layer", near)
    far_halo = lax.ppermute(far_edge, FLAT, far)

    window = span + 2 * HALO
    cells_held = layers * span * breadth
    own_field = jax.ShapeDtypeStruct((per_row, span * layers, LANES), jnp.float32)
    field = pltpu.VMEM((per_row, window * layers, LANES), jnp.float32)
    staged = call(
        stage_kernel, (own_field,) * 9,
        [in_smem] * 3 + [in_vmem] * (1 + groups), [pltpu.VMEM(own_field.shape, jnp.float32)],
        60 * cells_held, 40 * cells_held,
    )(ks_table, alpha_table, store_table, land, *received)
    head_shape = jax.ShapeDtypeStruct((held, span, breadth), jnp.float32)
    *heads, top = call(
        flow_kernel,
        (head_shape,) * groups + (jax.ShapeDtypeStruct((span, breadth), jnp.float32),),
        [in_smem] * 3 + [in_vmem] * (5 + len(staged)),
        [field] * 12
        + [pltpu.VMEM((window, breadth), jnp.float32)]
        + [pltpu.VMEM((window * per_row, LANES), jnp.float32)] * 2,
        200 * cells_held, 60 * cells_held,
    )(ks_table, alpha_table, store_table, land, near_halo, far_halo, diag, rhs, *staged)
    tops = exchange([top] * groups)
    backs = exchange(heads)

    packed = pltpu.VMEM((slots // groups, LANES), jnp.float32)
    partial = call(
        functools.partial(inflow_kernel, reach_rows),
        jax.ShapeDtypeStruct((tiles * reach_rows, node_count), jnp.float32),
        [in_vmem] * (5 + groups),
        [packed] * 3 + [pltpu.VMEM((across * per_row, LANES), jnp.float32)],
        4 * across * breadth * slots * node_count // groups, 8 * node_bytes,
    )(cells, bed, slot_section, cross_owner, cross_local, *tops)
    partial, *backs = lax.optimization_barrier((partial, *backs))
    terms = lax.all_to_all(partial.reshape(tiles, reach_rows, node_count), "tile", 0, 0)
    head = call(
        head_kernel, jax.ShapeDtypeStruct(head_start.shape, jnp.float32), [in_vmem] * groups,
        [pltpu.SemaphoreType.DMA((groups,))], 0, 2 * field_bytes, out_specs=in_hbm,
    )(*backs)
    return head, jnp.sum(terms, axis=0)[:, :node_count // groups]


def solution(mesh):
    placed = (
        P("layer", "tile", None),
        P("layer", "tile", None),
        P("tile", None),
        P(),
        P(),
        P(),
        P("tile", None),
        P("tile", None),
        P("tile", None),
        P("tile", None, None),
        P("tile", None, None),
    )
    return jax.shard_map(
        on_device,
        mesh=mesh,
        in_specs=placed,
        out_specs=(P("layer", "tile", None), P("tile", "layer")),
        check_vma=False,
    )
```

```python
import functools

import jax
import jax.numpy as jnp
from jax import lax
from jax.experimental import pallas as pl
from jax.experimental.pallas import tpu as pltpu
from jax.sharding import PartitionSpec as P

ITERS = 2
SWEEPS = 3

LATERAL = 1.0
VERTICAL = 2.0
GRAVITY = 1.0

HALO = ITERS * SWEEPS
BLOCK = 64
LANES = 128
VMEM_LIMIT = 32 * 1024 * 1024
VMEM_MOST = 60 * 1024 * 1024
FLAT = ("tile", "layer")

in_vmem = pl.BlockSpec(memory_space=pltpu.VMEM)
in_hbm = pl.BlockSpec(memory_space=pltpu.HBM)
in_smem = pl.BlockSpec(memory_space=pltpu.SMEM)


def bf16_pieces(value, count):
    pieces = []
    for _ in range(count):
        piece = value.astype(jnp.bfloat16)
        pieces.append(piece)
        value = value - piece.astype(jnp.float32)
    return pieces


def reciprocal(value):
    guess = pl.reciprocal(value, approx=True)
    return guess * (2.0 - value * guess)


def names_of(size):
    index = lax.broadcasted_iota(jnp.int32, (16, LANES), 0)
    return [(index + start).astype(jnp.float32).astype(jnp.bfloat16) for start in range(0, size, 16)]


def one_hot(row, names):
    one = jnp.ones((16, LANES), jnp.bfloat16)
    zero = jnp.zeros((16, LANES), jnp.bfloat16)
    return [jnp.maximum(one - jnp.abs(row - name), zero) for name in names]


def row_copies(ref, first, place):
    rows = ref[pl.ds(pl.multiple_of(first + place // 8 * 8, 8), 8), :]
    return jnp.broadcast_to(rows[place % 8:place % 8 + 1, :], (16, LANES)).astype(jnp.bfloat16)


def position():
    tile, layer = lax.axis_index("tile"), lax.axis_index("layer")
    groups = lax.axis_size("layer")
    flip = lax.rem(tile, 2)
    return layer, flip, jnp.where(flip == 1, groups - 1 - layer, layer)


def span_at(flip, groups, layer):
    return jnp.where(flip == 1, groups - 1 - layer, layer)


def split_cells(cells, first_row, breadth, width):
    local = cells - first_row * breadth
    shift = width.bit_length() - 1
    block = jnp.where(cells < 0, -1, local >> shift)
    return block.astype(jnp.float32), (local & (width - 1)).astype(jnp.float32)


def river_kernel(
    breadth, span, cells_ref, bed_ref, section_ref, reach_ref,
    diag_ref, rhs_ref, slot_section_ref, block_sc, spot_sc, dhigh_sc, dlow_sc, rhigh_sc, rlow_sc, sum_sc,
):
    _, _, number = position()
    rows = section_ref.shape[0]
    slots = reach_ref.shape[1]
    index = lax.broadcasted_iota(jnp.int32, (rows, slots), 0)
    pick = jnp.where(index == reach_ref[...], 1.0, 0.0).astype(jnp.bfloat16)
    picked = jnp.zeros(slot_section_ref.shape, jnp.float32)
    for piece in bf16_pieces(section_ref[...], 3):
        picked = picked + lax.dot_general(
            pick, piece, (((0,), (0,)), ((), ())), preferred_element_type=jnp.float32
        )
    slot_section_ref[...] = picked

    block, spot = split_cells(cells_ref[...], number * span, breadth, BLOCK)
    block_sc[...] = block
    spot_sc[...] = spot
    bed = bed_ref[...]
    for value, high_sc, low_sc in ((bed, dhigh_sc, dlow_sc), (bed * picked, rhigh_sc, rlow_sc)):
        high, low = bf16_pieces(value, 2)
        high_sc[...] = high.astype(jnp.float32)
        low_sc[...] = low.astype(jnp.float32)
    share = LANES // BLOCK
    blocks = share * diag_ref.shape[0]
    group = 32
    block_names, spot_names = names_of(blocks), names_of(BLOCK)

    def matmul(first, places):
        left, right = [], []
        for place in places:
            left.append(jnp.concatenate(one_hot(row_copies(block_sc, first, place), block_names), axis=0))
            hot = one_hot(row_copies(spot_sc, first, place), spot_names)
            values = [row_copies(ref, first, place) for ref in (dhigh_sc, dlow_sc, rhigh_sc, rlow_sc)]
            right.append(jnp.concatenate([tile * value for value in values for tile in hot], axis=0))
        return lax.dot_general(
            jnp.concatenate(left, axis=1),
            jnp.concatenate(right, axis=1),
            (((1,), (1,)), ((), ())),
            preferred_element_type=jnp.float32,
        )

    def step(count, total):
        first = count * group
        half = group // 2
        return total + (matmul(first, range(half)) + matmul(first, range(half, group)))

    total = lax.fori_loop(0, slots // group, step, jnp.zeros((blocks, 4 * BLOCK), jnp.float32))
    low_half = lax.broadcasted_iota(jnp.int32, diag_ref.shape, 1) < BLOCK
    for count, ref in ((0, diag_ref), (1, rhs_ref)):
        part = total[:, count * LANES:(count + 1) * LANES]
        sum_sc[...] = part + pltpu.roll(part, BLOCK, 1)
        ref[...] = jnp.where(
            low_half, sum_sc[pl.ds(0, blocks // share, stride=share), :], sum_sc[pl.ds(1, blocks // share, stride=share), :]
        )


def edge_kernel(land_ref, diag_ref, rhs_ref, *refs):
    block_refs, (near_ref, far_ref) = refs[:-2], refs[-2:]
    _, held, span, breadth = block_refs[0].shape
    _, _, number = position()
    odd = lax.rem(number, 2) == 1
    per_row = breadth // LANES

    def put_edges(entry, top, bottom, lanes=slice(None)):
        near_ref[pl.ds(entry * HALO, HALO), lanes] = jnp.where(odd, top, bottom)
        far_ref[pl.ds(entry * HALO, HALO), lanes] = jnp.where(odd, bottom, top)

    entry = 0
    for kind in range(2):
        for block_ref in block_refs:
            for held_layer in range(held):
                put_edges(entry, block_ref[kind, held_layer, :HALO, :], block_ref[kind, held_layer, span - HALO:, :])
                entry += 1
    put_edges(entry, land_ref[:HALO, :], land_ref[span - HALO:, :])
    for ref in (diag_ref, rhs_ref):
        entry += 1
        for part in range(per_row):
            top = ref[pl.ds(part, HALO, stride=per_row), :]
            bottom = ref[pl.ds((span - HALO) * per_row + part, HALO, stride=per_row), :]
            put_edges(entry, top, bottom, slice(part * LANES, (part + 1) * LANES))


def spread_kernel(section_hbm, owner_hbm, local_hbm, spread_ref, reach_ref, section_ref, owner_ref, local_ref, sems):
    pairs = ((section_hbm, section_ref), (owner_hbm, owner_ref), (local_hbm, local_ref))
    copies = [pltpu.make_async_copy(here, there, sems.at[k]) for k, (here, there) in enumerate(pairs)]
    for copy in copies:
        copy.start()
    for copy in copies:
        copy.wait()
    for tile in range(spread_ref.shape[0]):
        spread_ref[tile] = section_ref[...]
    reach_ref[...] = owner_ref[...] * section_ref.shape[0] + local_ref[...]


def prepare_kernel(head_hbm, soil_hbm, land_hbm, after_hbm, *refs):
    del after_hbm
    groups = lax.axis_size("layer")
    block_hbms, land_out_ref = refs[:groups], refs[groups]
    soil_ref, soil_float_ref, land_ref, in_sems, head_sems, soil_sems = refs[groups + 1:]
    held, across, _ = soil_ref.shape
    span = across // groups
    own, flip, _ = position()

    def rows_of(target):
        return pl.ds(pl.multiple_of(span_at(flip, groups, target) * span, span), span)

    copies = [pltpu.make_async_copy(soil_hbm.at[layer], soil_ref.at[layer], in_sems.at[layer]) for layer in range(held)]
    copies.append(pltpu.make_async_copy(land_hbm.at[rows_of(own), :], land_ref, in_sems.at[held]))
    heads = [
        pltpu.make_async_copy(head_hbm.at[:, rows_of(own ^ step), :], block_hbm.at[0], head_sems.at[step])
        for step, block_hbm in enumerate(block_hbms)
    ]
    for copy in copies + heads:
        copy.start()
    for layer in range(held):
        copies[layer].wait()
        soil_float_ref[layer] = soil_ref[layer].astype(jnp.float32)
    soils = [
        pltpu.make_async_copy(soil_float_ref.at[:, rows_of(own ^ step), :], block_hbm.at[1], soil_sems.at[step])
        for step, block_hbm in enumerate(block_hbms)
    ]
    for copy in soils:
        copy.start()
    copies[held].wait()
    land_out_ref[...] = land_ref[...].astype(jnp.float32)
    for copy in heads + soils:
        copy.wait()


class Rows:
    def __init__(self, layers, breadth):
        self.layers, self.breadth, self.per_row = layers, breadth, breadth // LANES

    def get(self, ref, row):
        spot = pl.ds(row * self.layers, self.layers)
        return jnp.concatenate([ref[part, spot, :] for part in range(self.per_row)], axis=1)

    def put(self, ref, row, value):
        spot = pl.ds(row * self.layers, self.layers)
        for part in range(self.per_row):
            ref[part, spot, :] = value[:, part * LANES:(part + 1) * LANES]

    def put_layer(self, ref, layer, row, value):
        for part in range(self.per_row):
            spot = pl.ds(row * self.layers + layer, value.shape[0], stride=self.layers)
            ref[part, spot, :] = value[:, part * LANES:(part + 1) * LANES]

    def east(self, field):
        return pltpu.roll(field, self.breadth - 1, 1)

    def west(self, field):
        return pltpu.roll(field, 1, 1)

    def below(self, field):
        return pltpu.roll(field, self.layers - 1, 0)

    def above(self, field):
        return pltpu.roll(field, 1, 0)


class Joined:
    def __init__(self, rows, own, full, first, last):
        self.rows, self.own, self.full, self.first, self.last = rows, own, full, first, last

    def get(self, row):
        if self.first <= row < self.last:
            return self.rows.get(self.own, row - self.first)
        return self.rows.get(self.full, row)

    def put(self, row, value):
        self.rows.put(self.full, row, value)


class Faces:
    def __init__(self, rows, land, lands):
        self.rows, self.lands = rows, lands
        lx_ref, ly_ref, lz_ref = lands
        count = land.shape[0]
        level = lax.broadcasted_iota(jnp.int32, (rows.layers, rows.breadth), 0)
        self.not_bottom = level < rows.layers - 1
        not_last = lax.broadcasted_iota(jnp.int32, land.shape, 1) < rows.breadth - 1
        lx_ref[pl.ds(0, count - 1), :] = 2.0 * LATERAL * land[:count - 1] * land[1:]
        ly_ref[...] = jnp.where(not_last, 2.0 * LATERAL * land * rows.east(land), 0.0)
        lz_ref[...] = 2.0 * VERTICAL * land * land

    def conduct(self, ks, alpha, head):
        return ks * jnp.exp(alpha * jnp.minimum(head, 0.0))

    def face(self, land, here, there):
        return land * (here * there) * reciprocal(here + there)

    def between_rows(self, row, here, there):
        return self.face(self.lands[0][pl.ds(row, 1), :], here, there)

    def in_row(self, row, here):
        rows = self.rows
        wy = self.face(self.lands[1][pl.ds(row, 1), :], here, rows.east(here))
        wz = self.face(self.lands[2][pl.ds(row, 1), :], here, rows.below(here))
        wz = jnp.where(self.not_bottom, wz, 0.0)
        wz_above = rows.above(wz)
        return wy, wz, wy + rows.west(wy) + wz + wz_above, GRAVITY * (wz_above - wz)


def lane_tables(refs, layers):
    lane = lax.broadcasted_iota(jnp.int32, (layers, LANES), 1)
    tables = []
    for ref in refs:
        table = jnp.zeros((layers, LANES), jnp.float32)
        for kind in range(ref.shape[0]):
            table = jnp.where(lane == kind, ref[kind], table)
        tables.append(table)
    return tables


def look_up(rows, table, soil):
    parts = [
        jnp.take_along_axis(table, soil[:, part * LANES:(part + 1) * LANES], axis=1, mode="promise_in_bounds")
        for part in range(rows.per_row)
    ]
    return jnp.concatenate(parts, axis=1)


def stage_kernel(ks_ref, alpha_ref, store_ref, land_ref, *refs):
    groups = lax.axis_size("layer")
    own, _, _ = position()
    block_refs = refs[:groups]
    first_out, ks_out, alpha_out, store_out, wx_out, wy_out, wz_out, diag_out, base_out, soil_sc, *lands = refs[groups:]
    _, held, span, breadth = block_refs[0].shape
    layers = groups * held
    rows = Rows(layers, breadth)
    faces = Faces(rows, land_ref[...], lands)

    for step, block_ref in enumerate(block_refs):
        for held_layer in range(held):
            layer = (own ^ step) * held + held_layer
            rows.put_layer(first_out, layer, 0, block_ref[0, held_layer])
            rows.put_layer(soil_sc, layer, 0, block_ref[1, held_layer])
    tables = lane_tables((ks_ref, alpha_ref, store_ref), layers)
    before = None
    for row in range(span):
        soil = rows.get(soil_sc, row).astype(jnp.int32)
        ks, alpha, store = [look_up(rows, table, soil) for table in tables]
        first = rows.get(first_out, row)
        here = faces.conduct(ks, alpha, first)
        wy, wz, diagonal, gravity = faces.in_row(row, here)
        for ref, value in (
            (ks_out, ks), (alpha_out, alpha), (store_out, store), (wy_out, wy), (wz_out, wz),
            (diag_out, store + diagonal), (base_out, store * first + gravity),
        ):
            rows.put(ref, row, value)
        if row > 0:
            rows.put(wx_out, row - 1, faces.between_rows(row - 1, before, here))
        before = here


def flow_kernel(kst_ref, alphat_ref, storet_ref, land_ref, near_ref, far_ref, diag_ref, rhs_ref, *refs):
    groups = lax.axis_size("layer")
    own, _, number = position()
    end = (number == 0) | (number == groups - 1)
    far_partner = jnp.where(end, own, own ^ (groups - 1))
    first_ref, ks_ref, alpha_ref, store_ref, wx_ref, wy_ref, wz_ref, partial_ref, gravity_ref = refs[:9]
    head_refs, top_ref = refs[9:9 + groups], refs[9 + groups]
    (
        first_sc, soil_sc, ks_sc, alpha_sc, store_sc, wx_sc, wy_sc, wz_sc, base_sc, inv_sc, ping_sc, pong_sc,
        land_sc, dtop_sc, rtop_sc, *lands,
    ) = refs[10 + groups:]
    held, span, breadth = head_refs[0].shape
    layers = groups * held
    window = span + 2 * HALO
    last_own = HALO + span
    rows = Rows(layers, breadth)
    side = HALO * rows.per_row

    land_sc[pl.ds(HALO, span), :] = land_ref[...]
    dtop_sc[pl.ds(side, span * rows.per_row), :] = diag_ref[...]
    rtop_sc[pl.ds(side, span * rows.per_row), :] = rhs_ref[...]

    def put_halo(ref, partner, row):
        def entry(number):
            return ref[pl.ds(number * HALO, HALO), :]

        for count in range(layers):
            layer = (partner ^ (count // held)) * held + count % held
            rows.put_layer(first_sc, layer, row, entry(count))
            rows.put_layer(soil_sc, layer, row, entry(layers + count))
        land_sc[pl.ds(row, HALO), :] = entry(2 * layers)
        for count, top_sc in ((2 * layers + 1, dtop_sc), (2 * layers + 2, rtop_sc)):
            value = entry(count)
            for part in range(rows.per_row):
                spot = pl.ds(row * rows.per_row + part, HALO, stride=rows.per_row)
                top_sc[spot, :] = value[:, part * LANES:(part + 1) * LANES]

    for odd, above_ref, below_ref in ((0, far_ref, near_ref), (1, near_ref, far_ref)):
        @pl.when(lax.rem(number, 2) == odd)
        def _(above_ref=above_ref, below_ref=below_ref):
            for ref, row in ((above_ref, 0), (below_ref, last_own)):
                put_halo(ref, own ^ 1 if ref is near_ref else far_partner, row)

    faces = Faces(rows, land_sc[...], lands)
    tables = lane_tables((kst_ref, alphat_ref, storet_ref), layers)
    for row in [*range(HALO), *range(last_own, window)]:
        soil = rows.get(soil_sc, row).astype(jnp.int32)
        for table, ref in zip(tables, (ks_sc, alpha_sc, store_sc)):
            rows.put(ref, row, look_up(rows, table, soil))

    def joined(own, full, last=last_own):
        return Joined(rows, own, full, HALO, last)

    first, ks, alpha, store = [
        joined(own, full)
        for own, full in ((first_ref, first_sc), (ks_ref, ks_sc), (alpha_ref, alpha_sc), (store_ref, store_sc))
    ]
    top = lax.broadcasted_iota(jnp.int32, (layers, breadth), 0) == 0

    def riv_row(ref, row):
        parts = [
            jnp.broadcast_to(ref[pl.ds(row * rows.per_row + part, 1), :], (layers, LANES))
            for part in range(rows.per_row)
        ]
        return jnp.where(top, jnp.concatenate(parts, axis=1), 0.0)

    def finish(row, diagonal, base):
        rows.put(inv_sc, row, reciprocal(diagonal + riv_row(dtop_sc, row)))
        rows.put(base_sc, row, base + riv_row(rtop_sc, row))

    def conduct(now, row):
        return faces.conduct(ks.get(row), alpha.get(row), now.get(row))

    def sweep(now, later_ref, weights, begin, stop):
        wx_of, wy_of, wz_of = weights
        before, here, wx_before = now.get(begin - 1), now.get(begin), wx_of.get(begin - 1)
        for row in range(begin, stop):
            after = now.get(row + 1)
            wx, wy, wz = wx_of.get(row), wy_of.get(row), wz_of.get(row)
            total = rows.get(base_sc, row) + wx_before * before + wx * after
            total = total + wy * rows.east(here) + rows.west(wy * here)
            total = total + wz * rows.below(here) + rows.above(wz * here)
            rows.put(later_ref, row, total * rows.get(inv_sc, row))
            before, here, wx_before = here, after, wx

    now, spare = first, [ping_sc, pong_sc]
    begin, stop = 0, window
    for picard in range(ITERS):
        early = picard == 0
        wx_of = joined(wx_ref, wx_sc, last_own - 1 if early else HALO)
        wy_of, wz_of = [joined(own, full, last_own if early else HALO) for own, full in ((wy_ref, wy_sc), (wz_ref, wz_sc))]
        before, wx_before = None, None
        for row in range(begin, stop):
            staged = early and HALO <= row < last_own
            here = conduct(now, row) if not staged or row in (HALO, last_own - 1) else None
            if row > begin:
                if early and HALO <= row - 1 < last_own - 1:
                    wx = wx_of.get(row - 1)
                else:
                    wx = faces.between_rows(row - 1, before, here)
                    wx_of.put(row - 1, wx)
                if row - 1 > begin:
                    diagonal, base = pending
                    finish(row - 1, diagonal + wx_before + wx, base)
                wx_before = wx
            if staged:
                pending = rows.get(partial_ref, row - HALO), rows.get(gravity_ref, row - HALO)
            elif begin < row < stop - 1:
                wy, wz, diagonal, gravity = faces.in_row(row, here)
                wy_of.put(row, wy)
                wz_of.put(row, wz)
                pending = store.get(row) + diagonal, store.get(row) * first.get(row) + gravity
            before = here
        for _ in range(SWEEPS):
            begin, stop = begin + 1, stop - 1
            later_ref = spare[0]
            sweep(now, later_ref, (wx_of, wy_of, wz_of), begin, stop)
            spare = [spare[1], later_ref]
            now = joined(None, later_ref, HALO)
    for part in range(rows.per_row):
        lanes = pl.ds(part * LANES, LANES)
        top_ref[:, lanes] = later_ref[part, pl.ds(HALO * layers, span, stride=layers), :]
        for step, head_ref in enumerate(head_refs):
            for held_layer in range(held):
                layer = (own ^ step) * held + held_layer
                head_ref[held_layer, :, lanes] = later_ref[part, pl.ds(HALO * layers + layer, span, stride=layers), :]


def inflow_kernel(reach_rows, cells_ref, bed_ref, slot_section_ref, reach_ref, *refs):
    groups = lax.axis_size("layer")
    own_layer, flip, _ = position()
    top_refs = refs[:groups]
    out_ref, block_sc, lane_sc, found_sc, turned_sc = refs[groups:]
    span, breadth = top_refs[0].shape
    per_row = breadth // LANES
    blocks = groups * span * per_row
    slots = cells_ref.shape[0]
    quarter = LANES // groups
    packed = slots // groups
    for step, top_ref in enumerate(top_refs):
        number = span_at(flip, groups, own_layer ^ step)
        for part in range(per_row):
            spot = pl.ds(number * span * per_row + part, span, stride=per_row)
            turned_sc[spot, :] = top_ref[:, part * LANES:(part + 1) * LANES]

    own = lax.broadcasted_iota(jnp.int32, (packed, LANES), 1) // quarter

    def pack(ref):
        result = None
        for number in range(groups):
            shift = lax.rem((number + groups - own_layer) * quarter, LANES)
            moved = pltpu.roll(ref[pl.ds(number * packed, packed), :], shift, 1)
            result = moved if result is None else jnp.where(own == number, moved, result)
        return result

    cells = pack(cells_ref)
    block, lane = split_cells(cells, 0, breadth, LANES)
    block_sc[...] = block
    lane_sc[...] = lane
    table = jnp.concatenate(bf16_pieces(turned_sc[...].T, 2), axis=1)
    group = 32
    names = names_of(blocks)
    index = lax.broadcasted_iota(jnp.int32, (8, LANES), 0).astype(jnp.float32)

    def step(count, _):
        first = pl.multiple_of(count * group, group)
        for pair in range(0, group, 2):
            hots = jnp.concatenate(
                [
                    jnp.concatenate(one_hot(row_copies(block_sc, first, place), names), axis=0)
                    for place in (pair, pair + 1)
                ],
                axis=1,
            )
            found = lax.dot_general(
                table, jnp.concatenate([hots, hots], axis=0), (((1,), (0,)), ((), ())),
                preferred_element_type=jnp.float32,
            )
            for place in (pair, pair + 1):
                rows = lane_sc[pl.ds(first + place // 8 * 8, 8), :]
                lanes = jnp.broadcast_to(rows[place % 8:place % 8 + 1, :], (8, LANES))
                mine = found[:, (place - pair) * LANES:(place - pair + 1) * LANES]
                total = jnp.zeros((8, LANES), jnp.float32)
                for start in range(0, LANES, 8):
                    total = total + jnp.where(lanes == index + float(start), mine[start:start + 8], 0.0)
                found_sc[pl.ds(first + place, 1), :] = jnp.sum(total, axis=0, keepdims=True)
        return 0

    lax.fori_loop(0, packed // group, step, 0)
    slot_in = jnp.where(cells >= 0, pack(bed_ref) * (found_sc[...] - pack(slot_section_ref)), 0.0)
    spread = jnp.concatenate(
        [slot_in if number == 0 else pltpu.roll(slot_in, LANES - number * quarter, 1) for number in range(groups)],
        axis=0,
    )
    in_quarter = lax.broadcasted_iota(jnp.int32, spread.shape, 1) < quarter
    pieces = bf16_pieces(jnp.where(in_quarter, spread, 0.0), 3)
    fold = reach_rows // groups
    index = lax.broadcasted_iota(jnp.int32, (out_ref.shape[0], slots), 0)
    index = index // fold * reach_rows + lax.rem(index, fold)
    result = None
    for number in range(groups):
        put = jnp.where(index + number * fold == reach_ref[...], 1.0, 0.0).astype(jnp.bfloat16)
        total = jnp.zeros(out_ref.shape, jnp.float32)
        for piece in pieces:
            total = total + lax.dot_general(
                put, piece, (((1,), (0,)), ((), ())), preferred_element_type=jnp.float32
            )
        result = total if result is None else result + pltpu.roll(total, number * quarter, 1)
    out_ref[...] = result


def sum_kernel(terms_ref, inflow_ref):
    total = terms_ref[0]
    for tile in range(1, terms_ref.shape[0]):
        total = total + terms_ref[tile]
    fold, quarter = total.shape[0], inflow_ref.shape[1]
    for number in range(inflow_ref.shape[0] // fold):
        lanes = slice(number * quarter, (number + 1) * quarter)
        inflow_ref[pl.ds(number * fold, fold), :] = total[:, lanes]


def head_kernel(*refs):
    groups = lax.axis_size("layer")
    back_refs, (head_hbm, sems) = refs[:groups], refs[groups:]
    _, span, _ = back_refs[0].shape
    own, flip, _ = position()
    copies = []
    for step, back_ref in enumerate(back_refs):
        rows = pl.ds(pl.multiple_of(span_at(flip, groups, own ^ step) * span, span), span)
        copies.append(pltpu.make_async_copy(back_ref, head_hbm.at[:, rows, :], sems.at[step]))
        copies[-1].start()
    for copy in copies:
        copy.wait()


def call(kernel, out_shape, in_specs, scratch, micros, vmem=VMEM_LIMIT, out_specs=None):
    single = not isinstance(out_shape, (tuple, list))
    return pl.pallas_call(
        kernel,
        out_shape=out_shape,
        in_specs=in_specs,
        out_specs=out_specs or (in_vmem if single else tuple(in_vmem for _ in out_shape)),
        scratch_shapes=scratch,
        compiler_params=pltpu.CompilerParams(vmem_limit_bytes=vmem),
        cost_estimate=pl.CostEstimate(flops=int(micros * 1.15e9), bytes_accessed=0, transcendentals=0),
    )


def on_device(
    head_start,
    soil_class,
    land_mask,
    ks_table,
    alpha_table,
    store_table,
    section,
    cross_owner,
    cross_local,
    node_cell,
    bed_cond,
):
    held, across, breadth = head_start.shape
    reach_rows, node_count = section.shape
    tiles = lax.axis_size("tile")
    groups = lax.axis_size("layer")
    layers = held * groups
    span = across // groups
    per_row = breadth // LANES
    blocks = span * per_row
    near = [(i, i ^ 1) for i in range(groups)]
    far = []
    for upper in range(tiles):
        far += [(upper * groups + i, upper * groups + (i ^ (groups - 1))) for i in range(1, groups - 1)]
        if upper + 1 < tiles:
            index = groups - 1 if upper % 2 == 0 else 0
            one, two = upper * groups + index, (upper + 1) * groups + index
            far += [(one, two), (two, one)]

    cells = node_cell[0]
    bed = bed_cond[0]
    slots = cells.shape[0]

    def exchange(parts):
        received = [parts[0]]
        for step in range(1, groups):
            received.append(lax.ppermute(parts[step], "layer", [(i, i ^ step) for i in range(groups)]))
        return received

    spread, reach = call(
        spread_kernel,
        (
            jax.ShapeDtypeStruct((tiles, reach_rows, node_count), jnp.float32),
            jax.ShapeDtypeStruct(cross_owner.shape, jnp.int32),
        ),
        [in_hbm] * 3,
        [
            pltpu.VMEM(section.shape, jnp.float32),
            pltpu.VMEM(cross_owner.shape, jnp.int32),
            pltpu.VMEM(cross_owner.shape, jnp.int32),
            pltpu.SemaphoreType.DMA((3,)),
        ],
        1, VMEM_MOST,
    )(section, cross_owner, cross_local)
    whole_section = lax.all_to_all(spread, "tile", 0, 0).reshape(tiles * reach_rows, node_count)
    *own_blocks, land = call(
        prepare_kernel,
        (jax.ShapeDtypeStruct((2, held, span, breadth), jnp.float32),) * groups
        + (jax.ShapeDtypeStruct((span, breadth), jnp.float32),),
        [in_hbm] * 4,
        [
            pltpu.VMEM(soil_class.shape, jnp.int32),
            pltpu.VMEM(soil_class.shape, jnp.float32),
            pltpu.VMEM((span, breadth), jnp.int32),
            pltpu.SemaphoreType.DMA((held + 1,)),
            pltpu.SemaphoreType.DMA((groups,)),
            pltpu.SemaphoreType.DMA((groups,)),
        ],
        2, VMEM_MOST, (in_hbm,) * groups + (in_vmem,),
    )(head_start, soil_class, land_mask, spread)
    received = exchange(own_blocks)

    node_scratch = pltpu.VMEM((slots, LANES), jnp.float32)
    riv_shape = jax.ShapeDtypeStruct((blocks, LANES), jnp.float32)
    diag, rhs, slot_section = call(
        functools.partial(river_kernel, breadth, span),
        (riv_shape, riv_shape, jax.ShapeDtypeStruct((slots, node_count), jnp.float32)),
        [in_vmem] * 4,
        [node_scratch] * 6 + [pltpu.VMEM((span * breadth // BLOCK, LANES), jnp.float32)],
        7,
    )(cells, bed, whole_section, reach)
    edges = jax.ShapeDtypeStruct(((2 * layers + 3) * HALO, breadth), jnp.float32)
    near_edge, far_edge = call(
        edge_kernel, (edges, edges), [in_vmem] * (3 + groups), [], 0.1,
    )(land, diag, rhs, *received)
    near_halo = lax.ppermute(near_edge, "layer", near)
    far_halo = lax.ppermute(far_edge, FLAT, far)

    window = span + 2 * HALO
    own_field = jax.ShapeDtypeStruct((per_row, span * layers, LANES), jnp.float32)
    field = pltpu.VMEM((per_row, window * layers, LANES), jnp.float32)
    staged = call(
        stage_kernel, (own_field,) * 9,
        [in_smem] * 3 + [in_vmem] * (1 + groups),
        [pltpu.VMEM(own_field.shape, jnp.float32)] + [pltpu.VMEM((span, breadth), jnp.float32)] * 3,
        2.5,
    )(ks_table, alpha_table, store_table, land, *received)
    head_shape = jax.ShapeDtypeStruct((held, span, breadth), jnp.float32)
    *heads, top = call(
        flow_kernel,
        (head_shape,) * groups + (jax.ShapeDtypeStruct((span, breadth), jnp.float32),),
        [in_smem] * 3 + [in_vmem] * (5 + len(staged)),
        [field] * 12
        + [pltpu.VMEM((window, breadth), jnp.float32)]
        + [pltpu.VMEM((window * per_row, LANES), jnp.float32)] * 2
        + [pltpu.VMEM((window, breadth), jnp.float32)] * 3,
        5,
    )(ks_table, alpha_table, store_table, land, near_halo, far_halo, diag, rhs, *staged)
    tops = exchange([top] * groups)
    backs = exchange(heads)

    fold = reach_rows // groups
    packed = pltpu.VMEM((slots // groups, LANES), jnp.float32)
    partial = call(
        functools.partial(inflow_kernel, reach_rows),
        jax.ShapeDtypeStruct((tiles * fold, node_count), jnp.float32),
        [in_vmem] * (4 + groups),
        [packed] * 3 + [pltpu.VMEM((across * per_row, LANES), jnp.float32)],
        3,
    )(cells, bed, slot_section, reach, *tops)
    partial, *backs = lax.optimization_barrier((partial, *backs))
    terms = lax.all_to_all(partial.reshape(tiles, fold, node_count), "tile", 0, 0)
    head = call(
        head_kernel, jax.ShapeDtypeStruct(head_start.shape, jnp.float32), [in_vmem] * groups,
        [pltpu.SemaphoreType.DMA((groups,))], 0.7, out_specs=in_hbm,
    )(*backs)
    inflow_shape = jax.ShapeDtypeStruct((reach_rows, node_count // groups), jnp.float32)
    return head, call(sum_kernel, inflow_shape, [in_vmem], [], 0.1)(terms)


def solution(mesh):
    placed = (
        P("layer", "tile", None),
        P("layer", "tile", None),
        P("tile", None),
        P(),
        P(),
        P(),
        P("tile", None),
        P("tile", None),
        P("tile", None),
        P("tile", None, None),
        P("tile", None, None),
    )
    return jax.shard_map(
        on_device,
        mesh=mesh,
        in_specs=placed,
        out_specs=(P("layer", "tile", None), P("tile", "layer")),
        check_vma=False,
    )
```

```python
import functools

import jax
import jax.numpy as jnp
from jax import lax
from jax.experimental import pallas as pl
from jax.experimental.pallas import tpu as pltpu
from jax.sharding import PartitionSpec as P

ITERS = 2
SWEEPS = 3

LATERAL = 1.0
VERTICAL = 2.0
GRAVITY = 1.0

HALO = ITERS * SWEEPS
BLOCK = 64
LANES = 128
VMEM_LIMIT = 32 * 1024 * 1024
VMEM_MOST = 60 * 1024 * 1024
FLAT = ("tile", "layer")

in_vmem = pl.BlockSpec(memory_space=pltpu.VMEM)
in_hbm = pl.BlockSpec(memory_space=pltpu.HBM)
in_smem = pl.BlockSpec(memory_space=pltpu.SMEM)


def bf16_pieces(value, count):
    pieces = []
    for _ in range(count):
        piece = value.astype(jnp.bfloat16)
        pieces.append(piece)
        value = value - piece.astype(jnp.float32)
    return pieces


def reciprocal(value):
    guess = pl.reciprocal(value, approx=True)
    return guess * (2.0 - value * guess)


def names_of(size):
    index = lax.broadcasted_iota(jnp.int32, (16, LANES), 0)
    return [(index + start).astype(jnp.float32).astype(jnp.bfloat16) for start in range(0, size, 16)]


def one_hot(row, names):
    one = jnp.ones((16, LANES), jnp.bfloat16)
    zero = jnp.zeros((16, LANES), jnp.bfloat16)
    return [jnp.maximum(one - jnp.abs(row - name), zero) for name in names]


def row_copies(ref, first, place):
    rows = ref[pl.ds(pl.multiple_of(first + place // 8 * 8, 8), 8), :]
    return jnp.broadcast_to(rows[place % 8:place % 8 + 1, :], (16, LANES)).astype(jnp.bfloat16)


def position():
    tile, layer = lax.axis_index("tile"), lax.axis_index("layer")
    groups = lax.axis_size("layer")
    flip = lax.rem(tile, 2)
    return layer, flip, jnp.where(flip == 1, groups - 1 - layer, layer)


def span_at(flip, groups, layer):
    return jnp.where(flip == 1, groups - 1 - layer, layer)


def split_cells(cells, first_row, breadth, width):
    local = cells - first_row * breadth
    shift = width.bit_length() - 1
    block = jnp.where(cells < 0, -1, local >> shift)
    return block.astype(jnp.float32), (local & (width - 1)).astype(jnp.float32)


def river_kernel(
    breadth, span, stride, cells_ref, bed_ref, section_ref,
    diag_ref, rhs_ref, slot_section_ref, reach_ref, block_sc, spot_sc, dhigh_sc, dlow_sc, rhigh_sc, rlow_sc, sum_sc,
):
    _, _, number = position()
    rows = section_ref.shape[0]
    slots = reach_ref.shape[1]
    first = (lax.axis_index("tile") + 1) * stride - 8
    own_rows = section_ref[pl.ds(pl.multiple_of(first, 8), 8), :]
    reach = jnp.concatenate([own_rows[k:k + 1, :] for k in range(slots // LANES)], axis=1)
    reach_ref[...] = reach
    index = lax.broadcasted_iota(jnp.int32, (rows, slots), 0).astype(jnp.float32)
    pick = jnp.where(index == reach, 1.0, 0.0).astype(jnp.bfloat16)
    picked = jnp.zeros(slot_section_ref.shape, jnp.float32)
    for piece in bf16_pieces(section_ref[...], 3):
        picked = picked + lax.dot_general(
            pick, piece, (((0,), (0,)), ((), ())), preferred_element_type=jnp.float32
        )
    slot_section_ref[...] = picked

    block, spot = split_cells(cells_ref[...], number * span, breadth, BLOCK)
    block_sc[...] = block
    spot_sc[...] = spot
    bed = bed_ref[...]
    for value, high_sc, low_sc in ((bed, dhigh_sc, dlow_sc), (bed * picked, rhigh_sc, rlow_sc)):
        high, low = bf16_pieces(value, 2)
        high_sc[...] = high.astype(jnp.float32)
        low_sc[...] = low.astype(jnp.float32)
    share = LANES // BLOCK
    blocks = share * diag_ref.shape[0]
    group = 64
    block_names, spot_names = names_of(blocks), names_of(BLOCK)

    def matmul(first, places):
        left, right = [], []
        for place in places:
            left.append(jnp.concatenate(one_hot(row_copies(block_sc, first, place), block_names), axis=0))
            hot = one_hot(row_copies(spot_sc, first, place), spot_names)
            values = [row_copies(ref, first, place) for ref in (dhigh_sc, dlow_sc, rhigh_sc, rlow_sc)]
            right.append(jnp.concatenate([tile * value for value in values for tile in hot], axis=0))
        return lax.dot_general(
            jnp.concatenate(left, axis=1),
            jnp.concatenate(right, axis=1),
            (((1,), (1,)), ((), ())),
            preferred_element_type=jnp.float32,
        )

    def step(count, total):
        first = count * group
        half = group // 2
        return total + (matmul(first, range(half)) + matmul(first, range(half, group)))

    total = lax.fori_loop(0, slots // group, step, jnp.zeros((blocks, 4 * BLOCK), jnp.float32))
    low_half = lax.broadcasted_iota(jnp.int32, diag_ref.shape, 1) < BLOCK
    for count, ref in ((0, diag_ref), (1, rhs_ref)):
        part = total[:, count * LANES:(count + 1) * LANES]
        sum_sc[...] = part + pltpu.roll(part, BLOCK, 1)
        ref[...] = jnp.where(
            low_half, sum_sc[pl.ds(0, blocks // share, stride=share), :], sum_sc[pl.ds(1, blocks // share, stride=share), :]
        )


def edge_kernel(land_ref, diag_ref, rhs_ref, *refs):
    block_refs, (near_ref, far_ref) = refs[:-2], refs[-2:]
    _, held, span, breadth = block_refs[0].shape
    _, _, number = position()
    odd = lax.rem(number, 2) == 1
    per_row = breadth // LANES

    def put_edges(entry, top, bottom, lanes=slice(None)):
        near_ref[pl.ds(entry * HALO, HALO), lanes] = jnp.where(odd, top, bottom)
        far_ref[pl.ds(entry * HALO, HALO), lanes] = jnp.where(odd, bottom, top)

    entry = 0
    for kind in range(2):
        for block_ref in block_refs:
            for held_layer in range(held):
                put_edges(entry, block_ref[kind, held_layer, :HALO, :], block_ref[kind, held_layer, span - HALO:, :])
                entry += 1
    put_edges(entry, land_ref[:HALO, :], land_ref[span - HALO:, :])
    for ref in (diag_ref, rhs_ref):
        entry += 1
        for part in range(per_row):
            top = ref[pl.ds(part, HALO, stride=per_row), :]
            bottom = ref[pl.ds((span - HALO) * per_row + part, HALO, stride=per_row), :]
            put_edges(entry, top, bottom, slice(part * LANES, (part + 1) * LANES))


def spread_kernel(section_hbm, owner_hbm, local_hbm, spread_ref, section_ref, owner_ref, local_ref, sems):
    pairs = ((section_hbm, section_ref), (owner_hbm, owner_ref), (local_hbm, local_ref))
    copies = [pltpu.make_async_copy(here, there, sems.at[k]) for k, (here, there) in enumerate(pairs)]
    for copy in copies:
        copy.start()
    for copy in copies:
        copy.wait()
    tiles, stride, _ = spread_ref.shape
    reach_rows = section_ref.shape[0]
    reach = (owner_ref[...] * stride + local_ref[...]).astype(jnp.float32)
    parts = [reach[:, start:start + LANES] for start in range(0, reach.shape[1], LANES)]
    parts.append(jnp.zeros((stride - reach_rows - len(parts), LANES), jnp.float32))
    payload = jnp.concatenate([section_ref[...], *parts], axis=0)
    for tile in range(tiles):
        spread_ref[tile] = payload


def prepare_kernel(head_hbm, soil_hbm, land_hbm, after_hbm, *refs):
    del after_hbm
    groups = lax.axis_size("layer")
    block_hbms, land_out_ref = refs[:groups], refs[groups]
    head_ref, soil_ref, soil_float_ref, land_ref, head_sems, soil_sems, land_sem, out_sems = refs[groups + 1:]
    held, across, _ = soil_ref.shape
    span = across // groups
    own, flip, _ = position()

    def rows_of(target):
        return pl.ds(pl.multiple_of(span_at(flip, groups, target) * span, span), span)

    soils = [pltpu.make_async_copy(soil_hbm.at[k], soil_ref.at[k], soil_sems.at[k]) for k in range(held)]
    heads = [pltpu.make_async_copy(head_hbm.at[k], head_ref.at[k], head_sems.at[k]) for k in range(held)]
    land = pltpu.make_async_copy(land_hbm.at[rows_of(own), :], land_ref, land_sem)
    for copy in (*heads, *soils, land):
        copy.start()
    outs = []

    def send(kind, field_ref):
        for step, block_hbm in enumerate(block_hbms):
            outs.append(
                pltpu.make_async_copy(
                    field_ref.at[:, rows_of(own ^ step), :], block_hbm.at[kind], out_sems.at[kind * groups + step]
                )
            )
            outs[-1].start()

    for copy in heads:
        copy.wait()
    send(0, head_ref)
    for layer, copy in enumerate(soils):
        copy.wait()
        soil_float_ref[layer] = soil_ref[layer].astype(jnp.float32)
    send(1, soil_float_ref)
    land.wait()
    land_out_ref[...] = land_ref[...].astype(jnp.float32)
    for copy in outs:
        copy.wait()


class Rows:
    def __init__(self, layers, breadth):
        self.layers, self.breadth, self.per_row = layers, breadth, breadth // LANES

    def get(self, ref, row):
        spot = pl.ds(row * self.layers, self.layers)
        return jnp.concatenate([ref[part, spot, :] for part in range(self.per_row)], axis=1)

    def put(self, ref, row, value):
        spot = pl.ds(row * self.layers, self.layers)
        for part in range(self.per_row):
            ref[part, spot, :] = value[:, part * LANES:(part + 1) * LANES]

    def put_layer(self, ref, layer, row, value):
        for part in range(self.per_row):
            spot = pl.ds(row * self.layers + layer, value.shape[0], stride=self.layers)
            ref[part, spot, :] = value[:, part * LANES:(part + 1) * LANES]

    def east(self, field):
        return pltpu.roll(field, self.breadth - 1, 1)

    def west(self, field):
        return pltpu.roll(field, 1, 1)

    def below(self, field):
        return pltpu.roll(field, self.layers - 1, 0)

    def above(self, field):
        return pltpu.roll(field, 1, 0)


class Joined:
    def __init__(self, rows, own, full, first, last):
        self.rows, self.own, self.full, self.first, self.last = rows, own, full, first, last

    def get(self, row):
        if self.first <= row < self.last:
            return self.rows.get(self.own, row - self.first)
        return self.rows.get(self.full, row)

    def put(self, row, value):
        self.rows.put(self.full, row, value)


class Faces:
    def __init__(self, rows, land, lands):
        self.rows, self.lands = rows, lands
        lx_ref, ly_ref, lz_ref = lands
        count = land.shape[0]
        level = lax.broadcasted_iota(jnp.int32, (rows.layers, rows.breadth), 0)
        self.not_bottom = level < rows.layers - 1
        not_last = lax.broadcasted_iota(jnp.int32, land.shape, 1) < rows.breadth - 1
        lx_ref[pl.ds(0, count - 1), :] = 2.0 * LATERAL * land[:count - 1] * land[1:]
        ly_ref[...] = jnp.where(not_last, 2.0 * LATERAL * land * rows.east(land), 0.0)
        lz_ref[...] = 2.0 * VERTICAL * land * land

    def conduct(self, ks, alpha, head):
        return ks * jnp.exp(alpha * jnp.minimum(head, 0.0))

    def face(self, land, here, there):
        return land * (here * there) * reciprocal(here + there)

    def between_rows(self, row, here, there):
        return self.face(self.lands[0][pl.ds(row, 1), :], here, there)

    def in_row(self, row, here):
        rows = self.rows
        wy = self.face(self.lands[1][pl.ds(row, 1), :], here, rows.east(here))
        wz = self.face(self.lands[2][pl.ds(row, 1), :], here, rows.below(here))
        wz = jnp.where(self.not_bottom, wz, 0.0)
        wz_above = rows.above(wz)
        return wy, wz, wy + rows.west(wy) + wz + wz_above, GRAVITY * (wz_above - wz)


def lane_tables(refs, layers):
    lane = lax.broadcasted_iota(jnp.int32, (layers, LANES), 1)
    tables = []
    for ref in refs:
        table = jnp.zeros((layers, LANES), jnp.float32)
        for kind in range(ref.shape[0]):
            table = jnp.where(lane == kind, ref[kind], table)
        tables.append(table)
    return tables


def look_up(rows, table, soil):
    parts = [
        jnp.take_along_axis(table, soil[:, part * LANES:(part + 1) * LANES], axis=1, mode="promise_in_bounds")
        for part in range(rows.per_row)
    ]
    return jnp.concatenate(parts, axis=1)


def stage_kernel(ks_ref, alpha_ref, store_ref, land_ref, *refs):
    groups = lax.axis_size("layer")
    own, _, _ = position()
    block_refs = refs[:groups]
    first_out, ks_out, alpha_out, store_out, wx_out, wy_out, wz_out, diag_out, base_out, soil_sc, *lands = refs[groups:]
    _, held, span, breadth = block_refs[0].shape
    layers = groups * held
    rows = Rows(layers, breadth)
    faces = Faces(rows, land_ref[...], lands)

    for step, block_ref in enumerate(block_refs):
        for held_layer in range(held):
            layer = (own ^ step) * held + held_layer
            rows.put_layer(first_out, layer, 0, block_ref[0, held_layer])
            rows.put_layer(soil_sc, layer, 0, block_ref[1, held_layer])
    tables = lane_tables((ks_ref, alpha_ref, store_ref), layers)
    before = None
    for row in range(span):
        soil = rows.get(soil_sc, row).astype(jnp.int32)
        ks, alpha, store = [look_up(rows, table, soil) for table in tables]
        first = rows.get(first_out, row)
        here = faces.conduct(ks, alpha, first)
        wy, wz, diagonal, gravity = faces.in_row(row, here)
        for ref, value in (
            (ks_out, ks), (alpha_out, alpha), (store_out, store), (wy_out, wy), (wz_out, wz),
            (diag_out, store + diagonal), (base_out, store * first + gravity),
        ):
            rows.put(ref, row, value)
        if row > 0:
            rows.put(wx_out, row - 1, faces.between_rows(row - 1, before, here))
        before = here


def flow_kernel(kst_ref, alphat_ref, storet_ref, land_ref, near_ref, far_ref, diag_ref, rhs_ref, *refs):
    groups = lax.axis_size("layer")
    own, _, number = position()
    end = (number == 0) | (number == groups - 1)
    far_partner = jnp.where(end, own, own ^ (groups - 1))
    first_ref, ks_ref, alpha_ref, store_ref, wx_ref, wy_ref, wz_ref, partial_ref, gravity_ref = refs[:9]
    head_refs, top_ref = refs[9:9 + groups], refs[9 + groups]
    (
        first_sc, soil_sc, ks_sc, alpha_sc, store_sc, wx_sc, wy_sc, wz_sc, base_sc, inv_sc, ping_sc, pong_sc,
        land_sc, dtop_sc, rtop_sc, *lands,
    ) = refs[10 + groups:]
    held, span, breadth = head_refs[0].shape
    layers = groups * held
    window = span + 2 * HALO
    last_own = HALO + span
    rows = Rows(layers, breadth)
    side = HALO * rows.per_row

    land_sc[pl.ds(HALO, span), :] = land_ref[...]
    dtop_sc[pl.ds(side, span * rows.per_row), :] = diag_ref[...]
    rtop_sc[pl.ds(side, span * rows.per_row), :] = rhs_ref[...]

    def put_halo(ref, partner, row):
        def entry(number):
            return ref[pl.ds(number * HALO, HALO), :]

        for count in range(layers):
            layer = (partner ^ (count // held)) * held + count % held
            rows.put_layer(first_sc, layer, row, entry(count))
            rows.put_layer(soil_sc, layer, row, entry(layers + count))
        land_sc[pl.ds(row, HALO), :] = entry(2 * layers)
        for count, top_sc in ((2 * layers + 1, dtop_sc), (2 * layers + 2, rtop_sc)):
            value = entry(count)
            for part in range(rows.per_row):
                spot = pl.ds(row * rows.per_row + part, HALO, stride=rows.per_row)
                top_sc[spot, :] = value[:, part * LANES:(part + 1) * LANES]

    for odd, above_ref, below_ref in ((0, far_ref, near_ref), (1, near_ref, far_ref)):
        @pl.when(lax.rem(number, 2) == odd)
        def _(above_ref=above_ref, below_ref=below_ref):
            for ref, row in ((above_ref, 0), (below_ref, last_own)):
                put_halo(ref, own ^ 1 if ref is near_ref else far_partner, row)

    faces = Faces(rows, land_sc[...], lands)
    tables = lane_tables((kst_ref, alphat_ref, storet_ref), layers)
    for row in [*range(HALO), *range(last_own, window)]:
        soil = rows.get(soil_sc, row).astype(jnp.int32)
        for table, ref in zip(tables, (ks_sc, alpha_sc, store_sc)):
            rows.put(ref, row, look_up(rows, table, soil))

    def joined(own, full, last=last_own):
        return Joined(rows, own, full, HALO, last)

    first, ks, alpha, store = [
        joined(own, full)
        for own, full in ((first_ref, first_sc), (ks_ref, ks_sc), (alpha_ref, alpha_sc), (store_ref, store_sc))
    ]
    top = lax.broadcasted_iota(jnp.int32, (layers, breadth), 0) == 0

    def riv_row(ref, row):
        parts = [
            jnp.broadcast_to(ref[pl.ds(row * rows.per_row + part, 1), :], (layers, LANES))
            for part in range(rows.per_row)
        ]
        return jnp.where(top, jnp.concatenate(parts, axis=1), 0.0)

    def finish(row, diagonal, base):
        rows.put(inv_sc, row, reciprocal(diagonal + riv_row(dtop_sc, row)))
        rows.put(base_sc, row, base + riv_row(rtop_sc, row))

    def conduct(now, row):
        return faces.conduct(ks.get(row), alpha.get(row), now.get(row))

    def sweep(now, later_ref, weights, begin, stop):
        wx_of, wy_of, wz_of = weights
        before, here, wx_before = now.get(begin - 1), now.get(begin), wx_of.get(begin - 1)
        for row in range(begin, stop):
            after = now.get(row + 1)
            wx, wy, wz = wx_of.get(row), wy_of.get(row), wz_of.get(row)
            total = rows.get(base_sc, row) + wx_before * before + wx * after
            total = total + wy * rows.east(here) + rows.west(wy * here)
            total = total + wz * rows.below(here) + rows.above(wz * here)
            rows.put(later_ref, row, total * rows.get(inv_sc, row))
            before, here, wx_before = here, after, wx

    now, spare = first, [ping_sc, pong_sc]
    begin, stop = 0, window
    for picard in range(ITERS):
        early = picard == 0
        wx_of = joined(wx_ref, wx_sc, last_own - 1 if early else HALO)
        wy_of, wz_of = [joined(own, full, last_own if early else HALO) for own, full in ((wy_ref, wy_sc), (wz_ref, wz_sc))]
        before, wx_before = None, None
        for row in range(begin, stop):
            staged = early and HALO <= row < last_own
            here = conduct(now, row) if not staged or row in (HALO, last_own - 1) else None
            if row > begin:
                if early and HALO <= row - 1 < last_own - 1:
                    wx = wx_of.get(row - 1)
                else:
                    wx = faces.between_rows(row - 1, before, here)
                    wx_of.put(row - 1, wx)
                if row - 1 > begin:
                    diagonal, base = pending
                    finish(row - 1, diagonal + wx_before + wx, base)
                wx_before = wx
            if staged:
                pending = rows.get(partial_ref, row - HALO), rows.get(gravity_ref, row - HALO)
            elif begin < row < stop - 1:
                wy, wz, diagonal, gravity = faces.in_row(row, here)
                wy_of.put(row, wy)
                wz_of.put(row, wz)
                pending = store.get(row) + diagonal, store.get(row) * first.get(row) + gravity
            before = here
        for _ in range(SWEEPS):
            begin, stop = begin + 1, stop - 1
            later_ref = spare[0]
            sweep(now, later_ref, (wx_of, wy_of, wz_of), begin, stop)
            spare = [spare[1], later_ref]
            now = joined(None, later_ref, HALO)
    for part in range(rows.per_row):
        lanes = pl.ds(part * LANES, LANES)
        top_ref[:, lanes] = later_ref[part, pl.ds(HALO * layers, span, stride=layers), :]
        for step, head_ref in enumerate(head_refs):
            for held_layer in range(held):
                layer = (own ^ step) * held + held_layer
                head_ref[held_layer, :, lanes] = later_ref[part, pl.ds(HALO * layers + layer, span, stride=layers), :]


def inflow_kernel(reach_rows, stride, cells_ref, bed_ref, slot_section_ref, reach_ref, *refs):
    groups = lax.axis_size("layer")
    own_layer, flip, _ = position()
    top_refs = refs[:groups]
    out_ref, block_sc, lane_sc, found_sc, turned_sc = refs[groups:]
    span, breadth = top_refs[0].shape
    per_row = breadth // LANES
    blocks = groups * span * per_row
    slots = cells_ref.shape[0]
    quarter = LANES // groups
    packed = slots // groups
    for step, top_ref in enumerate(top_refs):
        number = span_at(flip, groups, own_layer ^ step)
        for part in range(per_row):
            spot = pl.ds(number * span * per_row + part, span, stride=per_row)
            turned_sc[spot, :] = top_ref[:, part * LANES:(part + 1) * LANES]

    own = lax.broadcasted_iota(jnp.int32, (packed, LANES), 1) // quarter

    def pack(ref):
        result = None
        for number in range(groups):
            shift = lax.rem((number + groups - own_layer) * quarter, LANES)
            moved = pltpu.roll(ref[pl.ds(number * packed, packed), :], shift, 1)
            result = moved if result is None else jnp.where(own == number, moved, result)
        return result

    cells = pack(cells_ref)
    block, lane = split_cells(cells, 0, breadth, LANES)
    block_sc[...] = block
    lane_sc[...] = lane
    table = jnp.concatenate(bf16_pieces(turned_sc[...].T, 2), axis=0)
    group = 32
    names = names_of(blocks)
    index = lax.broadcasted_iota(jnp.int32, (8, LANES), 0).astype(jnp.float32)

    def step(count, _):
        first = pl.multiple_of(count * group, group)
        for pair in range(0, group, 2):
            hots = jnp.concatenate(
                [
                    jnp.concatenate(one_hot(row_copies(block_sc, first, place), names), axis=0)
                    for place in (pair, pair + 1)
                ],
                axis=1,
            )
            found = lax.dot_general(
                table, hots, (((1,), (0,)), ((), ())), preferred_element_type=jnp.float32
            )
            found = found[:LANES] + found[LANES:]
            for place in (pair, pair + 1):
                rows = lane_sc[pl.ds(first + place // 8 * 8, 8), :]
                lanes = jnp.broadcast_to(rows[place % 8:place % 8 + 1, :], (8, LANES))
                mine = found[:, (place - pair) * LANES:(place - pair + 1) * LANES]
                total = jnp.zeros((8, LANES), jnp.float32)
                for start in range(0, LANES, 8):
                    total = total + jnp.where(lanes == index + float(start), mine[start:start + 8], 0.0)
                found_sc[pl.ds(first + place, 1), :] = jnp.sum(total, axis=0, keepdims=True)
        return 0

    lax.fori_loop(0, packed // group, step, 0)
    slot_in = jnp.where(cells >= 0, pack(bed_ref) * (found_sc[...] - pack(slot_section_ref)), 0.0)
    spread = jnp.concatenate(
        [slot_in if number == 0 else pltpu.roll(slot_in, LANES - number * quarter, 1) for number in range(groups)],
        axis=0,
    )
    in_quarter = lax.broadcasted_iota(jnp.int32, spread.shape, 1) < quarter
    pieces = bf16_pieces(jnp.where(in_quarter, spread, 0.0), 3)
    fold = reach_rows // groups
    index = lax.broadcasted_iota(jnp.int32, (out_ref.shape[0], slots), 0)
    index = index // fold * stride + lax.rem(index, fold)
    result = None
    for number in range(groups):
        name = (index + number * fold).astype(jnp.float32)
        put = jnp.where(name == reach_ref[...], 1.0, 0.0).astype(jnp.bfloat16)
        total = jnp.zeros(out_ref.shape, jnp.float32)
        for piece in pieces:
            total = total + lax.dot_general(
                put, piece, (((1,), (0,)), ((), ())), preferred_element_type=jnp.float32
            )
        result = total if result is None else result + pltpu.roll(total, number * quarter, 1)
    out_ref[...] = result


def sum_kernel(terms_ref, inflow_ref):
    total = terms_ref[0]
    for tile in range(1, terms_ref.shape[0]):
        total = total + terms_ref[tile]
    fold, quarter = total.shape[0], inflow_ref.shape[1]
    for number in range(inflow_ref.shape[0] // fold):
        lanes = slice(number * quarter, (number + 1) * quarter)
        inflow_ref[pl.ds(number * fold, fold), :] = total[:, lanes]


def head_kernel(*refs):
    groups = lax.axis_size("layer")
    back_refs, (head_hbm, sems) = refs[:groups], refs[groups:]
    _, span, _ = back_refs[0].shape
    own, flip, _ = position()
    copies = []
    for step, back_ref in enumerate(back_refs):
        rows = pl.ds(pl.multiple_of(span_at(flip, groups, own ^ step) * span, span), span)
        copies.append(pltpu.make_async_copy(back_ref, head_hbm.at[:, rows, :], sems.at[step]))
        copies[-1].start()
    for copy in copies:
        copy.wait()


def call(kernel, out_shape, in_specs, scratch, micros, vmem=VMEM_LIMIT, out_specs=None):
    single = not isinstance(out_shape, (tuple, list))
    return pl.pallas_call(
        kernel,
        out_shape=out_shape,
        in_specs=in_specs,
        out_specs=out_specs or (in_vmem if single else tuple(in_vmem for _ in out_shape)),
        scratch_shapes=scratch,
        compiler_params=pltpu.CompilerParams(vmem_limit_bytes=vmem),
        cost_estimate=pl.CostEstimate(flops=int(micros * 1.15e9), bytes_accessed=0, transcendentals=0),
    )


def on_device(
    head_start,
    soil_class,
    land_mask,
    ks_table,
    alpha_table,
    store_table,
    section,
    cross_owner,
    cross_local,
    node_cell,
    bed_cond,
):
    held, across, breadth = head_start.shape
    reach_rows, node_count = section.shape
    tiles = lax.axis_size("tile")
    groups = lax.axis_size("layer")
    layers = held * groups
    span = across // groups
    per_row = breadth // LANES
    blocks = span * per_row
    near = [(i, i ^ 1) for i in range(groups)]
    far = []
    for upper in range(tiles):
        far += [(upper * groups + i, upper * groups + (i ^ (groups - 1))) for i in range(1, groups - 1)]
        if upper + 1 < tiles:
            index = groups - 1 if upper % 2 == 0 else 0
            one, two = upper * groups + index, (upper + 1) * groups + index
            far += [(one, two), (two, one)]

    cells = node_cell[0]
    bed = bed_cond[0]
    slots = cells.shape[0]

    def exchange(parts):
        received = [parts[0]]
        for step in range(1, groups):
            received.append(lax.ppermute(parts[step], "layer", [(i, i ^ step) for i in range(groups)]))
        return received

    stride = reach_rows + 8
    spread = call(
        spread_kernel, jax.ShapeDtypeStruct((tiles, stride, node_count), jnp.float32), [in_hbm] * 3,
        [
            pltpu.VMEM(section.shape, jnp.float32),
            pltpu.VMEM(cross_owner.shape, jnp.int32),
            pltpu.VMEM(cross_owner.shape, jnp.int32),
            pltpu.SemaphoreType.DMA((3,)),
        ],
        1, VMEM_MOST,
    )(section, cross_owner, cross_local)
    whole_section = lax.all_to_all(spread, "tile", 0, 0).reshape(tiles * stride, node_count)
    *own_blocks, land = call(
        prepare_kernel,
        (jax.ShapeDtypeStruct((2, held, span, breadth), jnp.float32),) * groups
        + (jax.ShapeDtypeStruct((span, breadth), jnp.float32),),
        [in_hbm] * 4,
        [
            pltpu.VMEM(head_start.shape, jnp.float32),
            pltpu.VMEM(soil_class.shape, jnp.int32),
            pltpu.VMEM(soil_class.shape, jnp.float32),
            pltpu.VMEM((span, breadth), jnp.int32),
            pltpu.SemaphoreType.DMA((held,)),
            pltpu.SemaphoreType.DMA((held,)),
            pltpu.SemaphoreType.DMA(()),
            pltpu.SemaphoreType.DMA((2 * groups,)),
        ],
        2, VMEM_MOST, (in_hbm,) * groups + (in_vmem,),
    )(head_start, soil_class, land_mask, spread)
    received = exchange(own_blocks)

    node_scratch = pltpu.VMEM((slots, LANES), jnp.float32)
    riv_shape = jax.ShapeDtypeStruct((blocks, LANES), jnp.float32)
    diag, rhs, slot_section, reach = call(
        functools.partial(river_kernel, breadth, span, stride),
        (
            riv_shape,
            riv_shape,
            jax.ShapeDtypeStruct((slots, node_count), jnp.float32),
            jax.ShapeDtypeStruct((1, slots), jnp.float32),
        ),
        [in_vmem] * 3,
        [node_scratch] * 6 + [pltpu.VMEM((span * breadth // BLOCK, LANES), jnp.float32)],
        7,
    )(cells, bed, whole_section)
    edges = jax.ShapeDtypeStruct(((2 * layers + 3) * HALO, breadth), jnp.float32)
    near_edge, far_edge = call(
        edge_kernel, (edges, edges), [in_vmem] * (3 + groups), [], 0.1,
    )(land, diag, rhs, *received)
    near_halo = lax.ppermute(near_edge, "layer", near)
    far_halo = lax.ppermute(far_edge, FLAT, far)

    window = span + 2 * HALO
    own_field = jax.ShapeDtypeStruct((per_row, span * layers, LANES), jnp.float32)
    field = pltpu.VMEM((per_row, window * layers, LANES), jnp.float32)
    staged = call(
        stage_kernel, (own_field,) * 9,
        [in_smem] * 3 + [in_vmem] * (1 + groups),
        [pltpu.VMEM(own_field.shape, jnp.float32)] + [pltpu.VMEM((span, breadth), jnp.float32)] * 3,
        2.5,
    )(ks_table, alpha_table, store_table, land, *received)
    head_shape = jax.ShapeDtypeStruct((held, span, breadth), jnp.float32)
    *heads, top = call(
        flow_kernel,
        (head_shape,) * groups + (jax.ShapeDtypeStruct((span, breadth), jnp.float32),),
        [in_smem] * 3 + [in_vmem] * (5 + len(staged)),
        [field] * 12
        + [pltpu.VMEM((window, breadth), jnp.float32)]
        + [pltpu.VMEM((window * per_row, LANES), jnp.float32)] * 2
        + [pltpu.VMEM((window, breadth), jnp.float32)] * 3,
        5,
    )(ks_table, alpha_table, store_table, land, near_halo, far_halo, diag, rhs, *staged)
    tops = exchange([top] * groups)
    backs = exchange(heads)

    fold = reach_rows // groups
    packed = pltpu.VMEM((slots // groups, LANES), jnp.float32)
    partial = call(
        functools.partial(inflow_kernel, reach_rows, stride),
        jax.ShapeDtypeStruct((tiles * fold, node_count), jnp.float32),
        [in_vmem] * (4 + groups),
        [packed] * 3 + [pltpu.VMEM((across * per_row, LANES), jnp.float32)],
        3,
    )(cells, bed, slot_section, reach, *tops)
    partial, *backs = lax.optimization_barrier((partial, *backs))
    terms = lax.all_to_all(partial.reshape(tiles, fold, node_count), "tile", 0, 0)
    head = call(
        head_kernel, jax.ShapeDtypeStruct(head_start.shape, jnp.float32), [in_vmem] * groups,
        [pltpu.SemaphoreType.DMA((groups,))], 0.7, out_specs=in_hbm,
    )(*backs)
    inflow_shape = jax.ShapeDtypeStruct((reach_rows, node_count // groups), jnp.float32)
    return head, call(sum_kernel, inflow_shape, [in_vmem], [], 0.1)(terms)


def solution(mesh):
    placed = (
        P("layer", "tile", None),
        P("layer", "tile", None),
        P("tile", None),
        P(),
        P(),
        P(),
        P("tile", None),
        P("tile", None),
        P("tile", None),
        P("tile", None, None),
        P("tile", None, None),
    )
    return jax.shard_map(
        on_device,
        mesh=mesh,
        in_specs=placed,
        out_specs=(P("layer", "tile", None), P("tile", "layer")),
        check_vma=False,
    )
```

```python
import functools

import jax
import jax.numpy as jnp
from jax import lax
from jax.experimental import pallas as pl
from jax.experimental.pallas import tpu as pltpu
from jax.sharding import PartitionSpec as P

ITERS = 2
SWEEPS = 3

LATERAL = 1.0
VERTICAL = 2.0
GRAVITY = 1.0

HALO = ITERS * SWEEPS
BLOCK = 64
LANES = 128
VMEM_LIMIT = 32 * 1024 * 1024
VMEM_MOST = 60 * 1024 * 1024
FLAT = ("tile", "layer")

in_vmem = pl.BlockSpec(memory_space=pltpu.VMEM)
in_hbm = pl.BlockSpec(memory_space=pltpu.HBM)
in_smem = pl.BlockSpec(memory_space=pltpu.SMEM)


def bf16_pieces(value, count):
    pieces = []
    for _ in range(count):
        piece = value.astype(jnp.bfloat16)
        pieces.append(piece)
        value = value - piece.astype(jnp.float32)
    return pieces


def reciprocal(value):
    guess = pl.reciprocal(value, approx=True)
    return guess * (2.0 - value * guess)


def names_of(size):
    index = lax.broadcasted_iota(jnp.int32, (16, LANES), 0)
    return [(index + start).astype(jnp.float32).astype(jnp.bfloat16) for start in range(0, size, 16)]


def one_hot(row, names):
    one = jnp.ones((16, LANES), jnp.bfloat16)
    zero = jnp.zeros((16, LANES), jnp.bfloat16)
    return [jnp.maximum(one - jnp.abs(row - name), zero) for name in names]


def row_copies(ref, first, place):
    rows = ref[pl.ds(pl.multiple_of(first + place // 8 * 8, 8), 8), :]
    return jnp.broadcast_to(rows[place % 8:place % 8 + 1, :], (16, LANES)).astype(jnp.bfloat16)


def position():
    tile, layer = lax.axis_index("tile"), lax.axis_index("layer")
    groups = lax.axis_size("layer")
    flip = lax.rem(tile, 2)
    return layer, flip, jnp.where(flip == 1, groups - 1 - layer, layer)


def span_at(flip, groups, layer):
    return jnp.where(flip == 1, groups - 1 - layer, layer)


def split_cells(cells, first_row, breadth, width):
    local = cells - first_row * breadth
    shift = width.bit_length() - 1
    block = jnp.where(cells < 0, -1, local >> shift)
    return block.astype(jnp.float32), (local & (width - 1)).astype(jnp.float32)


def river_kernel(
    breadth, span, stride, cells_ref, bed_ref, section_ref,
    diag_ref, rhs_ref, slot_section_ref, reach_ref, block_sc, spot_sc, dhigh_sc, dlow_sc, rhigh_sc, rlow_sc, sum_sc,
):
    _, _, number = position()
    rows = section_ref.shape[0]
    slots = reach_ref.shape[1]
    first = (lax.axis_index("tile") + 1) * stride - 8
    own_rows = section_ref[pl.ds(pl.multiple_of(first, 8), 8), :]
    reach = jnp.concatenate([own_rows[k:k + 1, :] for k in range(slots // LANES)], axis=1)
    reach_ref[...] = reach
    index = lax.broadcasted_iota(jnp.int32, (rows, slots), 0).astype(jnp.float32)
    pick = jnp.where(index == reach, 1.0, 0.0).astype(jnp.bfloat16)
    picked = jnp.zeros(slot_section_ref.shape, jnp.float32)
    for piece in bf16_pieces(section_ref[...], 3):
        picked = picked + lax.dot_general(
            pick, piece, (((0,), (0,)), ((), ())), preferred_element_type=jnp.float32
        )
    slot_section_ref[...] = picked

    block, spot = split_cells(cells_ref[...], number * span, breadth, BLOCK)
    block_sc[...] = block
    spot_sc[...] = spot
    bed = bed_ref[...]
    for value, high_sc, low_sc in ((bed, dhigh_sc, dlow_sc), (bed * picked, rhigh_sc, rlow_sc)):
        high, low = bf16_pieces(value, 2)
        high_sc[...] = high.astype(jnp.float32)
        low_sc[...] = low.astype(jnp.float32)
    share = LANES // BLOCK
    blocks = share * diag_ref.shape[0]
    group = 64
    block_names, spot_names = names_of(blocks), names_of(BLOCK)

    def matmul(first, places):
        left, right = [], []
        for place in places:
            left.append(jnp.concatenate(one_hot(row_copies(block_sc, first, place), block_names), axis=0))
            hot = one_hot(row_copies(spot_sc, first, place), spot_names)
            values = [row_copies(ref, first, place) for ref in (dhigh_sc, dlow_sc, rhigh_sc, rlow_sc)]
            right.append(jnp.concatenate([tile * value for value in values for tile in hot], axis=0))
        return lax.dot_general(
            jnp.concatenate(left, axis=1),
            jnp.concatenate(right, axis=1),
            (((1,), (1,)), ((), ())),
            preferred_element_type=jnp.float32,
        )

    def step(count, total):
        first = count * group
        half = group // 2
        return total + (matmul(first, range(half)) + matmul(first, range(half, group)))

    total = lax.fori_loop(0, slots // group, step, jnp.zeros((blocks, 4 * BLOCK), jnp.float32))
    low_half = lax.broadcasted_iota(jnp.int32, diag_ref.shape, 1) < BLOCK
    for count, ref in ((0, diag_ref), (1, rhs_ref)):
        part = total[:, count * LANES:(count + 1) * LANES]
        sum_sc[...] = part + pltpu.roll(part, BLOCK, 1)
        ref[...] = jnp.where(
            low_half, sum_sc[pl.ds(0, blocks // share, stride=share), :], sum_sc[pl.ds(1, blocks // share, stride=share), :]
        )


def edge_kernel(land_ref, diag_ref, rhs_ref, *refs):
    block_refs, (near_ref, far_ref) = refs[:-2], refs[-2:]
    _, held, span, breadth = block_refs[0].shape
    _, _, number = position()
    odd = lax.rem(number, 2) == 1
    per_row = breadth // LANES

    def put_edges(entry, top, bottom, lanes=slice(None)):
        near_ref[pl.ds(entry * HALO, HALO), lanes] = jnp.where(odd, top, bottom)
        far_ref[pl.ds(entry * HALO, HALO), lanes] = jnp.where(odd, bottom, top)

    entry = 0
    for kind in range(2):
        for block_ref in block_refs:
            for held_layer in range(held):
                put_edges(entry, block_ref[kind, held_layer, :HALO, :], block_ref[kind, held_layer, span - HALO:, :])
                entry += 1
    put_edges(entry, land_ref[:HALO, :], land_ref[span - HALO:, :])
    for ref in (diag_ref, rhs_ref):
        entry += 1
        for part in range(per_row):
            top = ref[pl.ds(part, HALO, stride=per_row), :]
            bottom = ref[pl.ds((span - HALO) * per_row + part, HALO, stride=per_row), :]
            put_edges(entry, top, bottom, slice(part * LANES, (part + 1) * LANES))


def spread_kernel(section_hbm, owner_hbm, local_hbm, spread_ref, section_ref, owner_ref, local_ref, sems):
    pairs = ((section_hbm, section_ref), (owner_hbm, owner_ref), (local_hbm, local_ref))
    copies = [pltpu.make_async_copy(here, there, sems.at[k]) for k, (here, there) in enumerate(pairs)]
    for copy in copies:
        copy.start()
    for copy in copies:
        copy.wait()
    tiles, stride, _ = spread_ref.shape
    reach_rows = section_ref.shape[0]
    reach = (owner_ref[...] * stride + local_ref[...]).astype(jnp.float32)
    parts = [reach[:, start:start + LANES] for start in range(0, reach.shape[1], LANES)]
    parts.append(jnp.zeros((stride - reach_rows - len(parts), LANES), jnp.float32))
    payload = jnp.concatenate([section_ref[...], *parts], axis=0)
    for tile in range(tiles):
        spread_ref[tile] = payload


def prepare_kernel(head_ref, soil_ref, land_ref, after_ref, *refs):
    del after_ref
    groups = lax.axis_size("layer")
    block_refs, land_out_ref = refs[:groups], refs[groups]
    held, across, _ = head_ref.shape
    span = across // groups
    own, flip, _ = position()

    def rows_of(target):
        return pl.ds(pl.multiple_of(span_at(flip, groups, target) * span, span), span)

    land_out_ref[...] = land_ref[rows_of(own), :].astype(jnp.float32)
    for step, block_ref in enumerate(block_refs):
        rows = rows_of(own ^ step)
        for layer in range(held):
            block_ref[0, layer] = head_ref[layer, rows, :]
            block_ref[1, layer] = soil_ref[layer, rows, :].astype(jnp.float32)


class Rows:
    def __init__(self, layers, breadth):
        self.layers, self.breadth, self.per_row = layers, breadth, breadth // LANES

    def get(self, ref, row):
        spot = pl.ds(row * self.layers, self.layers)
        return jnp.concatenate([ref[part, spot, :] for part in range(self.per_row)], axis=1)

    def put(self, ref, row, value):
        spot = pl.ds(row * self.layers, self.layers)
        for part in range(self.per_row):
            ref[part, spot, :] = value[:, part * LANES:(part + 1) * LANES]

    def put_layer(self, ref, layer, row, value):
        for part in range(self.per_row):
            spot = pl.ds(row * self.layers + layer, value.shape[0], stride=self.layers)
            ref[part, spot, :] = value[:, part * LANES:(part + 1) * LANES]

    def east(self, field):
        return pltpu.roll(field, self.breadth - 1, 1)

    def west(self, field):
        return pltpu.roll(field, 1, 1)

    def below(self, field):
        return pltpu.roll(field, self.layers - 1, 0)

    def above(self, field):
        return pltpu.roll(field, 1, 0)


class Joined:
    def __init__(self, rows, own, full, first, last):
        self.rows, self.own, self.full, self.first, self.last = rows, own, full, first, last

    def holds(self, row):
        return self.first <= row < self.last

    def get(self, row):
        if self.holds(row):
            return self.rows.get(self.own, row - HALO)
        return self.rows.get(self.full, row)

    def put(self, row, value):
        self.rows.put(self.full, row, value)


def relax_row(rows, row, head, weights, wx_before, base, inverse):
    before, here, after = head
    wx, wy, wz = [field.get(row) for field in weights]
    total = base.get(row) + wx_before * before + wx * after
    total = total + wy * rows.east(here) + rows.west(wy * here)
    total = total + wz * rows.below(here) + rows.above(wz * here)
    return total * inverse.get(row), wx


def river_row(rows, ref, row, top):
    parts = [
        jnp.broadcast_to(ref[pl.ds(row * rows.per_row + part, 1), :], (rows.layers, LANES))
        for part in range(rows.per_row)
    ]
    return jnp.where(top, jnp.concatenate(parts, axis=1), 0.0)


class Faces:
    def __init__(self, rows, land, lands):
        self.rows, self.lands = rows, lands
        lx_ref, ly_ref, lz_ref = lands
        count = land.shape[0]
        level = lax.broadcasted_iota(jnp.int32, (rows.layers, rows.breadth), 0)
        self.not_bottom = level < rows.layers - 1
        not_last = lax.broadcasted_iota(jnp.int32, land.shape, 1) < rows.breadth - 1
        lx_ref[pl.ds(0, count - 1), :] = 2.0 * LATERAL * land[:count - 1] * land[1:]
        ly_ref[...] = jnp.where(not_last, 2.0 * LATERAL * land * rows.east(land), 0.0)
        lz_ref[...] = 2.0 * VERTICAL * land * land

    def conduct(self, ks, alpha, head):
        return ks * jnp.exp(alpha * jnp.minimum(head, 0.0))

    def face(self, land, here, there):
        return land * (here * there) * reciprocal(here + there)

    def between_rows(self, row, here, there):
        return self.face(self.lands[0][pl.ds(row, 1), :], here, there)

    def in_row(self, row, here):
        rows = self.rows
        wy = self.face(self.lands[1][pl.ds(row, 1), :], here, rows.east(here))
        wz = self.face(self.lands[2][pl.ds(row, 1), :], here, rows.below(here))
        wz = jnp.where(self.not_bottom, wz, 0.0)
        wz_above = rows.above(wz)
        return wy, wz, wy + rows.west(wy) + wz + wz_above, GRAVITY * (wz_above - wz)


def lane_tables(refs, layers):
    lane = lax.broadcasted_iota(jnp.int32, (layers, LANES), 1)
    tables = []
    for ref in refs:
        table = jnp.zeros((layers, LANES), jnp.float32)
        for kind in range(ref.shape[0]):
            table = jnp.where(lane == kind, ref[kind], table)
        tables.append(table)
    return tables


def look_up(rows, table, soil):
    parts = [
        jnp.take_along_axis(table, soil[:, part * LANES:(part + 1) * LANES], axis=1, mode="promise_in_bounds")
        for part in range(rows.per_row)
    ]
    return jnp.concatenate(parts, axis=1)


def stage_kernel(ks_ref, alpha_ref, store_ref, land_ref, diag_ref, rhs_ref, *refs):
    groups = lax.axis_size("layer")
    own, _, _ = position()
    block_refs, refs = refs[:groups], refs[groups:]
    first_out, ks_out, alpha_out, store_out = refs[:4]
    fields = [refs[4 + 5 * picard:9 + 5 * picard] for picard in range(ITERS)]
    head_outs = refs[4 + 5 * ITERS:4 + 5 * ITERS + HALO]
    soil_sc, *lands = refs[4 + 5 * ITERS + HALO:]
    _, held, span, breadth = block_refs[0].shape
    layers = groups * held
    rows = Rows(layers, breadth)
    faces = Faces(rows, land_ref[...], lands)
    top = lax.broadcasted_iota(jnp.int32, (layers, breadth), 0) == 0

    for step, block_ref in enumerate(block_refs):
        for held_layer in range(held):
            layer = (own ^ step) * held + held_layer
            rows.put_layer(first_out, layer, 0, block_ref[0, held_layer])
            rows.put_layer(soil_sc, layer, 0, block_ref[1, held_layer])
    tables = lane_tables((ks_ref, alpha_ref, store_ref), layers)
    for row in range(span):
        soil = rows.get(soil_sc, row).astype(jnp.int32)
        for table, out in zip(tables, (ks_out, alpha_out, store_out)):
            rows.put(out, row, look_up(rows, table, soil))

    now, begin, stop, done = first_out, 0, span, 0
    for wx_out, wy_out, wz_out, inv_out, base_out in fields:
        before = None
        for row in range(begin, stop):
            here = faces.conduct(rows.get(ks_out, row), rows.get(alpha_out, row), rows.get(now, row))
            wy, wz, diagonal, gravity = faces.in_row(row, here)
            rows.put(wy_out, row, wy)
            rows.put(wz_out, row, wz)
            store = rows.get(store_out, row)
            sums = store + diagonal, store * rows.get(first_out, row) + gravity
            if row > begin:
                wx = faces.between_rows(row - 1, before[0], here)
                rows.put(wx_out, row - 1, wx)
                diagonal, base = before[1]
                if row - 1 > begin:
                    diagonal = reciprocal(diagonal + before[2] + wx + river_row(rows, diag_ref, row - 1, top))
                    base = base + river_row(rows, rhs_ref, row - 1, top)
                rows.put(inv_out, row - 1, diagonal)
                rows.put(base_out, row - 1, base)
            else:
                wx = None
            before = here, sums, wx
        rows.put(inv_out, stop - 1, before[1][0])
        rows.put(base_out, stop - 1, before[1][1])
        weights = [Joined(rows, None, ref, HALO, HALO) for ref in (wx_out, wy_out, wz_out)]
        base, inverse = [Joined(rows, None, ref, HALO, HALO) for ref in (base_out, inv_out)]
        for _ in range(SWEEPS):
            begin, stop = begin + 1, stop - 1
            head = rows.get(now, begin - 1), rows.get(now, begin)
            wx_before = rows.get(wx_out, begin - 1)
            for row in range(begin, stop):
                head = *head[-2:], rows.get(now, row + 1)
                value, wx_before = relax_row(rows, row, head, weights, wx_before, base, inverse)
                rows.put(head_outs[done], row, value)
            now = head_outs[done]
            done += 1


def flow_kernel(kst_ref, alphat_ref, storet_ref, land_ref, near_ref, far_ref, diag_ref, rhs_ref, *refs):
    groups = lax.axis_size("layer")
    own, _, number = position()
    end = (number == 0) | (number == groups - 1)
    far_partner = jnp.where(end, own, own ^ (groups - 1))
    first_ref, ks_ref, alpha_ref, store_ref = refs[:4]
    fields = [refs[4 + 5 * picard:9 + 5 * picard] for picard in range(ITERS)]
    staged_refs = refs[4 + 5 * ITERS:4 + 5 * ITERS + HALO]
    refs = refs[4 + 5 * ITERS + HALO:]
    head_refs, top_ref = refs[:groups], refs[groups]
    (
        first_sc, soil_sc, ks_sc, alpha_sc, store_sc, wx_sc, wy_sc, wz_sc, base_sc, inv_sc, ping_sc, pong_sc,
        land_sc, dtop_sc, rtop_sc, *lands,
    ) = refs[1 + groups:]
    held, span, breadth = head_refs[0].shape
    layers = groups * held
    window = span + 2 * HALO
    last_own = HALO + span
    rows = Rows(layers, breadth)
    side = HALO * rows.per_row

    land_sc[pl.ds(HALO, span), :] = land_ref[...]
    dtop_sc[pl.ds(side, span * rows.per_row), :] = diag_ref[...]
    rtop_sc[pl.ds(side, span * rows.per_row), :] = rhs_ref[...]

    def put_halo(ref, partner, row):
        def entry(number):
            return ref[pl.ds(number * HALO, HALO), :]

        for count in range(layers):
            layer = (partner ^ (count // held)) * held + count % held
            rows.put_layer(first_sc, layer, row, entry(count))
            rows.put_layer(soil_sc, layer, row, entry(layers + count))
        land_sc[pl.ds(row, HALO), :] = entry(2 * layers)
        for count, top_sc in ((2 * layers + 1, dtop_sc), (2 * layers + 2, rtop_sc)):
            value = entry(count)
            for part in range(rows.per_row):
                spot = pl.ds(row * rows.per_row + part, HALO, stride=rows.per_row)
                top_sc[spot, :] = value[:, part * LANES:(part + 1) * LANES]

    for odd, above_ref, below_ref in ((0, far_ref, near_ref), (1, near_ref, far_ref)):
        @pl.when(lax.rem(number, 2) == odd)
        def _(above_ref=above_ref, below_ref=below_ref):
            for ref, row in ((above_ref, 0), (below_ref, last_own)):
                put_halo(ref, own ^ 1 if ref is near_ref else far_partner, row)

    faces = Faces(rows, land_sc[...], lands)
    tables = lane_tables((kst_ref, alphat_ref, storet_ref), layers)
    for row in [*range(HALO), *range(last_own, window)]:
        soil = rows.get(soil_sc, row).astype(jnp.int32)
        for table, ref in zip(tables, (ks_sc, alpha_sc, store_sc)):
            rows.put(ref, row, look_up(rows, table, soil))

    first, ks, alpha, store = [
        Joined(rows, held_ref, full, HALO, last_own)
        for held_ref, full in ((first_ref, first_sc), (ks_ref, ks_sc), (alpha_ref, alpha_sc), (store_ref, store_sc))
    ]
    top = lax.broadcasted_iota(jnp.int32, (layers, breadth), 0) == 0

    now, begin, stop, done = first, 0, window, 0
    for wx_ref, wy_ref, wz_ref, inv_ref, base_ref in fields:
        low, high = HALO + done, last_own - done
        wx_of = Joined(rows, wx_ref, wx_sc, low, high - 1)
        wy_of, wz_of = Joined(rows, wy_ref, wy_sc, low, high), Joined(rows, wz_ref, wz_sc, low, high)
        inverse, base = [
            Joined(rows, held_ref, full, low + 1, high - 1) for held_ref, full in ((inv_ref, inv_sc), (base_ref, base_sc))
        ]
        here_before, wx_before, sums_before = None, None, None
        for row in range(begin, stop):
            at_end = row in (low, high - 1)
            here, sums = None, None
            if not wy_of.holds(row) or at_end:
                here = faces.conduct(ks.get(row), alpha.get(row), now.get(row))
            if at_end:
                sums = rows.get(inv_ref, row - HALO), rows.get(base_ref, row - HALO)
            elif not wy_of.holds(row) and begin < row < stop - 1:
                wy, wz, diagonal, gravity = faces.in_row(row, here)
                wy_of.put(row, wy)
                wz_of.put(row, wz)
                sums = store.get(row) + diagonal, store.get(row) * first.get(row) + gravity
            if row > begin:
                if wx_of.holds(row - 1):
                    wx = wx_of.get(row - 1)
                else:
                    wx = faces.between_rows(row - 1, here_before, here)
                    wx_of.put(row - 1, wx)
                if sums_before is not None:
                    diagonal = sums_before[0] + wx_before + wx + river_row(rows, dtop_sc, row - 1, top)
                    inverse.put(row - 1, reciprocal(diagonal))
                    base.put(row - 1, sums_before[1] + river_row(rows, rtop_sc, row - 1, top))
                wx_before = wx
            here_before, sums_before = here, sums
        for _ in range(SWEEPS):
            begin, stop = begin + 1, stop - 1
            later = Joined(rows, staged_refs[done], (ping_sc, pong_sc)[done % 2], HALO + done + 1, last_own - done - 1)
            done += 1
            for row in range(begin, stop):
                if not later.holds(row):
                    head = now.get(row - 1), now.get(row), now.get(row + 1)
                    value, _ = relax_row(rows, row, head, (wx_of, wy_of, wz_of), wx_of.get(row - 1), base, inverse)
                    later.put(row, value)
            now = later
    for row in range(now.first, now.last):
        now.put(row, now.get(row))
    for part in range(rows.per_row):
        lanes = pl.ds(part * LANES, LANES)
        top_ref[:, lanes] = now.full[part, pl.ds(HALO * layers, span, stride=layers), :]
        for step, head_ref in enumerate(head_refs):
            for held_layer in range(held):
                layer = (own ^ step) * held + held_layer
                head_ref[held_layer, :, lanes] = now.full[part, pl.ds(HALO * layers + layer, span, stride=layers), :]


def inflow_kernel(reach_rows, stride, cells_ref, bed_ref, slot_section_ref, reach_ref, *refs):
    groups = lax.axis_size("layer")
    own_layer, flip, _ = position()
    top_refs = refs[:groups]
    out_ref, block_sc, lane_sc, found_sc, turned_sc = refs[groups:]
    span, breadth = top_refs[0].shape
    per_row = breadth // LANES
    blocks = groups * span * per_row
    slots = cells_ref.shape[0]
    quarter = LANES // groups
    packed = slots // groups
    for step, top_ref in enumerate(top_refs):
        number = span_at(flip, groups, own_layer ^ step)
        for part in range(per_row):
            spot = pl.ds(number * span * per_row + part, span, stride=per_row)
            turned_sc[spot, :] = top_ref[:, part * LANES:(part + 1) * LANES]

    own = lax.broadcasted_iota(jnp.int32, (packed, LANES), 1) // quarter

    def pack(ref):
        result = None
        for number in range(groups):
            shift = lax.rem((number + groups - own_layer) * quarter, LANES)
            moved = pltpu.roll(ref[pl.ds(number * packed, packed), :], shift, 1)
            result = moved if result is None else jnp.where(own == number, moved, result)
        return result

    cells = pack(cells_ref)
    block, lane = split_cells(cells, 0, breadth, LANES)
    block_sc[...] = block
    lane_sc[...] = lane
    table = jnp.concatenate(bf16_pieces(turned_sc[...].T, 2), axis=0)
    group = 32
    names = names_of(blocks)
    index = lax.broadcasted_iota(jnp.int32, (8, LANES), 0).astype(jnp.float32)

    def step(count, _):
        first = pl.multiple_of(count * group, group)
        for pair in range(0, group, 2):
            hots = jnp.concatenate(
                [
                    jnp.concatenate(one_hot(row_copies(block_sc, first, place), names), axis=0)
                    for place in (pair, pair + 1)
                ],
                axis=1,
            )
            found = lax.dot_general(
                table, hots, (((1,), (0,)), ((), ())), preferred_element_type=jnp.float32
            )
            found = found[:LANES] + found[LANES:]
            for place in (pair, pair + 1):
                rows = lane_sc[pl.ds(first + place // 8 * 8, 8), :]
                lanes = jnp.broadcast_to(rows[place % 8:place % 8 + 1, :], (8, LANES))
                mine = found[:, (place - pair) * LANES:(place - pair + 1) * LANES]
                total = jnp.zeros((8, LANES), jnp.float32)
                for start in range(0, LANES, 8):
                    total = total + jnp.where(lanes == index + float(start), mine[start:start + 8], 0.0)
                found_sc[pl.ds(first + place, 1), :] = jnp.sum(total, axis=0, keepdims=True)
        return 0

    lax.fori_loop(0, packed // group, step, 0)
    slot_in = jnp.where(cells >= 0, pack(bed_ref) * (found_sc[...] - pack(slot_section_ref)), 0.0)
    spread = jnp.concatenate(
        [slot_in if number == 0 else pltpu.roll(slot_in, LANES - number * quarter, 1) for number in range(groups)],
        axis=0,
    )
    in_quarter = lax.broadcasted_iota(jnp.int32, spread.shape, 1) < quarter
    pieces = bf16_pieces(jnp.where(in_quarter, spread, 0.0), 3)
    fold = reach_rows // groups
    index = lax.broadcasted_iota(jnp.int32, (out_ref.shape[0], slots), 0)
    index = index // fold * stride + lax.rem(index, fold)
    result = None
    for number in range(groups):
        name = (index + number * fold).astype(jnp.float32)
        put = jnp.where(name == reach_ref[...], 1.0, 0.0).astype(jnp.bfloat16)
        total = jnp.zeros(out_ref.shape, jnp.float32)
        for piece in pieces:
            total = total + lax.dot_general(
                put, piece, (((1,), (0,)), ((), ())), preferred_element_type=jnp.float32
            )
        result = total if result is None else result + pltpu.roll(total, number * quarter, 1)
    out_ref[...] = result


def sum_kernel(terms_ref, inflow_ref):
    total = terms_ref[0]
    for tile in range(1, terms_ref.shape[0]):
        total = total + terms_ref[tile]
    fold, quarter = total.shape[0], inflow_ref.shape[1]
    for number in range(inflow_ref.shape[0] // fold):
        lanes = slice(number * quarter, (number + 1) * quarter)
        inflow_ref[pl.ds(number * fold, fold), :] = total[:, lanes]


def head_kernel(*refs):
    groups = lax.axis_size("layer")
    back_refs, (head_hbm, sems) = refs[:groups], refs[groups:]
    _, span, _ = back_refs[0].shape
    own, flip, _ = position()
    copies = []
    for step, back_ref in enumerate(back_refs):
        rows = pl.ds(pl.multiple_of(span_at(flip, groups, own ^ step) * span, span), span)
        copies.append(pltpu.make_async_copy(back_ref, head_hbm.at[:, rows, :], sems.at[step]))
        copies[-1].start()
    for copy in copies:
        copy.wait()


def call(kernel, out_shape, in_specs, scratch, micros, vmem=VMEM_LIMIT, out_specs=None):
    single = not isinstance(out_shape, (tuple, list))
    return pl.pallas_call(
        kernel,
        out_shape=out_shape,
        in_specs=in_specs,
        out_specs=out_specs or (in_vmem if single else tuple(in_vmem for _ in out_shape)),
        scratch_shapes=scratch,
        compiler_params=pltpu.CompilerParams(vmem_limit_bytes=vmem),
        cost_estimate=pl.CostEstimate(flops=int(micros * 1.15e9), bytes_accessed=0, transcendentals=0),
    )


def on_device(
    head_start,
    soil_class,
    land_mask,
    ks_table,
    alpha_table,
    store_table,
    section,
    cross_owner,
    cross_local,
    node_cell,
    bed_cond,
):
    held, across, breadth = head_start.shape
    reach_rows, node_count = section.shape
    tiles = lax.axis_size("tile")
    groups = lax.axis_size("layer")
    layers = held * groups
    span = across // groups
    per_row = breadth // LANES
    blocks = span * per_row
    near = [(i, i ^ 1) for i in range(groups)]
    far = []
    for upper in range(tiles):
        far += [(upper * groups + i, upper * groups + (i ^ (groups - 1))) for i in range(1, groups - 1)]
        if upper + 1 < tiles:
            index = groups - 1 if upper % 2 == 0 else 0
            one, two = upper * groups + index, (upper + 1) * groups + index
            far += [(one, two), (two, one)]

    cells = node_cell[0]
    bed = bed_cond[0]
    slots = cells.shape[0]

    def exchange(parts):
        received = [parts[0]]
        for step in range(1, groups):
            received.append(lax.ppermute(parts[step], "layer", [(i, i ^ step) for i in range(groups)]))
        return received

    stride = reach_rows + 8
    spread = call(
        spread_kernel, jax.ShapeDtypeStruct((tiles, stride, node_count), jnp.float32), [in_hbm] * 3,
        [
            pltpu.VMEM(section.shape, jnp.float32),
            pltpu.VMEM(cross_owner.shape, jnp.int32),
            pltpu.VMEM(cross_owner.shape, jnp.int32),
            pltpu.SemaphoreType.DMA((3,)),
        ],
        1, VMEM_MOST,
    )(section, cross_owner, cross_local)
    whole_section = lax.all_to_all(spread, "tile", 0, 0).reshape(tiles * stride, node_count)
    *own_blocks, land = call(
        prepare_kernel,
        (jax.ShapeDtypeStruct((2, held, span, breadth), jnp.float32),) * groups
        + (jax.ShapeDtypeStruct((span, breadth), jnp.float32),),
        [in_vmem] * 3 + [in_hbm], [], 0.5,
    )(head_start, soil_class, land_mask, spread)
    received = exchange(own_blocks)

    node_scratch = pltpu.VMEM((slots, LANES), jnp.float32)
    riv_shape = jax.ShapeDtypeStruct((blocks, LANES), jnp.float32)
    diag, rhs, slot_section, reach = call(
        functools.partial(river_kernel, breadth, span, stride),
        (
            riv_shape,
            riv_shape,
            jax.ShapeDtypeStruct((slots, node_count), jnp.float32),
            jax.ShapeDtypeStruct((1, slots), jnp.float32),
        ),
        [in_vmem] * 3,
        [node_scratch] * 6 + [pltpu.VMEM((span * breadth // BLOCK, LANES), jnp.float32)],
        7,
    )(cells, bed, whole_section)
    edges = jax.ShapeDtypeStruct(((2 * layers + 3) * HALO, breadth), jnp.float32)
    near_edge, far_edge = call(
        edge_kernel, (edges, edges), [in_vmem] * (3 + groups), [], 0.1,
    )(land, diag, rhs, *received)
    near_halo = lax.ppermute(near_edge, "layer", near)
    far_halo = lax.ppermute(far_edge, FLAT, far)

    window = span + 2 * HALO
    own_field = jax.ShapeDtypeStruct((per_row, span * layers, LANES), jnp.float32)
    field = pltpu.VMEM((per_row, window * layers, LANES), jnp.float32)
    staged = call(
        stage_kernel, (own_field,) * (4 + 5 * ITERS + HALO), [in_smem] * 3 + [in_vmem] * (3 + groups),
        [pltpu.VMEM(own_field.shape, jnp.float32)] + [pltpu.VMEM((span, breadth), jnp.float32)] * 3,
        4,
    )(ks_table, alpha_table, store_table, land, diag, rhs, *received)
    head_shape = jax.ShapeDtypeStruct((held, span, breadth), jnp.float32)
    *heads, top = call(
        flow_kernel,
        (head_shape,) * groups + (jax.ShapeDtypeStruct((span, breadth), jnp.float32),),
        [in_smem] * 3 + [in_vmem] * (5 + len(staged)),
        [field] * 12
        + [pltpu.VMEM((window, breadth), jnp.float32)]
        + [pltpu.VMEM((window * per_row, LANES), jnp.float32)] * 2
        + [pltpu.VMEM((window, breadth), jnp.float32)] * 3,
        3,
    )(ks_table, alpha_table, store_table, land, near_halo, far_halo, diag, rhs, *staged)
    tops = exchange([top] * groups)
    backs = exchange(heads)

    fold = reach_rows // groups
    packed = pltpu.VMEM((slots // groups, LANES), jnp.float32)
    partial = call(
        functools.partial(inflow_kernel, reach_rows, stride),
        jax.ShapeDtypeStruct((tiles * fold, node_count), jnp.float32),
        [in_vmem] * (4 + groups),
        [packed] * 3 + [pltpu.VMEM((across * per_row, LANES), jnp.float32)],
        3,
    )(cells, bed, slot_section, reach, *tops)
    partial, *backs = lax.optimization_barrier((partial, *backs))
    terms = lax.all_to_all(partial.reshape(tiles, fold, node_count), "tile", 0, 0)
    head = call(
        head_kernel, jax.ShapeDtypeStruct(head_start.shape, jnp.float32), [in_vmem] * groups,
        [pltpu.SemaphoreType.DMA((groups,))], 0.7, out_specs=in_hbm,
    )(*backs)
    inflow_shape = jax.ShapeDtypeStruct((reach_rows, node_count // groups), jnp.float32)
    return head, call(sum_kernel, inflow_shape, [in_vmem], [], 0.1)(terms)


def solution(mesh):
    placed = (
        P("layer", "tile", None),
        P("layer", "tile", None),
        P("tile", None),
        P(),
        P(),
        P(),
        P("tile", None),
        P("tile", None),
        P("tile", None),
        P("tile", None, None),
        P("tile", None, None),
    )
    return jax.shard_map(
        on_device,
        mesh=mesh,
        in_specs=placed,
        out_specs=(P("layer", "tile", None), P("tile", "layer")),
        check_vma=False,
    )
```

```python
import functools

import jax
import jax.numpy as jnp
from jax import lax
from jax.experimental import pallas as pl
from jax.experimental.pallas import tpu as pltpu
from jax.sharding import PartitionSpec as P

ITERS = 2
SWEEPS = 3

LATERAL = 1.0
VERTICAL = 2.0
GRAVITY = 1.0

HALO = ITERS * SWEEPS
BLOCK = 64
LANES = 128
VMEM_LIMIT = 32 * 1024 * 1024
VMEM_MOST = 60 * 1024 * 1024
FLAT = ("tile", "layer")

in_vmem = pl.BlockSpec(memory_space=pltpu.VMEM)
in_hbm = pl.BlockSpec(memory_space=pltpu.HBM)
in_smem = pl.BlockSpec(memory_space=pltpu.SMEM)


def bf16_pieces(value, count):
    pieces = []
    for _ in range(count):
        piece = value.astype(jnp.bfloat16)
        pieces.append(piece)
        value = value - piece.astype(jnp.float32)
    return pieces


def reciprocal(value):
    guess = pl.reciprocal(value, approx=True)
    return guess * (2.0 - value * guess)


def names_of(size):
    index = lax.broadcasted_iota(jnp.int32, (16, LANES), 0)
    return [(index + start).astype(jnp.float32).astype(jnp.bfloat16) for start in range(0, size, 16)]


def one_hot(row, names):
    one = jnp.ones((16, LANES), jnp.bfloat16)
    zero = jnp.zeros((16, LANES), jnp.bfloat16)
    return [jnp.maximum(one - jnp.abs(row - name), zero) for name in names]


def row_copies(ref, first, place):
    rows = ref[pl.ds(pl.multiple_of(first + place // 8 * 8, 8), 8), :]
    return jnp.broadcast_to(rows[place % 8:place % 8 + 1, :], (16, LANES)).astype(jnp.bfloat16)


def position():
    tile, layer = lax.axis_index("tile"), lax.axis_index("layer")
    groups = lax.axis_size("layer")
    flip = lax.rem(tile, 2)
    return layer, flip, jnp.where(flip == 1, groups - 1 - layer, layer)


def span_at(flip, groups, layer):
    return jnp.where(flip == 1, groups - 1 - layer, layer)


def split_cells(cells, first_row, breadth, width):
    local = cells - first_row * breadth
    shift = width.bit_length() - 1
    block = jnp.where(cells < 0, -1, local >> shift)
    return block.astype(jnp.float32), (local & (width - 1)).astype(jnp.float32)


def node_kernel(breadth, span, cells_ref, bed_ref, after_ref, *refs):
    del after_ref
    block_ref, spot_ref, high_ref, low_ref, lane_ref, bed_out_ref, hots_ref, block_sc = refs
    groups = lax.axis_size("layer")
    own_layer, _, number = position()
    cells, bed = cells_ref[...], bed_ref[...]
    block_ref[...], spot_ref[...] = split_cells(cells, number * span, breadth, BLOCK)
    high, low = bf16_pieces(bed, 2)
    high_ref[...] = high.astype(jnp.float32)
    low_ref[...] = low.astype(jnp.float32)

    packed_cells = pack_quarter(cells, groups, own_layer)
    bed_out_ref[...] = jnp.where(packed_cells >= 0, pack_quarter(bed, groups, own_layer), 0.0)
    block_sc[...], lane_ref[...] = split_cells(packed_cells, 0, breadth, LANES)
    names = names_of(hots_ref.shape[0])
    for row in range(block_sc.shape[0]):
        for tile, hot in enumerate(one_hot(row_copies(block_sc, 0, row), names)):
            hots_ref[pl.ds(tile * 16, 16), pl.ds(row * LANES, LANES)] = hot


def pack_quarter(field, groups, own_layer):
    quarter = LANES // groups
    packed = field.shape[0] // groups
    own = lax.broadcasted_iota(jnp.int32, (packed, LANES), 1) // quarter
    result = None
    for number in range(groups):
        shift = lax.rem((number + groups - own_layer) * quarter, LANES)
        moved = pltpu.roll(field[number * packed:(number + 1) * packed], shift, 1)
        result = moved if result is None else jnp.where(own == number, moved, result)
    return result


def river_kernel(
    stride, bed_ref, section_ref, block_ref, spot_ref, dhigh_ref, dlow_ref,
    diag_ref, rhs_ref, slot_section_ref, reach_ref, rhigh_sc, rlow_sc, sum_sc,
):
    rows = section_ref.shape[0]
    slots = reach_ref.shape[1]
    first = (lax.axis_index("tile") + 1) * stride - 8
    own_rows = section_ref[pl.ds(pl.multiple_of(first, 8), 8), :]
    reach = jnp.concatenate([own_rows[k:k + 1, :] for k in range(slots // LANES)], axis=1)
    reach_ref[...] = reach
    index = lax.broadcasted_iota(jnp.int32, (rows, slots), 0).astype(jnp.float32)
    pick = jnp.where(index == reach, 1.0, 0.0).astype(jnp.bfloat16)
    picked = jnp.zeros(slot_section_ref.shape, jnp.float32)
    for piece in bf16_pieces(section_ref[...], 3):
        picked = picked + lax.dot_general(
            pick, piece, (((0,), (0,)), ((), ())), preferred_element_type=jnp.float32
        )
    slot_section_ref[...] = picked

    high, low = bf16_pieces(bed_ref[...] * picked, 2)
    rhigh_sc[...] = high.astype(jnp.float32)
    rlow_sc[...] = low.astype(jnp.float32)
    share = LANES // BLOCK
    blocks = share * diag_ref.shape[0]
    group = 64
    block_names, spot_names = names_of(blocks), names_of(BLOCK)

    def matmul(first, places):
        left, right = [], []
        for place in places:
            left.append(jnp.concatenate(one_hot(row_copies(block_ref, first, place), block_names), axis=0))
            hot = one_hot(row_copies(spot_ref, first, place), spot_names)
            values = [row_copies(ref, first, place) for ref in (dhigh_ref, dlow_ref, rhigh_sc, rlow_sc)]
            right.append(jnp.concatenate([tile * value for value in values for tile in hot], axis=0))
        return lax.dot_general(
            jnp.concatenate(left, axis=1),
            jnp.concatenate(right, axis=1),
            (((1,), (1,)), ((), ())),
            preferred_element_type=jnp.float32,
        )

    def step(count, total):
        first = count * group
        half = group // 2
        return total + (matmul(first, range(half)) + matmul(first, range(half, group)))

    total = lax.fori_loop(0, slots // group, step, jnp.zeros((blocks, 4 * BLOCK), jnp.float32))
    low_half = lax.broadcasted_iota(jnp.int32, diag_ref.shape, 1) < BLOCK
    for count, ref in ((0, diag_ref), (1, rhs_ref)):
        part = total[:, count * LANES:(count + 1) * LANES]
        sum_sc[...] = part + pltpu.roll(part, BLOCK, 1)
        ref[...] = jnp.where(
            low_half, sum_sc[pl.ds(0, blocks // share, stride=share), :], sum_sc[pl.ds(1, blocks // share, stride=share), :]
        )


def edge_kernel(land_ref, diag_ref, rhs_ref, *refs):
    block_refs, (near_ref, far_ref) = refs[:-2], refs[-2:]
    _, held, span, breadth = block_refs[0].shape
    _, _, number = position()
    odd = lax.rem(number, 2) == 1
    per_row = breadth // LANES

    def put_edges(entry, top, bottom, lanes=slice(None)):
        near_ref[pl.ds(entry * HALO, HALO), lanes] = jnp.where(odd, top, bottom)
        far_ref[pl.ds(entry * HALO, HALO), lanes] = jnp.where(odd, bottom, top)

    entry = 0
    for kind in range(2):
        for block_ref in block_refs:
            for held_layer in range(held):
                put_edges(entry, block_ref[kind, held_layer, :HALO, :], block_ref[kind, held_layer, span - HALO:, :])
                entry += 1
    put_edges(entry, land_ref[:HALO, :], land_ref[span - HALO:, :])
    for ref in (diag_ref, rhs_ref):
        entry += 1
        for part in range(per_row):
            top = ref[pl.ds(part, HALO, stride=per_row), :]
            bottom = ref[pl.ds((span - HALO) * per_row + part, HALO, stride=per_row), :]
            put_edges(entry, top, bottom, slice(part * LANES, (part + 1) * LANES))


def spread_kernel(section_hbm, owner_hbm, local_hbm, spread_ref, section_ref, owner_ref, local_ref, sems):
    pairs = ((section_hbm, section_ref), (owner_hbm, owner_ref), (local_hbm, local_ref))
    copies = [pltpu.make_async_copy(here, there, sems.at[k]) for k, (here, there) in enumerate(pairs)]
    for copy in copies:
        copy.start()
    for copy in copies:
        copy.wait()
    tiles, stride, _ = spread_ref.shape
    reach_rows = section_ref.shape[0]
    reach = (owner_ref[...] * stride + local_ref[...]).astype(jnp.float32)
    parts = [reach[:, start:start + LANES] for start in range(0, reach.shape[1], LANES)]
    parts.append(jnp.zeros((stride - reach_rows - len(parts), LANES), jnp.float32))
    payload = jnp.concatenate([section_ref[...], *parts], axis=0)
    for tile in range(tiles):
        spread_ref[tile] = payload


def prepare_kernel(head_ref, soil_ref, land_ref, after_ref, *refs):
    del after_ref
    groups = lax.axis_size("layer")
    block_refs, land_out_ref = refs[:groups], refs[groups]
    held, across, _ = head_ref.shape
    span = across // groups
    own, flip, _ = position()

    def rows_of(target):
        return pl.ds(pl.multiple_of(span_at(flip, groups, target) * span, span), span)

    land_out_ref[...] = land_ref[rows_of(own), :].astype(jnp.float32)
    for step, block_ref in enumerate(block_refs):
        rows = rows_of(own ^ step)
        for layer in range(held):
            block_ref[0, layer] = head_ref[layer, rows, :]
            block_ref[1, layer] = soil_ref[layer, rows, :].astype(jnp.float32)


class Rows:
    def __init__(self, layers, breadth):
        self.layers, self.breadth, self.per_row = layers, breadth, breadth // LANES

    def get(self, ref, row):
        spot = pl.ds(row * self.layers, self.layers)
        return jnp.concatenate([ref[part, spot, :] for part in range(self.per_row)], axis=1)

    def put(self, ref, row, value):
        spot = pl.ds(row * self.layers, self.layers)
        for part in range(self.per_row):
            ref[part, spot, :] = value[:, part * LANES:(part + 1) * LANES]

    def put_layer(self, ref, layer, row, value):
        for part in range(self.per_row):
            spot = pl.ds(row * self.layers + layer, value.shape[0], stride=self.layers)
            ref[part, spot, :] = value[:, part * LANES:(part + 1) * LANES]

    def east(self, field):
        return pltpu.roll(field, self.breadth - 1, 1)

    def west(self, field):
        return pltpu.roll(field, 1, 1)

    def below(self, field):
        return pltpu.roll(field, self.layers - 1, 0)

    def above(self, field):
        return pltpu.roll(field, 1, 0)


class Joined:
    def __init__(self, rows, own, full, first, last):
        self.rows, self.own, self.full, self.first, self.last = rows, own, full, first, last

    def holds(self, row):
        return self.first <= row < self.last

    def get(self, row):
        if self.holds(row):
            return self.rows.get(self.own, row - HALO)
        return self.rows.get(self.full, row)

    def put(self, row, value):
        self.rows.put(self.full, row, value)


def relax_row(rows, row, head, weights, wx_before, base, inverse):
    before, here, after = head
    wx, wy, wz = [field.get(row) for field in weights]
    total = base.get(row) + wx_before * before + wx * after
    total = total + wy * rows.east(here) + rows.west(wy * here)
    total = total + wz * rows.below(here) + rows.above(wz * here)
    return total * inverse.get(row), wx


def river_row(rows, ref, row, top):
    parts = [
        jnp.broadcast_to(ref[pl.ds(row * rows.per_row + part, 1), :], (rows.layers, LANES))
        for part in range(rows.per_row)
    ]
    return jnp.where(top, jnp.concatenate(parts, axis=1), 0.0)


class Faces:
    def __init__(self, rows, land, lands):
        self.rows, self.lands = rows, lands
        lx_ref, ly_ref, lz_ref = lands
        count = land.shape[0]
        level = lax.broadcasted_iota(jnp.int32, (rows.layers, rows.breadth), 0)
        self.not_bottom = level < rows.layers - 1
        not_last = lax.broadcasted_iota(jnp.int32, land.shape, 1) < rows.breadth - 1
        lx_ref[pl.ds(0, count - 1), :] = 2.0 * LATERAL * land[:count - 1] * land[1:]
        ly_ref[...] = jnp.where(not_last, 2.0 * LATERAL * land * rows.east(land), 0.0)
        lz_ref[...] = 2.0 * VERTICAL * land * land

    def conduct(self, ks, alpha, head):
        return ks * jnp.exp(alpha * jnp.minimum(head, 0.0))

    def face(self, land, here, there):
        return land * (here * there) * reciprocal(here + there)

    def between_rows(self, row, here, there):
        return self.face(self.lands[0][pl.ds(row, 1), :], here, there)

    def in_row(self, row, here):
        rows = self.rows
        wy = self.face(self.lands[1][pl.ds(row, 1), :], here, rows.east(here))
        wz = self.face(self.lands[2][pl.ds(row, 1), :], here, rows.below(here))
        wz = jnp.where(self.not_bottom, wz, 0.0)
        wz_above = rows.above(wz)
        return wy, wz, wy + rows.west(wy) + wz + wz_above, GRAVITY * (wz_above - wz)


def lane_tables(refs, layers):
    lane = lax.broadcasted_iota(jnp.int32, (layers, LANES), 1)
    tables = []
    for ref in refs:
        table = jnp.zeros((layers, LANES), jnp.float32)
        for kind in range(ref.shape[0]):
            table = jnp.where(lane == kind, ref[kind], table)
        tables.append(table)
    return tables


def look_up(rows, table, soil):
    parts = [
        jnp.take_along_axis(table, soil[:, part * LANES:(part + 1) * LANES], axis=1, mode="promise_in_bounds")
        for part in range(rows.per_row)
    ]
    return jnp.concatenate(parts, axis=1)


def stage_kernel(ks_ref, alpha_ref, store_ref, land_ref, diag_ref, rhs_ref, *refs):
    groups = lax.axis_size("layer")
    own, _, _ = position()
    block_refs, refs = refs[:groups], refs[groups:]
    first_out, ks_out, alpha_out, store_out = refs[:4]
    fields = [refs[4 + 5 * picard:9 + 5 * picard] for picard in range(ITERS)]
    head_outs = refs[4 + 5 * ITERS:4 + 5 * ITERS + HALO]
    soil_sc, *lands = refs[4 + 5 * ITERS + HALO:]
    _, held, span, breadth = block_refs[0].shape
    layers = groups * held
    rows = Rows(layers, breadth)
    faces = Faces(rows, land_ref[...], lands)
    top = lax.broadcasted_iota(jnp.int32, (layers, breadth), 0) == 0

    for step, block_ref in enumerate(block_refs):
        for held_layer in range(held):
            layer = (own ^ step) * held + held_layer
            rows.put_layer(first_out, layer, 0, block_ref[0, held_layer])
            rows.put_layer(soil_sc, layer, 0, block_ref[1, held_layer])
    tables = lane_tables((ks_ref, alpha_ref, store_ref), layers)
    for row in range(span):
        soil = rows.get(soil_sc, row).astype(jnp.int32)
        for table, out in zip(tables, (ks_out, alpha_out, store_out)):
            rows.put(out, row, look_up(rows, table, soil))

    now, begin, stop, done = first_out, 0, span, 0
    for wx_out, wy_out, wz_out, inv_out, base_out in fields:
        before = None
        for row in range(begin, stop):
            here = faces.conduct(rows.get(ks_out, row), rows.get(alpha_out, row), rows.get(now, row))
            wy, wz, diagonal, gravity = faces.in_row(row, here)
            rows.put(wy_out, row, wy)
            rows.put(wz_out, row, wz)
            store = rows.get(store_out, row)
            sums = store + diagonal, store * rows.get(first_out, row) + gravity
            if row > begin:
                wx = faces.between_rows(row - 1, before[0], here)
                rows.put(wx_out, row - 1, wx)
                diagonal, base = before[1]
                if row - 1 > begin:
                    diagonal = reciprocal(diagonal + before[2] + wx + river_row(rows, diag_ref, row - 1, top))
                    base = base + river_row(rows, rhs_ref, row - 1, top)
                rows.put(inv_out, row - 1, diagonal)
                rows.put(base_out, row - 1, base)
            else:
                wx = None
            before = here, sums, wx
        rows.put(inv_out, stop - 1, before[1][0])
        rows.put(base_out, stop - 1, before[1][1])
        weights = [Joined(rows, None, ref, HALO, HALO) for ref in (wx_out, wy_out, wz_out)]
        base, inverse = [Joined(rows, None, ref, HALO, HALO) for ref in (base_out, inv_out)]
        for _ in range(SWEEPS):
            begin, stop = begin + 1, stop - 1
            head = rows.get(now, begin - 1), rows.get(now, begin)
            wx_before = rows.get(wx_out, begin - 1)
            for row in range(begin, stop):
                head = *head[-2:], rows.get(now, row + 1)
                value, wx_before = relax_row(rows, row, head, weights, wx_before, base, inverse)
                rows.put(head_outs[done], row, value)
            now = head_outs[done]
            done += 1


def flow_kernel(kst_ref, alphat_ref, storet_ref, land_ref, far_ref, near_ref, diag_ref, rhs_ref, *refs):
    groups = lax.axis_size("layer")
    own, _, number = position()
    end = (number == 0) | (number == groups - 1)
    far_partner = jnp.where(end, own, own ^ (groups - 1))
    first_ref, ks_ref, alpha_ref, store_ref = refs[:4]
    fields = [refs[4 + 5 * picard:9 + 5 * picard] for picard in range(ITERS)]
    staged_refs = refs[4 + 5 * ITERS:4 + 5 * ITERS + HALO]
    refs = refs[4 + 5 * ITERS + HALO:]
    head_refs, top_ref = refs[:groups], refs[groups]
    (
        first_sc, soil_sc, ks_sc, alpha_sc, store_sc, wx_sc, wy_sc, wz_sc, base_sc, inv_sc, ping_sc, pong_sc,
        land_sc, dtop_sc, rtop_sc, *lands,
    ) = refs[1 + groups:]
    held, span, breadth = head_refs[0].shape
    layers = groups * held
    window = span + 2 * HALO
    last_own = HALO + span
    rows = Rows(layers, breadth)
    side = HALO * rows.per_row

    land_sc[pl.ds(HALO, span), :] = land_ref[...]
    dtop_sc[pl.ds(side, span * rows.per_row), :] = diag_ref[...]
    rtop_sc[pl.ds(side, span * rows.per_row), :] = rhs_ref[...]

    def put_halo(ref, partner, row):
        def entry(number):
            return ref[pl.ds(number * HALO, HALO), :]

        for count in range(layers):
            layer = (partner ^ (count // held)) * held + count % held
            rows.put_layer(first_sc, layer, row, entry(count))
            rows.put_layer(soil_sc, layer, row, entry(layers + count))
        land_sc[pl.ds(row, HALO), :] = entry(2 * layers)
        for count, top_sc in ((2 * layers + 1, dtop_sc), (2 * layers + 2, rtop_sc)):
            value = entry(count)
            for part in range(rows.per_row):
                spot = pl.ds(row * rows.per_row + part, HALO, stride=rows.per_row)
                top_sc[spot, :] = value[:, part * LANES:(part + 1) * LANES]

    for odd, above_ref, below_ref in ((0, far_ref, near_ref), (1, near_ref, far_ref)):
        @pl.when(lax.rem(number, 2) == odd)
        def _(above_ref=above_ref, below_ref=below_ref):
            for ref, row in ((above_ref, 0), (below_ref, last_own)):
                put_halo(ref, own ^ 1 if ref is near_ref else far_partner, row)

    faces = Faces(rows, land_sc[...], lands)
    tables = lane_tables((kst_ref, alphat_ref, storet_ref), layers)
    for row in [*range(HALO), *range(last_own, window)]:
        soil = rows.get(soil_sc, row).astype(jnp.int32)
        for table, ref in zip(tables, (ks_sc, alpha_sc, store_sc)):
            rows.put(ref, row, look_up(rows, table, soil))

    first, ks, alpha, store = [
        Joined(rows, held_ref, full, HALO, last_own)
        for held_ref, full in ((first_ref, first_sc), (ks_ref, ks_sc), (alpha_ref, alpha_sc), (store_ref, store_sc))
    ]
    top = lax.broadcasted_iota(jnp.int32, (layers, breadth), 0) == 0

    now, begin, stop, done = first, 0, window, 0
    for wx_ref, wy_ref, wz_ref, inv_ref, base_ref in fields:
        low, high = HALO + done, last_own - done
        wx_of = Joined(rows, wx_ref, wx_sc, low, high - 1)
        wy_of, wz_of = Joined(rows, wy_ref, wy_sc, low, high), Joined(rows, wz_ref, wz_sc, low, high)
        inverse, base = [
            Joined(rows, held_ref, full, low + 1, high - 1) for held_ref, full in ((inv_ref, inv_sc), (base_ref, base_sc))
        ]
        here_before, wx_before, sums_before = None, None, None
        for row in range(begin, stop):
            at_end = row in (low, high - 1)
            here, sums = None, None
            if not wy_of.holds(row) or at_end:
                here = faces.conduct(ks.get(row), alpha.get(row), now.get(row))
            if at_end:
                sums = rows.get(inv_ref, row - HALO), rows.get(base_ref, row - HALO)
            elif not wy_of.holds(row) and begin < row < stop - 1:
                wy, wz, diagonal, gravity = faces.in_row(row, here)
                wy_of.put(row, wy)
                wz_of.put(row, wz)
                sums = store.get(row) + diagonal, store.get(row) * first.get(row) + gravity
            if row > begin:
                if wx_of.holds(row - 1):
                    wx = wx_of.get(row - 1)
                else:
                    wx = faces.between_rows(row - 1, here_before, here)
                    wx_of.put(row - 1, wx)
                if sums_before is not None:
                    diagonal = sums_before[0] + wx_before + wx + river_row(rows, dtop_sc, row - 1, top)
                    inverse.put(row - 1, reciprocal(diagonal))
                    base.put(row - 1, sums_before[1] + river_row(rows, rtop_sc, row - 1, top))
                wx_before = wx
            here_before, sums_before = here, sums
        for _ in range(SWEEPS):
            begin, stop = begin + 1, stop - 1
            later = Joined(rows, staged_refs[done], (ping_sc, pong_sc)[done % 2], HALO + done + 1, last_own - done - 1)
            done += 1
            for row in range(begin, stop):
                if not later.holds(row):
                    head = now.get(row - 1), now.get(row), now.get(row + 1)
                    value, _ = relax_row(rows, row, head, (wx_of, wy_of, wz_of), wx_of.get(row - 1), base, inverse)
                    later.put(row, value)
            now = later
    for row in range(now.first, now.last):
        now.put(row, now.get(row))
    for part in range(rows.per_row):
        lanes = pl.ds(part * LANES, LANES)
        top_ref[:, lanes] = now.full[part, pl.ds(HALO * layers, span, stride=layers), :]
        for step, head_ref in enumerate(head_refs):
            for held_layer in range(held):
                layer = (own ^ step) * held + held_layer
                head_ref[held_layer, :, lanes] = now.full[part, pl.ds(HALO * layers + layer, span, stride=layers), :]


def inflow_kernel(reach_rows, stride, lane_ref, bed_ref, hots_ref, slot_section_ref, reach_ref, *refs):
    groups = lax.axis_size("layer")
    own_layer, flip, _ = position()
    top_refs = refs[:groups]
    out_ref, found_sc, turned_sc = refs[groups:]
    span, breadth = top_refs[0].shape
    per_row = breadth // LANES
    slots = reach_ref.shape[1]
    quarter = LANES // groups
    for step, top_ref in enumerate(top_refs):
        number = span_at(flip, groups, own_layer ^ step)
        for part in range(per_row):
            spot = pl.ds(number * span * per_row + part, span, stride=per_row)
            turned_sc[spot, :] = top_ref[:, part * LANES:(part + 1) * LANES]
    table = jnp.concatenate(bf16_pieces(turned_sc[...].T, 2), axis=0)
    index = lax.broadcasted_iota(jnp.int32, (8, LANES), 0).astype(jnp.float32)
    for pair in range(0, lane_ref.shape[0], 2):
        found = lax.dot_general(
            table, hots_ref[:, pl.ds(pair * LANES, 2 * LANES)], (((1,), (0,)), ((), ())),
            preferred_element_type=jnp.float32,
        )
        found = found[:LANES] + found[LANES:]
        for row in (pair, pair + 1):
            lanes = jnp.broadcast_to(lane_ref[pl.ds(row, 1), :], (8, LANES))
            mine = found[:, (row - pair) * LANES:(row - pair + 1) * LANES]
            total = jnp.zeros((8, LANES), jnp.float32)
            for start in range(0, LANES, 8):
                total = total + jnp.where(lanes == index + float(start), mine[start:start + 8], 0.0)
            found_sc[pl.ds(row, 1), :] = jnp.sum(total, axis=0, keepdims=True)
    slot_in = bed_ref[...] * (found_sc[...] - pack_quarter(slot_section_ref[...], groups, own_layer))
    spread = jnp.concatenate(
        [slot_in if number == 0 else pltpu.roll(slot_in, LANES - number * quarter, 1) for number in range(groups)],
        axis=0,
    )
    in_quarter = lax.broadcasted_iota(jnp.int32, spread.shape, 1) < quarter
    pieces = bf16_pieces(jnp.where(in_quarter, spread, 0.0), 3)
    fold = reach_rows // groups
    index = lax.broadcasted_iota(jnp.int32, (out_ref.shape[0], slots), 0)
    index = index // fold * stride + lax.rem(index, fold)
    result = None
    for number in range(groups):
        name = (index + number * fold).astype(jnp.float32)
        put = jnp.where(name == reach_ref[...], 1.0, 0.0).astype(jnp.bfloat16)
        total = jnp.zeros(out_ref.shape, jnp.float32)
        for piece in pieces:
            total = total + lax.dot_general(
                put, piece, (((1,), (0,)), ((), ())), preferred_element_type=jnp.float32
            )
        result = total if result is None else result + pltpu.roll(total, number * quarter, 1)
    out_ref[...] = result


def sum_kernel(terms_ref, inflow_ref):
    total = terms_ref[0]
    for tile in range(1, terms_ref.shape[0]):
        total = total + terms_ref[tile]
    fold, quarter = total.shape[0], inflow_ref.shape[1]
    for number in range(inflow_ref.shape[0] // fold):
        lanes = slice(number * quarter, (number + 1) * quarter)
        inflow_ref[pl.ds(number * fold, fold), :] = total[:, lanes]


def head_kernel(*refs):
    groups = lax.axis_size("layer")
    back_refs, (head_hbm, sems) = refs[:groups], refs[groups:]
    _, span, _ = back_refs[0].shape
    own, flip, _ = position()
    copies = []
    for step, back_ref in enumerate(back_refs):
        rows = pl.ds(pl.multiple_of(span_at(flip, groups, own ^ step) * span, span), span)
        copies.append(pltpu.make_async_copy(back_ref, head_hbm.at[:, rows, :], sems.at[step]))
        copies[-1].start()
    for copy in copies:
        copy.wait()


def call(kernel, out_shape, in_specs, scratch, micros, vmem=VMEM_LIMIT, out_specs=None):
    single = not isinstance(out_shape, (tuple, list))
    return pl.pallas_call(
        kernel,
        out_shape=out_shape,
        in_specs=in_specs,
        out_specs=out_specs or (in_vmem if single else tuple(in_vmem for _ in out_shape)),
        scratch_shapes=scratch,
        compiler_params=pltpu.CompilerParams(vmem_limit_bytes=vmem),
        cost_estimate=pl.CostEstimate(flops=int(micros * 1.15e9), bytes_accessed=0, transcendentals=0),
    )


def on_device(
    head_start,
    soil_class,
    land_mask,
    ks_table,
    alpha_table,
    store_table,
    section,
    cross_owner,
    cross_local,
    node_cell,
    bed_cond,
):
    held, across, breadth = head_start.shape
    reach_rows, node_count = section.shape
    tiles = lax.axis_size("tile")
    groups = lax.axis_size("layer")
    layers = held * groups
    span = across // groups
    per_row = breadth // LANES
    blocks = span * per_row
    near = [(i, i ^ 1) for i in range(groups)]
    far = []
    for upper in range(tiles):
        far += [(upper * groups + i, upper * groups + (i ^ (groups - 1))) for i in range(1, groups - 1)]
        if upper + 1 < tiles:
            index = groups - 1 if upper % 2 == 0 else 0
            one, two = upper * groups + index, (upper + 1) * groups + index
            far += [(one, two), (two, one)]

    cells = node_cell[0]
    bed = bed_cond[0]
    slots = cells.shape[0]

    def exchange(parts):
        received = [parts[0]]
        for step in range(1, groups):
            received.append(lax.ppermute(parts[step], "layer", [(i, i ^ step) for i in range(groups)]))
        return received

    stride = reach_rows + 8
    spread = call(
        spread_kernel, jax.ShapeDtypeStruct((tiles, stride, node_count), jnp.float32), [in_hbm] * 3,
        [
            pltpu.VMEM(section.shape, jnp.float32),
            pltpu.VMEM(cross_owner.shape, jnp.int32),
            pltpu.VMEM(cross_owner.shape, jnp.int32),
            pltpu.SemaphoreType.DMA((3,)),
        ],
        1, VMEM_MOST,
    )(section, cross_owner, cross_local)
    whole_section = lax.all_to_all(spread, "tile", 0, 0).reshape(tiles * stride, node_count)
    *own_blocks, land = call(
        prepare_kernel,
        (jax.ShapeDtypeStruct((2, held, span, breadth), jnp.float32),) * groups
        + (jax.ShapeDtypeStruct((span, breadth), jnp.float32),),
        [in_vmem] * 3 + [in_hbm], [], 0.5,
    )(head_start, soil_class, land_mask, spread)
    received = exchange(own_blocks)

    node_scratch = pltpu.VMEM((slots, LANES), jnp.float32)
    riv_shape = jax.ShapeDtypeStruct((blocks, LANES), jnp.float32)
    field = jax.ShapeDtypeStruct((slots, LANES), jnp.float32)
    packed = jax.ShapeDtypeStruct((slots // groups, LANES), jnp.float32)
    *parts, lanes, bed_packed, hots = call(
        functools.partial(node_kernel, breadth, span),
        (field,) * 4 + (packed,) * 2
        + (jax.ShapeDtypeStruct((across * per_row, slots // groups * LANES), jnp.bfloat16),),
        [in_vmem] * 3, [pltpu.VMEM(packed.shape, jnp.float32)], 1,
    )(cells, bed, land)
    diag, rhs, slot_section, reach = call(
        functools.partial(river_kernel, stride),
        (riv_shape, riv_shape, field, jax.ShapeDtypeStruct((1, slots), jnp.float32)),
        [in_vmem] * 6, [node_scratch] * 2 + [pltpu.VMEM((span * breadth // BLOCK, LANES), jnp.float32)], 7,
    )(bed, whole_section, *parts)
    edges = jax.ShapeDtypeStruct(((2 * layers + 3) * HALO, breadth), jnp.float32)
    near_edge, far_edge = call(
        edge_kernel, (edges, edges), [in_vmem] * (3 + groups), [], 0.1,
    )(land, diag, rhs, *received)
    far_halo = lax.ppermute(far_edge, FLAT, far)
    near_halo = lax.ppermute(near_edge, "layer", near)

    window = span + 2 * HALO
    own_field = jax.ShapeDtypeStruct((per_row, span * layers, LANES), jnp.float32)
    field = pltpu.VMEM((per_row, window * layers, LANES), jnp.float32)
    staged = call(
        stage_kernel, (own_field,) * (4 + 5 * ITERS + HALO), [in_smem] * 3 + [in_vmem] * (3 + groups),
        [pltpu.VMEM(own_field.shape, jnp.float32)] + [pltpu.VMEM((span, breadth), jnp.float32)] * 3,
        4,
    )(ks_table, alpha_table, store_table, land, diag, rhs, *received)
    head_shape = jax.ShapeDtypeStruct((held, span, breadth), jnp.float32)
    *heads, top = call(
        flow_kernel,
        (head_shape,) * groups + (jax.ShapeDtypeStruct((span, breadth), jnp.float32),),
        [in_smem] * 3 + [in_vmem] * (5 + len(staged)),
        [field] * 12
        + [pltpu.VMEM((window, breadth), jnp.float32)]
        + [pltpu.VMEM((window * per_row, LANES), jnp.float32)] * 2
        + [pltpu.VMEM((window, breadth), jnp.float32)] * 3,
        3,
    )(ks_table, alpha_table, store_table, land, far_halo, near_halo, diag, rhs, *staged)
    tops = exchange([top] * groups)
    backs = exchange(heads)

    fold = reach_rows // groups
    partial = call(
        functools.partial(inflow_kernel, reach_rows, stride),
        jax.ShapeDtypeStruct((tiles * fold, node_count), jnp.float32), [in_vmem] * (5 + groups),
        [pltpu.VMEM(packed.shape, jnp.float32), pltpu.VMEM((across * per_row, LANES), jnp.float32)], 3,
    )(lanes, bed_packed, hots, slot_section, reach, *tops)
    partial, *backs = lax.optimization_barrier((partial, *backs))
    terms = lax.all_to_all(partial.reshape(tiles, fold, node_count), "tile", 0, 0)
    head = call(
        head_kernel, jax.ShapeDtypeStruct(head_start.shape, jnp.float32), [in_vmem] * groups,
        [pltpu.SemaphoreType.DMA((groups,))], 0.7, out_specs=in_hbm,
    )(*backs)
    inflow_shape = jax.ShapeDtypeStruct((reach_rows, node_count // groups), jnp.float32)
    return head, call(sum_kernel, inflow_shape, [in_vmem], [], 0.1)(terms)


def solution(mesh):
    placed = (
        P("layer", "tile", None),
        P("layer", "tile", None),
        P("tile", None),
        P(),
        P(),
        P(),
        P("tile", None),
        P("tile", None),
        P("tile", None),
        P("tile", None, None),
        P("tile", None, None),
    )
    return jax.shard_map(
        on_device,
        mesh=mesh,
        in_specs=placed,
        out_specs=(P("layer", "tile", None), P("tile", "layer")),
        check_vma=False,
    )
```

```python
import functools

import jax
import jax.numpy as jnp
from jax import lax
from jax.experimental import pallas as pl
from jax.experimental.pallas import tpu as pltpu
from jax.sharding import PartitionSpec as P

ITERS = 2
SWEEPS = 3

LATERAL = 1.0
VERTICAL = 2.0
GRAVITY = 1.0

HALO = ITERS * SWEEPS
BLOCK = 64
LANES = 128
VMEM_LIMIT = 32 * 1024 * 1024
VMEM_MOST = 60 * 1024 * 1024
FLAT = ("tile", "layer")

in_vmem = pl.BlockSpec(memory_space=pltpu.VMEM)
in_hbm = pl.BlockSpec(memory_space=pltpu.HBM)
in_smem = pl.BlockSpec(memory_space=pltpu.SMEM)


def bf16_pieces(value, count):
    pieces = []
    for _ in range(count):
        piece = value.astype(jnp.bfloat16)
        pieces.append(piece)
        value = value - piece.astype(jnp.float32)
    return pieces


def reciprocal(value):
    guess = pl.reciprocal(value, approx=True)
    return guess * (2.0 - value * guess)


def names_of(size):
    index = lax.broadcasted_iota(jnp.int32, (16, LANES), 0)
    return [(index + start).astype(jnp.float32).astype(jnp.bfloat16) for start in range(0, size, 16)]


def one_hot(row, names):
    one = jnp.ones((16, LANES), jnp.bfloat16)
    zero = jnp.zeros((16, LANES), jnp.bfloat16)
    return [jnp.maximum(one - jnp.abs(row - name), zero) for name in names]


def row_copies(ref, first, place):
    rows = ref[pl.ds(pl.multiple_of(first + place // 8 * 8, 8), 8), :]
    return jnp.broadcast_to(rows[place % 8:place % 8 + 1, :], (16, LANES)).astype(jnp.bfloat16)


def position():
    tile, layer = lax.axis_index("tile"), lax.axis_index("layer")
    groups = lax.axis_size("layer")
    flip = lax.rem(tile, 2)
    return layer, flip, jnp.where(flip == 1, groups - 1 - layer, layer)


def span_at(flip, groups, layer):
    return jnp.where(flip == 1, groups - 1 - layer, layer)


def split_cells(cells, first_row, breadth, width):
    local = cells - first_row * breadth
    shift = width.bit_length() - 1
    block = jnp.where(cells < 0, -1, local >> shift)
    return block.astype(jnp.float32), (local & (width - 1)).astype(jnp.float32)


def river_kernel(
    breadth, span, stride, cells_ref, bed_ref, section_ref,
    diag_ref, rhs_ref, slot_section_ref, reach_ref, block_sc, spot_sc, dhigh_sc, dlow_sc, rhigh_sc, rlow_sc, sum_sc,
):
    _, _, number = position()
    rows = section_ref.shape[0]
    slots = reach_ref.shape[1]
    first = (lax.axis_index("tile") + 1) * stride - 8
    own_rows = section_ref[pl.ds(pl.multiple_of(first, 8), 8), :]
    reach = jnp.concatenate([own_rows[k:k + 1, :] for k in range(slots // LANES)], axis=1)
    reach_ref[...] = reach
    index = lax.broadcasted_iota(jnp.int32, (rows, slots), 0).astype(jnp.float32)
    pick = jnp.where(index == reach, 1.0, 0.0).astype(jnp.bfloat16)
    picked = jnp.zeros(slot_section_ref.shape, jnp.float32)
    for piece in bf16_pieces(section_ref[...], 3):
        picked = picked + lax.dot_general(
            pick, piece, (((0,), (0,)), ((), ())), preferred_element_type=jnp.float32
        )
    slot_section_ref[...] = picked

    block, spot = split_cells(cells_ref[...], number * span, breadth, BLOCK)
    block_sc[...] = block
    spot_sc[...] = spot
    bed = bed_ref[...]
    for value, high_sc, low_sc in ((bed, dhigh_sc, dlow_sc), (bed * picked, rhigh_sc, rlow_sc)):
        high, low = bf16_pieces(value, 2)
        high_sc[...] = high.astype(jnp.float32)
        low_sc[...] = low.astype(jnp.float32)
    share = LANES // BLOCK
    blocks = share * diag_ref.shape[0]
    group = 64
    block_names, spot_names = names_of(blocks), names_of(BLOCK)

    def matmul(first, places):
        left, right = [], []
        for place in places:
            left.append(jnp.concatenate(one_hot(row_copies(block_sc, first, place), block_names), axis=0))
            hot = one_hot(row_copies(spot_sc, first, place), spot_names)
            values = [row_copies(ref, first, place) for ref in (dhigh_sc, dlow_sc, rhigh_sc, rlow_sc)]
            right.append(jnp.concatenate([tile * value for value in values for tile in hot], axis=0))
        return lax.dot_general(
            jnp.concatenate(left, axis=1),
            jnp.concatenate(right, axis=1),
            (((1,), (1,)), ((), ())),
            preferred_element_type=jnp.float32,
        )

    def step(count, total):
        first = count * group
        half = group // 2
        return total + (matmul(first, range(half)) + matmul(first, range(half, group)))

    total = lax.fori_loop(0, slots // group, step, jnp.zeros((blocks, 4 * BLOCK), jnp.float32))
    low_half = lax.broadcasted_iota(jnp.int32, diag_ref.shape, 1) < BLOCK
    for count, ref in ((0, diag_ref), (1, rhs_ref)):
        part = total[:, count * LANES:(count + 1) * LANES]
        sum_sc[...] = part + pltpu.roll(part, BLOCK, 1)
        ref[...] = jnp.where(
            low_half, sum_sc[pl.ds(0, blocks // share, stride=share), :], sum_sc[pl.ds(1, blocks // share, stride=share), :]
        )


def edge_kernel(land_ref, diag_ref, rhs_ref, *refs):
    block_refs, (near_ref, far_ref) = refs[:-2], refs[-2:]
    _, held, span, breadth = block_refs[0].shape
    _, _, number = position()
    odd = lax.rem(number, 2) == 1
    per_row = breadth // LANES

    def put_edges(entry, top, bottom, lanes=slice(None)):
        near_ref[pl.ds(entry * HALO, HALO), lanes] = jnp.where(odd, top, bottom)
        far_ref[pl.ds(entry * HALO, HALO), lanes] = jnp.where(odd, bottom, top)

    entry = 0
    for kind in range(2):
        for block_ref in block_refs:
            for held_layer in range(held):
                put_edges(entry, block_ref[kind, held_layer, :HALO, :], block_ref[kind, held_layer, span - HALO:, :])
                entry += 1
    put_edges(entry, land_ref[:HALO, :], land_ref[span - HALO:, :])
    for ref in (diag_ref, rhs_ref):
        entry += 1
        for part in range(per_row):
            top = ref[pl.ds(part, HALO, stride=per_row), :]
            bottom = ref[pl.ds((span - HALO) * per_row + part, HALO, stride=per_row), :]
            put_edges(entry, top, bottom, slice(part * LANES, (part + 1) * LANES))


def spread_kernel(section_hbm, owner_hbm, local_hbm, spread_ref, section_ref, owner_ref, local_ref, sems):
    pairs = ((section_hbm, section_ref), (owner_hbm, owner_ref), (local_hbm, local_ref))
    copies = [pltpu.make_async_copy(here, there, sems.at[k]) for k, (here, there) in enumerate(pairs)]
    for copy in copies:
        copy.start()
    for copy in copies:
        copy.wait()
    tiles, stride, _ = spread_ref.shape
    reach_rows = section_ref.shape[0]
    reach = (owner_ref[...] * stride + local_ref[...]).astype(jnp.float32)
    parts = [reach[:, start:start + LANES] for start in range(0, reach.shape[1], LANES)]
    parts.append(jnp.zeros((stride - reach_rows - len(parts), LANES), jnp.float32))
    payload = jnp.concatenate([section_ref[...], *parts], axis=0)
    for tile in range(tiles):
        spread_ref[tile] = payload


def prepare_kernel(head_ref, soil_ref, land_ref, after_ref, *refs):
    del after_ref
    groups = lax.axis_size("layer")
    block_refs, land_out_ref = refs[:groups], refs[groups]
    held, across, _ = head_ref.shape
    span = across // groups
    own, flip, _ = position()

    def rows_of(target):
        return pl.ds(pl.multiple_of(span_at(flip, groups, target) * span, span), span)

    land_out_ref[...] = land_ref[rows_of(own), :].astype(jnp.float32)
    for step, block_ref in enumerate(block_refs):
        rows = rows_of(own ^ step)
        for layer in range(held):
            block_ref[0, layer] = head_ref[layer, rows, :]
            block_ref[1, layer] = soil_ref[layer, rows, :].astype(jnp.float32)


class Rows:
    def __init__(self, layers, breadth):
        self.layers, self.breadth, self.per_row = layers, breadth, breadth // LANES

    def get(self, ref, row):
        spot = pl.ds(row * self.layers, self.layers)
        return jnp.concatenate([ref[part, spot, :] for part in range(self.per_row)], axis=1)

    def put(self, ref, row, value):
        spot = pl.ds(row * self.layers, self.layers)
        for part in range(self.per_row):
            ref[part, spot, :] = value[:, part * LANES:(part + 1) * LANES]

    def put_layer(self, ref, layer, row, value):
        for part in range(self.per_row):
            spot = pl.ds(row * self.layers + layer, value.shape[0], stride=self.layers)
            ref[part, spot, :] = value[:, part * LANES:(part + 1) * LANES]

    def east(self, field):
        return pltpu.roll(field, self.breadth - 1, 1)

    def west(self, field):
        return pltpu.roll(field, 1, 1)

    def below(self, field):
        return pltpu.roll(field, self.layers - 1, 0)

    def above(self, field):
        return pltpu.roll(field, 1, 0)


class Joined:
    def __init__(self, rows, own, full, first, last):
        self.rows, self.own, self.full, self.first, self.last = rows, own, full, first, last

    def holds(self, row):
        return self.first <= row < self.last

    def get(self, row):
        if self.holds(row):
            return self.rows.get(self.own, row - HALO)
        return self.rows.get(self.full, row)

    def put(self, row, value):
        self.rows.put(self.full, row, value)


def relax_row(rows, row, head, weights, wx_before, base, inverse):
    before, here, after = head
    wx, wy, wz = [field.get(row) for field in weights]
    total = base.get(row) + wx_before * before + wx * after
    total = total + wy * rows.east(here) + rows.west(wy * here)
    total = total + wz * rows.below(here) + rows.above(wz * here)
    return total * inverse.get(row), wx


def river_row(rows, ref, row, top):
    parts = [
        jnp.broadcast_to(ref[pl.ds(row * rows.per_row + part, 1), :], (rows.layers, LANES))
        for part in range(rows.per_row)
    ]
    return jnp.where(top, jnp.concatenate(parts, axis=1), 0.0)


class Faces:
    def __init__(self, rows, land, lands):
        self.rows, self.lands = rows, lands
        lx_ref, ly_ref, lz_ref = lands
        count = land.shape[0]
        level = lax.broadcasted_iota(jnp.int32, (rows.layers, rows.breadth), 0)
        self.not_bottom = level < rows.layers - 1
        not_last = lax.broadcasted_iota(jnp.int32, land.shape, 1) < rows.breadth - 1
        lx_ref[pl.ds(0, count - 1), :] = 2.0 * LATERAL * land[:count - 1] * land[1:]
        ly_ref[...] = jnp.where(not_last, 2.0 * LATERAL * land * rows.east(land), 0.0)
        lz_ref[...] = 2.0 * VERTICAL * land * land

    def conduct(self, ks, alpha, head):
        return ks * jnp.exp(alpha * jnp.minimum(head, 0.0))

    def face(self, land, here, there):
        return land * (here * there) * reciprocal(here + there)

    def between_rows(self, row, here, there):
        return self.face(self.lands[0][pl.ds(row, 1), :], here, there)

    def in_row(self, row, here):
        rows = self.rows
        wy = self.face(self.lands[1][pl.ds(row, 1), :], here, rows.east(here))
        wz = self.face(self.lands[2][pl.ds(row, 1), :], here, rows.below(here))
        wz = jnp.where(self.not_bottom, wz, 0.0)
        wz_above = rows.above(wz)
        return wy, wz, wy + rows.west(wy) + wz + wz_above, GRAVITY * (wz_above - wz)


def lane_tables(refs, layers):
    lane = lax.broadcasted_iota(jnp.int32, (layers, LANES), 1)
    tables = []
    for ref in refs:
        table = jnp.zeros((layers, LANES), jnp.float32)
        for kind in range(ref.shape[0]):
            table = jnp.where(lane == kind, ref[kind], table)
        tables.append(table)
    return tables


def look_up(rows, table, soil):
    parts = [
        jnp.take_along_axis(table, soil[:, part * LANES:(part + 1) * LANES], axis=1, mode="promise_in_bounds")
        for part in range(rows.per_row)
    ]
    return jnp.concatenate(parts, axis=1)


def stage_kernel(ks_ref, alpha_ref, store_ref, land_ref, diag_ref, rhs_ref, *refs):
    groups = lax.axis_size("layer")
    own, _, _ = position()
    block_refs, refs = refs[:groups], refs[groups:]
    first_out, ks_out, alpha_out, store_out = refs[:4]
    fields = [refs[4 + 5 * picard:9 + 5 * picard] for picard in range(ITERS)]
    head_outs = refs[4 + 5 * ITERS:4 + 5 * ITERS + HALO]
    soil_sc, *lands = refs[4 + 5 * ITERS + HALO:]
    _, held, span, breadth = block_refs[0].shape
    layers = groups * held
    rows = Rows(layers, breadth)
    faces = Faces(rows, land_ref[...], lands)
    top = lax.broadcasted_iota(jnp.int32, (layers, breadth), 0) == 0

    for step, block_ref in enumerate(block_refs):
        for held_layer in range(held):
            layer = (own ^ step) * held + held_layer
            rows.put_layer(first_out, layer, 0, block_ref[0, held_layer])
            rows.put_layer(soil_sc, layer, 0, block_ref[1, held_layer])
    tables = lane_tables((ks_ref, alpha_ref, store_ref), layers)
    for row in range(span):
        soil = rows.get(soil_sc, row).astype(jnp.int32)
        for table, out in zip(tables, (ks_out, alpha_out, store_out)):
            rows.put(out, row, look_up(rows, table, soil))

    now, begin, stop, done = first_out, 0, span, 0
    for wx_out, wy_out, wz_out, inv_out, base_out in fields:
        before = None
        for row in range(begin, stop):
            here = faces.conduct(rows.get(ks_out, row), rows.get(alpha_out, row), rows.get(now, row))
            wy, wz, diagonal, gravity = faces.in_row(row, here)
            rows.put(wy_out, row, wy)
            rows.put(wz_out, row, wz)
            store = rows.get(store_out, row)
            sums = store + diagonal, store * rows.get(first_out, row) + gravity
            if row > begin:
                wx = faces.between_rows(row - 1, before[0], here)
                rows.put(wx_out, row - 1, wx)
                diagonal, base = before[1]
                if row - 1 > begin:
                    diagonal = reciprocal(diagonal + before[2] + wx + river_row(rows, diag_ref, row - 1, top))
                    base = base + river_row(rows, rhs_ref, row - 1, top)
                rows.put(inv_out, row - 1, diagonal)
                rows.put(base_out, row - 1, base)
            else:
                wx = None
            before = here, sums, wx
        rows.put(inv_out, stop - 1, before[1][0])
        rows.put(base_out, stop - 1, before[1][1])
        weights = [Joined(rows, None, ref, HALO, HALO) for ref in (wx_out, wy_out, wz_out)]
        base, inverse = [Joined(rows, None, ref, HALO, HALO) for ref in (base_out, inv_out)]
        for _ in range(SWEEPS):
            begin, stop = begin + 1, stop - 1
            head = rows.get(now, begin - 1), rows.get(now, begin)
            wx_before = rows.get(wx_out, begin - 1)
            for row in range(begin, stop):
                head = *head[-2:], rows.get(now, row + 1)
                value, wx_before = relax_row(rows, row, head, weights, wx_before, base, inverse)
                rows.put(head_outs[done], row, value)
            now = head_outs[done]
            done += 1


def flow_kernel(kst_ref, alphat_ref, storet_ref, land_ref, far_ref, near_ref, diag_ref, rhs_ref, *refs):
    groups = lax.axis_size("layer")
    own, _, number = position()
    end = (number == 0) | (number == groups - 1)
    far_partner = jnp.where(end, own, own ^ (groups - 1))
    first_ref, ks_ref, alpha_ref, store_ref = refs[:4]
    fields = [refs[4 + 5 * picard:9 + 5 * picard] for picard in range(ITERS)]
    staged_refs = refs[4 + 5 * ITERS:4 + 5 * ITERS + HALO]
    refs = refs[4 + 5 * ITERS + HALO:]
    head_refs, top_ref = refs[:groups], refs[groups]
    (
        first_sc, soil_sc, ks_sc, alpha_sc, store_sc, wx_sc, wy_sc, wz_sc, base_sc, inv_sc, ping_sc, pong_sc,
        land_sc, dtop_sc, rtop_sc, *lands,
    ) = refs[1 + groups:]
    held, span, breadth = head_refs[0].shape
    layers = groups * held
    window = span + 2 * HALO
    last_own = HALO + span
    rows = Rows(layers, breadth)
    side = HALO * rows.per_row

    land_sc[pl.ds(HALO, span), :] = land_ref[...]
    dtop_sc[pl.ds(side, span * rows.per_row), :] = diag_ref[...]
    rtop_sc[pl.ds(side, span * rows.per_row), :] = rhs_ref[...]

    def put_halo(ref, partner, row):
        def entry(number):
            return ref[pl.ds(number * HALO, HALO), :]

        for count in range(layers):
            layer = (partner ^ (count // held)) * held + count % held
            rows.put_layer(first_sc, layer, row, entry(count))
            rows.put_layer(soil_sc, layer, row, entry(layers + count))
        land_sc[pl.ds(row, HALO), :] = entry(2 * layers)
        for count, top_sc in ((2 * layers + 1, dtop_sc), (2 * layers + 2, rtop_sc)):
            value = entry(count)
            for part in range(rows.per_row):
                spot = pl.ds(row * rows.per_row + part, HALO, stride=rows.per_row)
                top_sc[spot, :] = value[:, part * LANES:(part + 1) * LANES]

    for odd, above_ref, below_ref in ((0, far_ref, near_ref), (1, near_ref, far_ref)):
        @pl.when(lax.rem(number, 2) == odd)
        def _(above_ref=above_ref, below_ref=below_ref):
            for ref, row in ((above_ref, 0), (below_ref, last_own)):
                put_halo(ref, own ^ 1 if ref is near_ref else far_partner, row)

    faces = Faces(rows, land_sc[...], lands)
    tables = lane_tables((kst_ref, alphat_ref, storet_ref), layers)
    for row in [*range(HALO), *range(last_own, window)]:
        soil = rows.get(soil_sc, row).astype(jnp.int32)
        for table, ref in zip(tables, (ks_sc, alpha_sc, store_sc)):
            rows.put(ref, row, look_up(rows, table, soil))

    first, ks, alpha, store = [
        Joined(rows, held_ref, full, HALO, last_own)
        for held_ref, full in ((first_ref, first_sc), (ks_ref, ks_sc), (alpha_ref, alpha_sc), (store_ref, store_sc))
    ]
    top = lax.broadcasted_iota(jnp.int32, (layers, breadth), 0) == 0

    now, begin, stop, done = first, 0, window, 0
    for wx_ref, wy_ref, wz_ref, inv_ref, base_ref in fields:
        low, high = HALO + done, last_own - done
        wx_of = Joined(rows, wx_ref, wx_sc, low, high - 1)
        wy_of, wz_of = Joined(rows, wy_ref, wy_sc, low, high), Joined(rows, wz_ref, wz_sc, low, high)
        inverse, base = [
            Joined(rows, held_ref, full, low + 1, high - 1) for held_ref, full in ((inv_ref, inv_sc), (base_ref, base_sc))
        ]
        here_before, wx_before, sums_before = None, None, None
        for row in range(begin, stop):
            at_end = row in (low, high - 1)
            here, sums = None, None
            if not wy_of.holds(row) or at_end:
                here = faces.conduct(ks.get(row), alpha.get(row), now.get(row))
            if at_end:
                sums = rows.get(inv_ref, row - HALO), rows.get(base_ref, row - HALO)
            elif not wy_of.holds(row) and begin < row < stop - 1:
                wy, wz, diagonal, gravity = faces.in_row(row, here)
                wy_of.put(row, wy)
                wz_of.put(row, wz)
                sums = store.get(row) + diagonal, store.get(row) * first.get(row) + gravity
            if row > begin:
                if wx_of.holds(row - 1):
                    wx = wx_of.get(row - 1)
                else:
                    wx = faces.between_rows(row - 1, here_before, here)
                    wx_of.put(row - 1, wx)
                if sums_before is not None:
                    diagonal = sums_before[0] + wx_before + wx + river_row(rows, dtop_sc, row - 1, top)
                    inverse.put(row - 1, reciprocal(diagonal))
                    base.put(row - 1, sums_before[1] + river_row(rows, rtop_sc, row - 1, top))
                wx_before = wx
            here_before, sums_before = here, sums
        for _ in range(SWEEPS):
            begin, stop = begin + 1, stop - 1
            later = Joined(rows, staged_refs[done], (ping_sc, pong_sc)[done % 2], HALO + done + 1, last_own - done - 1)
            done += 1
            for row in range(begin, stop):
                if not later.holds(row):
                    head = now.get(row - 1), now.get(row), now.get(row + 1)
                    value, _ = relax_row(rows, row, head, (wx_of, wy_of, wz_of), wx_of.get(row - 1), base, inverse)
                    later.put(row, value)
            now = later
    for row in range(now.first, now.last):
        now.put(row, now.get(row))
    for part in range(rows.per_row):
        lanes = pl.ds(part * LANES, LANES)
        top_ref[:, lanes] = now.full[part, pl.ds(HALO * layers, span, stride=layers), :]
        for step, head_ref in enumerate(head_refs):
            for held_layer in range(held):
                layer = (own ^ step) * held + held_layer
                head_ref[held_layer, :, lanes] = now.full[part, pl.ds(HALO * layers + layer, span, stride=layers), :]


def inflow_kernel(reach_rows, stride, cells_ref, bed_ref, slot_section_ref, reach_ref, *refs):
    groups = lax.axis_size("layer")
    own_layer, flip, _ = position()
    top_refs = refs[:groups]
    out_ref, block_sc, lane_sc, found_sc, turned_sc = refs[groups:]
    span, breadth = top_refs[0].shape
    per_row = breadth // LANES
    blocks = groups * span * per_row
    slots = cells_ref.shape[0]
    quarter = LANES // groups
    packed = slots // groups
    for step, top_ref in enumerate(top_refs):
        number = span_at(flip, groups, own_layer ^ step)
        for part in range(per_row):
            spot = pl.ds(number * span * per_row + part, span, stride=per_row)
            turned_sc[spot, :] = top_ref[:, part * LANES:(part + 1) * LANES]

    own = lax.broadcasted_iota(jnp.int32, (packed, LANES), 1) // quarter

    def pack(ref):
        result = None
        for number in range(groups):
            shift = lax.rem((number + groups - own_layer) * quarter, LANES)
            moved = pltpu.roll(ref[pl.ds(number * packed, packed), :], shift, 1)
            result = moved if result is None else jnp.where(own == number, moved, result)
        return result

    cells = pack(cells_ref)
    block, lane = split_cells(cells, 0, breadth, LANES)
    block_sc[...] = block
    lane_sc[...] = lane
    table = jnp.concatenate(bf16_pieces(turned_sc[...].T, 2), axis=0)
    names = names_of(blocks)
    index = lax.broadcasted_iota(jnp.int32, (8, LANES), 0).astype(jnp.float32)
    for pair in range(0, packed, 2):
        hots = jnp.concatenate(
            [jnp.concatenate(one_hot(row_copies(block_sc, 0, row), names), axis=0) for row in (pair, pair + 1)], axis=1
        )
        found = lax.dot_general(
            table, hots, (((1,), (0,)), ((), ())), preferred_element_type=jnp.float32
        )
        found = found[:LANES] + found[LANES:]
        for row in (pair, pair + 1):
            lanes = jnp.broadcast_to(lane_sc[pl.ds(row, 1), :], (8, LANES))
            mine = found[:, (row - pair) * LANES:(row - pair + 1) * LANES]
            total = jnp.zeros((8, LANES), jnp.float32)
            for start in range(0, LANES, 8):
                total = total + jnp.where(lanes == index + float(start), mine[start:start + 8], 0.0)
            found_sc[pl.ds(row, 1), :] = jnp.sum(total, axis=0, keepdims=True)
    slot_in = jnp.where(cells >= 0, pack(bed_ref) * (found_sc[...] - pack(slot_section_ref)), 0.0)
    spread = jnp.concatenate(
        [slot_in if number == 0 else pltpu.roll(slot_in, LANES - number * quarter, 1) for number in range(groups)],
        axis=0,
    )
    in_quarter = lax.broadcasted_iota(jnp.int32, spread.shape, 1) < quarter
    pieces = bf16_pieces(jnp.where(in_quarter, spread, 0.0), 3)
    fold = reach_rows // groups
    index = lax.broadcasted_iota(jnp.int32, (out_ref.shape[0], slots), 0)
    index = index // fold * stride + lax.rem(index, fold)
    result = None
    for number in range(groups):
        name = (index + number * fold).astype(jnp.float32)
        put = jnp.where(name == reach_ref[...], 1.0, 0.0).astype(jnp.bfloat16)
        total = jnp.zeros(out_ref.shape, jnp.float32)
        for piece in pieces:
            total = total + lax.dot_general(
                put, piece, (((1,), (0,)), ((), ())), preferred_element_type=jnp.float32
            )
        result = total if result is None else result + pltpu.roll(total, number * quarter, 1)
    out_ref[...] = result


def sum_kernel(terms_ref, inflow_ref):
    total = terms_ref[0]
    for tile in range(1, terms_ref.shape[0]):
        total = total + terms_ref[tile]
    fold, quarter = total.shape[0], inflow_ref.shape[1]
    for number in range(inflow_ref.shape[0] // fold):
        lanes = slice(number * quarter, (number + 1) * quarter)
        inflow_ref[pl.ds(number * fold, fold), :] = total[:, lanes]


def head_kernel(*refs):
    groups = lax.axis_size("layer")
    back_refs, (head_hbm, sems) = refs[:groups], refs[groups:]
    _, span, _ = back_refs[0].shape
    own, flip, _ = position()
    copies = []
    for step, back_ref in enumerate(back_refs):
        rows = pl.ds(pl.multiple_of(span_at(flip, groups, own ^ step) * span, span), span)
        copies.append(pltpu.make_async_copy(back_ref, head_hbm.at[:, rows, :], sems.at[step]))
        copies[-1].start()
    for copy in copies:
        copy.wait()


def call(kernel, out_shape, in_specs, scratch, micros, vmem=VMEM_LIMIT, out_specs=None):
    single = not isinstance(out_shape, (tuple, list))
    return pl.pallas_call(
        kernel,
        out_shape=out_shape,
        in_specs=in_specs,
        out_specs=out_specs or (in_vmem if single else tuple(in_vmem for _ in out_shape)),
        scratch_shapes=scratch,
        compiler_params=pltpu.CompilerParams(vmem_limit_bytes=vmem),
        cost_estimate=pl.CostEstimate(flops=int(micros * 1.15e9), bytes_accessed=0, transcendentals=0),
    )


def on_device(
    head_start,
    soil_class,
    land_mask,
    ks_table,
    alpha_table,
    store_table,
    section,
    cross_owner,
    cross_local,
    node_cell,
    bed_cond,
):
    held, across, breadth = head_start.shape
    reach_rows, node_count = section.shape
    tiles = lax.axis_size("tile")
    groups = lax.axis_size("layer")
    layers = held * groups
    span = across // groups
    per_row = breadth // LANES
    blocks = span * per_row
    near = [(i, i ^ 1) for i in range(groups)]
    far = []
    for upper in range(tiles):
        far += [(upper * groups + i, upper * groups + (i ^ (groups - 1))) for i in range(1, groups - 1)]
        if upper + 1 < tiles:
            index = groups - 1 if upper % 2 == 0 else 0
            one, two = upper * groups + index, (upper + 1) * groups + index
            far += [(one, two), (two, one)]

    cells = node_cell[0]
    bed = bed_cond[0]
    slots = cells.shape[0]

    def exchange(parts):
        received = [parts[0]]
        for step in range(1, groups):
            received.append(lax.ppermute(parts[step], "layer", [(i, i ^ step) for i in range(groups)]))
        return received

    stride = reach_rows + 8
    spread = call(
        spread_kernel, jax.ShapeDtypeStruct((tiles, stride, node_count), jnp.float32), [in_hbm] * 3,
        [
            pltpu.VMEM(section.shape, jnp.float32),
            pltpu.VMEM(cross_owner.shape, jnp.int32),
            pltpu.VMEM(cross_owner.shape, jnp.int32),
            pltpu.SemaphoreType.DMA((3,)),
        ],
        1, VMEM_MOST,
    )(section, cross_owner, cross_local)
    whole_section = lax.all_to_all(spread, "tile", 0, 0).reshape(tiles * stride, node_count)
    *own_blocks, land = call(
        prepare_kernel,
        (jax.ShapeDtypeStruct((2, held, span, breadth), jnp.float32),) * groups
        + (jax.ShapeDtypeStruct((span, breadth), jnp.float32),),
        [in_vmem] * 3 + [in_hbm], [], 0.5,
    )(head_start, soil_class, land_mask, spread)
    received = exchange(own_blocks)

    node_scratch = pltpu.VMEM((slots, LANES), jnp.float32)
    riv_shape = jax.ShapeDtypeStruct((blocks, LANES), jnp.float32)
    diag, rhs, slot_section, reach = call(
        functools.partial(river_kernel, breadth, span, stride),
        (
            riv_shape,
            riv_shape,
            jax.ShapeDtypeStruct((slots, node_count), jnp.float32),
            jax.ShapeDtypeStruct((1, slots), jnp.float32),
        ),
        [in_vmem] * 3,
        [node_scratch] * 6 + [pltpu.VMEM((span * breadth // BLOCK, LANES), jnp.float32)],
        7,
    )(cells, bed, whole_section)
    edges = jax.ShapeDtypeStruct(((2 * layers + 3) * HALO, breadth), jnp.float32)
    near_edge, far_edge = call(
        edge_kernel, (edges, edges), [in_vmem] * (3 + groups), [], 0.1,
    )(land, diag, rhs, *received)
    far_halo = lax.ppermute(far_edge, FLAT, far)
    near_halo = lax.ppermute(near_edge, "layer", near)

    window = span + 2 * HALO
    own_field = jax.ShapeDtypeStruct((per_row, span * layers, LANES), jnp.float32)
    field = pltpu.VMEM((per_row, window * layers, LANES), jnp.float32)
    staged = call(
        stage_kernel, (own_field,) * (4 + 5 * ITERS + HALO), [in_smem] * 3 + [in_vmem] * (3 + groups),
        [pltpu.VMEM(own_field.shape, jnp.float32)] + [pltpu.VMEM((span, breadth), jnp.float32)] * 3,
        4,
    )(ks_table, alpha_table, store_table, land, diag, rhs, *received)
    head_shape = jax.ShapeDtypeStruct((held, span, breadth), jnp.float32)
    *heads, top = call(
        flow_kernel,
        (head_shape,) * groups + (jax.ShapeDtypeStruct((span, breadth), jnp.float32),),
        [in_smem] * 3 + [in_vmem] * (5 + len(staged)),
        [field] * 12
        + [pltpu.VMEM((window, breadth), jnp.float32)]
        + [pltpu.VMEM((window * per_row, LANES), jnp.float32)] * 2
        + [pltpu.VMEM((window, breadth), jnp.float32)] * 3,
        3,
    )(ks_table, alpha_table, store_table, land, far_halo, near_halo, diag, rhs, *staged)
    tops = exchange([top] * groups)
    backs = exchange(heads)

    fold = reach_rows // groups
    packed = pltpu.VMEM((slots // groups, LANES), jnp.float32)
    partial = call(
        functools.partial(inflow_kernel, reach_rows, stride),
        jax.ShapeDtypeStruct((tiles * fold, node_count), jnp.float32),
        [in_vmem] * (4 + groups),
        [packed] * 3 + [pltpu.VMEM((across * per_row, LANES), jnp.float32)],
        3,
    )(cells, bed, slot_section, reach, *tops)
    partial, *backs[:-1] = lax.optimization_barrier((partial, *backs[:-1]))
    terms = lax.all_to_all(partial.reshape(tiles, fold, node_count), "tile", 0, 0)
    head = call(
        head_kernel, jax.ShapeDtypeStruct(head_start.shape, jnp.float32), [in_vmem] * groups,
        [pltpu.SemaphoreType.DMA((groups,))], 0.7, out_specs=in_hbm,
    )(*backs)
    inflow_shape = jax.ShapeDtypeStruct((reach_rows, node_count // groups), jnp.float32)
    return head, call(sum_kernel, inflow_shape, [in_vmem], [], 0.1)(terms)


def solution(mesh):
    placed = (
        P("layer", "tile", None),
        P("layer", "tile", None),
        P("tile", None),
        P(),
        P(),
        P(),
        P("tile", None),
        P("tile", None),
        P("tile", None),
        P("tile", None, None),
        P("tile", None, None),
    )
    return jax.shard_map(
        on_device,
        mesh=mesh,
        in_specs=placed,
        out_specs=(P("layer", "tile", None), P("tile", "layer")),
        check_vma=False,
    )
```

```python
import functools

import jax
import jax.numpy as jnp
from jax import lax
from jax.experimental import pallas as pl
from jax.experimental.pallas import tpu as pltpu
from jax.sharding import PartitionSpec as P

ITERS = 2
SWEEPS = 3

LATERAL = 1.0
VERTICAL = 2.0
GRAVITY = 1.0

HALO = ITERS * SWEEPS
BLOCK = 64
LANES = 128
VMEM_LIMIT = 32 * 1024 * 1024
VMEM_MOST = 60 * 1024 * 1024
FLAT = ("tile", "layer")

in_vmem = pl.BlockSpec(memory_space=pltpu.VMEM)
in_hbm = pl.BlockSpec(memory_space=pltpu.HBM)
in_smem = pl.BlockSpec(memory_space=pltpu.SMEM)


def bf16_pieces(value, count):
    pieces = []
    for _ in range(count):
        piece = value.astype(jnp.bfloat16)
        pieces.append(piece)
        value = value - piece.astype(jnp.float32)
    return pieces


def reciprocal(value):
    guess = pl.reciprocal(value, approx=True)
    return guess * (2.0 - value * guess)


def names_of(size):
    index = lax.broadcasted_iota(jnp.int32, (16, LANES), 0)
    return [(index + start).astype(jnp.float32).astype(jnp.bfloat16) for start in range(0, size, 16)]


def one_hot(row, names):
    one = jnp.ones((16, LANES), jnp.bfloat16)
    zero = jnp.zeros((16, LANES), jnp.bfloat16)
    return [jnp.maximum(one - jnp.abs(row - name), zero) for name in names]


def row_copies(ref, first, place):
    rows = ref[pl.ds(pl.multiple_of(first + place // 8 * 8, 8), 8), :]
    return jnp.broadcast_to(rows[place % 8:place % 8 + 1, :], (16, LANES)).astype(jnp.bfloat16)


def position():
    tile, layer = lax.axis_index("tile"), lax.axis_index("layer")
    groups = lax.axis_size("layer")
    flip = lax.rem(tile, 2)
    return layer, flip, jnp.where(flip == 1, groups - 1 - layer, layer)


def span_at(flip, groups, layer):
    return jnp.where(flip == 1, groups - 1 - layer, layer)


def split_cells(cells, first_row, breadth, width):
    local = cells - first_row * breadth
    shift = width.bit_length() - 1
    block = jnp.where(cells < 0, -1, local >> shift)
    return block.astype(jnp.float32), (local & (width - 1)).astype(jnp.float32)


def river_kernel(
    breadth, span, stride, cells_ref, bed_ref, section_ref,
    diag_ref, rhs_ref, slot_section_ref, reach_ref, block_sc, spot_sc, dhigh_sc, dlow_sc, rhigh_sc, rlow_sc, sum_sc,
):
    _, _, number = position()
    rows = section_ref.shape[0]
    slots = reach_ref.shape[1]
    first = (lax.axis_index("tile") + 1) * stride - 8
    own_rows = section_ref[pl.ds(pl.multiple_of(first, 8), 8), :]
    reach = jnp.concatenate([own_rows[k:k + 1, :] for k in range(slots // LANES)], axis=1)
    reach_ref[...] = reach
    index = lax.broadcasted_iota(jnp.int32, (rows, slots), 0).astype(jnp.float32)
    pick = jnp.where(index == reach, 1.0, 0.0).astype(jnp.bfloat16)
    picked = jnp.zeros(slot_section_ref.shape, jnp.float32)
    for piece in bf16_pieces(section_ref[...], 3):
        picked = picked + lax.dot_general(
            pick, piece, (((0,), (0,)), ((), ())), preferred_element_type=jnp.float32
        )
    slot_section_ref[...] = picked

    block, spot = split_cells(cells_ref[...], number * span, breadth, BLOCK)
    block_sc[...] = block
    spot_sc[...] = spot
    bed = bed_ref[...]
    for value, high_sc, low_sc in ((bed, dhigh_sc, dlow_sc), (bed * picked, rhigh_sc, rlow_sc)):
        high, low = bf16_pieces(value, 2)
        high_sc[...] = high.astype(jnp.float32)
        low_sc[...] = low.astype(jnp.float32)
    share = LANES // BLOCK
    blocks = share * diag_ref.shape[0]
    group = 64
    block_names, spot_names = names_of(blocks), names_of(BLOCK)

    def matmul(first, places):
        left, right = [], []
        for place in places:
            left.append(jnp.concatenate(one_hot(row_copies(block_sc, first, place), block_names), axis=0))
            hot = one_hot(row_copies(spot_sc, first, place), spot_names)
            values = [row_copies(ref, first, place) for ref in (dhigh_sc, dlow_sc, rhigh_sc, rlow_sc)]
            right.append(jnp.concatenate([tile * value for value in values for tile in hot], axis=0))
        return lax.dot_general(
            jnp.concatenate(left, axis=1),
            jnp.concatenate(right, axis=1),
            (((1,), (1,)), ((), ())),
            preferred_element_type=jnp.float32,
        )

    def step(count, total):
        first = count * group
        half = group // 2
        return total + (matmul(first, range(half)) + matmul(first, range(half, group)))

    total = lax.fori_loop(0, slots // group, step, jnp.zeros((blocks, 4 * BLOCK), jnp.float32))
    low_half = lax.broadcasted_iota(jnp.int32, diag_ref.shape, 1) < BLOCK
    for count, ref in ((0, diag_ref), (1, rhs_ref)):
        part = total[:, count * LANES:(count + 1) * LANES]
        sum_sc[...] = part + pltpu.roll(part, BLOCK, 1)
        ref[...] = jnp.where(
            low_half, sum_sc[pl.ds(0, blocks // share, stride=share), :], sum_sc[pl.ds(1, blocks // share, stride=share), :]
        )


def edge_kernel(land_ref, diag_ref, rhs_ref, *refs):
    block_refs, (near_ref, far_ref) = refs[:-2], refs[-2:]
    _, held, span, breadth = block_refs[0].shape
    _, _, number = position()
    odd = lax.rem(number, 2) == 1
    per_row = breadth // LANES

    def put_edges(entry, top, bottom, lanes=slice(None)):
        near_ref[pl.ds(entry * HALO, HALO), lanes] = jnp.where(odd, top, bottom)
        far_ref[pl.ds(entry * HALO, HALO), lanes] = jnp.where(odd, bottom, top)

    entry = 0
    for kind in range(2):
        for block_ref in block_refs:
            for held_layer in range(held):
                put_edges(entry, block_ref[kind, held_layer, :HALO, :], block_ref[kind, held_layer, span - HALO:, :])
                entry += 1
    put_edges(entry, land_ref[:HALO, :], land_ref[span - HALO:, :])
    for ref in (diag_ref, rhs_ref):
        entry += 1
        for part in range(per_row):
            top = ref[pl.ds(part, HALO, stride=per_row), :]
            bottom = ref[pl.ds((span - HALO) * per_row + part, HALO, stride=per_row), :]
            put_edges(entry, top, bottom, slice(part * LANES, (part + 1) * LANES))
    rest = near_ref.shape[0] - (entry + 1) * HALO
    for ref in (near_ref, far_ref):
        ref[pl.ds((entry + 1) * HALO, rest), :] = jnp.zeros((rest, breadth), jnp.float32)


def spread_kernel(section_hbm, owner_hbm, local_hbm, spread_ref, section_ref, owner_ref, local_ref, sems):
    pairs = ((section_hbm, section_ref), (owner_hbm, owner_ref), (local_hbm, local_ref))
    copies = [pltpu.make_async_copy(here, there, sems.at[k]) for k, (here, there) in enumerate(pairs)]
    for copy in copies:
        copy.start()
    for copy in copies:
        copy.wait()
    tiles, stride, _ = spread_ref.shape
    reach_rows = section_ref.shape[0]
    reach = (owner_ref[...] * stride + local_ref[...]).astype(jnp.float32)
    parts = [reach[:, start:start + LANES] for start in range(0, reach.shape[1], LANES)]
    parts.append(jnp.zeros((stride - reach_rows - len(parts), LANES), jnp.float32))
    payload = jnp.concatenate([section_ref[...], *parts], axis=0)
    for tile in range(tiles):
        spread_ref[tile] = payload


def prepare_kernel(head_ref, soil_ref, land_ref, after_ref, *refs):
    del after_ref
    groups = lax.axis_size("layer")
    block_refs, land_out_ref = refs[:groups], refs[groups]
    held, across, _ = head_ref.shape
    span = across // groups
    own, flip, _ = position()

    def rows_of(target):
        return pl.ds(pl.multiple_of(span_at(flip, groups, target) * span, span), span)

    land_out_ref[...] = land_ref[rows_of(own), :].astype(jnp.float32)
    for step, block_ref in enumerate(block_refs):
        rows = rows_of(own ^ step)
        for layer in range(held):
            block_ref[0, layer] = head_ref[layer, rows, :]
            block_ref[1, layer] = soil_ref[layer, rows, :].astype(jnp.float32)


class Rows:
    def __init__(self, layers, breadth):
        self.layers, self.breadth, self.per_row = layers, breadth, breadth // LANES

    def get(self, ref, row):
        spot = pl.ds(row * self.layers, self.layers)
        return jnp.concatenate([ref[part, spot, :] for part in range(self.per_row)], axis=1)

    def put(self, ref, row, value):
        spot = pl.ds(row * self.layers, self.layers)
        for part in range(self.per_row):
            ref[part, spot, :] = value[:, part * LANES:(part + 1) * LANES]

    def put_layer(self, ref, layer, row, value):
        for part in range(self.per_row):
            spot = pl.ds(row * self.layers + layer, value.shape[0], stride=self.layers)
            ref[part, spot, :] = value[:, part * LANES:(part + 1) * LANES]

    def east(self, field):
        return pltpu.roll(field, self.breadth - 1, 1)

    def west(self, field):
        return pltpu.roll(field, 1, 1)

    def below(self, field):
        return pltpu.roll(field, self.layers - 1, 0)

    def above(self, field):
        return pltpu.roll(field, 1, 0)


class Joined:
    def __init__(self, rows, own, full, first, last):
        self.rows, self.own, self.full, self.first, self.last = rows, own, full, first, last

    def holds(self, row):
        return self.first <= row < self.last

    def get(self, row):
        if self.holds(row):
            return self.rows.get(self.own, row - HALO)
        return self.rows.get(self.full, row)

    def put(self, row, value):
        self.rows.put(self.full, row, value)


def relax_row(rows, row, head, weights, wx_before, base, inverse):
    before, here, after = head
    wx, wy, wz = [field.get(row) for field in weights]
    total = base.get(row) + wx_before * before + wx * after
    total = total + wy * rows.east(here) + rows.west(wy * here)
    total = total + wz * rows.below(here) + rows.above(wz * here)
    return total * inverse.get(row), wx


def river_row(rows, ref, row, top):
    parts = [
        jnp.broadcast_to(ref[pl.ds(row * rows.per_row + part, 1), :], (rows.layers, LANES))
        for part in range(rows.per_row)
    ]
    return jnp.where(top, jnp.concatenate(parts, axis=1), 0.0)


class Faces:
    def __init__(self, rows, land, lands):
        self.rows, self.lands = rows, lands
        lx_ref, ly_ref, lz_ref = lands
        count = land.shape[0]
        level = lax.broadcasted_iota(jnp.int32, (rows.layers, rows.breadth), 0)
        self.not_bottom = level < rows.layers - 1
        not_last = lax.broadcasted_iota(jnp.int32, land.shape, 1) < rows.breadth - 1
        lx_ref[pl.ds(0, count - 1), :] = 2.0 * LATERAL * land[:count - 1] * land[1:]
        ly_ref[...] = jnp.where(not_last, 2.0 * LATERAL * land * rows.east(land), 0.0)
        lz_ref[...] = 2.0 * VERTICAL * land * land

    def conduct(self, ks, alpha, head):
        return ks * jnp.exp(alpha * jnp.minimum(head, 0.0))

    def face(self, land, here, there):
        return land * (here * there) * reciprocal(here + there)

    def between_rows(self, row, here, there):
        return self.face(self.lands[0][pl.ds(row, 1), :], here, there)

    def in_row(self, row, here):
        rows = self.rows
        wy = self.face(self.lands[1][pl.ds(row, 1), :], here, rows.east(here))
        wz = self.face(self.lands[2][pl.ds(row, 1), :], here, rows.below(here))
        wz = jnp.where(self.not_bottom, wz, 0.0)
        wz_above = rows.above(wz)
        return wy, wz, wy + rows.west(wy) + wz + wz_above, GRAVITY * (wz_above - wz)


def lane_tables(refs, layers):
    lane = lax.broadcasted_iota(jnp.int32, (layers, LANES), 1)
    tables = []
    for ref in refs:
        table = jnp.zeros((layers, LANES), jnp.float32)
        for kind in range(ref.shape[0]):
            table = jnp.where(lane == kind, ref[kind], table)
        tables.append(table)
    return tables


def look_up(rows, table, soil):
    parts = [
        jnp.take_along_axis(table, soil[:, part * LANES:(part + 1) * LANES], axis=1, mode="promise_in_bounds")
        for part in range(rows.per_row)
    ]
    return jnp.concatenate(parts, axis=1)


def stage_kernel(ks_ref, alpha_ref, store_ref, land_ref, diag_ref, rhs_ref, *refs):
    groups = lax.axis_size("layer")
    own, _, _ = position()
    block_refs, refs = refs[:groups], refs[groups:]
    first_out, ks_out, alpha_out, store_out = refs[:4]
    fields = [refs[4 + 5 * picard:9 + 5 * picard] for picard in range(ITERS)]
    head_outs = refs[4 + 5 * ITERS:4 + 5 * ITERS + HALO]
    soil_sc, *lands = refs[4 + 5 * ITERS + HALO:]
    _, held, span, breadth = block_refs[0].shape
    layers = groups * held
    rows = Rows(layers, breadth)
    faces = Faces(rows, land_ref[...], lands)
    top = lax.broadcasted_iota(jnp.int32, (layers, breadth), 0) == 0

    for step, block_ref in enumerate(block_refs):
        for held_layer in range(held):
            layer = (own ^ step) * held + held_layer
            rows.put_layer(first_out, layer, 0, block_ref[0, held_layer])
            rows.put_layer(soil_sc, layer, 0, block_ref[1, held_layer])
    tables = lane_tables((ks_ref, alpha_ref, store_ref), layers)
    for row in range(span):
        soil = rows.get(soil_sc, row).astype(jnp.int32)
        for table, out in zip(tables, (ks_out, alpha_out, store_out)):
            rows.put(out, row, look_up(rows, table, soil))

    now, begin, stop, done = first_out, 0, span, 0
    for wx_out, wy_out, wz_out, inv_out, base_out in fields:
        before = None
        for row in range(begin, stop):
            here = faces.conduct(rows.get(ks_out, row), rows.get(alpha_out, row), rows.get(now, row))
            wy, wz, diagonal, gravity = faces.in_row(row, here)
            rows.put(wy_out, row, wy)
            rows.put(wz_out, row, wz)
            store = rows.get(store_out, row)
            sums = store + diagonal, store * rows.get(first_out, row) + gravity
            if row > begin:
                wx = faces.between_rows(row - 1, before[0], here)
                rows.put(wx_out, row - 1, wx)
                diagonal, base = before[1]
                if row - 1 > begin:
                    diagonal = reciprocal(diagonal + before[2] + wx + river_row(rows, diag_ref, row - 1, top))
                    base = base + river_row(rows, rhs_ref, row - 1, top)
                rows.put(inv_out, row - 1, diagonal)
                rows.put(base_out, row - 1, base)
            else:
                wx = None
            before = here, sums, wx
        rows.put(inv_out, stop - 1, before[1][0])
        rows.put(base_out, stop - 1, before[1][1])
        weights = [Joined(rows, None, ref, HALO, HALO) for ref in (wx_out, wy_out, wz_out)]
        base, inverse = [Joined(rows, None, ref, HALO, HALO) for ref in (base_out, inv_out)]
        for _ in range(SWEEPS):
            begin, stop = begin + 1, stop - 1
            head = rows.get(now, begin - 1), rows.get(now, begin)
            wx_before = rows.get(wx_out, begin - 1)
            for row in range(begin, stop):
                head = *head[-2:], rows.get(now, row + 1)
                value, wx_before = relax_row(rows, row, head, weights, wx_before, base, inverse)
                rows.put(head_outs[done], row, value)
            now = head_outs[done]
            done += 1


def flow_kernel(kst_ref, alphat_ref, storet_ref, land_ref, far_ref, near_ref, diag_ref, rhs_ref, *refs):
    groups = lax.axis_size("layer")
    own, _, number = position()
    end = (number == 0) | (number == groups - 1)
    far_partner = jnp.where(end, own, own ^ (groups - 1))
    tile, tiles = lax.axis_index("tile"), lax.axis_size("tile")
    outside = ((tile == 0) & (number == 0)) | ((tile == tiles - 1) & (number == groups - 1))
    first_ref, ks_ref, alpha_ref, store_ref = refs[:4]
    fields = [refs[4 + 5 * picard:9 + 5 * picard] for picard in range(ITERS)]
    staged_refs = refs[4 + 5 * ITERS:4 + 5 * ITERS + HALO]
    refs = refs[4 + 5 * ITERS + HALO:]
    head_refs, top_ref = refs[:groups], refs[groups]
    (
        first_sc, soil_sc, ks_sc, alpha_sc, store_sc, wx_sc, wy_sc, wz_sc, base_sc, inv_sc, ping_sc, pong_sc,
        land_sc, dtop_sc, rtop_sc, *lands,
    ) = refs[1 + groups:]
    held, span, breadth = head_refs[0].shape
    layers = groups * held
    window = span + 2 * HALO
    last_own = HALO + span
    rows = Rows(layers, breadth)
    side = HALO * rows.per_row

    land_sc[pl.ds(HALO, span), :] = land_ref[...]
    dtop_sc[pl.ds(side, span * rows.per_row), :] = diag_ref[...]
    rtop_sc[pl.ds(side, span * rows.per_row), :] = rhs_ref[...]

    def put_halo(ref, partner, row):
        def entry(number):
            return ref[pl.ds(number * HALO, HALO), :]

        for count in range(layers):
            layer = (partner ^ (count // held)) * held + count % held
            rows.put_layer(first_sc, layer, row, entry(count))
            rows.put_layer(soil_sc, layer, row, entry(layers + count))
        water = outside if ref is far_ref else False
        land_sc[pl.ds(row, HALO), :] = jnp.where(water, 0.0, entry(2 * layers))
        for count, top_sc in ((2 * layers + 1, dtop_sc), (2 * layers + 2, rtop_sc)):
            value = entry(count)
            for part in range(rows.per_row):
                spot = pl.ds(row * rows.per_row + part, HALO, stride=rows.per_row)
                top_sc[spot, :] = value[:, part * LANES:(part + 1) * LANES]

    for odd, above_ref, below_ref in ((0, far_ref, near_ref), (1, near_ref, far_ref)):
        @pl.when(lax.rem(number, 2) == odd)
        def _(above_ref=above_ref, below_ref=below_ref):
            for ref, row in ((above_ref, 0), (below_ref, last_own)):
                put_halo(ref, own ^ 1 if ref is near_ref else far_partner, row)

    faces = Faces(rows, land_sc[...], lands)
    tables = lane_tables((kst_ref, alphat_ref, storet_ref), layers)
    for row in [*range(HALO), *range(last_own, window)]:
        soil = rows.get(soil_sc, row).astype(jnp.int32)
        for table, ref in zip(tables, (ks_sc, alpha_sc, store_sc)):
            rows.put(ref, row, look_up(rows, table, soil))

    first, ks, alpha, store = [
        Joined(rows, held_ref, full, HALO, last_own)
        for held_ref, full in ((first_ref, first_sc), (ks_ref, ks_sc), (alpha_ref, alpha_sc), (store_ref, store_sc))
    ]
    top = lax.broadcasted_iota(jnp.int32, (layers, breadth), 0) == 0

    now, begin, stop, done = first, 0, window, 0
    for wx_ref, wy_ref, wz_ref, inv_ref, base_ref in fields:
        low, high = HALO + done, last_own - done
        wx_of = Joined(rows, wx_ref, wx_sc, low, high - 1)
        wy_of, wz_of = Joined(rows, wy_ref, wy_sc, low, high), Joined(rows, wz_ref, wz_sc, low, high)
        inverse, base = [
            Joined(rows, held_ref, full, low + 1, high - 1) for held_ref, full in ((inv_ref, inv_sc), (base_ref, base_sc))
        ]
        here_before, wx_before, sums_before = None, None, None
        for row in range(begin, stop):
            at_end = row in (low, high - 1)
            here, sums = None, None
            if not wy_of.holds(row) or at_end:
                here = faces.conduct(ks.get(row), alpha.get(row), now.get(row))
            if at_end:
                sums = rows.get(inv_ref, row - HALO), rows.get(base_ref, row - HALO)
            elif not wy_of.holds(row) and begin < row < stop - 1:
                wy, wz, diagonal, gravity = faces.in_row(row, here)
                wy_of.put(row, wy)
                wz_of.put(row, wz)
                sums = store.get(row) + diagonal, store.get(row) * first.get(row) + gravity
            if row > begin:
                if wx_of.holds(row - 1):
                    wx = wx_of.get(row - 1)
                else:
                    wx = faces.between_rows(row - 1, here_before, here)
                    wx_of.put(row - 1, wx)
                if sums_before is not None:
                    diagonal = sums_before[0] + wx_before + wx + river_row(rows, dtop_sc, row - 1, top)
                    inverse.put(row - 1, reciprocal(diagonal))
                    base.put(row - 1, sums_before[1] + river_row(rows, rtop_sc, row - 1, top))
                wx_before = wx
            here_before, sums_before = here, sums
        for _ in range(SWEEPS):
            begin, stop = begin + 1, stop - 1
            later = Joined(rows, staged_refs[done], (ping_sc, pong_sc)[done % 2], HALO + done + 1, last_own - done - 1)
            done += 1
            for row in range(begin, stop):
                if not later.holds(row):
                    head = now.get(row - 1), now.get(row), now.get(row + 1)
                    value, _ = relax_row(rows, row, head, (wx_of, wy_of, wz_of), wx_of.get(row - 1), base, inverse)
                    later.put(row, value)
            now = later
    for row in range(now.first, now.last):
        now.put(row, now.get(row))
    for part in range(rows.per_row):
        lanes = pl.ds(part * LANES, LANES)
        top_ref[:, lanes] = now.full[part, pl.ds(HALO * layers, span, stride=layers), :]
        for step, head_ref in enumerate(head_refs):
            for held_layer in range(held):
                layer = (own ^ step) * held + held_layer
                head_ref[held_layer, :, lanes] = now.full[part, pl.ds(HALO * layers + layer, span, stride=layers), :]


def inflow_kernel(reach_rows, stride, cells_ref, bed_ref, slot_section_ref, reach_ref, *refs):
    groups = lax.axis_size("layer")
    own_layer, flip, _ = position()
    top_refs = refs[:groups]
    out_ref, block_sc, lane_sc, found_sc, turned_sc = refs[groups:]
    span, breadth = top_refs[0].shape
    per_row = breadth // LANES
    blocks = groups * span * per_row
    slots = cells_ref.shape[0]
    quarter = LANES // groups
    packed = slots // groups
    for step, top_ref in enumerate(top_refs):
        number = span_at(flip, groups, own_layer ^ step)
        for part in range(per_row):
            spot = pl.ds(number * span * per_row + part, span, stride=per_row)
            turned_sc[spot, :] = top_ref[:, part * LANES:(part + 1) * LANES]

    own = lax.broadcasted_iota(jnp.int32, (packed, LANES), 1) // quarter

    def pack(ref):
        result = None
        for number in range(groups):
            shift = lax.rem((number + groups - own_layer) * quarter, LANES)
            moved = pltpu.roll(ref[pl.ds(number * packed, packed), :], shift, 1)
            result = moved if result is None else jnp.where(own == number, moved, result)
        return result

    cells = pack(cells_ref)
    block, lane = split_cells(cells, 0, breadth, LANES)
    block_sc[...] = block
    lane_sc[...] = lane
    table = jnp.concatenate(bf16_pieces(turned_sc[...].T, 2), axis=0)
    names = names_of(blocks)
    index = lax.broadcasted_iota(jnp.int32, (8, LANES), 0).astype(jnp.float32)
    for pair in range(0, packed, 2):
        hots = jnp.concatenate(
            [jnp.concatenate(one_hot(row_copies(block_sc, 0, row), names), axis=0) for row in (pair, pair + 1)], axis=1
        )
        found = lax.dot_general(
            table, hots, (((1,), (0,)), ((), ())), preferred_element_type=jnp.float32
        )
        found = found[:LANES] + found[LANES:]
        for row in (pair, pair + 1):
            lanes = jnp.broadcast_to(lane_sc[pl.ds(row, 1), :], (8, LANES))
            mine = found[:, (row - pair) * LANES:(row - pair + 1) * LANES]
            total = jnp.zeros((8, LANES), jnp.float32)
            for start in range(0, LANES, 8):
                total = total + jnp.where(lanes == index + float(start), mine[start:start + 8], 0.0)
            found_sc[pl.ds(row, 1), :] = jnp.sum(total, axis=0, keepdims=True)
    slot_in = jnp.where(cells >= 0, pack(bed_ref) * (found_sc[...] - pack(slot_section_ref)), 0.0)
    spread = jnp.concatenate(
        [slot_in if number == 0 else pltpu.roll(slot_in, LANES - number * quarter, 1) for number in range(groups)],
        axis=0,
    )
    in_quarter = lax.broadcasted_iota(jnp.int32, spread.shape, 1) < quarter
    pieces = bf16_pieces(jnp.where(in_quarter, spread, 0.0), 3)
    fold = reach_rows // groups
    index = lax.broadcasted_iota(jnp.int32, (out_ref.shape[0], slots), 0)
    index = index // fold * stride + lax.rem(index, fold)
    result = None
    for number in range(groups):
        name = (index + number * fold).astype(jnp.float32)
        put = jnp.where(name == reach_ref[...], 1.0, 0.0).astype(jnp.bfloat16)
        total = jnp.zeros(out_ref.shape, jnp.float32)
        for piece in pieces:
            total = total + lax.dot_general(
                put, piece, (((1,), (0,)), ((), ())), preferred_element_type=jnp.float32
            )
        result = total if result is None else result + pltpu.roll(total, number * quarter, 1)
    out_ref[...] = result


def sum_kernel(terms_ref, inflow_ref):
    total = terms_ref[0]
    for tile in range(1, terms_ref.shape[0]):
        total = total + terms_ref[tile]
    fold, quarter = total.shape[0], inflow_ref.shape[1]
    for number in range(inflow_ref.shape[0] // fold):
        lanes = slice(number * quarter, (number + 1) * quarter)
        inflow_ref[pl.ds(number * fold, fold), :] = total[:, lanes]


def head_kernel(*refs):
    groups = lax.axis_size("layer")
    back_refs, (head_hbm, sems) = refs[:groups], refs[groups:]
    _, span, _ = back_refs[0].shape
    own, flip, _ = position()
    copies = []
    for step, back_ref in enumerate(back_refs):
        rows = pl.ds(pl.multiple_of(span_at(flip, groups, own ^ step) * span, span), span)
        copies.append(pltpu.make_async_copy(back_ref, head_hbm.at[:, rows, :], sems.at[step]))
        copies[-1].start()
    for copy in copies:
        copy.wait()


def call(kernel, out_shape, in_specs, scratch, micros, vmem=VMEM_LIMIT, out_specs=None):
    single = not isinstance(out_shape, (tuple, list))
    return pl.pallas_call(
        kernel,
        out_shape=out_shape,
        in_specs=in_specs,
        out_specs=out_specs or (in_vmem if single else tuple(in_vmem for _ in out_shape)),
        scratch_shapes=scratch,
        compiler_params=pltpu.CompilerParams(vmem_limit_bytes=vmem),
        cost_estimate=pl.CostEstimate(flops=int(micros * 1.15e9), bytes_accessed=0, transcendentals=0),
    )


def on_device(
    head_start,
    soil_class,
    land_mask,
    ks_table,
    alpha_table,
    store_table,
    section,
    cross_owner,
    cross_local,
    node_cell,
    bed_cond,
):
    held, across, breadth = head_start.shape
    reach_rows, node_count = section.shape
    tiles = lax.axis_size("tile")
    groups = lax.axis_size("layer")
    layers = held * groups
    span = across // groups
    per_row = breadth // LANES
    blocks = span * per_row
    near = [(i, i ^ 1) for i in range(groups)]
    far = []
    for upper in range(tiles):
        far += [(upper * groups + i, upper * groups + (i ^ (groups - 1))) for i in range(1, groups - 1)]
        if upper + 1 < tiles:
            index = groups - 1 if upper % 2 == 0 else 0
            one, two = upper * groups + index, (upper + 1) * groups + index
            far += [(one, two), (two, one)]
    far += [(0, 0)]
    last = tiles * groups - (1 if tiles % 2 == 1 else groups)
    far += [(last, last)]

    cells = node_cell[0]
    bed = bed_cond[0]
    slots = cells.shape[0]

    def exchange(parts):
        received = [parts[0]]
        for step in range(1, groups):
            received.append(lax.ppermute(parts[step], "layer", [(i, i ^ step) for i in range(groups)]))
        return received

    stride = reach_rows + 8
    spread = call(
        spread_kernel, jax.ShapeDtypeStruct((tiles, stride, node_count), jnp.float32), [in_hbm] * 3,
        [
            pltpu.VMEM(section.shape, jnp.float32),
            pltpu.VMEM(cross_owner.shape, jnp.int32),
            pltpu.VMEM(cross_owner.shape, jnp.int32),
            pltpu.SemaphoreType.DMA((3,)),
        ],
        1, VMEM_MOST,
    )(section, cross_owner, cross_local)
    whole_section = lax.all_to_all(spread, "tile", 0, 0).reshape(tiles * stride, node_count)
    *own_blocks, land = call(
        prepare_kernel,
        (jax.ShapeDtypeStruct((2, held, span, breadth), jnp.float32),) * groups
        + (jax.ShapeDtypeStruct((span, breadth), jnp.float32),),
        [in_vmem] * 3 + [in_hbm], [], 0.5,
    )(head_start, soil_class, land_mask, spread)
    received = exchange(own_blocks)

    node_scratch = pltpu.VMEM((slots, LANES), jnp.float32)
    riv_shape = jax.ShapeDtypeStruct((blocks, LANES), jnp.float32)
    diag, rhs, slot_section, reach = call(
        functools.partial(river_kernel, breadth, span, stride),
        (
            riv_shape,
            riv_shape,
            jax.ShapeDtypeStruct((slots, node_count), jnp.float32),
            jax.ShapeDtypeStruct((1, slots), jnp.float32),
        ),
        [in_vmem] * 3,
        [node_scratch] * 6 + [pltpu.VMEM((span * breadth // BLOCK, LANES), jnp.float32)],
        7,
    )(cells, bed, whole_section)
    edges = jax.ShapeDtypeStruct((-(-(2 * layers + 3) * HALO // 8) * 8, breadth), jnp.float32)
    near_edge, far_edge = call(
        edge_kernel, (edges, edges), [in_vmem] * (3 + groups), [], 0.1,
    )(land, diag, rhs, *received)
    far_halo = lax.ppermute(far_edge, FLAT, far)
    near_halo = lax.ppermute(near_edge, "layer", near)

    window = span + 2 * HALO
    own_field = jax.ShapeDtypeStruct((per_row, span * layers, LANES), jnp.float32)
    field = pltpu.VMEM((per_row, window * layers, LANES), jnp.float32)
    staged = call(
        stage_kernel, (own_field,) * (4 + 5 * ITERS + HALO), [in_smem] * 3 + [in_vmem] * (3 + groups),
        [pltpu.VMEM(own_field.shape, jnp.float32)] + [pltpu.VMEM((span, breadth), jnp.float32)] * 3,
        4,
    )(ks_table, alpha_table, store_table, land, diag, rhs, *received)
    head_shape = jax.ShapeDtypeStruct((held, span, breadth), jnp.float32)
    *heads, top = call(
        flow_kernel,
        (head_shape,) * groups + (jax.ShapeDtypeStruct((span, breadth), jnp.float32),),
        [in_smem] * 3 + [in_vmem] * (5 + len(staged)),
        [field] * 12
        + [pltpu.VMEM((window, breadth), jnp.float32)]
        + [pltpu.VMEM((window * per_row, LANES), jnp.float32)] * 2
        + [pltpu.VMEM((window, breadth), jnp.float32)] * 3,
        3,
    )(ks_table, alpha_table, store_table, land, far_halo, near_halo, diag, rhs, *staged)
    tops = exchange([top] * groups)
    backs = exchange(heads)

    fold = reach_rows // groups
    packed = pltpu.VMEM((slots // groups, LANES), jnp.float32)
    partial = call(
        functools.partial(inflow_kernel, reach_rows, stride),
        jax.ShapeDtypeStruct((tiles * fold, node_count), jnp.float32),
        [in_vmem] * (4 + groups),
        [packed] * 3 + [pltpu.VMEM((across * per_row, LANES), jnp.float32)],
        3,
    )(cells, bed, slot_section, reach, *tops)
    partial, *backs[:-1] = lax.optimization_barrier((partial, *backs[:-1]))
    terms = lax.all_to_all(partial.reshape(tiles, fold, node_count), "tile", 0, 0)
    head = call(
        head_kernel, jax.ShapeDtypeStruct(head_start.shape, jnp.float32), [in_vmem] * groups,
        [pltpu.SemaphoreType.DMA((groups,))], 0.7, out_specs=in_hbm,
    )(*backs)
    inflow_shape = jax.ShapeDtypeStruct((reach_rows, node_count // groups), jnp.float32)
    return head, call(sum_kernel, inflow_shape, [in_vmem], [], 0.1)(terms)


def solution(mesh):
    placed = (
        P("layer", "tile", None),
        P("layer", "tile", None),
        P("tile", None),
        P(),
        P(),
        P(),
        P("tile", None),
        P("tile", None),
        P("tile", None),
        P("tile", None, None),
        P("tile", None, None),
    )
    return jax.shard_map(
        on_device,
        mesh=mesh,
        in_specs=placed,
        out_specs=(P("layer", "tile", None), P("tile", "layer")),
        check_vma=False,
    )
```

```python
import functools

import jax
import jax.numpy as jnp
from jax import lax
from jax.experimental import pallas as pl
from jax.experimental.pallas import tpu as pltpu
from jax.sharding import PartitionSpec as P

ITERS = 2
SWEEPS = 3

LATERAL = 1.0
VERTICAL = 2.0
GRAVITY = 1.0

HALO = ITERS * SWEEPS
BLOCK = 64
LANES = 128
VMEM_LIMIT = 32 * 1024 * 1024
VMEM_MOST = 60 * 1024 * 1024
FLAT = ("tile", "layer")

in_vmem = pl.BlockSpec(memory_space=pltpu.VMEM)
in_hbm = pl.BlockSpec(memory_space=pltpu.HBM)
in_smem = pl.BlockSpec(memory_space=pltpu.SMEM)


def bf16_pieces(value, count):
    pieces = []
    for _ in range(count):
        piece = value.astype(jnp.bfloat16)
        pieces.append(piece)
        value = value - piece.astype(jnp.float32)
    return pieces


def reciprocal(value):
    guess = pl.reciprocal(value, approx=True)
    return guess * (2.0 - value * guess)


def names_of(size):
    index = lax.broadcasted_iota(jnp.int32, (16, LANES), 0)
    return [(index + start).astype(jnp.float32).astype(jnp.bfloat16) for start in range(0, size, 16)]


def one_hot(row, names):
    one = jnp.ones((16, LANES), jnp.bfloat16)
    zero = jnp.zeros((16, LANES), jnp.bfloat16)
    return [jnp.maximum(one - jnp.abs(row - name), zero) for name in names]


def row_copies(ref, first, place):
    rows = ref[pl.ds(pl.multiple_of(first + place // 8 * 8, 8), 8), :]
    return jnp.broadcast_to(rows[place % 8:place % 8 + 1, :], (16, LANES)).astype(jnp.bfloat16)


def position():
    tile, layer = lax.axis_index("tile"), lax.axis_index("layer")
    groups = lax.axis_size("layer")
    flip = lax.rem(tile, 2)
    return layer, flip, jnp.where(flip == 1, groups - 1 - layer, layer)


def own_land(land_ref, span):
    _, _, number = position()
    return land_ref[pl.ds(pl.multiple_of(number * span, span), span), :].astype(jnp.float32)


def span_at(flip, groups, layer):
    return jnp.where(flip == 1, groups - 1 - layer, layer)


def split_cells(cells, first_row, breadth, width):
    local = cells - first_row * breadth
    shift = width.bit_length() - 1
    block = jnp.where(cells < 0, -1, local >> shift)
    return block.astype(jnp.float32), (local & (width - 1)).astype(jnp.float32)


GROUP = 64


def scatter_sum(group, blocks, block_ref, spot_ref, value_refs):
    block_names, spot_names = names_of(blocks), names_of(BLOCK)
    total = None
    for start in range(0, GROUP, GROUP // 2):
        left, right = [], []
        for place in range(start, start + GROUP // 2):
            left.append(jnp.concatenate(one_hot(row_copies(block_ref, group * GROUP, place), block_names), axis=0))
            hot = one_hot(row_copies(spot_ref, group * GROUP, place), spot_names)
            values = [row_copies(ref, group * GROUP, place) for ref in value_refs]
            right.append(jnp.concatenate([tile * value for value in values for tile in hot], axis=0))
        part = lax.dot_general(
            jnp.concatenate(left, axis=1),
            jnp.concatenate(right, axis=1),
            (((1,), (1,)), ((), ())),
            preferred_element_type=jnp.float32,
        )
        total = part if total is None else total + part
    return total


def scatter_range(first, last, blocks, block_ref, spot_ref, value_refs):
    def step(group, total):
        return total + scatter_sum(group, blocks, block_ref, spot_ref, value_refs)

    return lax.fori_loop(first, last, step, jnp.zeros((blocks, BLOCK * len(value_refs)), jnp.float32))


def early_groups(slots):
    return slots // GROUP // 2


def early_kernel(breadth, span, cells_ref, bed_ref, block_ref, spot_ref, high_ref, low_ref, early_ref):
    _, _, number = position()
    block_ref[...], spot_ref[...] = split_cells(cells_ref[...], number * span, breadth, BLOCK)
    high, low = bf16_pieces(bed_ref[...], 2)
    high_ref[...] = high.astype(jnp.float32)
    low_ref[...] = low.astype(jnp.float32)
    early_ref[...] = scatter_range(
        0, early_groups(cells_ref.shape[0]), early_ref.shape[0], block_ref, spot_ref, (high_ref, low_ref)
    )


def river_kernel(
    stride, bed_ref, section_ref, block_ref, spot_ref, dhigh_ref, dlow_ref, early_ref,
    diag_ref, rhs_ref, slot_section_ref, reach_ref, rhigh_sc, rlow_sc, sum_sc,
):
    rows = section_ref.shape[0]
    slots = reach_ref.shape[1]
    first = (lax.axis_index("tile") + 1) * stride - 8
    own_rows = section_ref[pl.ds(pl.multiple_of(first, 8), 8), :]
    reach = jnp.concatenate([own_rows[k:k + 1, :] for k in range(slots // LANES)], axis=1)
    reach_ref[...] = reach
    index = lax.broadcasted_iota(jnp.int32, (rows, slots), 0).astype(jnp.float32)
    pick = jnp.where(index == reach, 1.0, 0.0).astype(jnp.bfloat16)
    picked = jnp.zeros(slot_section_ref.shape, jnp.float32)
    for piece in bf16_pieces(section_ref[...], 3):
        picked = picked + lax.dot_general(
            pick, piece, (((0,), (0,)), ((), ())), preferred_element_type=jnp.float32
        )
    slot_section_ref[...] = picked
    high, low = bf16_pieces(bed_ref[...] * picked, 2)
    rhigh_sc[...] = high.astype(jnp.float32)
    rlow_sc[...] = low.astype(jnp.float32)

    share = LANES // BLOCK
    blocks = share * diag_ref.shape[0]
    middle = early_groups(slots)
    rhs_only = scatter_range(0, middle, blocks, block_ref, spot_ref, (rhigh_sc, rlow_sc))
    both = scatter_range(
        middle, slots // GROUP, blocks, block_ref, spot_ref, (dhigh_ref, dlow_ref, rhigh_sc, rlow_sc)
    )
    low_half = lax.broadcasted_iota(jnp.int32, diag_ref.shape, 1) < BLOCK
    for part, ref in ((both[:, :LANES] + early_ref[...], diag_ref), (both[:, LANES:] + rhs_only, rhs_ref)):
        sum_sc[...] = part + pltpu.roll(part, BLOCK, 1)
        ref[...] = jnp.where(
            low_half, sum_sc[pl.ds(0, blocks // share, stride=share), :], sum_sc[pl.ds(1, blocks // share, stride=share), :]
        )


def edge_kernel(land_ref, diag_ref, rhs_ref, *refs):
    block_refs, (near_ref, far_ref) = refs[:-2], refs[-2:]
    _, held, span, breadth = block_refs[0].shape
    _, _, number = position()
    odd = lax.rem(number, 2) == 1
    per_row = breadth // LANES

    def put_edges(entry, top, bottom, lanes=slice(None)):
        near_ref[pl.ds(entry * HALO, HALO), lanes] = jnp.where(odd, top, bottom)
        far_ref[pl.ds(entry * HALO, HALO), lanes] = jnp.where(odd, bottom, top)

    entry = 0
    for kind in range(2):
        for block_ref in block_refs:
            for held_layer in range(held):
                put_edges(entry, block_ref[kind, held_layer, :HALO, :], block_ref[kind, held_layer, span - HALO:, :])
                entry += 1
    land = own_land(land_ref, span)
    put_edges(entry, land[:HALO], land[span - HALO:])
    for ref in (diag_ref, rhs_ref):
        entry += 1
        for part in range(per_row):
            top = ref[pl.ds(part, HALO, stride=per_row), :]
            bottom = ref[pl.ds((span - HALO) * per_row + part, HALO, stride=per_row), :]
            put_edges(entry, top, bottom, slice(part * LANES, (part + 1) * LANES))
    rest = near_ref.shape[0] - (entry + 1) * HALO
    for ref in (near_ref, far_ref):
        ref[pl.ds((entry + 1) * HALO, rest), :] = jnp.zeros((rest, breadth), jnp.float32)


def spread_kernel(section_hbm, owner_hbm, local_hbm, spread_ref, section_ref, owner_ref, local_ref, sems):
    pairs = ((section_hbm, section_ref), (owner_hbm, owner_ref), (local_hbm, local_ref))
    copies = [pltpu.make_async_copy(here, there, sems.at[k]) for k, (here, there) in enumerate(pairs)]
    for copy in copies:
        copy.start()
    for copy in copies:
        copy.wait()
    tiles, stride, _ = spread_ref.shape
    reach_rows = section_ref.shape[0]
    reach = (owner_ref[...] * stride + local_ref[...]).astype(jnp.float32)
    parts = [reach[:, start:start + LANES] for start in range(0, reach.shape[1], LANES)]
    parts.append(jnp.zeros((stride - reach_rows - len(parts), LANES), jnp.float32))
    payload = jnp.concatenate([section_ref[...], *parts], axis=0)
    for tile in range(tiles):
        spread_ref[tile] = payload


def prepare_kernel(head_ref, soil_ref, after_ref, *refs):
    del after_ref
    groups = len(refs)
    held, across, _ = head_ref.shape
    span = across // groups
    own, flip, _ = position()

    def rows_of(target):
        return pl.ds(pl.multiple_of(span_at(flip, groups, target) * span, span), span)

    for step, block_ref in enumerate(refs):
        rows = rows_of(own ^ step)
        for layer in range(held):
            block_ref[0, layer] = head_ref[layer, rows, :]
            block_ref[1, layer] = soil_ref[layer, rows, :].astype(jnp.float32)


class Rows:
    def __init__(self, layers, breadth):
        self.layers, self.breadth, self.per_row = layers, breadth, breadth // LANES

    def get(self, ref, row):
        spot = pl.ds(row * self.layers, self.layers)
        return jnp.concatenate([ref[part, spot, :] for part in range(self.per_row)], axis=1)

    def put(self, ref, row, value):
        spot = pl.ds(row * self.layers, self.layers)
        for part in range(self.per_row):
            ref[part, spot, :] = value[:, part * LANES:(part + 1) * LANES]

    def put_layer(self, ref, layer, row, value):
        for part in range(self.per_row):
            spot = pl.ds(row * self.layers + layer, value.shape[0], stride=self.layers)
            ref[part, spot, :] = value[:, part * LANES:(part + 1) * LANES]

    def east(self, field):
        return pltpu.roll(field, self.breadth - 1, 1)

    def west(self, field):
        return pltpu.roll(field, 1, 1)

    def below(self, field):
        return pltpu.roll(field, self.layers - 1, 0)

    def above(self, field):
        return pltpu.roll(field, 1, 0)


class Joined:
    def __init__(self, rows, own, full, first, last):
        self.rows, self.own, self.full, self.first, self.last = rows, own, full, first, last

    def holds(self, row):
        return self.first <= row < self.last

    def get(self, row):
        if self.holds(row):
            return self.rows.get(self.own, row - HALO)
        return self.rows.get(self.full, row)

    def put(self, row, value):
        self.rows.put(self.full, row, value)


def relax_row(rows, row, head, weights, wx_before, base, inverse):
    before, here, after = head
    wx, wy, wz = [field.get(row) for field in weights]
    total = base.get(row) + wx_before * before + wx * after
    total = total + wy * rows.east(here) + rows.west(wy * here)
    total = total + wz * rows.below(here) + rows.above(wz * here)
    return total * inverse.get(row), wx


def river_row(rows, ref, row, top):
    parts = [
        jnp.broadcast_to(ref[pl.ds(row * rows.per_row + part, 1), :], (rows.layers, LANES))
        for part in range(rows.per_row)
    ]
    return jnp.where(top, jnp.concatenate(parts, axis=1), 0.0)


class Faces:
    def __init__(self, rows, land, lands):
        self.rows, self.lands = rows, lands
        lx_ref, ly_ref, lz_ref = lands
        count = land.shape[0]
        level = lax.broadcasted_iota(jnp.int32, (rows.layers, rows.breadth), 0)
        self.not_bottom = level < rows.layers - 1
        not_last = lax.broadcasted_iota(jnp.int32, land.shape, 1) < rows.breadth - 1
        lx_ref[pl.ds(0, count - 1), :] = 2.0 * LATERAL * land[:count - 1] * land[1:]
        ly_ref[...] = jnp.where(not_last, 2.0 * LATERAL * land * rows.east(land), 0.0)
        lz_ref[...] = 2.0 * VERTICAL * land * land

    def conduct(self, ks, alpha, head):
        return ks * jnp.exp(alpha * jnp.minimum(head, 0.0))

    def face(self, land, here, there):
        return land * (here * there) * reciprocal(here + there)

    def between_rows(self, row, here, there):
        return self.face(self.lands[0][pl.ds(row, 1), :], here, there)

    def in_row(self, row, here):
        rows = self.rows
        wy = self.face(self.lands[1][pl.ds(row, 1), :], here, rows.east(here))
        wz = self.face(self.lands[2][pl.ds(row, 1), :], here, rows.below(here))
        wz = jnp.where(self.not_bottom, wz, 0.0)
        wz_above = rows.above(wz)
        return wy, wz, wy + rows.west(wy) + wz + wz_above, GRAVITY * (wz_above - wz)


def lane_tables(refs, layers):
    lane = lax.broadcasted_iota(jnp.int32, (layers, LANES), 1)
    tables = []
    for ref in refs:
        table = jnp.zeros((layers, LANES), jnp.float32)
        for kind in range(ref.shape[0]):
            table = jnp.where(lane == kind, ref[kind], table)
        tables.append(table)
    return tables


def look_up(rows, table, soil):
    parts = [
        jnp.take_along_axis(table, soil[:, part * LANES:(part + 1) * LANES], axis=1, mode="promise_in_bounds")
        for part in range(rows.per_row)
    ]
    return jnp.concatenate(parts, axis=1)


def stage_kernel(ks_ref, alpha_ref, store_ref, land_ref, diag_ref, rhs_ref, *refs):
    groups = lax.axis_size("layer")
    own, _, _ = position()
    block_refs, refs = refs[:groups], refs[groups:]
    first_out, ks_out, alpha_out, store_out = refs[:4]
    fields = [refs[4 + 5 * picard:9 + 5 * picard] for picard in range(ITERS)]
    head_outs = refs[4 + 5 * ITERS:4 + 5 * ITERS + HALO]
    soil_sc, *lands = refs[4 + 5 * ITERS + HALO:]
    _, held, span, breadth = block_refs[0].shape
    layers = groups * held
    rows = Rows(layers, breadth)
    faces = Faces(rows, own_land(land_ref, span), lands)
    top = lax.broadcasted_iota(jnp.int32, (layers, breadth), 0) == 0

    for step, block_ref in enumerate(block_refs):
        for held_layer in range(held):
            layer = (own ^ step) * held + held_layer
            rows.put_layer(first_out, layer, 0, block_ref[0, held_layer])
            rows.put_layer(soil_sc, layer, 0, block_ref[1, held_layer])
    tables = lane_tables((ks_ref, alpha_ref, store_ref), layers)
    for row in range(span):
        soil = rows.get(soil_sc, row).astype(jnp.int32)
        for table, out in zip(tables, (ks_out, alpha_out, store_out)):
            rows.put(out, row, look_up(rows, table, soil))

    now, begin, stop, done = first_out, 0, span, 0
    for wx_out, wy_out, wz_out, inv_out, base_out in fields:
        before = None
        for row in range(begin, stop):
            here = faces.conduct(rows.get(ks_out, row), rows.get(alpha_out, row), rows.get(now, row))
            wy, wz, diagonal, gravity = faces.in_row(row, here)
            rows.put(wy_out, row, wy)
            rows.put(wz_out, row, wz)
            store = rows.get(store_out, row)
            sums = store + diagonal, store * rows.get(first_out, row) + gravity
            if row > begin:
                wx = faces.between_rows(row - 1, before[0], here)
                rows.put(wx_out, row - 1, wx)
                diagonal, base = before[1]
                if row - 1 > begin:
                    diagonal = reciprocal(diagonal + before[2] + wx + river_row(rows, diag_ref, row - 1, top))
                    base = base + river_row(rows, rhs_ref, row - 1, top)
                rows.put(inv_out, row - 1, diagonal)
                rows.put(base_out, row - 1, base)
            else:
                wx = None
            before = here, sums, wx
        rows.put(inv_out, stop - 1, before[1][0])
        rows.put(base_out, stop - 1, before[1][1])
        weights = [Joined(rows, None, ref, HALO, HALO) for ref in (wx_out, wy_out, wz_out)]
        base, inverse = [Joined(rows, None, ref, HALO, HALO) for ref in (base_out, inv_out)]
        for _ in range(SWEEPS):
            begin, stop = begin + 1, stop - 1
            head = rows.get(now, begin - 1), rows.get(now, begin)
            wx_before = rows.get(wx_out, begin - 1)
            for row in range(begin, stop):
                head = *head[-2:], rows.get(now, row + 1)
                value, wx_before = relax_row(rows, row, head, weights, wx_before, base, inverse)
                rows.put(head_outs[done], row, value)
            now = head_outs[done]
            done += 1


def flow_kernel(kst_ref, alphat_ref, storet_ref, land_ref, far_ref, near_ref, diag_ref, rhs_ref, *refs):
    groups = lax.axis_size("layer")
    own, _, number = position()
    end = (number == 0) | (number == groups - 1)
    far_partner = jnp.where(end, own, own ^ (groups - 1))
    tile, tiles = lax.axis_index("tile"), lax.axis_size("tile")
    outside = ((tile == 0) & (number == 0)) | ((tile == tiles - 1) & (number == groups - 1))
    first_ref, ks_ref, alpha_ref, store_ref = refs[:4]
    fields = [refs[4 + 5 * picard:9 + 5 * picard] for picard in range(ITERS)]
    staged_refs = refs[4 + 5 * ITERS:4 + 5 * ITERS + HALO]
    refs = refs[4 + 5 * ITERS + HALO:]
    head_refs, top_ref = refs[:groups], refs[groups]
    (
        first_sc, soil_sc, ks_sc, alpha_sc, store_sc, wx_sc, wy_sc, wz_sc, base_sc, inv_sc, ping_sc, pong_sc,
        land_sc, dtop_sc, rtop_sc, *lands,
    ) = refs[1 + groups:]
    held, span, breadth = head_refs[0].shape
    layers = groups * held
    window = span + 2 * HALO
    last_own = HALO + span
    rows = Rows(layers, breadth)
    side = HALO * rows.per_row

    land_sc[pl.ds(HALO, span), :] = own_land(land_ref, span)
    dtop_sc[pl.ds(side, span * rows.per_row), :] = diag_ref[...]
    rtop_sc[pl.ds(side, span * rows.per_row), :] = rhs_ref[...]

    def put_halo(ref, partner, row):
        def entry(number):
            return ref[pl.ds(number * HALO, HALO), :]

        for count in range(layers):
            layer = (partner ^ (count // held)) * held + count % held
            rows.put_layer(first_sc, layer, row, entry(count))
            rows.put_layer(soil_sc, layer, row, entry(layers + count))
        water = outside if ref is far_ref else False
        land_sc[pl.ds(row, HALO), :] = jnp.where(water, 0.0, entry(2 * layers))
        for count, top_sc in ((2 * layers + 1, dtop_sc), (2 * layers + 2, rtop_sc)):
            value = entry(count)
            for part in range(rows.per_row):
                spot = pl.ds(row * rows.per_row + part, HALO, stride=rows.per_row)
                top_sc[spot, :] = value[:, part * LANES:(part + 1) * LANES]

    for odd, above_ref, below_ref in ((0, far_ref, near_ref), (1, near_ref, far_ref)):
        @pl.when(lax.rem(number, 2) == odd)
        def _(above_ref=above_ref, below_ref=below_ref):
            for ref, row in ((above_ref, 0), (below_ref, last_own)):
                put_halo(ref, own ^ 1 if ref is near_ref else far_partner, row)

    faces = Faces(rows, land_sc[...], lands)
    tables = lane_tables((kst_ref, alphat_ref, storet_ref), layers)
    for row in [*range(HALO), *range(last_own, window)]:
        soil = rows.get(soil_sc, row).astype(jnp.int32)
        for table, ref in zip(tables, (ks_sc, alpha_sc, store_sc)):
            rows.put(ref, row, look_up(rows, table, soil))

    first, ks, alpha, store = [
        Joined(rows, held_ref, full, HALO, last_own)
        for held_ref, full in ((first_ref, first_sc), (ks_ref, ks_sc), (alpha_ref, alpha_sc), (store_ref, store_sc))
    ]
    top = lax.broadcasted_iota(jnp.int32, (layers, breadth), 0) == 0

    now, begin, stop, done = first, 0, window, 0
    for wx_ref, wy_ref, wz_ref, inv_ref, base_ref in fields:
        low, high = HALO + done, last_own - done
        wx_of = Joined(rows, wx_ref, wx_sc, low, high - 1)
        wy_of, wz_of = Joined(rows, wy_ref, wy_sc, low, high), Joined(rows, wz_ref, wz_sc, low, high)
        inverse, base = [
            Joined(rows, held_ref, full, low + 1, high - 1) for held_ref, full in ((inv_ref, inv_sc), (base_ref, base_sc))
        ]
        here_before, wx_before, sums_before = None, None, None
        for row in range(begin, stop):
            at_end = row in (low, high - 1)
            here, sums = None, None
            if not wy_of.holds(row) or at_end:
                here = faces.conduct(ks.get(row), alpha.get(row), now.get(row))
            if at_end:
                sums = rows.get(inv_ref, row - HALO), rows.get(base_ref, row - HALO)
            elif not wy_of.holds(row) and begin < row < stop - 1:
                wy, wz, diagonal, gravity = faces.in_row(row, here)
                wy_of.put(row, wy)
                wz_of.put(row, wz)
                sums = store.get(row) + diagonal, store.get(row) * first.get(row) + gravity
            if row > begin:
                if wx_of.holds(row - 1):
                    wx = wx_of.get(row - 1)
                else:
                    wx = faces.between_rows(row - 1, here_before, here)
                    wx_of.put(row - 1, wx)
                if sums_before is not None:
                    diagonal = sums_before[0] + wx_before + wx + river_row(rows, dtop_sc, row - 1, top)
                    inverse.put(row - 1, reciprocal(diagonal))
                    base.put(row - 1, sums_before[1] + river_row(rows, rtop_sc, row - 1, top))
                wx_before = wx
            here_before, sums_before = here, sums
        for _ in range(SWEEPS):
            begin, stop = begin + 1, stop - 1
            later = Joined(rows, staged_refs[done], (ping_sc, pong_sc)[done % 2], HALO + done + 1, last_own - done - 1)
            done += 1
            for row in range(begin, stop):
                if not later.holds(row):
                    head = now.get(row - 1), now.get(row), now.get(row + 1)
                    value, _ = relax_row(rows, row, head, (wx_of, wy_of, wz_of), wx_of.get(row - 1), base, inverse)
                    later.put(row, value)
            now = later
    for row in range(now.first, now.last):
        now.put(row, now.get(row))
    for part in range(rows.per_row):
        lanes = pl.ds(part * LANES, LANES)
        top_ref[:, lanes] = now.full[part, pl.ds(HALO * layers, span, stride=layers), :]
        for step, head_ref in enumerate(head_refs):
            for held_layer in range(held):
                layer = (own ^ step) * held + held_layer
                head_ref[held_layer, :, lanes] = now.full[part, pl.ds(HALO * layers + layer, span, stride=layers), :]


def inflow_kernel(reach_rows, stride, cells_ref, bed_ref, slot_section_ref, reach_ref, *refs):
    groups = lax.axis_size("layer")
    own_layer, flip, _ = position()
    top_refs = refs[:groups]
    out_ref, block_sc, lane_sc, found_sc, turned_sc = refs[groups:]
    span, breadth = top_refs[0].shape
    per_row = breadth // LANES
    blocks = groups * span * per_row
    slots = cells_ref.shape[0]
    quarter = LANES // groups
    packed = slots // groups
    for step, top_ref in enumerate(top_refs):
        number = span_at(flip, groups, own_layer ^ step)
        for part in range(per_row):
            spot = pl.ds(number * span * per_row + part, span, stride=per_row)
            turned_sc[spot, :] = top_ref[:, part * LANES:(part + 1) * LANES]

    own = lax.broadcasted_iota(jnp.int32, (packed, LANES), 1) // quarter

    def pack(ref):
        result = None
        for number in range(groups):
            shift = lax.rem((number + groups - own_layer) * quarter, LANES)
            moved = pltpu.roll(ref[pl.ds(number * packed, packed), :], shift, 1)
            result = moved if result is None else jnp.where(own == number, moved, result)
        return result

    cells = pack(cells_ref)
    block, lane = split_cells(cells, 0, breadth, LANES)
    block_sc[...] = block
    lane_sc[...] = lane
    table = jnp.concatenate(bf16_pieces(turned_sc[...].T, 2), axis=0)
    names = names_of(blocks)
    index = lax.broadcasted_iota(jnp.int32, (8, LANES), 0).astype(jnp.float32)
    for pair in range(0, packed, 2):
        hots = jnp.concatenate(
            [jnp.concatenate(one_hot(row_copies(block_sc, 0, row), names), axis=0) for row in (pair, pair + 1)], axis=1
        )
        found = lax.dot_general(
            table, hots, (((1,), (0,)), ((), ())), preferred_element_type=jnp.float32
        )
        found = found[:LANES] + found[LANES:]
        for row in (pair, pair + 1):
            lanes = jnp.broadcast_to(lane_sc[pl.ds(row, 1), :], (8, LANES))
            mine = found[:, (row - pair) * LANES:(row - pair + 1) * LANES]
            total = jnp.zeros((8, LANES), jnp.float32)
            for start in range(0, LANES, 8):
                total = total + jnp.where(lanes == index + float(start), mine[start:start + 8], 0.0)
            found_sc[pl.ds(row, 1), :] = jnp.sum(total, axis=0, keepdims=True)
    slot_in = jnp.where(cells >= 0, pack(bed_ref) * (found_sc[...] - pack(slot_section_ref)), 0.0)
    spread = jnp.concatenate(
        [slot_in if number == 0 else pltpu.roll(slot_in, LANES - number * quarter, 1) for number in range(groups)],
        axis=0,
    )
    in_quarter = lax.broadcasted_iota(jnp.int32, spread.shape, 1) < quarter
    pieces = bf16_pieces(jnp.where(in_quarter, spread, 0.0), 3)
    fold = reach_rows // groups
    index = lax.broadcasted_iota(jnp.int32, (out_ref.shape[0], slots), 0)
    index = index // fold * stride + lax.rem(index, fold)
    result = None
    for number in range(groups):
        name = (index + number * fold).astype(jnp.float32)
        put = jnp.where(name == reach_ref[...], 1.0, 0.0).astype(jnp.bfloat16)
        total = jnp.zeros(out_ref.shape, jnp.float32)
        for piece in pieces:
            total = total + lax.dot_general(
                put, piece, (((1,), (0,)), ((), ())), preferred_element_type=jnp.float32
            )
        result = total if result is None else result + pltpu.roll(total, number * quarter, 1)
    out_ref[...] = result


def sum_kernel(terms_ref, inflow_ref):
    total = terms_ref[0]
    for tile in range(1, terms_ref.shape[0]):
        total = total + terms_ref[tile]
    fold, quarter = total.shape[0], inflow_ref.shape[1]
    for number in range(inflow_ref.shape[0] // fold):
        lanes = slice(number * quarter, (number + 1) * quarter)
        inflow_ref[pl.ds(number * fold, fold), :] = total[:, lanes]


def head_kernel(*refs):
    groups = lax.axis_size("layer")
    back_refs, (head_hbm, sems) = refs[:groups], refs[groups:]
    _, span, _ = back_refs[0].shape
    own, flip, _ = position()
    copies = []
    for step, back_ref in enumerate(back_refs):
        rows = pl.ds(pl.multiple_of(span_at(flip, groups, own ^ step) * span, span), span)
        copies.append(pltpu.make_async_copy(back_ref, head_hbm.at[:, rows, :], sems.at[step]))
        copies[-1].start()
    for copy in copies:
        copy.wait()


def call(kernel, out_shape, in_specs, scratch, micros, vmem=VMEM_LIMIT, out_specs=None):
    single = not isinstance(out_shape, (tuple, list))
    return pl.pallas_call(
        kernel,
        out_shape=out_shape,
        in_specs=in_specs,
        out_specs=out_specs or (in_vmem if single else tuple(in_vmem for _ in out_shape)),
        scratch_shapes=scratch,
        compiler_params=pltpu.CompilerParams(vmem_limit_bytes=vmem),
        cost_estimate=pl.CostEstimate(flops=int(micros * 1.15e9), bytes_accessed=0, transcendentals=0),
    )


def on_device(
    head_start,
    soil_class,
    land_mask,
    ks_table,
    alpha_table,
    store_table,
    section,
    cross_owner,
    cross_local,
    node_cell,
    bed_cond,
):
    held, across, breadth = head_start.shape
    reach_rows, node_count = section.shape
    tiles = lax.axis_size("tile")
    groups = lax.axis_size("layer")
    layers = held * groups
    span = across // groups
    per_row = breadth // LANES
    blocks = span * per_row
    near = [(i, i ^ 1) for i in range(groups)]
    far = []
    for upper in range(tiles):
        far += [(upper * groups + i, upper * groups + (i ^ (groups - 1))) for i in range(1, groups - 1)]
        if upper + 1 < tiles:
            index = groups - 1 if upper % 2 == 0 else 0
            one, two = upper * groups + index, (upper + 1) * groups + index
            far += [(one, two), (two, one)]
    far += [(0, 0)]
    last = tiles * groups - (1 if tiles % 2 == 1 else groups)
    far += [(last, last)]

    cells = node_cell[0]
    bed = bed_cond[0]
    slots = cells.shape[0]

    def exchange(parts):
        received = [parts[0]]
        for step in range(1, groups):
            received.append(lax.ppermute(parts[step], "layer", [(i, i ^ step) for i in range(groups)]))
        return received

    stride = reach_rows + 8
    spread = call(
        spread_kernel, jax.ShapeDtypeStruct((tiles, stride, node_count), jnp.float32), [in_hbm] * 3,
        [
            pltpu.VMEM(section.shape, jnp.float32),
            pltpu.VMEM(cross_owner.shape, jnp.int32),
            pltpu.VMEM(cross_owner.shape, jnp.int32),
            pltpu.SemaphoreType.DMA((3,)),
        ],
        1, VMEM_MOST,
    )(section, cross_owner, cross_local)
    whole_section = lax.all_to_all(spread, "tile", 0, 0).reshape(tiles * stride, node_count)
    own_blocks = call(
        prepare_kernel,
        (jax.ShapeDtypeStruct((2, held, span, breadth), jnp.float32),) * groups,
        [in_vmem] * 2 + [in_hbm], [], 0.5,
    )(head_start, soil_class, spread)
    received = exchange(own_blocks)

    node_scratch = pltpu.VMEM((slots, LANES), jnp.float32)
    riv_shape = jax.ShapeDtypeStruct((blocks, LANES), jnp.float32)
    node_field = jax.ShapeDtypeStruct((slots, LANES), jnp.float32)
    groups_of_cells = span * breadth // BLOCK
    early = call(
        functools.partial(early_kernel, breadth, span),
        (node_field,) * 4 + (jax.ShapeDtypeStruct((groups_of_cells, LANES), jnp.float32),), [in_vmem] * 2, [], 2.5,
    )(cells, bed)
    diag, rhs, slot_section, reach = call(
        functools.partial(river_kernel, stride),
        (riv_shape, riv_shape, node_field, jax.ShapeDtypeStruct((1, slots), jnp.float32)),
        [in_vmem] * 7, [node_scratch] * 2 + [pltpu.VMEM((groups_of_cells, LANES), jnp.float32)], 6,
    )(bed, whole_section, *early)
    edges = jax.ShapeDtypeStruct((-(-(2 * layers + 3) * HALO // 8) * 8, breadth), jnp.float32)
    near_edge, far_edge = call(
        edge_kernel, (edges, edges), [in_vmem] * (3 + groups), [], 0.1,
    )(land_mask, diag, rhs, *received)
    far_halo = lax.ppermute(far_edge, FLAT, far)
    near_halo = lax.ppermute(near_edge, "layer", near)

    window = span + 2 * HALO
    own_field = jax.ShapeDtypeStruct((per_row, span * layers, LANES), jnp.float32)
    field = pltpu.VMEM((per_row, window * layers, LANES), jnp.float32)
    staged = call(
        stage_kernel, (own_field,) * (4 + 5 * ITERS + HALO), [in_smem] * 3 + [in_vmem] * (3 + groups),
        [pltpu.VMEM(own_field.shape, jnp.float32)] + [pltpu.VMEM((span, breadth), jnp.float32)] * 3,
        4,
    )(ks_table, alpha_table, store_table, land_mask, diag, rhs, *received)
    head_shape = jax.ShapeDtypeStruct((held, span, breadth), jnp.float32)
    *heads, top = call(
        flow_kernel,
        (head_shape,) * groups + (jax.ShapeDtypeStruct((span, breadth), jnp.float32),),
        [in_smem] * 3 + [in_vmem] * (5 + len(staged)),
        [field] * 12
        + [pltpu.VMEM((window, breadth), jnp.float32)]
        + [pltpu.VMEM((window * per_row, LANES), jnp.float32)] * 2
        + [pltpu.VMEM((window, breadth), jnp.float32)] * 3,
        3,
    )(ks_table, alpha_table, store_table, land_mask, far_halo, near_halo, diag, rhs, *staged)
    tops = exchange([top] * groups)
    backs = exchange(heads)

    fold = reach_rows // groups
    packed = pltpu.VMEM((slots // groups, LANES), jnp.float32)
    partial = call(
        functools.partial(inflow_kernel, reach_rows, stride),
        jax.ShapeDtypeStruct((tiles * fold, node_count), jnp.float32),
        [in_vmem] * (4 + groups),
        [packed] * 3 + [pltpu.VMEM((across * per_row, LANES), jnp.float32)],
        3,
    )(cells, bed, slot_section, reach, *tops)
    partial, *backs[:-1] = lax.optimization_barrier((partial, *backs[:-1]))
    terms = lax.all_to_all(partial.reshape(tiles, fold, node_count), "tile", 0, 0)
    head = call(
        head_kernel, jax.ShapeDtypeStruct(head_start.shape, jnp.float32), [in_vmem] * groups,
        [pltpu.SemaphoreType.DMA((groups,))], 0.7, out_specs=in_hbm,
    )(*backs)
    inflow_shape = jax.ShapeDtypeStruct((reach_rows, node_count // groups), jnp.float32)
    return head, call(sum_kernel, inflow_shape, [in_vmem], [], 0.1)(terms)


def solution(mesh):
    placed = (
        P("layer", "tile", None),
        P("layer", "tile", None),
        P("tile", None),
        P(),
        P(),
        P(),
        P("tile", None),
        P("tile", None),
        P("tile", None),
        P("tile", None, None),
        P("tile", None, None),
    )
    return jax.shard_map(
        on_device,
        mesh=mesh,
        in_specs=placed,
        out_specs=(P("layer", "tile", None), P("tile", "layer")),
        check_vma=False,
    )
```

```python
import functools

import jax
import jax.numpy as jnp
from jax import lax
from jax.experimental import pallas as pl
from jax.experimental.pallas import tpu as pltpu
from jax.sharding import PartitionSpec as P

ITERS = 2
SWEEPS = 3

LATERAL = 1.0
VERTICAL = 2.0
GRAVITY = 1.0

HALO = ITERS * SWEEPS
BLOCK = 64
LANES = 128
VMEM_LIMIT = 32 * 1024 * 1024
VMEM_MOST = 60 * 1024 * 1024
FLAT = ("tile", "layer")

in_vmem = pl.BlockSpec(memory_space=pltpu.VMEM)
in_hbm = pl.BlockSpec(memory_space=pltpu.HBM)
in_smem = pl.BlockSpec(memory_space=pltpu.SMEM)


def bf16_pieces(value, count):
    pieces = []
    for _ in range(count):
        piece = value.astype(jnp.bfloat16)
        pieces.append(piece)
        value = value - piece.astype(jnp.float32)
    return pieces


def reciprocal(value):
    guess = pl.reciprocal(value, approx=True)
    return guess * (2.0 - value * guess)


def names_of(size):
    index = lax.broadcasted_iota(jnp.int32, (16, LANES), 0)
    return [(index + start).astype(jnp.float32).astype(jnp.bfloat16) for start in range(0, size, 16)]


def one_hot(row, names):
    one = jnp.ones((16, LANES), jnp.bfloat16)
    zero = jnp.zeros((16, LANES), jnp.bfloat16)
    return [jnp.maximum(one - jnp.abs(row - name), zero) for name in names]


def row_copies(ref, first, place):
    rows = ref[pl.ds(pl.multiple_of(first + place // 8 * 8, 8), 8), :]
    return jnp.broadcast_to(rows[place % 8:place % 8 + 1, :], (16, LANES)).astype(jnp.bfloat16)


def position():
    tile, layer = lax.axis_index("tile"), lax.axis_index("layer")
    groups = lax.axis_size("layer")
    flip = lax.rem(tile, 2)
    return layer, flip, jnp.where(flip == 1, groups - 1 - layer, layer)


def own_land(land_ref, span):
    _, _, number = position()
    return land_ref[pl.ds(pl.multiple_of(number * span, span), span), :].astype(jnp.float32)


def span_at(flip, groups, layer):
    return jnp.where(flip == 1, groups - 1 - layer, layer)


def split_cells(cells, first_row, breadth, width):
    local = cells - first_row * breadth
    shift = width.bit_length() - 1
    block = jnp.where(cells < 0, -1, local >> shift)
    return block.astype(jnp.float32), (local & (width - 1)).astype(jnp.float32)


GROUP = 64


def scatter_sum(group, blocks, block_ref, spot_ref, value_refs):
    block_names, spot_names = names_of(blocks), names_of(BLOCK)
    total = None
    for start in range(0, GROUP, GROUP // 2):
        left, right = [], []
        for place in range(start, start + GROUP // 2):
            left.append(jnp.concatenate(one_hot(row_copies(block_ref, group * GROUP, place), block_names), axis=0))
            hot = one_hot(row_copies(spot_ref, group * GROUP, place), spot_names)
            values = [row_copies(ref, group * GROUP, place) for ref in value_refs]
            right.append(jnp.concatenate([tile * value for value in values for tile in hot], axis=0))
        part = lax.dot_general(
            jnp.concatenate(left, axis=1),
            jnp.concatenate(right, axis=1),
            (((1,), (1,)), ((), ())),
            preferred_element_type=jnp.float32,
        )
        total = part if total is None else total + part
    return total


def scatter_range(first, last, blocks, block_ref, spot_ref, value_refs):
    def step(group, total):
        return total + scatter_sum(group, blocks, block_ref, spot_ref, value_refs)

    return lax.fori_loop(first, last, step, jnp.zeros((blocks, BLOCK * len(value_refs)), jnp.float32))


def early_groups(slots):
    return slots // GROUP * 3 // 4


def early_kernel(breadth, span, cells_ref, bed_ref, block_ref, spot_ref, high_ref, low_ref, early_ref):
    _, _, number = position()
    block_ref[...], spot_ref[...] = split_cells(cells_ref[...], number * span, breadth, BLOCK)
    high, low = bf16_pieces(bed_ref[...], 2)
    high_ref[...] = high.astype(jnp.float32)
    low_ref[...] = low.astype(jnp.float32)
    early_ref[...] = scatter_range(
        0, early_groups(cells_ref.shape[0]), early_ref.shape[0], block_ref, spot_ref, (high_ref, low_ref)
    )


def river_kernel(
    stride, bed_ref, section_ref, block_ref, spot_ref, dhigh_ref, dlow_ref, early_ref,
    diag_ref, rhs_ref, slot_section_ref, reach_ref, rhigh_sc, rlow_sc, sum_sc,
):
    rows = section_ref.shape[0]
    slots = reach_ref.shape[1]
    first = (lax.axis_index("tile") + 1) * stride - 8
    own_rows = section_ref[pl.ds(pl.multiple_of(first, 8), 8), :]
    reach = jnp.concatenate([own_rows[k:k + 1, :] for k in range(slots // LANES)], axis=1)
    reach_ref[...] = reach
    index = lax.broadcasted_iota(jnp.int32, (rows, slots), 0).astype(jnp.float32)
    pick = jnp.where(index == reach, 1.0, 0.0).astype(jnp.bfloat16)
    picked = jnp.zeros(slot_section_ref.shape, jnp.float32)
    for piece in bf16_pieces(section_ref[...], 3):
        picked = picked + lax.dot_general(
            pick, piece, (((0,), (0,)), ((), ())), preferred_element_type=jnp.float32
        )
    slot_section_ref[...] = picked
    high, low = bf16_pieces(bed_ref[...] * picked, 2)
    rhigh_sc[...] = high.astype(jnp.float32)
    rlow_sc[...] = low.astype(jnp.float32)

    share = LANES // BLOCK
    blocks = share * diag_ref.shape[0]
    middle = early_groups(slots)
    rhs_only = scatter_range(0, middle, blocks, block_ref, spot_ref, (rhigh_sc, rlow_sc))
    both = scatter_range(
        middle, slots // GROUP, blocks, block_ref, spot_ref, (dhigh_ref, dlow_ref, rhigh_sc, rlow_sc)
    )
    low_half = lax.broadcasted_iota(jnp.int32, diag_ref.shape, 1) < BLOCK
    for part, ref in ((both[:, :LANES] + early_ref[...], diag_ref), (both[:, LANES:] + rhs_only, rhs_ref)):
        sum_sc[...] = part + pltpu.roll(part, BLOCK, 1)
        ref[...] = jnp.where(
            low_half, sum_sc[pl.ds(0, blocks // share, stride=share), :], sum_sc[pl.ds(1, blocks // share, stride=share), :]
        )


def edge_kernel(land_ref, diag_ref, rhs_ref, *refs):
    block_refs, (near_head_ref, near_ref, far_head_ref, far_ref) = refs[:-4], refs[-4:]
    _, held, span, breadth = block_refs[0].shape
    _, _, number = position()
    odd = lax.rem(number, 2) == 1
    per_row = breadth // LANES

    def put_edges(to_near, to_far, entry, top, bottom, lanes=slice(None)):
        to_near[pl.ds(entry * HALO, HALO), lanes] = jnp.where(odd, top, bottom)
        to_far[pl.ds(entry * HALO, HALO), lanes] = jnp.where(odd, bottom, top)

    for kind, to in enumerate(((near_head_ref, far_head_ref), (near_ref, far_ref))):
        for step, block_ref in enumerate(block_refs):
            for held_layer in range(held):
                field = block_ref.at[kind, held_layer]
                put_edges(*to, step * held + held_layer, field[:HALO, :], field[span - HALO:, :])
    entry = len(block_refs) * held
    land = own_land(land_ref, span)
    put_edges(near_ref, far_ref, entry, land[:HALO], land[span - HALO:])
    for ref in (diag_ref, rhs_ref):
        entry += 1
        for part in range(per_row):
            top = ref[pl.ds(part, HALO, stride=per_row), :]
            bottom = ref[pl.ds((span - HALO) * per_row + part, HALO, stride=per_row), :]
            put_edges(near_ref, far_ref, entry, top, bottom, slice(part * LANES, (part + 1) * LANES))
    rest = near_ref.shape[0] - (entry + 1) * HALO
    for ref in (near_ref, far_ref):
        ref[pl.ds((entry + 1) * HALO, rest), :] = jnp.zeros((rest, breadth), jnp.float32)


def spread_kernel(section_hbm, owner_hbm, local_hbm, spread_ref, section_ref, owner_ref, local_ref, sems):
    pairs = ((section_hbm, section_ref), (owner_hbm, owner_ref), (local_hbm, local_ref))
    copies = [pltpu.make_async_copy(here, there, sems.at[k]) for k, (here, there) in enumerate(pairs)]
    for copy in copies:
        copy.start()
    for copy in copies:
        copy.wait()
    tiles, stride, _ = spread_ref.shape
    reach_rows = section_ref.shape[0]
    reach = (owner_ref[...] * stride + local_ref[...]).astype(jnp.float32)
    parts = [reach[:, start:start + LANES] for start in range(0, reach.shape[1], LANES)]
    parts.append(jnp.zeros((stride - reach_rows - len(parts), LANES), jnp.float32))
    payload = jnp.concatenate([section_ref[...], *parts], axis=0)
    for tile in range(tiles):
        spread_ref[tile] = payload


def prepare_kernel(head_ref, soil_ref, after_ref, *refs):
    del after_ref
    groups = len(refs)
    held, across, _ = head_ref.shape
    span = across // groups
    own, flip, _ = position()

    def rows_of(target):
        return pl.ds(pl.multiple_of(span_at(flip, groups, target) * span, span), span)

    for step, block_ref in enumerate(refs):
        rows = rows_of(own ^ step)
        for layer in range(held):
            block_ref[0, layer] = head_ref[layer, rows, :]
            block_ref[1, layer] = soil_ref[layer, rows, :].astype(jnp.float32)


class Rows:
    def __init__(self, layers, breadth):
        self.layers, self.breadth, self.per_row = layers, breadth, breadth // LANES

    def get(self, ref, row):
        spot = pl.ds(row * self.layers, self.layers)
        return jnp.concatenate([ref[part, spot, :] for part in range(self.per_row)], axis=1)

    def put(self, ref, row, value):
        spot = pl.ds(row * self.layers, self.layers)
        for part in range(self.per_row):
            ref[part, spot, :] = value[:, part * LANES:(part + 1) * LANES]

    def put_layer(self, ref, layer, row, value):
        for part in range(self.per_row):
            spot = pl.ds(row * self.layers + layer, value.shape[0], stride=self.layers)
            ref[part, spot, :] = value[:, part * LANES:(part + 1) * LANES]

    def east(self, field):
        return pltpu.roll(field, self.breadth - 1, 1)

    def west(self, field):
        return pltpu.roll(field, 1, 1)

    def below(self, field):
        return pltpu.roll(field, self.layers - 1, 0)

    def above(self, field):
        return pltpu.roll(field, 1, 0)


class Joined:
    def __init__(self, rows, own, full, first, last):
        self.rows, self.own, self.full, self.first, self.last = rows, own, full, first, last

    def holds(self, row):
        return self.first <= row < self.last

    def get(self, row):
        if self.holds(row):
            return self.rows.get(self.own, row - HALO)
        return self.rows.get(self.full, row)

    def put(self, row, value):
        self.rows.put(self.full, row, value)


def relax_row(rows, row, head, weights, wx_before, base, inverse):
    before, here, after = head
    wx, wy, wz = [field.get(row) for field in weights]
    total = base.get(row) + wx_before * before + wx * after
    total = total + wy * rows.east(here) + rows.west(wy * here)
    total = total + wz * rows.below(here) + rows.above(wz * here)
    return total * inverse.get(row), wx


def river_row(rows, ref, row, top):
    parts = [
        jnp.broadcast_to(ref[pl.ds(row * rows.per_row + part, 1), :], (rows.layers, LANES))
        for part in range(rows.per_row)
    ]
    return jnp.where(top, jnp.concatenate(parts, axis=1), 0.0)


class Faces:
    def __init__(self, rows, land, lands):
        self.rows, self.lands = rows, lands
        lx_ref, ly_ref, lz_ref = lands
        count = land.shape[0]
        level = lax.broadcasted_iota(jnp.int32, (rows.layers, rows.breadth), 0)
        self.not_bottom = level < rows.layers - 1
        not_last = lax.broadcasted_iota(jnp.int32, land.shape, 1) < rows.breadth - 1
        lx_ref[pl.ds(0, count - 1), :] = 2.0 * LATERAL * land[:count - 1] * land[1:]
        ly_ref[...] = jnp.where(not_last, 2.0 * LATERAL * land * rows.east(land), 0.0)
        lz_ref[...] = 2.0 * VERTICAL * land * land

    def conduct(self, ks, alpha, head):
        return ks * jnp.exp(alpha * jnp.minimum(head, 0.0))

    def face(self, land, here, there):
        return land * (here * there) * reciprocal(here + there)

    def between_rows(self, row, here, there):
        return self.face(self.lands[0][pl.ds(row, 1), :], here, there)

    def in_row(self, row, here):
        rows = self.rows
        wy = self.face(self.lands[1][pl.ds(row, 1), :], here, rows.east(here))
        wz = self.face(self.lands[2][pl.ds(row, 1), :], here, rows.below(here))
        wz = jnp.where(self.not_bottom, wz, 0.0)
        wz_above = rows.above(wz)
        return wy, wz, wy + rows.west(wy) + wz + wz_above, GRAVITY * (wz_above - wz)


def lane_tables(refs, layers):
    lane = lax.broadcasted_iota(jnp.int32, (layers, LANES), 1)
    tables = []
    for ref in refs:
        table = jnp.zeros((layers, LANES), jnp.float32)
        for kind in range(ref.shape[0]):
            table = jnp.where(lane == kind, ref[kind], table)
        tables.append(table)
    return tables


def look_up(rows, table, soil):
    parts = [
        jnp.take_along_axis(table, soil[:, part * LANES:(part + 1) * LANES], axis=1, mode="promise_in_bounds")
        for part in range(rows.per_row)
    ]
    return jnp.concatenate(parts, axis=1)


def stage_kernel(ks_ref, alpha_ref, store_ref, land_ref, diag_ref, rhs_ref, *refs):
    groups = lax.axis_size("layer")
    own, _, _ = position()
    block_refs, refs = refs[:groups], refs[groups:]
    first_out, ks_out, alpha_out, store_out = refs[:4]
    fields = [refs[4 + 5 * picard:9 + 5 * picard] for picard in range(ITERS)]
    head_outs = refs[4 + 5 * ITERS:4 + 5 * ITERS + HALO]
    soil_sc, *lands = refs[4 + 5 * ITERS + HALO:]
    _, held, span, breadth = block_refs[0].shape
    layers = groups * held
    rows = Rows(layers, breadth)
    faces = Faces(rows, own_land(land_ref, span), lands)
    top = lax.broadcasted_iota(jnp.int32, (layers, breadth), 0) == 0

    for step, block_ref in enumerate(block_refs):
        for held_layer in range(held):
            layer = (own ^ step) * held + held_layer
            rows.put_layer(first_out, layer, 0, block_ref[0, held_layer])
            rows.put_layer(soil_sc, layer, 0, block_ref[1, held_layer])
    tables = lane_tables((ks_ref, alpha_ref, store_ref), layers)
    for row in range(span):
        soil = rows.get(soil_sc, row).astype(jnp.int32)
        for table, out in zip(tables, (ks_out, alpha_out, store_out)):
            rows.put(out, row, look_up(rows, table, soil))

    now, begin, stop, done = first_out, 0, span, 0
    for wx_out, wy_out, wz_out, inv_out, base_out in fields:
        before = None
        for row in range(begin, stop):
            here = faces.conduct(rows.get(ks_out, row), rows.get(alpha_out, row), rows.get(now, row))
            wy, wz, diagonal, gravity = faces.in_row(row, here)
            rows.put(wy_out, row, wy)
            rows.put(wz_out, row, wz)
            store = rows.get(store_out, row)
            sums = store + diagonal, store * rows.get(first_out, row) + gravity
            if row > begin:
                wx = faces.between_rows(row - 1, before[0], here)
                rows.put(wx_out, row - 1, wx)
                diagonal, base = before[1]
                if row - 1 > begin:
                    diagonal = reciprocal(diagonal + before[2] + wx + river_row(rows, diag_ref, row - 1, top))
                    base = base + river_row(rows, rhs_ref, row - 1, top)
                rows.put(inv_out, row - 1, diagonal)
                rows.put(base_out, row - 1, base)
            else:
                wx = None
            before = here, sums, wx
        rows.put(inv_out, stop - 1, before[1][0])
        rows.put(base_out, stop - 1, before[1][1])
        weights = [Joined(rows, None, ref, HALO, HALO) for ref in (wx_out, wy_out, wz_out)]
        base, inverse = [Joined(rows, None, ref, HALO, HALO) for ref in (base_out, inv_out)]
        for _ in range(SWEEPS):
            begin, stop = begin + 1, stop - 1
            head = rows.get(now, begin - 1), rows.get(now, begin)
            wx_before = rows.get(wx_out, begin - 1)
            for row in range(begin, stop):
                head = *head[-2:], rows.get(now, row + 1)
                value, wx_before = relax_row(rows, row, head, weights, wx_before, base, inverse)
                rows.put(head_outs[done], row, value)
            now = head_outs[done]
            done += 1


def flow_kernel(
    kst_ref, alphat_ref, storet_ref, land_ref, far_head_ref, far_ref, near_head_ref, near_ref, diag_ref, rhs_ref, *refs,
):
    groups = lax.axis_size("layer")
    own, _, number = position()
    end = (number == 0) | (number == groups - 1)
    far_partner = jnp.where(end, own, own ^ (groups - 1))
    tile, tiles = lax.axis_index("tile"), lax.axis_size("tile")
    outside = ((tile == 0) & (number == 0)) | ((tile == tiles - 1) & (number == groups - 1))
    first_ref, ks_ref, alpha_ref, store_ref = refs[:4]
    fields = [refs[4 + 5 * picard:9 + 5 * picard] for picard in range(ITERS)]
    staged_refs = refs[4 + 5 * ITERS:4 + 5 * ITERS + HALO]
    refs = refs[4 + 5 * ITERS + HALO:]
    head_refs, top_ref = refs[:groups], refs[groups]
    (
        first_sc, soil_sc, ks_sc, alpha_sc, store_sc, wx_sc, wy_sc, wz_sc, base_sc, inv_sc, ping_sc, pong_sc,
        land_sc, dtop_sc, rtop_sc, *lands,
    ) = refs[1 + groups:]
    held, span, breadth = head_refs[0].shape
    layers = groups * held
    window = span + 2 * HALO
    last_own = HALO + span
    rows = Rows(layers, breadth)
    side = HALO * rows.per_row

    land_sc[pl.ds(HALO, span), :] = own_land(land_ref, span)
    dtop_sc[pl.ds(side, span * rows.per_row), :] = diag_ref[...]
    rtop_sc[pl.ds(side, span * rows.per_row), :] = rhs_ref[...]

    def put_halo(refs, partner, water, row):
        def entry(ref, number):
            return ref[pl.ds(number * HALO, HALO), :]

        head, rest = refs
        for count in range(layers):
            layer = (partner ^ (count // held)) * held + count % held
            rows.put_layer(first_sc, layer, row, entry(head, count))
            rows.put_layer(soil_sc, layer, row, entry(rest, count))
        land_sc[pl.ds(row, HALO), :] = jnp.where(water, 0.0, entry(rest, layers))
        for count, top_sc in ((layers + 1, dtop_sc), (layers + 2, rtop_sc)):
            value = entry(rest, count)
            for part in range(rows.per_row):
                spot = pl.ds(row * rows.per_row + part, HALO, stride=rows.per_row)
                top_sc[spot, :] = value[:, part * LANES:(part + 1) * LANES]

    far = (far_head_ref, far_ref), far_partner, outside
    near = (near_head_ref, near_ref), own ^ 1, False
    for odd, above, below in ((0, far, near), (1, near, far)):
        @pl.when(lax.rem(number, 2) == odd)
        def _(above=above, below=below):
            put_halo(*above, 0)
            put_halo(*below, last_own)

    faces = Faces(rows, land_sc[...], lands)
    tables = lane_tables((kst_ref, alphat_ref, storet_ref), layers)
    for row in [*range(HALO), *range(last_own, window)]:
        soil = rows.get(soil_sc, row).astype(jnp.int32)
        for table, ref in zip(tables, (ks_sc, alpha_sc, store_sc)):
            rows.put(ref, row, look_up(rows, table, soil))

    first, ks, alpha, store = [
        Joined(rows, held_ref, full, HALO, last_own)
        for held_ref, full in ((first_ref, first_sc), (ks_ref, ks_sc), (alpha_ref, alpha_sc), (store_ref, store_sc))
    ]
    top = lax.broadcasted_iota(jnp.int32, (layers, breadth), 0) == 0

    now, begin, stop, done = first, 0, window, 0
    for wx_ref, wy_ref, wz_ref, inv_ref, base_ref in fields:
        low, high = HALO + done, last_own - done
        wx_of = Joined(rows, wx_ref, wx_sc, low, high - 1)
        wy_of, wz_of = Joined(rows, wy_ref, wy_sc, low, high), Joined(rows, wz_ref, wz_sc, low, high)
        inverse, base = [
            Joined(rows, held_ref, full, low + 1, high - 1) for held_ref, full in ((inv_ref, inv_sc), (base_ref, base_sc))
        ]
        here_before, wx_before, sums_before = None, None, None
        for row in range(begin, stop):
            at_end = row in (low, high - 1)
            here, sums = None, None
            if not wy_of.holds(row) or at_end:
                here = faces.conduct(ks.get(row), alpha.get(row), now.get(row))
            if at_end:
                sums = rows.get(inv_ref, row - HALO), rows.get(base_ref, row - HALO)
            elif not wy_of.holds(row) and begin < row < stop - 1:
                wy, wz, diagonal, gravity = faces.in_row(row, here)
                wy_of.put(row, wy)
                wz_of.put(row, wz)
                sums = store.get(row) + diagonal, store.get(row) * first.get(row) + gravity
            if row > begin:
                if wx_of.holds(row - 1):
                    wx = wx_of.get(row - 1)
                else:
                    wx = faces.between_rows(row - 1, here_before, here)
                    wx_of.put(row - 1, wx)
                if sums_before is not None:
                    diagonal = sums_before[0] + wx_before + wx + river_row(rows, dtop_sc, row - 1, top)
                    inverse.put(row - 1, reciprocal(diagonal))
                    base.put(row - 1, sums_before[1] + river_row(rows, rtop_sc, row - 1, top))
                wx_before = wx
            here_before, sums_before = here, sums
        for _ in range(SWEEPS):
            begin, stop = begin + 1, stop - 1
            later = Joined(rows, staged_refs[done], (ping_sc, pong_sc)[done % 2], HALO + done + 1, last_own - done - 1)
            done += 1
            for row in range(begin, stop):
                if not later.holds(row):
                    head = now.get(row - 1), now.get(row), now.get(row + 1)
                    value, _ = relax_row(rows, row, head, (wx_of, wy_of, wz_of), wx_of.get(row - 1), base, inverse)
                    later.put(row, value)
            now = later
    for row in range(now.first, now.last):
        now.put(row, now.get(row))
    for part in range(rows.per_row):
        lanes = pl.ds(part * LANES, LANES)
        top_ref[:, lanes] = now.full[part, pl.ds(HALO * layers, span, stride=layers), :]
        for step, head_ref in enumerate(head_refs):
            for held_layer in range(held):
                layer = (own ^ step) * held + held_layer
                head_ref[held_layer, :, lanes] = now.full[part, pl.ds(HALO * layers + layer, span, stride=layers), :]


def inflow_kernel(reach_rows, stride, cells_ref, bed_ref, slot_section_ref, reach_ref, *refs):
    groups = lax.axis_size("layer")
    own_layer, flip, _ = position()
    top_refs = refs[:groups]
    out_ref, block_sc, lane_sc, found_sc, turned_sc = refs[groups:]
    span, breadth = top_refs[0].shape
    per_row = breadth // LANES
    blocks = groups * span * per_row
    slots = cells_ref.shape[0]
    quarter = LANES // groups
    packed = slots // groups
    for step, top_ref in enumerate(top_refs):
        number = span_at(flip, groups, own_layer ^ step)
        for part in range(per_row):
            spot = pl.ds(number * span * per_row + part, span, stride=per_row)
            turned_sc[spot, :] = top_ref[:, part * LANES:(part + 1) * LANES]

    own = lax.broadcasted_iota(jnp.int32, (packed, LANES), 1) // quarter

    def pack(ref):
        result = None
        for number in range(groups):
            shift = lax.rem((number + groups - own_layer) * quarter, LANES)
            moved = pltpu.roll(ref[pl.ds(number * packed, packed), :], shift, 1)
            result = moved if result is None else jnp.where(own == number, moved, result)
        return result

    cells = pack(cells_ref)
    block, lane = split_cells(cells, 0, breadth, LANES)
    block_sc[...] = block
    lane_sc[...] = lane
    table = jnp.concatenate(bf16_pieces(turned_sc[...].T, 2), axis=0)
    names = names_of(blocks)
    index = lax.broadcasted_iota(jnp.int32, (8, LANES), 0).astype(jnp.float32)
    for pair in range(0, packed, 2):
        hots = jnp.concatenate(
            [jnp.concatenate(one_hot(row_copies(block_sc, 0, row), names), axis=0) for row in (pair, pair + 1)], axis=1
        )
        found = lax.dot_general(
            table, hots, (((1,), (0,)), ((), ())), preferred_element_type=jnp.float32
        )
        found = found[:LANES] + found[LANES:]
        for row in (pair, pair + 1):
            lanes = jnp.broadcast_to(lane_sc[pl.ds(row, 1), :], (8, LANES))
            mine = found[:, (row - pair) * LANES:(row - pair + 1) * LANES]
            total = jnp.zeros((8, LANES), jnp.float32)
            for start in range(0, LANES, 8):
                total = total + jnp.where(lanes == index + float(start), mine[start:start + 8], 0.0)
            found_sc[pl.ds(row, 1), :] = jnp.sum(total, axis=0, keepdims=True)
    slot_in = jnp.where(cells >= 0, pack(bed_ref) * (found_sc[...] - pack(slot_section_ref)), 0.0)
    spread = jnp.concatenate(
        [slot_in if number == 0 else pltpu.roll(slot_in, LANES - number * quarter, 1) for number in range(groups)],
        axis=0,
    )
    in_quarter = lax.broadcasted_iota(jnp.int32, spread.shape, 1) < quarter
    pieces = bf16_pieces(jnp.where(in_quarter, spread, 0.0), 3)
    fold = reach_rows // groups
    index = lax.broadcasted_iota(jnp.int32, (out_ref.shape[0], slots), 0)
    index = index // fold * stride + lax.rem(index, fold)
    result = None
    for number in range(groups):
        name = (index + number * fold).astype(jnp.float32)
        put = jnp.where(name == reach_ref[...], 1.0, 0.0).astype(jnp.bfloat16)
        total = jnp.zeros(out_ref.shape, jnp.float32)
        for piece in pieces:
            total = total + lax.dot_general(
                put, piece, (((1,), (0,)), ((), ())), preferred_element_type=jnp.float32
            )
        result = total if result is None else result + pltpu.roll(total, number * quarter, 1)
    out_ref[...] = result


def sum_kernel(terms_ref, inflow_ref):
    total = terms_ref[0]
    for tile in range(1, terms_ref.shape[0]):
        total = total + terms_ref[tile]
    fold, quarter = total.shape[0], inflow_ref.shape[1]
    for number in range(inflow_ref.shape[0] // fold):
        lanes = slice(number * quarter, (number + 1) * quarter)
        inflow_ref[pl.ds(number * fold, fold), :] = total[:, lanes]


def head_kernel(*refs):
    groups = lax.axis_size("layer")
    back_refs, (head_hbm, sems) = refs[:groups], refs[groups:]
    _, span, _ = back_refs[0].shape
    own, flip, _ = position()
    copies = []
    for step, back_ref in enumerate(back_refs):
        rows = pl.ds(pl.multiple_of(span_at(flip, groups, own ^ step) * span, span), span)
        copies.append(pltpu.make_async_copy(back_ref, head_hbm.at[:, rows, :], sems.at[step]))
        copies[-1].start()
    for copy in copies:
        copy.wait()


def call(kernel, out_shape, in_specs, scratch, micros, vmem=VMEM_LIMIT, out_specs=None):
    single = not isinstance(out_shape, (tuple, list))
    return pl.pallas_call(
        kernel,
        out_shape=out_shape,
        in_specs=in_specs,
        out_specs=out_specs or (in_vmem if single else tuple(in_vmem for _ in out_shape)),
        scratch_shapes=scratch,
        compiler_params=pltpu.CompilerParams(vmem_limit_bytes=vmem),
        cost_estimate=pl.CostEstimate(flops=int(micros * 1.15e9), bytes_accessed=0, transcendentals=0),
    )


def on_device(
    head_start,
    soil_class,
    land_mask,
    ks_table,
    alpha_table,
    store_table,
    section,
    cross_owner,
    cross_local,
    node_cell,
    bed_cond,
):
    held, across, breadth = head_start.shape
    reach_rows, node_count = section.shape
    tiles = lax.axis_size("tile")
    groups = lax.axis_size("layer")
    layers = held * groups
    span = across // groups
    per_row = breadth // LANES
    blocks = span * per_row
    near = [(i, i ^ 1) for i in range(groups)]
    far = []
    for upper in range(tiles):
        far += [(upper * groups + i, upper * groups + (i ^ (groups - 1))) for i in range(1, groups - 1)]
        if upper + 1 < tiles:
            index = groups - 1 if upper % 2 == 0 else 0
            one, two = upper * groups + index, (upper + 1) * groups + index
            far += [(one, two), (two, one)]
    far += [(0, 0)]
    last = tiles * groups - (1 if tiles % 2 == 1 else groups)
    far += [(last, last)]

    cells = node_cell[0]
    bed = bed_cond[0]
    slots = cells.shape[0]

    def exchange(parts):
        received = [parts[0]]
        for step in range(1, groups):
            received.append(lax.ppermute(parts[step], "layer", [(i, i ^ step) for i in range(groups)]))
        return received

    stride = reach_rows + 8
    spread = call(
        spread_kernel, jax.ShapeDtypeStruct((tiles, stride, node_count), jnp.float32), [in_hbm] * 3,
        [
            pltpu.VMEM(section.shape, jnp.float32),
            pltpu.VMEM(cross_owner.shape, jnp.int32),
            pltpu.VMEM(cross_owner.shape, jnp.int32),
            pltpu.SemaphoreType.DMA((3,)),
        ],
        1, VMEM_MOST,
    )(section, cross_owner, cross_local)
    whole_section = lax.all_to_all(spread, "tile", 0, 0).reshape(tiles * stride, node_count)
    own_blocks = call(
        prepare_kernel,
        (jax.ShapeDtypeStruct((2, held, span, breadth), jnp.float32),) * groups,
        [in_vmem] * 2 + [in_hbm], [], 0.5,
    )(head_start, soil_class, spread)
    received = exchange(own_blocks)

    node_scratch = pltpu.VMEM((slots, LANES), jnp.float32)
    riv_shape = jax.ShapeDtypeStruct((blocks, LANES), jnp.float32)
    node_field = jax.ShapeDtypeStruct((slots, LANES), jnp.float32)
    groups_of_cells = span * breadth // BLOCK
    early = call(
        functools.partial(early_kernel, breadth, span),
        (node_field,) * 4 + (jax.ShapeDtypeStruct((groups_of_cells, LANES), jnp.float32),), [in_vmem] * 2, [], 2.5,
    )(cells, bed)
    diag, rhs, slot_section, reach = call(
        functools.partial(river_kernel, stride),
        (riv_shape, riv_shape, node_field, jax.ShapeDtypeStruct((1, slots), jnp.float32)),
        [in_vmem] * 7, [node_scratch] * 2 + [pltpu.VMEM((groups_of_cells, LANES), jnp.float32)], 6,
    )(bed, whole_section, *early)
    edges = (
        jax.ShapeDtypeStruct((layers * HALO, breadth), jnp.float32),
        jax.ShapeDtypeStruct((-(-(layers + 3) * HALO // 8) * 8, breadth), jnp.float32),
    )
    edge_parts = call(
        edge_kernel, edges * 2, [in_vmem] * (3 + groups), [], 0.1,
    )(land_mask, diag, rhs, *received)
    far_halo = [lax.ppermute(part, FLAT, far) for part in edge_parts[2:]]
    near_halo = [lax.ppermute(part, "layer", near) for part in edge_parts[:2]]

    window = span + 2 * HALO
    own_field = jax.ShapeDtypeStruct((per_row, span * layers, LANES), jnp.float32)
    field = pltpu.VMEM((per_row, window * layers, LANES), jnp.float32)
    staged = call(
        stage_kernel, (own_field,) * (4 + 5 * ITERS + HALO), [in_smem] * 3 + [in_vmem] * (3 + groups),
        [pltpu.VMEM(own_field.shape, jnp.float32)] + [pltpu.VMEM((span, breadth), jnp.float32)] * 3,
        4,
    )(ks_table, alpha_table, store_table, land_mask, diag, rhs, *received)
    head_shape = jax.ShapeDtypeStruct((held, span, breadth), jnp.float32)
    *heads, top = call(
        flow_kernel,
        (head_shape,) * groups + (jax.ShapeDtypeStruct((span, breadth), jnp.float32),),
        [in_smem] * 3 + [in_vmem] * (7 + len(staged)),
        [field] * 12
        + [pltpu.VMEM((window, breadth), jnp.float32)]
        + [pltpu.VMEM((window * per_row, LANES), jnp.float32)] * 2
        + [pltpu.VMEM((window, breadth), jnp.float32)] * 3,
        3,
    )(ks_table, alpha_table, store_table, land_mask, *far_halo, *near_halo, diag, rhs, *staged)
    tops = exchange([top] * groups)
    backs = exchange(heads)

    fold = reach_rows // groups
    packed = pltpu.VMEM((slots // groups, LANES), jnp.float32)
    partial = call(
        functools.partial(inflow_kernel, reach_rows, stride),
        jax.ShapeDtypeStruct((tiles * fold, node_count), jnp.float32),
        [in_vmem] * (4 + groups),
        [packed] * 3 + [pltpu.VMEM((across * per_row, LANES), jnp.float32)],
        3,
    )(cells, bed, slot_section, reach, *tops)
    partial, *backs[:-1] = lax.optimization_barrier((partial, *backs[:-1]))
    terms = lax.all_to_all(partial.reshape(tiles, fold, node_count), "tile", 0, 0)
    head = call(
        head_kernel, jax.ShapeDtypeStruct(head_start.shape, jnp.float32), [in_vmem] * groups,
        [pltpu.SemaphoreType.DMA((groups,))], 0.7, out_specs=in_hbm,
    )(*backs)
    inflow_shape = jax.ShapeDtypeStruct((reach_rows, node_count // groups), jnp.float32)
    return head, call(sum_kernel, inflow_shape, [in_vmem], [], 0.1)(terms)


def solution(mesh):
    placed = (
        P("layer", "tile", None),
        P("layer", "tile", None),
        P("tile", None),
        P(),
        P(),
        P(),
        P("tile", None),
        P("tile", None),
        P("tile", None),
        P("tile", None, None),
        P("tile", None, None),
    )
    return jax.shard_map(
        on_device,
        mesh=mesh,
        in_specs=placed,
        out_specs=(P("layer", "tile", None), P("tile", "layer")),
        check_vma=False,
    )
```

```python
import functools

import jax
import jax.numpy as jnp
from jax import lax
from jax.experimental import pallas as pl
from jax.experimental.pallas import tpu as pltpu
from jax.sharding import PartitionSpec as P

ITERS = 2
SWEEPS = 3

LATERAL = 1.0
VERTICAL = 2.0
GRAVITY = 1.0

HALO = ITERS * SWEEPS
BLOCK = 64
LANES = 128
VMEM_LIMIT = 32 * 1024 * 1024
VMEM_MOST = 60 * 1024 * 1024
FLAT = ("tile", "layer")

in_vmem = pl.BlockSpec(memory_space=pltpu.VMEM)
in_hbm = pl.BlockSpec(memory_space=pltpu.HBM)
in_smem = pl.BlockSpec(memory_space=pltpu.SMEM)


def bf16_pieces(value, count):
    pieces = []
    for _ in range(count):
        piece = value.astype(jnp.bfloat16)
        pieces.append(piece)
        value = value - piece.astype(jnp.float32)
    return pieces


def reciprocal(value):
    guess = pl.reciprocal(value, approx=True)
    return guess * (2.0 - value * guess)


def names_of(size):
    index = lax.broadcasted_iota(jnp.int32, (16, LANES), 0)
    return [(index + start).astype(jnp.float32).astype(jnp.bfloat16) for start in range(0, size, 16)]


def one_hot(row, names):
    one = jnp.ones((16, LANES), jnp.bfloat16)
    zero = jnp.zeros((16, LANES), jnp.bfloat16)
    return [jnp.maximum(one - jnp.abs(row - name), zero) for name in names]


def row_copies(ref, first, place):
    rows = ref[pl.ds(pl.multiple_of(first + place // 8 * 8, 8), 8), :]
    return jnp.broadcast_to(rows[place % 8:place % 8 + 1, :], (16, LANES)).astype(jnp.bfloat16)


def position():
    tile, layer = lax.axis_index("tile"), lax.axis_index("layer")
    groups = lax.axis_size("layer")
    flip = lax.rem(tile, 2)
    return layer, flip, jnp.where(flip == 1, groups - 1 - layer, layer)


def own_land(land_ref, span):
    _, _, number = position()
    return land_ref[pl.ds(pl.multiple_of(number * span, span), span), :].astype(jnp.float32)


def span_at(flip, groups, layer):
    return jnp.where(flip == 1, groups - 1 - layer, layer)


def split_cells(cells, first_row, breadth, width):
    local = cells - first_row * breadth
    shift = width.bit_length() - 1
    block = jnp.where(cells < 0, -1, local >> shift)
    return block.astype(jnp.float32), (local & (width - 1)).astype(jnp.float32)


GROUP = 64


def scatter_sum(group, blocks, block_ref, spot_ref, value_refs):
    block_names, spot_names = names_of(blocks), names_of(BLOCK)
    total = None
    for start in range(0, GROUP, GROUP // 2):
        left, right = [], []
        for place in range(start, start + GROUP // 2):
            left.append(jnp.concatenate(one_hot(row_copies(block_ref, group * GROUP, place), block_names), axis=0))
            hot = one_hot(row_copies(spot_ref, group * GROUP, place), spot_names)
            values = [row_copies(ref, group * GROUP, place) for ref in value_refs]
            right.append(jnp.concatenate([tile * value for value in values for tile in hot], axis=0))
        part = lax.dot_general(
            jnp.concatenate(left, axis=1),
            jnp.concatenate(right, axis=1),
            (((1,), (1,)), ((), ())),
            preferred_element_type=jnp.float32,
        )
        total = part if total is None else total + part
    return total


def scatter_range(first, last, blocks, block_ref, spot_ref, value_refs):
    def step(group, total):
        return total + scatter_sum(group, blocks, block_ref, spot_ref, value_refs)

    return lax.fori_loop(first, last, step, jnp.zeros((blocks, BLOCK * len(value_refs)), jnp.float32))


def early_groups(slots):
    return slots // GROUP * 3 // 4


def early_kernel(breadth, span, cells_ref, bed_ref, block_ref, spot_ref, high_ref, low_ref, early_ref):
    _, _, number = position()
    block_ref[...], spot_ref[...] = split_cells(cells_ref[...], number * span, breadth, BLOCK)
    high, low = bf16_pieces(bed_ref[...], 2)
    high_ref[...] = high.astype(jnp.float32)
    low_ref[...] = low.astype(jnp.float32)
    early_ref[...] = scatter_range(
        0, early_groups(cells_ref.shape[0]), early_ref.shape[0], block_ref, spot_ref, (high_ref, low_ref)
    )


def river_kernel(
    stride, bed_ref, section_ref, block_ref, spot_ref, dhigh_ref, dlow_ref, early_ref,
    diag_ref, rhs_ref, slot_section_ref, reach_ref, rhigh_sc, rlow_sc, sum_sc,
):
    rows = section_ref.shape[0]
    slots = reach_ref.shape[1]
    first = (lax.axis_index("tile") + 1) * stride - 8
    own_rows = section_ref[pl.ds(pl.multiple_of(first, 8), 8), :]
    reach = jnp.concatenate([own_rows[k:k + 1, :] for k in range(slots // LANES)], axis=1)
    reach_ref[...] = reach
    index = lax.broadcasted_iota(jnp.int32, (rows, slots), 0).astype(jnp.float32)
    pick = jnp.where(index == reach, 1.0, 0.0).astype(jnp.bfloat16)
    picked = jnp.zeros(slot_section_ref.shape, jnp.float32)
    for piece in bf16_pieces(section_ref[...], 3):
        picked = picked + lax.dot_general(
            pick, piece, (((0,), (0,)), ((), ())), preferred_element_type=jnp.float32
        )
    slot_section_ref[...] = picked
    high, low = bf16_pieces(bed_ref[...] * picked, 2)
    rhigh_sc[...] = high.astype(jnp.float32)
    rlow_sc[...] = low.astype(jnp.float32)

    share = LANES // BLOCK
    blocks = share * diag_ref.shape[0]
    middle = early_groups(slots)
    rhs_only = scatter_range(0, middle, blocks, block_ref, spot_ref, (rhigh_sc, rlow_sc))
    both = scatter_range(
        middle, slots // GROUP, blocks, block_ref, spot_ref, (dhigh_ref, dlow_ref, rhigh_sc, rlow_sc)
    )
    low_half = lax.broadcasted_iota(jnp.int32, diag_ref.shape, 1) < BLOCK
    for part, ref in ((both[:, :LANES] + early_ref[...], diag_ref), (both[:, LANES:] + rhs_only, rhs_ref)):
        sum_sc[...] = part + pltpu.roll(part, BLOCK, 1)
        ref[...] = jnp.where(
            low_half, sum_sc[pl.ds(0, blocks // share, stride=share), :], sum_sc[pl.ds(1, blocks // share, stride=share), :]
        )


def edge_kernel(land_ref, diag_ref, rhs_ref, *refs):
    block_refs, (near_ref, far_ref) = refs[:-2], refs[-2:]
    _, held, span, breadth = block_refs[0].shape
    _, _, number = position()
    odd = lax.rem(number, 2) == 1
    per_row = breadth // LANES

    def put_edges(entry, top, bottom, lanes=slice(None)):
        near_ref[pl.ds(entry * HALO, HALO), lanes] = jnp.where(odd, top, bottom)
        far_ref[pl.ds(entry * HALO, HALO), lanes] = jnp.where(odd, bottom, top)

    entry = 0
    for kind in range(2):
        for block_ref in block_refs:
            for held_layer in range(held):
                put_edges(entry, block_ref[kind, held_layer, :HALO, :], block_ref[kind, held_layer, span - HALO:, :])
                entry += 1
    land = own_land(land_ref, span)
    put_edges(entry, land[:HALO], land[span - HALO:])
    for ref in (diag_ref, rhs_ref):
        entry += 1
        for part in range(per_row):
            top = ref[pl.ds(part, HALO, stride=per_row), :]
            bottom = ref[pl.ds((span - HALO) * per_row + part, HALO, stride=per_row), :]
            put_edges(entry, top, bottom, slice(part * LANES, (part + 1) * LANES))
    rest = near_ref.shape[0] - (entry + 1) * HALO
    for ref in (near_ref, far_ref):
        ref[pl.ds((entry + 1) * HALO, rest), :] = jnp.zeros((rest, breadth), jnp.float32)


def spread_kernel(section_hbm, owner_hbm, local_hbm, spread_ref, section_ref, owner_ref, local_ref, sems):
    pairs = ((section_hbm, section_ref), (owner_hbm, owner_ref), (local_hbm, local_ref))
    copies = [pltpu.make_async_copy(here, there, sems.at[k]) for k, (here, there) in enumerate(pairs)]
    for copy in copies:
        copy.start()
    for copy in copies:
        copy.wait()
    tiles, stride, _ = spread_ref.shape
    reach_rows = section_ref.shape[0]
    reach = (owner_ref[...] * stride + local_ref[...]).astype(jnp.float32)
    parts = [reach[:, start:start + LANES] for start in range(0, reach.shape[1], LANES)]
    parts.append(jnp.zeros((stride - reach_rows - len(parts), LANES), jnp.float32))
    payload = jnp.concatenate([section_ref[...], *parts], axis=0)
    for tile in range(tiles):
        spread_ref[tile] = payload


def prepare_kernel(head_ref, soil_ref, after_ref, *refs):
    del after_ref
    groups = len(refs)
    held, across, _ = head_ref.shape
    span = across // groups
    own, flip, _ = position()

    def rows_of(target):
        return pl.ds(pl.multiple_of(span_at(flip, groups, target) * span, span), span)

    for step, block_ref in enumerate(refs):
        rows = rows_of(own ^ step)
        for layer in range(held):
            block_ref[0, layer] = head_ref[layer, rows, :]
            block_ref[1, layer] = soil_ref[layer, rows, :].astype(jnp.float32)


class Rows:
    def __init__(self, layers, breadth):
        self.layers, self.breadth, self.per_row = layers, breadth, breadth // LANES

    def get(self, ref, row):
        spot = pl.ds(row * self.layers, self.layers)
        return jnp.concatenate([ref[part, spot, :] for part in range(self.per_row)], axis=1)

    def put(self, ref, row, value):
        spot = pl.ds(row * self.layers, self.layers)
        for part in range(self.per_row):
            ref[part, spot, :] = value[:, part * LANES:(part + 1) * LANES]

    def put_layer(self, ref, layer, row, value):
        for part in range(self.per_row):
            spot = pl.ds(row * self.layers + layer, value.shape[0], stride=self.layers)
            ref[part, spot, :] = value[:, part * LANES:(part + 1) * LANES]

    def east(self, field):
        return pltpu.roll(field, self.breadth - 1, 1)

    def west(self, field):
        return pltpu.roll(field, 1, 1)

    def below(self, field):
        return pltpu.roll(field, self.layers - 1, 0)

    def above(self, field):
        return pltpu.roll(field, 1, 0)


class Joined:
    def __init__(self, rows, own, full, first, last):
        self.rows, self.own, self.full, self.first, self.last = rows, own, full, first, last

    def holds(self, row):
        return self.first <= row < self.last

    def get(self, row):
        if self.holds(row):
            return self.rows.get(self.own, row - HALO)
        return self.rows.get(self.full, row)

    def put(self, row, value):
        self.rows.put(self.full, row, value)


def relax_row(rows, row, head, weights, wx_before, base, inverse):
    before, here, after = head
    wx, wy, wz = [field.get(row) for field in weights]
    total = base.get(row) + wx_before * before + wx * after
    total = total + wy * rows.east(here) + rows.west(wy * here)
    total = total + wz * rows.below(here) + rows.above(wz * here)
    return total * inverse.get(row), wx


def river_row(rows, ref, row, top):
    parts = [
        jnp.broadcast_to(ref[pl.ds(row * rows.per_row + part, 1), :], (rows.layers, LANES))
        for part in range(rows.per_row)
    ]
    return jnp.where(top, jnp.concatenate(parts, axis=1), 0.0)


class Faces:
    def __init__(self, rows, land, lands):
        self.rows, self.lands = rows, lands
        lx_ref, ly_ref, lz_ref = lands
        count = land.shape[0]
        level = lax.broadcasted_iota(jnp.int32, (rows.layers, rows.breadth), 0)
        self.not_bottom = level < rows.layers - 1
        not_last = lax.broadcasted_iota(jnp.int32, land.shape, 1) < rows.breadth - 1
        lx_ref[pl.ds(0, count - 1), :] = 2.0 * LATERAL * land[:count - 1] * land[1:]
        ly_ref[...] = jnp.where(not_last, 2.0 * LATERAL * land * rows.east(land), 0.0)
        lz_ref[...] = 2.0 * VERTICAL * land * land

    def conduct(self, ks, alpha, head):
        return ks * jnp.exp(alpha * jnp.minimum(head, 0.0))

    def face(self, land, here, there):
        return land * (here * there) * reciprocal(here + there)

    def between_rows(self, row, here, there):
        return self.face(self.lands[0][pl.ds(row, 1), :], here, there)

    def in_row(self, row, here):
        rows = self.rows
        wy = self.face(self.lands[1][pl.ds(row, 1), :], here, rows.east(here))
        wz = self.face(self.lands[2][pl.ds(row, 1), :], here, rows.below(here))
        wz = jnp.where(self.not_bottom, wz, 0.0)
        wz_above = rows.above(wz)
        return wy, wz, wy + rows.west(wy) + wz + wz_above, GRAVITY * (wz_above - wz)


def lane_tables(refs, layers):
    lane = lax.broadcasted_iota(jnp.int32, (layers, LANES), 1)
    tables = []
    for ref in refs:
        table = jnp.zeros((layers, LANES), jnp.float32)
        for kind in range(ref.shape[0]):
            table = jnp.where(lane == kind, ref[kind], table)
        tables.append(table)
    return tables


def look_up(rows, table, soil):
    parts = [
        jnp.take_along_axis(table, soil[:, part * LANES:(part + 1) * LANES], axis=1, mode="promise_in_bounds")
        for part in range(rows.per_row)
    ]
    return jnp.concatenate(parts, axis=1)


def stage_kernel(ks_ref, alpha_ref, store_ref, land_ref, diag_ref, rhs_ref, *refs):
    groups = lax.axis_size("layer")
    own, _, _ = position()
    block_refs, refs = refs[:groups], refs[groups:]
    first_out, ks_out, alpha_out, store_out = refs[:4]
    fields = [refs[4 + 5 * picard:9 + 5 * picard] for picard in range(ITERS)]
    head_outs = refs[4 + 5 * ITERS:4 + 5 * ITERS + HALO]
    soil_sc, *lands = refs[4 + 5 * ITERS + HALO:]
    _, held, span, breadth = block_refs[0].shape
    layers = groups * held
    rows = Rows(layers, breadth)
    faces = Faces(rows, own_land(land_ref, span), lands)
    top = lax.broadcasted_iota(jnp.int32, (layers, breadth), 0) == 0

    for step, block_ref in enumerate(block_refs):
        for held_layer in range(held):
            layer = (own ^ step) * held + held_layer
            rows.put_layer(first_out, layer, 0, block_ref[0, held_layer])
            rows.put_layer(soil_sc, layer, 0, block_ref[1, held_layer])
    tables = lane_tables((ks_ref, alpha_ref, store_ref), layers)
    for row in range(span):
        soil = rows.get(soil_sc, row).astype(jnp.int32)
        for table, out in zip(tables, (ks_out, alpha_out, store_out)):
            rows.put(out, row, look_up(rows, table, soil))

    now, begin, stop, done = first_out, 0, span, 0
    for wx_out, wy_out, wz_out, inv_out, base_out in fields:
        before = None
        for row in range(begin, stop):
            here = faces.conduct(rows.get(ks_out, row), rows.get(alpha_out, row), rows.get(now, row))
            wy, wz, diagonal, gravity = faces.in_row(row, here)
            rows.put(wy_out, row, wy)
            rows.put(wz_out, row, wz)
            store = rows.get(store_out, row)
            sums = store + diagonal, store * rows.get(first_out, row) + gravity
            if row > begin:
                wx = faces.between_rows(row - 1, before[0], here)
                rows.put(wx_out, row - 1, wx)
                diagonal, base = before[1]
                if row - 1 > begin:
                    diagonal = reciprocal(diagonal + before[2] + wx + river_row(rows, diag_ref, row - 1, top))
                    base = base + river_row(rows, rhs_ref, row - 1, top)
                rows.put(inv_out, row - 1, diagonal)
                rows.put(base_out, row - 1, base)
            else:
                wx = None
            before = here, sums, wx
        rows.put(inv_out, stop - 1, before[1][0])
        rows.put(base_out, stop - 1, before[1][1])
        weights = [Joined(rows, None, ref, HALO, HALO) for ref in (wx_out, wy_out, wz_out)]
        base, inverse = [Joined(rows, None, ref, HALO, HALO) for ref in (base_out, inv_out)]
        for _ in range(SWEEPS):
            begin, stop = begin + 1, stop - 1
            head = rows.get(now, begin - 1), rows.get(now, begin)
            wx_before = rows.get(wx_out, begin - 1)
            for row in range(begin, stop):
                head = *head[-2:], rows.get(now, row + 1)
                value, wx_before = relax_row(rows, row, head, weights, wx_before, base, inverse)
                rows.put(head_outs[done], row, value)
            now = head_outs[done]
            done += 1


def flow_kernel(kst_ref, alphat_ref, storet_ref, land_ref, far_ref, near_ref, diag_ref, rhs_ref, *refs):
    groups = lax.axis_size("layer")
    own, _, number = position()
    end = (number == 0) | (number == groups - 1)
    far_partner = jnp.where(end, own, own ^ (groups - 1))
    tile, tiles = lax.axis_index("tile"), lax.axis_size("tile")
    outside = ((tile == 0) & (number == 0)) | ((tile == tiles - 1) & (number == groups - 1))
    first_ref, ks_ref, alpha_ref, store_ref = refs[:4]
    fields = [refs[4 + 5 * picard:9 + 5 * picard] for picard in range(ITERS)]
    staged_refs = refs[4 + 5 * ITERS:4 + 5 * ITERS + HALO]
    refs = refs[4 + 5 * ITERS + HALO:]
    head_refs, top_ref = refs[:groups], refs[groups]
    (
        first_sc, soil_sc, ks_sc, alpha_sc, store_sc, wx_sc, wy_sc, wz_sc, base_sc, inv_sc, ping_sc, pong_sc,
        land_sc, dtop_sc, rtop_sc, *lands,
    ) = refs[1 + groups:]
    held, span, breadth = head_refs[0].shape
    layers = groups * held
    window = span + 2 * HALO
    last_own = HALO + span
    rows = Rows(layers, breadth)
    side = HALO * rows.per_row

    land_sc[pl.ds(HALO, span), :] = own_land(land_ref, span)
    dtop_sc[pl.ds(side, span * rows.per_row), :] = diag_ref[...]
    rtop_sc[pl.ds(side, span * rows.per_row), :] = rhs_ref[...]

    def put_halo(ref, partner, row):
        def entry(number):
            return ref[pl.ds(number * HALO, HALO), :]

        for count in range(layers):
            layer = (partner ^ (count // held)) * held + count % held
            rows.put_layer(first_sc, layer, row, entry(count))
            rows.put_layer(soil_sc, layer, row, entry(layers + count))
        water = outside if ref is far_ref else False
        land_sc[pl.ds(row, HALO), :] = jnp.where(water, 0.0, entry(2 * layers))
        for count, top_sc in ((2 * layers + 1, dtop_sc), (2 * layers + 2, rtop_sc)):
            value = entry(count)
            for part in range(rows.per_row):
                spot = pl.ds(row * rows.per_row + part, HALO, stride=rows.per_row)
                top_sc[spot, :] = value[:, part * LANES:(part + 1) * LANES]

    for odd, above_ref, below_ref in ((0, far_ref, near_ref), (1, near_ref, far_ref)):
        @pl.when(lax.rem(number, 2) == odd)
        def _(above_ref=above_ref, below_ref=below_ref):
            for ref, row in ((above_ref, 0), (below_ref, last_own)):
                put_halo(ref, own ^ 1 if ref is near_ref else far_partner, row)

    faces = Faces(rows, land_sc[...], lands)
    tables = lane_tables((kst_ref, alphat_ref, storet_ref), layers)
    for row in [*range(HALO), *range(last_own, window)]:
        soil = rows.get(soil_sc, row).astype(jnp.int32)
        for table, ref in zip(tables, (ks_sc, alpha_sc, store_sc)):
            rows.put(ref, row, look_up(rows, table, soil))

    first, ks, alpha, store = [
        Joined(rows, held_ref, full, HALO, last_own)
        for held_ref, full in ((first_ref, first_sc), (ks_ref, ks_sc), (alpha_ref, alpha_sc), (store_ref, store_sc))
    ]
    top = lax.broadcasted_iota(jnp.int32, (layers, breadth), 0) == 0

    now, begin, stop, done = first, 0, window, 0
    for wx_ref, wy_ref, wz_ref, inv_ref, base_ref in fields:
        low, high = HALO + done, last_own - done
        wx_of = Joined(rows, wx_ref, wx_sc, low, high - 1)
        wy_of, wz_of = Joined(rows, wy_ref, wy_sc, low, high), Joined(rows, wz_ref, wz_sc, low, high)
        inverse, base = [
            Joined(rows, held_ref, full, low + 1, high - 1) for held_ref, full in ((inv_ref, inv_sc), (base_ref, base_sc))
        ]
        here_before, wx_before, sums_before = None, None, None
        for row in range(begin, stop):
            at_end = row in (low, high - 1)
            here, sums = None, None
            if not wy_of.holds(row) or at_end:
                here = faces.conduct(ks.get(row), alpha.get(row), now.get(row))
            if at_end:
                sums = rows.get(inv_ref, row - HALO), rows.get(base_ref, row - HALO)
            elif not wy_of.holds(row) and begin < row < stop - 1:
                wy, wz, diagonal, gravity = faces.in_row(row, here)
                wy_of.put(row, wy)
                wz_of.put(row, wz)
                sums = store.get(row) + diagonal, store.get(row) * first.get(row) + gravity
            if row > begin:
                if wx_of.holds(row - 1):
                    wx = wx_of.get(row - 1)
                else:
                    wx = faces.between_rows(row - 1, here_before, here)
                    wx_of.put(row - 1, wx)
                if sums_before is not None:
                    diagonal = sums_before[0] + wx_before + wx + river_row(rows, dtop_sc, row - 1, top)
                    inverse.put(row - 1, reciprocal(diagonal))
                    base.put(row - 1, sums_before[1] + river_row(rows, rtop_sc, row - 1, top))
                wx_before = wx
            here_before, sums_before = here, sums
        for _ in range(SWEEPS):
            begin, stop = begin + 1, stop - 1
            later = Joined(rows, staged_refs[done], (ping_sc, pong_sc)[done % 2], HALO + done + 1, last_own - done - 1)
            done += 1
            for row in range(begin, stop):
                if not later.holds(row):
                    head = now.get(row - 1), now.get(row), now.get(row + 1)
                    value, _ = relax_row(rows, row, head, (wx_of, wy_of, wz_of), wx_of.get(row - 1), base, inverse)
                    later.put(row, value)
            now = later
    for row in range(now.first, now.last):
        now.put(row, now.get(row))
    for part in range(rows.per_row):
        lanes = pl.ds(part * LANES, LANES)
        top_ref[:, lanes] = now.full[part, pl.ds(HALO * layers, span, stride=layers), :]
        for step, head_ref in enumerate(head_refs):
            for held_layer in range(held):
                layer = (own ^ step) * held + held_layer
                head_ref[held_layer, :, lanes] = now.full[part, pl.ds(HALO * layers + layer, span, stride=layers), :]


def inflow_kernel(reach_rows, stride, cells_ref, bed_ref, slot_section_ref, reach_ref, *refs):
    groups = lax.axis_size("layer")
    own_layer, flip, _ = position()
    top_refs = refs[:groups]
    out_ref, block_sc, lane_sc, found_sc, turned_sc = refs[groups:]
    span, breadth = top_refs[0].shape
    per_row = breadth // LANES
    blocks = groups * span * per_row
    slots = cells_ref.shape[0]
    quarter = LANES // groups
    packed = slots // groups
    for step, top_ref in enumerate(top_refs):
        number = span_at(flip, groups, own_layer ^ step)
        for part in range(per_row):
            spot = pl.ds(number * span * per_row + part, span, stride=per_row)
            turned_sc[spot, :] = top_ref[:, part * LANES:(part + 1) * LANES]

    own = lax.broadcasted_iota(jnp.int32, (packed, LANES), 1) // quarter

    def pack(ref):
        result = None
        for number in range(groups):
            shift = lax.rem((number + groups - own_layer) * quarter, LANES)
            moved = pltpu.roll(ref[pl.ds(number * packed, packed), :], shift, 1)
            result = moved if result is None else jnp.where(own == number, moved, result)
        return result

    cells = pack(cells_ref)
    block, lane = split_cells(cells, 0, breadth, LANES)
    block_sc[...] = block
    lane_sc[...] = lane
    table = jnp.concatenate(bf16_pieces(turned_sc[...].T, 2), axis=0)
    names = names_of(blocks)
    index = lax.broadcasted_iota(jnp.int32, (8, LANES), 0).astype(jnp.float32)
    for pair in range(0, packed, 2):
        hots = jnp.concatenate(
            [jnp.concatenate(one_hot(row_copies(block_sc, 0, row), names), axis=0) for row in (pair, pair + 1)], axis=1
        )
        found = lax.dot_general(
            table, hots, (((1,), (0,)), ((), ())), preferred_element_type=jnp.float32
        )
        found = found[:LANES] + found[LANES:]
        for row in (pair, pair + 1):
            lanes = jnp.broadcast_to(lane_sc[pl.ds(row, 1), :], (8, LANES))
            mine = found[:, (row - pair) * LANES:(row - pair + 1) * LANES]
            total = jnp.zeros((8, LANES), jnp.float32)
            for start in range(0, LANES, 8):
                total = total + jnp.where(lanes == index + float(start), mine[start:start + 8], 0.0)
            found_sc[pl.ds(row, 1), :] = jnp.sum(total, axis=0, keepdims=True)
    slot_in = jnp.where(cells >= 0, pack(bed_ref) * (found_sc[...] - pack(slot_section_ref)), 0.0)
    spread = jnp.concatenate(
        [slot_in if number == 0 else pltpu.roll(slot_in, LANES - number * quarter, 1) for number in range(groups)],
        axis=0,
    )
    in_quarter = lax.broadcasted_iota(jnp.int32, spread.shape, 1) < quarter
    pieces = bf16_pieces(jnp.where(in_quarter, spread, 0.0), 3)
    fold = reach_rows // groups
    index = lax.broadcasted_iota(jnp.int32, (out_ref.shape[0], slots), 0)
    index = index // fold * stride + lax.rem(index, fold)
    result = None
    for number in range(groups):
        name = (index + number * fold).astype(jnp.float32)
        put = jnp.where(name == reach_ref[...], 1.0, 0.0).astype(jnp.bfloat16)
        total = jnp.zeros(out_ref.shape, jnp.float32)
        for piece in pieces:
            total = total + lax.dot_general(
                put, piece, (((1,), (0,)), ((), ())), preferred_element_type=jnp.float32
            )
        result = total if result is None else result + pltpu.roll(total, number * quarter, 1)
    out_ref[...] = result


def sum_kernel(terms_ref, inflow_ref):
    total = terms_ref[0]
    for tile in range(1, terms_ref.shape[0]):
        total = total + terms_ref[tile]
    fold, quarter = total.shape[0], inflow_ref.shape[1]
    for number in range(inflow_ref.shape[0] // fold):
        lanes = slice(number * quarter, (number + 1) * quarter)
        inflow_ref[pl.ds(number * fold, fold), :] = total[:, lanes]


def head_kernel(*refs):
    groups = lax.axis_size("layer")
    back_refs, (head_hbm, sems) = refs[:groups], refs[groups:]
    _, span, _ = back_refs[0].shape
    own, flip, _ = position()
    copies = []
    for step, back_ref in enumerate(back_refs):
        rows = pl.ds(pl.multiple_of(span_at(flip, groups, own ^ step) * span, span), span)
        copies.append(pltpu.make_async_copy(back_ref, head_hbm.at[:, rows, :], sems.at[step]))
        copies[-1].start()
    for copy in copies:
        copy.wait()


def call(kernel, out_shape, in_specs, scratch, micros, vmem=VMEM_LIMIT, out_specs=None):
    single = not isinstance(out_shape, (tuple, list))
    return pl.pallas_call(
        kernel,
        out_shape=out_shape,
        in_specs=in_specs,
        out_specs=out_specs or (in_vmem if single else tuple(in_vmem for _ in out_shape)),
        scratch_shapes=scratch,
        compiler_params=pltpu.CompilerParams(vmem_limit_bytes=vmem),
        cost_estimate=pl.CostEstimate(flops=int(micros * 1.15e9), bytes_accessed=0, transcendentals=0),
    )


def on_device(
    head_start,
    soil_class,
    land_mask,
    ks_table,
    alpha_table,
    store_table,
    section,
    cross_owner,
    cross_local,
    node_cell,
    bed_cond,
):
    held, across, breadth = head_start.shape
    reach_rows, node_count = section.shape
    tiles = lax.axis_size("tile")
    groups = lax.axis_size("layer")
    layers = held * groups
    span = across // groups
    per_row = breadth // LANES
    blocks = span * per_row
    near = [(i, i ^ 1) for i in range(groups)]
    far = []
    for upper in range(tiles):
        far += [(upper * groups + i, upper * groups + (i ^ (groups - 1))) for i in range(1, groups - 1)]
        if upper + 1 < tiles:
            index = groups - 1 if upper % 2 == 0 else 0
            one, two = upper * groups + index, (upper + 1) * groups + index
            far += [(one, two), (two, one)]
    far += [(0, 0)]
    last = tiles * groups - (1 if tiles % 2 == 1 else groups)
    far += [(last, last)]

    cells = node_cell[0]
    bed = bed_cond[0]
    slots = cells.shape[0]

    def exchange(parts):
        received = [parts[0]]
        for step in range(1, groups):
            received.append(lax.ppermute(parts[step], "layer", [(i, i ^ step) for i in range(groups)]))
        return received

    stride = reach_rows + 8
    spread = call(
        spread_kernel, jax.ShapeDtypeStruct((tiles, stride, node_count), jnp.float32), [in_hbm] * 3,
        [
            pltpu.VMEM(section.shape, jnp.float32),
            pltpu.VMEM(cross_owner.shape, jnp.int32),
            pltpu.VMEM(cross_owner.shape, jnp.int32),
            pltpu.SemaphoreType.DMA((3,)),
        ],
        1, VMEM_MOST,
    )(section, cross_owner, cross_local)
    whole_section = lax.all_to_all(spread, "tile", 0, 0).reshape(tiles * stride, node_count)
    own_blocks = call(
        prepare_kernel,
        (jax.ShapeDtypeStruct((2, held, span, breadth), jnp.float32),) * groups,
        [in_vmem] * 2 + [in_hbm], [], 0.5,
    )(head_start, soil_class, spread)
    received = exchange(own_blocks)

    node_scratch = pltpu.VMEM((slots, LANES), jnp.float32)
    riv_shape = jax.ShapeDtypeStruct((blocks, LANES), jnp.float32)
    node_field = jax.ShapeDtypeStruct((slots, LANES), jnp.float32)
    groups_of_cells = span * breadth // BLOCK
    early = call(
        functools.partial(early_kernel, breadth, span),
        (node_field,) * 4 + (jax.ShapeDtypeStruct((groups_of_cells, LANES), jnp.float32),), [in_vmem] * 2, [], 2.5,
    )(cells, bed)
    diag, rhs, slot_section, reach = call(
        functools.partial(river_kernel, stride),
        (riv_shape, riv_shape, node_field, jax.ShapeDtypeStruct((1, slots), jnp.float32)),
        [in_vmem] * 7, [node_scratch] * 2 + [pltpu.VMEM((groups_of_cells, LANES), jnp.float32)], 6,
    )(bed, whole_section, *early)
    edges = jax.ShapeDtypeStruct((-(-(2 * layers + 3) * HALO // 8) * 8, breadth), jnp.float32)
    near_edge, far_edge = call(
        edge_kernel, (edges, edges), [in_vmem] * (3 + groups), [], 0.1,
    )(land_mask, diag, rhs, *received)
    far_halo = lax.ppermute(far_edge, FLAT, far)
    near_halo = lax.ppermute(near_edge, "layer", near)

    window = span + 2 * HALO
    own_field = jax.ShapeDtypeStruct((per_row, span * layers, LANES), jnp.float32)
    field = pltpu.VMEM((per_row, window * layers, LANES), jnp.float32)
    staged = call(
        stage_kernel, (own_field,) * (4 + 5 * ITERS + HALO), [in_smem] * 3 + [in_vmem] * (3 + groups),
        [pltpu.VMEM(own_field.shape, jnp.float32)] + [pltpu.VMEM((span, breadth), jnp.float32)] * 3,
        4,
    )(ks_table, alpha_table, store_table, land_mask, diag, rhs, *received)
    head_shape = jax.ShapeDtypeStruct((held, span, breadth), jnp.float32)
    *heads, top = call(
        flow_kernel,
        (head_shape,) * groups + (jax.ShapeDtypeStruct((span, breadth), jnp.float32),),
        [in_smem] * 3 + [in_vmem] * (5 + len(staged)),
        [field] * 12
        + [pltpu.VMEM((window, breadth), jnp.float32)]
        + [pltpu.VMEM((window * per_row, LANES), jnp.float32)] * 2
        + [pltpu.VMEM((window, breadth), jnp.float32)] * 3,
        3,
    )(ks_table, alpha_table, store_table, land_mask, far_halo, near_halo, diag, rhs, *staged)
    tops = exchange([top] * groups)
    backs = exchange(heads)

    fold = reach_rows // groups
    packed = pltpu.VMEM((slots // groups, LANES), jnp.float32)
    partial = call(
        functools.partial(inflow_kernel, reach_rows, stride),
        jax.ShapeDtypeStruct((tiles * fold, node_count), jnp.float32),
        [in_vmem] * (4 + groups),
        [packed] * 3 + [pltpu.VMEM((across * per_row, LANES), jnp.float32)],
        3,
    )(cells, bed, slot_section, reach, *tops)
    partial, *backs[:-1] = lax.optimization_barrier((partial, *backs[:-1]))
    terms = lax.all_to_all(partial.reshape(tiles, fold, node_count), "tile", 0, 0)
    head = call(
        head_kernel, jax.ShapeDtypeStruct(head_start.shape, jnp.float32), [in_vmem] * groups,
        [pltpu.SemaphoreType.DMA((groups,))], 0.7, out_specs=in_hbm,
    )(*backs)
    inflow_shape = jax.ShapeDtypeStruct((reach_rows, node_count // groups), jnp.float32)
    return head, call(sum_kernel, inflow_shape, [in_vmem], [], 0.1)(terms)


def solution(mesh):
    placed = (
        P("layer", "tile", None),
        P("layer", "tile", None),
        P("tile", None),
        P(),
        P(),
        P(),
        P("tile", None),
        P("tile", None),
        P("tile", None),
        P("tile", None, None),
        P("tile", None, None),
    )
    return jax.shard_map(
        on_device,
        mesh=mesh,
        in_specs=placed,
        out_specs=(P("layer", "tile", None), P("tile", "layer")),
        check_vma=False,
    )
```

```python
import functools

import jax
import jax.numpy as jnp
from jax import lax
from jax.experimental import pallas as pl
from jax.experimental.pallas import tpu as pltpu
from jax.sharding import PartitionSpec as P

ITERS = 2
SWEEPS = 3

LATERAL = 1.0
VERTICAL = 2.0
GRAVITY = 1.0

HALO = ITERS * SWEEPS
BLOCK = 64
LANES = 128
VMEM_LIMIT = 32 * 1024 * 1024
VMEM_MOST = 60 * 1024 * 1024
FLAT = ("tile", "layer")

in_vmem = pl.BlockSpec(memory_space=pltpu.VMEM)
in_hbm = pl.BlockSpec(memory_space=pltpu.HBM)
in_smem = pl.BlockSpec(memory_space=pltpu.SMEM)


def bf16_pieces(value, count):
    pieces = []
    for _ in range(count):
        piece = value.astype(jnp.bfloat16)
        pieces.append(piece)
        value = value - piece.astype(jnp.float32)
    return pieces


def reciprocal(value):
    guess = pl.reciprocal(value, approx=True)
    return guess * (2.0 - value * guess)


def names_of(size):
    index = lax.broadcasted_iota(jnp.int32, (16, LANES), 0)
    return [(index + start).astype(jnp.float32).astype(jnp.bfloat16) for start in range(0, size, 16)]


def one_hot(row, names):
    one = jnp.ones((16, LANES), jnp.bfloat16)
    zero = jnp.zeros((16, LANES), jnp.bfloat16)
    return [jnp.maximum(one - jnp.abs(row - name), zero) for name in names]


def row_copies(ref, first, place):
    rows = ref[pl.ds(pl.multiple_of(first + place // 8 * 8, 8), 8), :]
    return jnp.broadcast_to(rows[place % 8:place % 8 + 1, :], (16, LANES)).astype(jnp.bfloat16)


def position():
    tile, layer = lax.axis_index("tile"), lax.axis_index("layer")
    groups = lax.axis_size("layer")
    flip = lax.rem(tile, 2)
    return layer, flip, jnp.where(flip == 1, groups - 1 - layer, layer)


def own_land(land_ref, span):
    _, _, number = position()
    return land_ref[pl.ds(pl.multiple_of(number * span, span), span), :].astype(jnp.float32)


def span_at(flip, groups, layer):
    return jnp.where(flip == 1, groups - 1 - layer, layer)


def split_cells(cells, first_row, breadth, width):
    local = cells - first_row * breadth
    shift = width.bit_length() - 1
    block = jnp.where(cells < 0, -1, local >> shift)
    return block.astype(jnp.float32), (local & (width - 1)).astype(jnp.float32)


GROUP = 64


def scatter_sum(group, blocks, block_ref, spot_ref, value_refs):
    block_names, spot_names = names_of(blocks), names_of(BLOCK)
    total = None
    for start in range(0, GROUP, GROUP // 2):
        left, right = [], []
        for place in range(start, start + GROUP // 2):
            left.append(jnp.concatenate(one_hot(row_copies(block_ref, group * GROUP, place), block_names), axis=0))
            hot = one_hot(row_copies(spot_ref, group * GROUP, place), spot_names)
            values = [row_copies(ref, group * GROUP, place) for ref in value_refs]
            right.append(jnp.concatenate([tile * value for value in values for tile in hot], axis=0))
        part = lax.dot_general(
            jnp.concatenate(left, axis=1),
            jnp.concatenate(right, axis=1),
            (((1,), (1,)), ((), ())),
            preferred_element_type=jnp.float32,
        )
        total = part if total is None else total + part
    return total


def scatter_range(first, last, blocks, block_ref, spot_ref, value_refs):
    def step(group, total):
        return total + scatter_sum(group, blocks, block_ref, spot_ref, value_refs)

    return lax.fori_loop(first, last, step, jnp.zeros((blocks, BLOCK * len(value_refs)), jnp.float32))


def early_kernel(breadth, span, cells_ref, bed_ref, block_ref, spot_ref, diag_ref, high_ref, low_ref, sum_sc):
    _, _, number = position()
    block_ref[...], spot_ref[...] = split_cells(cells_ref[...], number * span, breadth, BLOCK)
    high, low = bf16_pieces(bed_ref[...], 2)
    high_ref[...] = high.astype(jnp.float32)
    low_ref[...] = low.astype(jnp.float32)
    put_sums(diag_ref, sum_sc, block_ref, spot_ref, (high_ref, low_ref))


def put_sums(out_ref, sum_sc, block_ref, spot_ref, piece_refs):
    share = LANES // BLOCK
    blocks = share * out_ref.shape[0]
    part = scatter_range(0, block_ref.shape[0] // GROUP, blocks, block_ref, spot_ref, piece_refs)
    sum_sc[...] = part + pltpu.roll(part, BLOCK, 1)
    low_half = lax.broadcasted_iota(jnp.int32, out_ref.shape, 1) < BLOCK
    out_ref[...] = jnp.where(
        low_half, sum_sc[pl.ds(0, blocks // share, stride=share), :], sum_sc[pl.ds(1, blocks // share, stride=share), :]
    )


def river_kernel(
    stride, bed_ref, section_ref, block_ref, spot_ref, rhs_ref, slot_section_ref, reach_ref, rhigh_sc, rlow_sc, sum_sc,
):
    rows = section_ref.shape[0]
    slots = reach_ref.shape[1]
    first = (lax.axis_index("tile") + 1) * stride - 8
    own_rows = section_ref[pl.ds(pl.multiple_of(first, 8), 8), :]
    reach = jnp.concatenate([own_rows[k:k + 1, :] for k in range(slots // LANES)], axis=1)
    reach_ref[...] = reach
    index = lax.broadcasted_iota(jnp.int32, (rows, slots), 0).astype(jnp.float32)
    pick = jnp.where(index == reach, 1.0, 0.0).astype(jnp.bfloat16)
    picked = jnp.zeros(slot_section_ref.shape, jnp.float32)
    for piece in bf16_pieces(section_ref[...], 3):
        picked = picked + lax.dot_general(
            pick, piece, (((0,), (0,)), ((), ())), preferred_element_type=jnp.float32
        )
    slot_section_ref[...] = picked
    high, low = bf16_pieces(bed_ref[...] * picked, 2)
    rhigh_sc[...] = high.astype(jnp.float32)
    rlow_sc[...] = low.astype(jnp.float32)

    put_sums(rhs_ref, sum_sc, block_ref, spot_ref, (rhigh_sc, rlow_sc))


def edge_kernel(land_ref, diag_ref, rhs_ref, *refs):
    block_refs, (near_ref, far_ref) = refs[:-2], refs[-2:]
    _, held, span, breadth = block_refs[0].shape
    _, _, number = position()
    odd = lax.rem(number, 2) == 1
    per_row = breadth // LANES

    def put_edges(entry, top, bottom, lanes=slice(None)):
        near_ref[pl.ds(entry * HALO, HALO), lanes] = jnp.where(odd, top, bottom)
        far_ref[pl.ds(entry * HALO, HALO), lanes] = jnp.where(odd, bottom, top)

    entry = 0
    for kind in range(2):
        for block_ref in block_refs:
            for held_layer in range(held):
                put_edges(entry, block_ref[kind, held_layer, :HALO, :], block_ref[kind, held_layer, span - HALO:, :])
                entry += 1
    land = own_land(land_ref, span)
    put_edges(entry, land[:HALO], land[span - HALO:])
    for ref in (diag_ref, rhs_ref):
        entry += 1
        for part in range(per_row):
            top = ref[pl.ds(part, HALO, stride=per_row), :]
            bottom = ref[pl.ds((span - HALO) * per_row + part, HALO, stride=per_row), :]
            put_edges(entry, top, bottom, slice(part * LANES, (part + 1) * LANES))
    rest = near_ref.shape[0] - (entry + 1) * HALO
    for ref in (near_ref, far_ref):
        ref[pl.ds((entry + 1) * HALO, rest), :] = jnp.zeros((rest, breadth), jnp.float32)


def spread_kernel(section_hbm, owner_hbm, local_hbm, spread_ref, section_ref, owner_ref, local_ref, sems):
    pairs = ((section_hbm, section_ref), (owner_hbm, owner_ref), (local_hbm, local_ref))
    copies = [pltpu.make_async_copy(here, there, sems.at[k]) for k, (here, there) in enumerate(pairs)]
    for copy in copies:
        copy.start()
    for copy in copies:
        copy.wait()
    tiles, stride, _ = spread_ref.shape
    reach_rows = section_ref.shape[0]
    reach = (owner_ref[...] * stride + local_ref[...]).astype(jnp.float32)
    parts = [reach[:, start:start + LANES] for start in range(0, reach.shape[1], LANES)]
    parts.append(jnp.zeros((stride - reach_rows - len(parts), LANES), jnp.float32))
    payload = jnp.concatenate([section_ref[...], *parts], axis=0)
    for tile in range(tiles):
        spread_ref[tile] = payload


def prepare_kernel(head_ref, soil_ref, after_ref, *refs):
    del after_ref
    groups = len(refs)
    held, across, _ = head_ref.shape
    span = across // groups
    own, flip, _ = position()

    def rows_of(target):
        return pl.ds(pl.multiple_of(span_at(flip, groups, target) * span, span), span)

    for step, block_ref in enumerate(refs):
        rows = rows_of(own ^ step)
        for layer in range(held):
            block_ref[0, layer] = head_ref[layer, rows, :]
            block_ref[1, layer] = soil_ref[layer, rows, :].astype(jnp.float32)


class Rows:
    def __init__(self, layers, breadth):
        self.layers, self.breadth, self.per_row = layers, breadth, breadth // LANES

    def get(self, ref, row):
        spot = pl.ds(row * self.layers, self.layers)
        return jnp.concatenate([ref[part, spot, :] for part in range(self.per_row)], axis=1)

    def put(self, ref, row, value):
        spot = pl.ds(row * self.layers, self.layers)
        for part in range(self.per_row):
            ref[part, spot, :] = value[:, part * LANES:(part + 1) * LANES]

    def put_layer(self, ref, layer, row, value):
        for part in range(self.per_row):
            spot = pl.ds(row * self.layers + layer, value.shape[0], stride=self.layers)
            ref[part, spot, :] = value[:, part * LANES:(part + 1) * LANES]

    def east(self, field):
        return pltpu.roll(field, self.breadth - 1, 1)

    def west(self, field):
        return pltpu.roll(field, 1, 1)

    def below(self, field):
        return pltpu.roll(field, self.layers - 1, 0)

    def above(self, field):
        return pltpu.roll(field, 1, 0)


class Joined:
    def __init__(self, rows, own, full, first, last):
        self.rows, self.own, self.full, self.first, self.last = rows, own, full, first, last

    def holds(self, row):
        return self.first <= row < self.last

    def get(self, row):
        if self.holds(row):
            return self.rows.get(self.own, row - HALO)
        return self.rows.get(self.full, row)

    def put(self, row, value):
        self.rows.put(self.full, row, value)


def relax_row(rows, row, head, weights, wx_before, base, inverse):
    before, here, after = head
    wx, wy, wz = [field.get(row) for field in weights]
    total = base.get(row) + wx_before * before + wx * after
    total = total + wy * rows.east(here) + rows.west(wy * here)
    total = total + wz * rows.below(here) + rows.above(wz * here)
    return total * inverse.get(row), wx


def river_row(rows, ref, row, top):
    parts = [
        jnp.broadcast_to(ref[pl.ds(row * rows.per_row + part, 1), :], (rows.layers, LANES))
        for part in range(rows.per_row)
    ]
    return jnp.where(top, jnp.concatenate(parts, axis=1), 0.0)


class Faces:
    def __init__(self, rows, land, lands):
        self.rows, self.lands = rows, lands
        lx_ref, ly_ref, lz_ref = lands
        count = land.shape[0]
        level = lax.broadcasted_iota(jnp.int32, (rows.layers, rows.breadth), 0)
        self.not_bottom = level < rows.layers - 1
        not_last = lax.broadcasted_iota(jnp.int32, land.shape, 1) < rows.breadth - 1
        lx_ref[pl.ds(0, count - 1), :] = 2.0 * LATERAL * land[:count - 1] * land[1:]
        ly_ref[...] = jnp.where(not_last, 2.0 * LATERAL * land * rows.east(land), 0.0)
        lz_ref[...] = 2.0 * VERTICAL * land * land

    def conduct(self, ks, alpha, head):
        return ks * jnp.exp(alpha * jnp.minimum(head, 0.0))

    def face(self, land, here, there):
        return land * (here * there) * reciprocal(here + there)

    def between_rows(self, row, here, there):
        return self.face(self.lands[0][pl.ds(row, 1), :], here, there)

    def in_row(self, row, here):
        rows = self.rows
        wy = self.face(self.lands[1][pl.ds(row, 1), :], here, rows.east(here))
        wz = self.face(self.lands[2][pl.ds(row, 1), :], here, rows.below(here))
        wz = jnp.where(self.not_bottom, wz, 0.0)
        wz_above = rows.above(wz)
        return wy, wz, wy + rows.west(wy) + wz + wz_above, GRAVITY * (wz_above - wz)


def lane_tables(refs, layers):
    lane = lax.broadcasted_iota(jnp.int32, (layers, LANES), 1)
    tables = []
    for ref in refs:
        table = jnp.zeros((layers, LANES), jnp.float32)
        for kind in range(ref.shape[0]):
            table = jnp.where(lane == kind, ref[kind], table)
        tables.append(table)
    return tables


def look_up(rows, table, soil):
    parts = [
        jnp.take_along_axis(table, soil[:, part * LANES:(part + 1) * LANES], axis=1, mode="promise_in_bounds")
        for part in range(rows.per_row)
    ]
    return jnp.concatenate(parts, axis=1)


def stage_kernel(ks_ref, alpha_ref, store_ref, land_ref, diag_ref, rhs_ref, *refs):
    groups = lax.axis_size("layer")
    own, _, _ = position()
    block_refs, refs = refs[:groups], refs[groups:]
    first_out, ks_out, alpha_out, store_out = refs[:4]
    fields = [refs[4 + 5 * picard:9 + 5 * picard] for picard in range(ITERS)]
    head_outs = refs[4 + 5 * ITERS:4 + 5 * ITERS + HALO]
    soil_sc, *lands = refs[4 + 5 * ITERS + HALO:]
    _, held, span, breadth = block_refs[0].shape
    layers = groups * held
    rows = Rows(layers, breadth)
    faces = Faces(rows, own_land(land_ref, span), lands)
    top = lax.broadcasted_iota(jnp.int32, (layers, breadth), 0) == 0

    for step, block_ref in enumerate(block_refs):
        for held_layer in range(held):
            layer = (own ^ step) * held + held_layer
            rows.put_layer(first_out, layer, 0, block_ref[0, held_layer])
            rows.put_layer(soil_sc, layer, 0, block_ref[1, held_layer])
    tables = lane_tables((ks_ref, alpha_ref, store_ref), layers)
    for row in range(span):
        soil = rows.get(soil_sc, row).astype(jnp.int32)
        for table, out in zip(tables, (ks_out, alpha_out, store_out)):
            rows.put(out, row, look_up(rows, table, soil))

    now, begin, stop, done = first_out, 0, span, 0
    for wx_out, wy_out, wz_out, inv_out, base_out in fields:
        before = None
        for row in range(begin, stop):
            here = faces.conduct(rows.get(ks_out, row), rows.get(alpha_out, row), rows.get(now, row))
            wy, wz, diagonal, gravity = faces.in_row(row, here)
            rows.put(wy_out, row, wy)
            rows.put(wz_out, row, wz)
            store = rows.get(store_out, row)
            sums = store + diagonal, store * rows.get(first_out, row) + gravity
            if row > begin:
                wx = faces.between_rows(row - 1, before[0], here)
                rows.put(wx_out, row - 1, wx)
                diagonal, base = before[1]
                if row - 1 > begin:
                    diagonal = reciprocal(diagonal + before[2] + wx + river_row(rows, diag_ref, row - 1, top))
                    base = base + river_row(rows, rhs_ref, row - 1, top)
                rows.put(inv_out, row - 1, diagonal)
                rows.put(base_out, row - 1, base)
            else:
                wx = None
            before = here, sums, wx
        rows.put(inv_out, stop - 1, before[1][0])
        rows.put(base_out, stop - 1, before[1][1])
        weights = [Joined(rows, None, ref, HALO, HALO) for ref in (wx_out, wy_out, wz_out)]
        base, inverse = [Joined(rows, None, ref, HALO, HALO) for ref in (base_out, inv_out)]
        for _ in range(SWEEPS):
            begin, stop = begin + 1, stop - 1
            head = rows.get(now, begin - 1), rows.get(now, begin)
            wx_before = rows.get(wx_out, begin - 1)
            for row in range(begin, stop):
                head = *head[-2:], rows.get(now, row + 1)
                value, wx_before = relax_row(rows, row, head, weights, wx_before, base, inverse)
                rows.put(head_outs[done], row, value)
            now = head_outs[done]
            done += 1


def flow_kernel(kst_ref, alphat_ref, storet_ref, land_ref, far_ref, near_ref, diag_ref, rhs_ref, *refs):
    groups = lax.axis_size("layer")
    own, _, number = position()
    end = (number == 0) | (number == groups - 1)
    far_partner = jnp.where(end, own, own ^ (groups - 1))
    tile, tiles = lax.axis_index("tile"), lax.axis_size("tile")
    outside = ((tile == 0) & (number == 0)) | ((tile == tiles - 1) & (number == groups - 1))
    first_ref, ks_ref, alpha_ref, store_ref = refs[:4]
    fields = [refs[4 + 5 * picard:9 + 5 * picard] for picard in range(ITERS)]
    staged_refs = refs[4 + 5 * ITERS:4 + 5 * ITERS + HALO]
    refs = refs[4 + 5 * ITERS + HALO:]
    head_refs, top_ref = refs[:groups], refs[groups]
    (
        first_sc, soil_sc, ks_sc, alpha_sc, store_sc, wx_sc, wy_sc, wz_sc, base_sc, inv_sc, ping_sc, pong_sc,
        land_sc, dtop_sc, rtop_sc, *lands,
    ) = refs[1 + groups:]
    held, span, breadth = head_refs[0].shape
    layers = groups * held
    window = span + 2 * HALO
    last_own = HALO + span
    rows = Rows(layers, breadth)
    side = HALO * rows.per_row

    land_sc[pl.ds(HALO, span), :] = own_land(land_ref, span)
    dtop_sc[pl.ds(side, span * rows.per_row), :] = diag_ref[...]
    rtop_sc[pl.ds(side, span * rows.per_row), :] = rhs_ref[...]

    def put_halo(ref, partner, row):
        def entry(number):
            return ref[pl.ds(number * HALO, HALO), :]

        for count in range(layers):
            layer = (partner ^ (count // held)) * held + count % held
            rows.put_layer(first_sc, layer, row, entry(count))
            rows.put_layer(soil_sc, layer, row, entry(layers + count))
        water = outside if ref is far_ref else False
        land_sc[pl.ds(row, HALO), :] = jnp.where(water, 0.0, entry(2 * layers))
        for count, top_sc in ((2 * layers + 1, dtop_sc), (2 * layers + 2, rtop_sc)):
            value = entry(count)
            for part in range(rows.per_row):
                spot = pl.ds(row * rows.per_row + part, HALO, stride=rows.per_row)
                top_sc[spot, :] = value[:, part * LANES:(part + 1) * LANES]

    for odd, above_ref, below_ref in ((0, far_ref, near_ref), (1, near_ref, far_ref)):
        @pl.when(lax.rem(number, 2) == odd)
        def _(above_ref=above_ref, below_ref=below_ref):
            for ref, row in ((above_ref, 0), (below_ref, last_own)):
                put_halo(ref, own ^ 1 if ref is near_ref else far_partner, row)

    faces = Faces(rows, land_sc[...], lands)
    tables = lane_tables((kst_ref, alphat_ref, storet_ref), layers)
    for row in [*range(HALO), *range(last_own, window)]:
        soil = rows.get(soil_sc, row).astype(jnp.int32)
        for table, ref in zip(tables, (ks_sc, alpha_sc, store_sc)):
            rows.put(ref, row, look_up(rows, table, soil))

    first, ks, alpha, store = [
        Joined(rows, held_ref, full, HALO, last_own)
        for held_ref, full in ((first_ref, first_sc), (ks_ref, ks_sc), (alpha_ref, alpha_sc), (store_ref, store_sc))
    ]
    top = lax.broadcasted_iota(jnp.int32, (layers, breadth), 0) == 0

    now, begin, stop, done = first, 0, window, 0
    for wx_ref, wy_ref, wz_ref, inv_ref, base_ref in fields:
        low, high = HALO + done, last_own - done
        wx_of = Joined(rows, wx_ref, wx_sc, low, high - 1)
        wy_of, wz_of = Joined(rows, wy_ref, wy_sc, low, high), Joined(rows, wz_ref, wz_sc, low, high)
        inverse, base = [
            Joined(rows, held_ref, full, low + 1, high - 1) for held_ref, full in ((inv_ref, inv_sc), (base_ref, base_sc))
        ]
        here_before, wx_before, sums_before = None, None, None
        for row in range(begin, stop):
            at_end = row in (low, high - 1)
            here, sums = None, None
            if not wy_of.holds(row) or at_end:
                here = faces.conduct(ks.get(row), alpha.get(row), now.get(row))
            if at_end:
                sums = rows.get(inv_ref, row - HALO), rows.get(base_ref, row - HALO)
            elif not wy_of.holds(row) and begin < row < stop - 1:
                wy, wz, diagonal, gravity = faces.in_row(row, here)
                wy_of.put(row, wy)
                wz_of.put(row, wz)
                sums = store.get(row) + diagonal, store.get(row) * first.get(row) + gravity
            if row > begin:
                if wx_of.holds(row - 1):
                    wx = wx_of.get(row - 1)
                else:
                    wx = faces.between_rows(row - 1, here_before, here)
                    wx_of.put(row - 1, wx)
                if sums_before is not None:
                    diagonal = sums_before[0] + wx_before + wx + river_row(rows, dtop_sc, row - 1, top)
                    inverse.put(row - 1, reciprocal(diagonal))
                    base.put(row - 1, sums_before[1] + river_row(rows, rtop_sc, row - 1, top))
                wx_before = wx
            here_before, sums_before = here, sums
        for _ in range(SWEEPS):
            begin, stop = begin + 1, stop - 1
            later = Joined(rows, staged_refs[done], (ping_sc, pong_sc)[done % 2], HALO + done + 1, last_own - done - 1)
            done += 1
            for row in range(begin, stop):
                if not later.holds(row):
                    head = now.get(row - 1), now.get(row), now.get(row + 1)
                    value, _ = relax_row(rows, row, head, (wx_of, wy_of, wz_of), wx_of.get(row - 1), base, inverse)
                    later.put(row, value)
            now = later
    for row in range(now.first, now.last):
        now.put(row, now.get(row))
    for part in range(rows.per_row):
        lanes = pl.ds(part * LANES, LANES)
        top_ref[:, lanes] = now.full[part, pl.ds(HALO * layers, span, stride=layers), :]
        for step, head_ref in enumerate(head_refs):
            for held_layer in range(held):
                layer = (own ^ step) * held + held_layer
                head_ref[held_layer, :, lanes] = now.full[part, pl.ds(HALO * layers + layer, span, stride=layers), :]


def inflow_kernel(reach_rows, stride, cells_ref, bed_ref, slot_section_ref, reach_ref, *refs):
    groups = lax.axis_size("layer")
    own_layer, flip, _ = position()
    top_refs = refs[:groups]
    out_ref, block_sc, lane_sc, found_sc, turned_sc = refs[groups:]
    span, breadth = top_refs[0].shape
    per_row = breadth // LANES
    blocks = groups * span * per_row
    slots = cells_ref.shape[0]
    quarter = LANES // groups
    packed = slots // groups
    for step, top_ref in enumerate(top_refs):
        number = span_at(flip, groups, own_layer ^ step)
        for part in range(per_row):
            spot = pl.ds(number * span * per_row + part, span, stride=per_row)
            turned_sc[spot, :] = top_ref[:, part * LANES:(part + 1) * LANES]

    own = lax.broadcasted_iota(jnp.int32, (packed, LANES), 1) // quarter

    def pack(ref):
        result = None
        for number in range(groups):
            shift = lax.rem((number + groups - own_layer) * quarter, LANES)
            moved = pltpu.roll(ref[pl.ds(number * packed, packed), :], shift, 1)
            result = moved if result is None else jnp.where(own == number, moved, result)
        return result

    cells = pack(cells_ref)
    block, lane = split_cells(cells, 0, breadth, LANES)
    block_sc[...] = block
    lane_sc[...] = lane
    table = jnp.concatenate(bf16_pieces(turned_sc[...].T, 2), axis=0)
    names = names_of(blocks)
    index = lax.broadcasted_iota(jnp.int32, (8, LANES), 0).astype(jnp.float32)
    for pair in range(0, packed, 2):
        hots = jnp.concatenate(
            [jnp.concatenate(one_hot(row_copies(block_sc, 0, row), names), axis=0) for row in (pair, pair + 1)], axis=1
        )
        found = lax.dot_general(
            table, hots, (((1,), (0,)), ((), ())), preferred_element_type=jnp.float32
        )
        found = found[:LANES] + found[LANES:]
        for row in (pair, pair + 1):
            lanes = jnp.broadcast_to(lane_sc[pl.ds(row, 1), :], (8, LANES))
            mine = found[:, (row - pair) * LANES:(row - pair + 1) * LANES]
            total = jnp.zeros((8, LANES), jnp.float32)
            for start in range(0, LANES, 8):
                total = total + jnp.where(lanes == index + float(start), mine[start:start + 8], 0.0)
            found_sc[pl.ds(row, 1), :] = jnp.sum(total, axis=0, keepdims=True)
    slot_in = jnp.where(cells >= 0, pack(bed_ref) * (found_sc[...] - pack(slot_section_ref)), 0.0)
    spread = jnp.concatenate(
        [slot_in if number == 0 else pltpu.roll(slot_in, LANES - number * quarter, 1) for number in range(groups)],
        axis=0,
    )
    in_quarter = lax.broadcasted_iota(jnp.int32, spread.shape, 1) < quarter
    pieces = bf16_pieces(jnp.where(in_quarter, spread, 0.0), 3)
    fold = reach_rows // groups
    index = lax.broadcasted_iota(jnp.int32, (out_ref.shape[0], slots), 0)
    index = index // fold * stride + lax.rem(index, fold)
    result = None
    for number in range(groups):
        name = (index + number * fold).astype(jnp.float32)
        put = jnp.where(name == reach_ref[...], 1.0, 0.0).astype(jnp.bfloat16)
        total = jnp.zeros(out_ref.shape, jnp.float32)
        for piece in pieces:
            total = total + lax.dot_general(
                put, piece, (((1,), (0,)), ((), ())), preferred_element_type=jnp.float32
            )
        result = total if result is None else result + pltpu.roll(total, number * quarter, 1)
    out_ref[...] = result


def sum_kernel(terms_ref, inflow_ref):
    total = terms_ref[0]
    for tile in range(1, terms_ref.shape[0]):
        total = total + terms_ref[tile]
    fold, quarter = total.shape[0], inflow_ref.shape[1]
    for number in range(inflow_ref.shape[0] // fold):
        lanes = slice(number * quarter, (number + 1) * quarter)
        inflow_ref[pl.ds(number * fold, fold), :] = total[:, lanes]


def head_kernel(*refs):
    groups = lax.axis_size("layer")
    back_refs, (head_hbm, sems) = refs[:groups], refs[groups:]
    _, span, _ = back_refs[0].shape
    own, flip, _ = position()
    copies = []
    for step, back_ref in enumerate(back_refs):
        rows = pl.ds(pl.multiple_of(span_at(flip, groups, own ^ step) * span, span), span)
        copies.append(pltpu.make_async_copy(back_ref, head_hbm.at[:, rows, :], sems.at[step]))
        copies[-1].start()
    for copy in copies:
        copy.wait()


def call(kernel, out_shape, in_specs, scratch, micros, vmem=VMEM_LIMIT, out_specs=None):
    single = not isinstance(out_shape, (tuple, list))
    return pl.pallas_call(
        kernel,
        out_shape=out_shape,
        in_specs=in_specs,
        out_specs=out_specs or (in_vmem if single else tuple(in_vmem for _ in out_shape)),
        scratch_shapes=scratch,
        compiler_params=pltpu.CompilerParams(vmem_limit_bytes=vmem),
        cost_estimate=pl.CostEstimate(flops=int(micros * 1.15e9), bytes_accessed=0, transcendentals=0),
    )


def on_device(
    head_start,
    soil_class,
    land_mask,
    ks_table,
    alpha_table,
    store_table,
    section,
    cross_owner,
    cross_local,
    node_cell,
    bed_cond,
):
    held, across, breadth = head_start.shape
    reach_rows, node_count = section.shape
    tiles = lax.axis_size("tile")
    groups = lax.axis_size("layer")
    layers = held * groups
    span = across // groups
    per_row = breadth // LANES
    blocks = span * per_row
    near = [(i, i ^ 1) for i in range(groups)]
    far = []
    for upper in range(tiles):
        far += [(upper * groups + i, upper * groups + (i ^ (groups - 1))) for i in range(1, groups - 1)]
        if upper + 1 < tiles:
            index = groups - 1 if upper % 2 == 0 else 0
            one, two = upper * groups + index, (upper + 1) * groups + index
            far += [(one, two), (two, one)]
    far += [(0, 0)]
    last = tiles * groups - (1 if tiles % 2 == 1 else groups)
    far += [(last, last)]

    cells = node_cell[0]
    bed = bed_cond[0]
    slots = cells.shape[0]

    def exchange(parts):
        received = [parts[0]]
        for step in range(1, groups):
            received.append(lax.ppermute(parts[step], "layer", [(i, i ^ step) for i in range(groups)]))
        return received

    stride = reach_rows + 8
    spread = call(
        spread_kernel, jax.ShapeDtypeStruct((tiles, stride, node_count), jnp.float32), [in_hbm] * 3,
        [
            pltpu.VMEM(section.shape, jnp.float32),
            pltpu.VMEM(cross_owner.shape, jnp.int32),
            pltpu.VMEM(cross_owner.shape, jnp.int32),
            pltpu.SemaphoreType.DMA((3,)),
        ],
        1, VMEM_MOST,
    )(section, cross_owner, cross_local)
    whole_section = lax.all_to_all(spread, "tile", 0, 0).reshape(tiles * stride, node_count)
    own_blocks = call(
        prepare_kernel,
        (jax.ShapeDtypeStruct((2, held, span, breadth), jnp.float32),) * groups,
        [in_vmem] * 2 + [in_hbm], [], 0.5,
    )(head_start, soil_class, spread)
    received = exchange(own_blocks)

    node_scratch = pltpu.VMEM((slots, LANES), jnp.float32)
    riv_shape = jax.ShapeDtypeStruct((blocks, LANES), jnp.float32)
    node_field = jax.ShapeDtypeStruct((slots, LANES), jnp.float32)
    groups_of_cells = span * breadth // BLOCK
    sums = pltpu.VMEM((groups_of_cells, LANES), jnp.float32)
    block_number, spot, diag = call(
        functools.partial(early_kernel, breadth, span), (node_field, node_field, riv_shape), [in_vmem] * 2,
        [node_scratch] * 2 + [sums], 3,
    )(cells, bed)
    rhs, slot_section, reach = call(
        functools.partial(river_kernel, stride),
        (riv_shape, node_field, jax.ShapeDtypeStruct((1, slots), jnp.float32)),
        [in_vmem] * 4, [node_scratch] * 2 + [sums], 5,
    )(bed, whole_section, block_number, spot)
    edges = jax.ShapeDtypeStruct((-(-(2 * layers + 3) * HALO // 8) * 8, breadth), jnp.float32)
    near_edge, far_edge = call(
        edge_kernel, (edges, edges), [in_vmem] * (3 + groups), [], 0.1,
    )(land_mask, diag, rhs, *received)
    far_halo = lax.ppermute(far_edge, FLAT, far)
    near_halo = lax.ppermute(near_edge, "layer", near)

    window = span + 2 * HALO
    own_field = jax.ShapeDtypeStruct((per_row, span * layers, LANES), jnp.float32)
    field = pltpu.VMEM((per_row, window * layers, LANES), jnp.float32)
    staged = call(
        stage_kernel, (own_field,) * (4 + 5 * ITERS + HALO), [in_smem] * 3 + [in_vmem] * (3 + groups),
        [pltpu.VMEM(own_field.shape, jnp.float32)] + [pltpu.VMEM((span, breadth), jnp.float32)] * 3,
        4,
    )(ks_table, alpha_table, store_table, land_mask, diag, rhs, *received)
    head_shape = jax.ShapeDtypeStruct((held, span, breadth), jnp.float32)
    *heads, top = call(
        flow_kernel,
        (head_shape,) * groups + (jax.ShapeDtypeStruct((span, breadth), jnp.float32),),
        [in_smem] * 3 + [in_vmem] * (5 + len(staged)),
        [field] * 12
        + [pltpu.VMEM((window, breadth), jnp.float32)]
        + [pltpu.VMEM((window * per_row, LANES), jnp.float32)] * 2
        + [pltpu.VMEM((window, breadth), jnp.float32)] * 3,
        3,
    )(ks_table, alpha_table, store_table, land_mask, far_halo, near_halo, diag, rhs, *staged)
    tops = exchange([top] * groups)
    backs = exchange(heads)

    fold = reach_rows // groups
    packed = pltpu.VMEM((slots // groups, LANES), jnp.float32)
    partial = call(
        functools.partial(inflow_kernel, reach_rows, stride),
        jax.ShapeDtypeStruct((tiles * fold, node_count), jnp.float32),
        [in_vmem] * (4 + groups),
        [packed] * 3 + [pltpu.VMEM((across * per_row, LANES), jnp.float32)],
        3,
    )(cells, bed, slot_section, reach, *tops)
    partial, *backs[:-1] = lax.optimization_barrier((partial, *backs[:-1]))
    terms = lax.all_to_all(partial.reshape(tiles, fold, node_count), "tile", 0, 0)
    head = call(
        head_kernel, jax.ShapeDtypeStruct(head_start.shape, jnp.float32), [in_vmem] * groups,
        [pltpu.SemaphoreType.DMA((groups,))], 0.7, out_specs=in_hbm,
    )(*backs)
    inflow_shape = jax.ShapeDtypeStruct((reach_rows, node_count // groups), jnp.float32)
    return head, call(sum_kernel, inflow_shape, [in_vmem], [], 0.1)(terms)


def solution(mesh):
    placed = (
        P("layer", "tile", None),
        P("layer", "tile", None),
        P("tile", None),
        P(),
        P(),
        P(),
        P("tile", None),
        P("tile", None),
        P("tile", None),
        P("tile", None, None),
        P("tile", None, None),
    )
    return jax.shard_map(
        on_device,
        mesh=mesh,
        in_specs=placed,
        out_specs=(P("layer", "tile", None), P("tile", "layer")),
        check_vma=False,
    )
```

```python
import functools

import jax
import jax.numpy as jnp
from jax import lax
from jax.experimental import pallas as pl
from jax.experimental.pallas import tpu as pltpu
from jax.sharding import PartitionSpec as P

ITERS = 2
SWEEPS = 3

LATERAL = 1.0
VERTICAL = 2.0
GRAVITY = 1.0

HALO = ITERS * SWEEPS
BLOCK = 64
LANES = 128
VMEM_LIMIT = 32 * 1024 * 1024
VMEM_MOST = 60 * 1024 * 1024
FLAT = ("tile", "layer")

in_vmem = pl.BlockSpec(memory_space=pltpu.VMEM)
in_hbm = pl.BlockSpec(memory_space=pltpu.HBM)
in_smem = pl.BlockSpec(memory_space=pltpu.SMEM)


def bf16_pieces(value, count):
    pieces = []
    for _ in range(count):
        piece = value.astype(jnp.bfloat16)
        pieces.append(piece)
        value = value - piece.astype(jnp.float32)
    return pieces


def reciprocal(value):
    guess = pl.reciprocal(value, approx=True)
    return guess * (2.0 - value * guess)


def names_of(size):
    index = lax.broadcasted_iota(jnp.int32, (16, LANES), 0)
    return [(index + start).astype(jnp.float32).astype(jnp.bfloat16) for start in range(0, size, 16)]


def one_hot(row, names):
    one = jnp.ones((16, LANES), jnp.bfloat16)
    zero = jnp.zeros((16, LANES), jnp.bfloat16)
    return [jnp.maximum(one - jnp.abs(row - name), zero) for name in names]


def row_copies(ref, first, place):
    rows = ref[pl.ds(pl.multiple_of(first + place // 8 * 8, 8), 8), :]
    return jnp.broadcast_to(rows[place % 8:place % 8 + 1, :], (16, LANES)).astype(jnp.bfloat16)


def position():
    tile, layer = lax.axis_index("tile"), lax.axis_index("layer")
    groups = lax.axis_size("layer")
    flip = lax.rem(tile, 2)
    return layer, flip, jnp.where(flip == 1, groups - 1 - layer, layer)


def own_land(land_ref, span):
    _, _, number = position()
    return land_ref[pl.ds(pl.multiple_of(number * span, span), span), :].astype(jnp.float32)


def span_at(flip, groups, layer):
    return jnp.where(flip == 1, groups - 1 - layer, layer)


def split_cells(cells, first_row, breadth, width):
    local = cells - first_row * breadth
    shift = width.bit_length() - 1
    block = jnp.where(cells < 0, -1, local >> shift)
    return block.astype(jnp.float32), (local & (width - 1)).astype(jnp.float32)


GROUP = 64


def scatter_sum(group, blocks, block_ref, spot_ref, value_refs):
    block_names, spot_names = names_of(blocks), names_of(BLOCK)
    total = None
    for start in range(0, GROUP, GROUP // 2):
        left, right = [], []
        for place in range(start, start + GROUP // 2):
            left.append(jnp.concatenate(one_hot(row_copies(block_ref, group * GROUP, place), block_names), axis=0))
            hot = one_hot(row_copies(spot_ref, group * GROUP, place), spot_names)
            values = [row_copies(ref, group * GROUP, place) for ref in value_refs]
            right.append(jnp.concatenate([tile * value for value in values for tile in hot], axis=0))
        part = lax.dot_general(
            jnp.concatenate(left, axis=1),
            jnp.concatenate(right, axis=1),
            (((1,), (1,)), ((), ())),
            preferred_element_type=jnp.float32,
        )
        total = part if total is None else total + part
    return total


def scatter_range(first, last, blocks, block_ref, spot_ref, value_refs):
    def step(group, total):
        return total + scatter_sum(group, blocks, block_ref, spot_ref, value_refs)

    return lax.fori_loop(first, last, step, jnp.zeros((blocks, BLOCK * len(value_refs)), jnp.float32))


def early_kernel(breadth, span, cells_ref, bed_ref, block_ref, spot_ref, diag_ref, high_ref, low_ref, sum_sc):
    _, _, number = position()
    block_ref[...], spot_ref[...] = split_cells(cells_ref[...], number * span, breadth, BLOCK)
    high, low = bf16_pieces(bed_ref[...], 2)
    high_ref[...] = high.astype(jnp.float32)
    low_ref[...] = low.astype(jnp.float32)
    put_sums(diag_ref, sum_sc, block_ref, spot_ref, (high_ref, low_ref))


def put_sums(out_ref, sum_sc, block_ref, spot_ref, piece_refs):
    share = LANES // BLOCK
    blocks = share * out_ref.shape[0]
    part = scatter_range(0, block_ref.shape[0] // GROUP, blocks, block_ref, spot_ref, piece_refs)
    sum_sc[...] = part + pltpu.roll(part, BLOCK, 1)
    low_half = lax.broadcasted_iota(jnp.int32, out_ref.shape, 1) < BLOCK
    out_ref[...] = jnp.where(
        low_half, sum_sc[pl.ds(0, blocks // share, stride=share), :], sum_sc[pl.ds(1, blocks // share, stride=share), :]
    )


def river_kernel(
    stride, bed_ref, section_ref, block_ref, spot_ref, rhs_ref, slot_section_ref, reach_ref, rhigh_sc, rlow_sc, sum_sc,
):
    rows = section_ref.shape[0]
    slots = reach_ref.shape[1]
    first = (lax.axis_index("tile") + 1) * stride - 8
    own_rows = section_ref[pl.ds(pl.multiple_of(first, 8), 8), :]
    reach = jnp.concatenate([own_rows[k:k + 1, :] for k in range(slots // LANES)], axis=1)
    reach_ref[...] = reach
    index = lax.broadcasted_iota(jnp.int32, (rows, slots), 0).astype(jnp.float32)
    pick = jnp.where(index == reach, 1.0, 0.0).astype(jnp.bfloat16)
    picked = jnp.zeros(slot_section_ref.shape, jnp.float32)
    for piece in bf16_pieces(section_ref[...], 3):
        picked = picked + lax.dot_general(
            pick, piece, (((0,), (0,)), ((), ())), preferred_element_type=jnp.float32
        )
    slot_section_ref[...] = picked
    high, low = bf16_pieces(bed_ref[...] * picked, 2)
    rhigh_sc[...] = high.astype(jnp.float32)
    rlow_sc[...] = low.astype(jnp.float32)

    put_sums(rhs_ref, sum_sc, block_ref, spot_ref, (rhigh_sc, rlow_sc))


def edge_kernel(land_ref, diag_ref, rhs_ref, *refs):
    block_refs, (near_ref, far_ref) = refs[:-2], refs[-2:]
    _, held, span, breadth = block_refs[0].shape
    _, _, number = position()
    odd = lax.rem(number, 2) == 1
    per_row = breadth // LANES

    def put_edges(entry, top, bottom, lanes=slice(None)):
        near_ref[pl.ds(entry * HALO, HALO), lanes] = jnp.where(odd, top, bottom)
        far_ref[pl.ds(entry * HALO, HALO), lanes] = jnp.where(odd, bottom, top)

    entry = 0
    for kind in range(2):
        for block_ref in block_refs:
            for held_layer in range(held):
                put_edges(entry, block_ref[kind, held_layer, :HALO, :], block_ref[kind, held_layer, span - HALO:, :])
                entry += 1
    land = own_land(land_ref, span)
    put_edges(entry, land[:HALO], land[span - HALO:])
    for ref in (diag_ref, rhs_ref):
        entry += 1
        for part in range(per_row):
            top = ref[pl.ds(part, HALO, stride=per_row), :]
            bottom = ref[pl.ds((span - HALO) * per_row + part, HALO, stride=per_row), :]
            put_edges(entry, top, bottom, slice(part * LANES, (part + 1) * LANES))
    rest = near_ref.shape[0] - (entry + 1) * HALO
    for ref in (near_ref, far_ref):
        ref[pl.ds((entry + 1) * HALO, rest), :] = jnp.zeros((rest, breadth), jnp.float32)


def spread_kernel(section_hbm, owner_hbm, local_hbm, spread_ref, section_ref, owner_ref, local_ref, sems):
    pairs = ((section_hbm, section_ref), (owner_hbm, owner_ref), (local_hbm, local_ref))
    copies = [pltpu.make_async_copy(here, there, sems.at[k]) for k, (here, there) in enumerate(pairs)]
    for copy in copies:
        copy.start()
    for copy in copies:
        copy.wait()
    tiles, stride, _ = spread_ref.shape
    reach_rows = section_ref.shape[0]
    reach = (owner_ref[...] * stride + local_ref[...]).astype(jnp.float32)
    parts = [reach[:, start:start + LANES] for start in range(0, reach.shape[1], LANES)]
    parts.append(jnp.zeros((stride - reach_rows - len(parts), LANES), jnp.float32))
    payload = jnp.concatenate([section_ref[...], *parts], axis=0)
    for tile in range(tiles):
        spread_ref[tile] = payload


def prepare_kernel(head_ref, soil_ref, after_ref, *refs):
    del after_ref
    groups = len(refs)
    held, across, _ = head_ref.shape
    span = across // groups
    own, flip, _ = position()

    def rows_of(target):
        return pl.ds(pl.multiple_of(span_at(flip, groups, target) * span, span), span)

    for step, block_ref in enumerate(refs):
        rows = rows_of(own ^ step)
        for layer in range(held):
            block_ref[0, layer] = head_ref[layer, rows, :]
            block_ref[1, layer] = soil_ref[layer, rows, :].astype(jnp.float32)


class Rows:
    def __init__(self, layers, breadth):
        self.layers, self.breadth, self.per_row = layers, breadth, breadth // LANES

    def get(self, ref, row):
        spot = pl.ds(row * self.layers, self.layers)
        return jnp.concatenate([ref[part, spot, :] for part in range(self.per_row)], axis=1)

    def put(self, ref, row, value):
        spot = pl.ds(row * self.layers, self.layers)
        for part in range(self.per_row):
            ref[part, spot, :] = value[:, part * LANES:(part + 1) * LANES]

    def put_layer(self, ref, layer, row, value):
        for part in range(self.per_row):
            spot = pl.ds(row * self.layers + layer, value.shape[0], stride=self.layers)
            ref[part, spot, :] = value[:, part * LANES:(part + 1) * LANES]

    def east(self, field):
        return pltpu.roll(field, self.breadth - 1, 1)

    def west(self, field):
        return pltpu.roll(field, 1, 1)

    def below(self, field):
        return pltpu.roll(field, self.layers - 1, 0)

    def above(self, field):
        return pltpu.roll(field, 1, 0)


class Joined:
    def __init__(self, rows, own, full, first, last):
        self.rows, self.own, self.full, self.first, self.last = rows, own, full, first, last

    def holds(self, row):
        return self.first <= row < self.last

    def get(self, row):
        if self.holds(row):
            return self.rows.get(self.own, row - HALO)
        return self.rows.get(self.full, row)

    def put(self, row, value):
        self.rows.put(self.full, row, value)


def relax_row(rows, row, head, weights, wx_before, base, inverse):
    before, here, after = head
    wx, wy, wz = [field.get(row) for field in weights]
    total = base.get(row) + wx_before * before + wx * after
    total = total + wy * rows.east(here) + rows.west(wy * here)
    total = total + wz * rows.below(here) + rows.above(wz * here)
    return total * inverse.get(row), wx


def river_row(rows, ref, row, top):
    parts = [
        jnp.broadcast_to(ref[pl.ds(row * rows.per_row + part, 1), :], (rows.layers, LANES))
        for part in range(rows.per_row)
    ]
    return jnp.where(top, jnp.concatenate(parts, axis=1), 0.0)


class Faces:
    def __init__(self, rows, land, lands):
        self.rows, self.lands = rows, lands
        lx_ref, ly_ref, lz_ref = lands
        count = land.shape[0]
        level = lax.broadcasted_iota(jnp.int32, (rows.layers, rows.breadth), 0)
        self.not_bottom = level < rows.layers - 1
        not_last = lax.broadcasted_iota(jnp.int32, land.shape, 1) < rows.breadth - 1
        lx_ref[pl.ds(0, count - 1), :] = 2.0 * LATERAL * land[:count - 1] * land[1:]
        ly_ref[...] = jnp.where(not_last, 2.0 * LATERAL * land * rows.east(land), 0.0)
        lz_ref[...] = 2.0 * VERTICAL * land * land

    def conduct(self, ks, alpha, head):
        return ks * jnp.exp(alpha * jnp.minimum(head, 0.0))

    def face(self, land, here, there):
        return land * (here * there) * reciprocal(here + there)

    def between_rows(self, row, here, there):
        return self.face(self.lands[0][pl.ds(row, 1), :], here, there)

    def in_row(self, row, here):
        rows = self.rows
        wy = self.face(self.lands[1][pl.ds(row, 1), :], here, rows.east(here))
        wz = self.face(self.lands[2][pl.ds(row, 1), :], here, rows.below(here))
        wz = jnp.where(self.not_bottom, wz, 0.0)
        wz_above = rows.above(wz)
        return wy, wz, wy + rows.west(wy) + wz + wz_above, GRAVITY * (wz_above - wz)


def lane_tables(refs, layers):
    lane = lax.broadcasted_iota(jnp.int32, (layers, LANES), 1)
    tables = []
    for ref in refs:
        table = jnp.zeros((layers, LANES), jnp.float32)
        for kind in range(ref.shape[0]):
            table = jnp.where(lane == kind, ref[kind], table)
        tables.append(table)
    return tables


def look_up(rows, table, soil):
    parts = [
        jnp.take_along_axis(table, soil[:, part * LANES:(part + 1) * LANES], axis=1, mode="promise_in_bounds")
        for part in range(rows.per_row)
    ]
    return jnp.concatenate(parts, axis=1)


def stage_kernel(ks_ref, alpha_ref, store_ref, land_ref, diag_ref, rhs_ref, *refs):
    groups = lax.axis_size("layer")
    own, _, _ = position()
    block_refs, refs = refs[:groups], refs[groups:]
    first_out, ks_out, alpha_out, store_out = refs[:4]
    fields = [refs[4 + 5 * picard:9 + 5 * picard] for picard in range(ITERS)]
    head_outs = refs[4 + 5 * ITERS:4 + 5 * ITERS + HALO]
    soil_sc, *lands = refs[4 + 5 * ITERS + HALO:]
    _, held, span, breadth = block_refs[0].shape
    layers = groups * held
    rows = Rows(layers, breadth)
    faces = Faces(rows, own_land(land_ref, span), lands)
    top = lax.broadcasted_iota(jnp.int32, (layers, breadth), 0) == 0

    for step, block_ref in enumerate(block_refs):
        for held_layer in range(held):
            layer = (own ^ step) * held + held_layer
            rows.put_layer(first_out, layer, 0, block_ref[0, held_layer])
            rows.put_layer(soil_sc, layer, 0, block_ref[1, held_layer])
    tables = lane_tables((ks_ref, alpha_ref, store_ref), layers)
    for row in range(span):
        soil = rows.get(soil_sc, row).astype(jnp.int32)
        for table, out in zip(tables, (ks_out, alpha_out, store_out)):
            rows.put(out, row, look_up(rows, table, soil))

    now, begin, stop, done = first_out, 0, span, 0
    for wx_out, wy_out, wz_out, inv_out, base_out in fields:
        before = None
        for row in range(begin, stop):
            here = faces.conduct(rows.get(ks_out, row), rows.get(alpha_out, row), rows.get(now, row))
            wy, wz, diagonal, gravity = faces.in_row(row, here)
            rows.put(wy_out, row, wy)
            rows.put(wz_out, row, wz)
            store = rows.get(store_out, row)
            sums = store + diagonal, store * rows.get(first_out, row) + gravity
            if row > begin:
                wx = faces.between_rows(row - 1, before[0], here)
                rows.put(wx_out, row - 1, wx)
                diagonal, base = before[1]
                if row - 1 > begin:
                    diagonal = reciprocal(diagonal + before[2] + wx + river_row(rows, diag_ref, row - 1, top))
                    base = base + river_row(rows, rhs_ref, row - 1, top)
                rows.put(inv_out, row - 1, diagonal)
                rows.put(base_out, row - 1, base)
            else:
                wx = None
            before = here, sums, wx
        rows.put(inv_out, stop - 1, before[1][0])
        rows.put(base_out, stop - 1, before[1][1])
        weights = [Joined(rows, None, ref, HALO, HALO) for ref in (wx_out, wy_out, wz_out)]
        base, inverse = [Joined(rows, None, ref, HALO, HALO) for ref in (base_out, inv_out)]
        for _ in range(SWEEPS):
            begin, stop = begin + 1, stop - 1
            head = rows.get(now, begin - 1), rows.get(now, begin)
            wx_before = rows.get(wx_out, begin - 1)
            for row in range(begin, stop):
                head = *head[-2:], rows.get(now, row + 1)
                value, wx_before = relax_row(rows, row, head, weights, wx_before, base, inverse)
                rows.put(head_outs[done], row, value)
            now = head_outs[done]
            done += 1


def flow_kernel(is_far, kst_ref, alphat_ref, storet_ref, land_ref, halo_ref, diag_ref, rhs_ref, *refs):
    groups = lax.axis_size("layer")
    own, _, number = position()
    end = (number == 0) | (number == groups - 1)
    far_partner = jnp.where(end, own, own ^ (groups - 1))
    tile, tiles = lax.axis_index("tile"), lax.axis_size("tile")
    outside = ((tile == 0) & (number == 0)) | ((tile == tiles - 1) & (number == groups - 1))
    partner, water = (far_partner, outside) if is_far else (own ^ 1, False)
    first_ref, ks_ref, alpha_ref, store_ref = refs[:4]
    fields = [refs[4 + 5 * picard:9 + 5 * picard] for picard in range(ITERS)]
    staged_refs = refs[4 + 5 * ITERS:4 + 5 * ITERS + HALO]
    refs = refs[4 + 5 * ITERS + HALO:]
    if is_far:
        near_ref, refs = refs[0], refs[1:]
        head_refs, top_ref, result_ref, refs = refs[:groups], refs[groups], refs[groups + 1], refs[groups + 2:]
        held = head_refs[0].shape[0]
    else:
        result_ref, refs = refs[0], refs[1:]
    (
        first_sc, soil_sc, ks_sc, alpha_sc, store_sc, wx_sc, wy_sc, wz_sc, base_sc, inv_sc, ping_sc, pong_sc,
        land_sc, dtop_sc, rtop_sc, *lands,
    ) = refs
    breadth = land_ref.shape[1]
    span = land_ref.shape[0] // groups
    layers = first_ref.shape[1] // span
    held = layers // groups
    window = span + 2 * HALO
    last_own = HALO + span
    rows = Rows(layers, breadth)
    side = HALO * rows.per_row

    land_sc[...] = jnp.zeros_like(land_sc)
    land_sc[pl.ds(HALO, span), :] = own_land(land_ref, span)
    dtop_sc[pl.ds(side, span * rows.per_row), :] = diag_ref[...]
    rtop_sc[pl.ds(side, span * rows.per_row), :] = rhs_ref[...]
    top = lax.broadcasted_iota(jnp.int32, (layers, breadth), 0) == 0

    def put_halo(row):
        def entry(number):
            return halo_ref[pl.ds(number * HALO, HALO), :]

        for count in range(layers):
            layer = (partner ^ (count // held)) * held + count % held
            rows.put_layer(first_sc, layer, row, entry(count))
            rows.put_layer(soil_sc, layer, row, entry(layers + count))
        land_sc[pl.ds(row, HALO), :] = jnp.where(water, 0.0, entry(2 * layers))
        for count, top_sc in ((2 * layers + 1, dtop_sc), (2 * layers + 2, rtop_sc)):
            value = entry(count)
            for part in range(rows.per_row):
                spot = pl.ds(row * rows.per_row + part, HALO, stride=rows.per_row)
                top_sc[spot, :] = value[:, part * LANES:(part + 1) * LANES]

    def one_side(above):
        halo = 0 if above else last_own
        put_halo(halo)
        faces = Faces(rows, land_sc[...], lands)
        tables = lane_tables((kst_ref, alphat_ref, storet_ref), layers)
        for row in range(halo, halo + HALO):
            soil = rows.get(soil_sc, row).astype(jnp.int32)
            for table, ref in zip(tables, (ks_sc, alpha_sc, store_sc)):
                rows.put(ref, row, look_up(rows, table, soil))
        first, ks, alpha, store = [
            Joined(rows, held_ref, full, HALO, last_own)
            for held_ref, full in ((first_ref, first_sc), (ks_ref, ks_sc), (alpha_ref, alpha_sc), (store_ref, store_sc))
        ]
        now, begin, stop, done = first, 0, window, 0
        for wx_ref, wy_ref, wz_ref, inv_ref, base_ref in fields:
            low, high = HALO + done, last_own - done
            wx_of = Joined(rows, wx_ref, wx_sc, low, high - 1)
            wy_of, wz_of = Joined(rows, wy_ref, wy_sc, low, high), Joined(rows, wz_ref, wz_sc, low, high)
            inverse, base = [
                Joined(rows, held_ref, full, low + 1, high - 1) for held_ref, full in ((inv_ref, inv_sc), (base_ref, base_sc))
            ]
            start, finish, last_staged = (begin, low + 2, low) if above else (high - 2, stop, high - 1)
            here_before, wx_before, sums_before = None, None, None
            for row in range(start, finish):
                here, sums = None, None
                if row == last_staged or not wy_of.holds(row):
                    here = faces.conduct(ks.get(row), alpha.get(row), now.get(row))
                if row == last_staged:
                    sums = rows.get(inv_ref, row - HALO), rows.get(base_ref, row - HALO)
                elif not wy_of.holds(row) and begin < row < stop - 1:
                    wy, wz, diagonal, gravity = faces.in_row(row, here)
                    wy_of.put(row, wy)
                    wz_of.put(row, wz)
                    sums = store.get(row) + diagonal, store.get(row) * first.get(row) + gravity
                if row > start:
                    if wx_of.holds(row - 1):
                        wx = wx_of.get(row - 1)
                    else:
                        wx = faces.between_rows(row - 1, here_before, here)
                        wx_of.put(row - 1, wx)
                    if sums_before is not None:
                        diagonal = sums_before[0] + wx_before + wx + river_row(rows, dtop_sc, row - 1, top)
                        inverse.put(row - 1, reciprocal(diagonal))
                        base.put(row - 1, sums_before[1] + river_row(rows, rtop_sc, row - 1, top))
                    wx_before = wx
                here_before, sums_before = here, sums
            for _ in range(SWEEPS):
                begin, stop = begin + 1, stop - 1
                later = Joined(
                    rows, staged_refs[done], (ping_sc, pong_sc)[done % 2], HALO + done + 1, last_own - done - 1
                )
                done += 1
                for row in range(begin, later.first) if above else range(later.last, stop):
                    head = now.get(row - 1), now.get(row), now.get(row + 1)
                    value, _ = relax_row(rows, row, head, (wx_of, wy_of, wz_of), wx_of.get(row - 1), base, inverse)
                    later.put(row, value)
                now = later
        mine = range(HALO, now.first) if above else range(now.last, last_own)
        for row in mine:
            rows.put(result_ref, row - HALO, now.get(row))
        if is_far:
            for row in range(HALO, last_own):
                if row not in mine:
                    other = staged_refs[-1] if now.holds(row) else near_ref
                    rows.put(result_ref, row - HALO, rows.get(other, row - HALO))

    odd = lax.rem(number, 2)
    for above in (True, False):
        @pl.when(odd == (1 if above != is_far else 0))
        def _(above=above):
            one_side(above)

    if is_far:
        for part in range(rows.per_row):
            lanes = pl.ds(part * LANES, LANES)
            top_ref[:, lanes] = result_ref[part, pl.ds(0, span, stride=layers), :]
            for step, head_ref in enumerate(head_refs):
                for held_layer in range(held):
                    layer = (own ^ step) * held + held_layer
                    head_ref[held_layer, :, lanes] = result_ref[part, pl.ds(layer, span, stride=layers), :]


def inflow_kernel(reach_rows, stride, cells_ref, bed_ref, slot_section_ref, reach_ref, *refs):
    groups = lax.axis_size("layer")
    own_layer, flip, _ = position()
    top_refs = refs[:groups]
    out_ref, block_sc, lane_sc, found_sc, turned_sc = refs[groups:]
    span, breadth = top_refs[0].shape
    per_row = breadth // LANES
    blocks = groups * span * per_row
    slots = cells_ref.shape[0]
    quarter = LANES // groups
    packed = slots // groups
    for step, top_ref in enumerate(top_refs):
        number = span_at(flip, groups, own_layer ^ step)
        for part in range(per_row):
            spot = pl.ds(number * span * per_row + part, span, stride=per_row)
            turned_sc[spot, :] = top_ref[:, part * LANES:(part + 1) * LANES]

    own = lax.broadcasted_iota(jnp.int32, (packed, LANES), 1) // quarter

    def pack(ref):
        result = None
        for number in range(groups):
            shift = lax.rem((number + groups - own_layer) * quarter, LANES)
            moved = pltpu.roll(ref[pl.ds(number * packed, packed), :], shift, 1)
            result = moved if result is None else jnp.where(own == number, moved, result)
        return result

    cells = pack(cells_ref)
    block, lane = split_cells(cells, 0, breadth, LANES)
    block_sc[...] = block
    lane_sc[...] = lane
    table = jnp.concatenate(bf16_pieces(turned_sc[...].T, 2), axis=0)
    names = names_of(blocks)
    index = lax.broadcasted_iota(jnp.int32, (8, LANES), 0).astype(jnp.float32)
    for pair in range(0, packed, 2):
        hots = jnp.concatenate(
            [jnp.concatenate(one_hot(row_copies(block_sc, 0, row), names), axis=0) for row in (pair, pair + 1)], axis=1
        )
        found = lax.dot_general(
            table, hots, (((1,), (0,)), ((), ())), preferred_element_type=jnp.float32
        )
        found = found[:LANES] + found[LANES:]
        for row in (pair, pair + 1):
            lanes = jnp.broadcast_to(lane_sc[pl.ds(row, 1), :], (8, LANES))
            mine = found[:, (row - pair) * LANES:(row - pair + 1) * LANES]
            total = jnp.zeros((8, LANES), jnp.float32)
            for start in range(0, LANES, 8):
                total = total + jnp.where(lanes == index + float(start), mine[start:start + 8], 0.0)
            found_sc[pl.ds(row, 1), :] = jnp.sum(total, axis=0, keepdims=True)
    slot_in = jnp.where(cells >= 0, pack(bed_ref) * (found_sc[...] - pack(slot_section_ref)), 0.0)
    spread = jnp.concatenate(
        [slot_in if number == 0 else pltpu.roll(slot_in, LANES - number * quarter, 1) for number in range(groups)],
        axis=0,
    )
    in_quarter = lax.broadcasted_iota(jnp.int32, spread.shape, 1) < quarter
    pieces = bf16_pieces(jnp.where(in_quarter, spread, 0.0), 3)
    fold = reach_rows // groups
    index = lax.broadcasted_iota(jnp.int32, (out_ref.shape[0], slots), 0)
    index = index // fold * stride + lax.rem(index, fold)
    result = None
    for number in range(groups):
        name = (index + number * fold).astype(jnp.float32)
        put = jnp.where(name == reach_ref[...], 1.0, 0.0).astype(jnp.bfloat16)
        total = jnp.zeros(out_ref.shape, jnp.float32)
        for piece in pieces:
            total = total + lax.dot_general(
                put, piece, (((1,), (0,)), ((), ())), preferred_element_type=jnp.float32
            )
        result = total if result is None else result + pltpu.roll(total, number * quarter, 1)
    out_ref[...] = result


def sum_kernel(terms_ref, inflow_ref):
    total = terms_ref[0]
    for tile in range(1, terms_ref.shape[0]):
        total = total + terms_ref[tile]
    fold, quarter = total.shape[0], inflow_ref.shape[1]
    for number in range(inflow_ref.shape[0] // fold):
        lanes = slice(number * quarter, (number + 1) * quarter)
        inflow_ref[pl.ds(number * fold, fold), :] = total[:, lanes]


def head_kernel(*refs):
    groups = lax.axis_size("layer")
    back_refs, (head_hbm, sems) = refs[:groups], refs[groups:]
    _, span, _ = back_refs[0].shape
    own, flip, _ = position()
    copies = []
    for step, back_ref in enumerate(back_refs):
        rows = pl.ds(pl.multiple_of(span_at(flip, groups, own ^ step) * span, span), span)
        copies.append(pltpu.make_async_copy(back_ref, head_hbm.at[:, rows, :], sems.at[step]))
        copies[-1].start()
    for copy in copies:
        copy.wait()


def call(kernel, out_shape, in_specs, scratch, micros, vmem=VMEM_LIMIT, out_specs=None):
    single = not isinstance(out_shape, (tuple, list))
    return pl.pallas_call(
        kernel,
        out_shape=out_shape,
        in_specs=in_specs,
        out_specs=out_specs or (in_vmem if single else tuple(in_vmem for _ in out_shape)),
        scratch_shapes=scratch,
        compiler_params=pltpu.CompilerParams(vmem_limit_bytes=vmem),
        cost_estimate=pl.CostEstimate(flops=int(micros * 1.15e9), bytes_accessed=0, transcendentals=0),
    )


def on_device(
    head_start,
    soil_class,
    land_mask,
    ks_table,
    alpha_table,
    store_table,
    section,
    cross_owner,
    cross_local,
    node_cell,
    bed_cond,
):
    held, across, breadth = head_start.shape
    reach_rows, node_count = section.shape
    tiles = lax.axis_size("tile")
    groups = lax.axis_size("layer")
    layers = held * groups
    span = across // groups
    per_row = breadth // LANES
    blocks = span * per_row
    near = [(i, i ^ 1) for i in range(groups)]
    far = []
    for upper in range(tiles):
        far += [(upper * groups + i, upper * groups + (i ^ (groups - 1))) for i in range(1, groups - 1)]
        if upper + 1 < tiles:
            index = groups - 1 if upper % 2 == 0 else 0
            one, two = upper * groups + index, (upper + 1) * groups + index
            far += [(one, two), (two, one)]
    far += [(0, 0)]
    last = tiles * groups - (1 if tiles % 2 == 1 else groups)
    far += [(last, last)]

    cells = node_cell[0]
    bed = bed_cond[0]
    slots = cells.shape[0]

    def exchange(parts):
        received = [parts[0]]
        for step in range(1, groups):
            received.append(lax.ppermute(parts[step], "layer", [(i, i ^ step) for i in range(groups)]))
        return received

    stride = reach_rows + 8
    spread = call(
        spread_kernel, jax.ShapeDtypeStruct((tiles, stride, node_count), jnp.float32), [in_hbm] * 3,
        [
            pltpu.VMEM(section.shape, jnp.float32),
            pltpu.VMEM(cross_owner.shape, jnp.int32),
            pltpu.VMEM(cross_owner.shape, jnp.int32),
            pltpu.SemaphoreType.DMA((3,)),
        ],
        1, VMEM_MOST,
    )(section, cross_owner, cross_local)
    whole_section = lax.all_to_all(spread, "tile", 0, 0).reshape(tiles * stride, node_count)
    own_blocks = call(
        prepare_kernel,
        (jax.ShapeDtypeStruct((2, held, span, breadth), jnp.float32),) * groups,
        [in_vmem] * 2 + [in_hbm], [], 0.5,
    )(head_start, soil_class, spread)
    received = exchange(own_blocks)

    node_scratch = pltpu.VMEM((slots, LANES), jnp.float32)
    riv_shape = jax.ShapeDtypeStruct((blocks, LANES), jnp.float32)
    node_field = jax.ShapeDtypeStruct((slots, LANES), jnp.float32)
    groups_of_cells = span * breadth // BLOCK
    sums = pltpu.VMEM((groups_of_cells, LANES), jnp.float32)
    block_number, spot, diag = call(
        functools.partial(early_kernel, breadth, span), (node_field, node_field, riv_shape), [in_vmem] * 2,
        [node_scratch] * 2 + [sums], 3,
    )(cells, bed)
    rhs, slot_section, reach = call(
        functools.partial(river_kernel, stride),
        (riv_shape, node_field, jax.ShapeDtypeStruct((1, slots), jnp.float32)),
        [in_vmem] * 4, [node_scratch] * 2 + [sums], 5,
    )(bed, whole_section, block_number, spot)
    edges = jax.ShapeDtypeStruct((-(-(2 * layers + 3) * HALO // 8) * 8, breadth), jnp.float32)
    near_edge, far_edge = call(
        edge_kernel, (edges, edges), [in_vmem] * (3 + groups), [], 0.1,
    )(land_mask, diag, rhs, *received)
    far_halo = lax.ppermute(far_edge, FLAT, far)
    near_halo = lax.ppermute(near_edge, "layer", near)

    window = span + 2 * HALO
    own_field = jax.ShapeDtypeStruct((per_row, span * layers, LANES), jnp.float32)
    field = pltpu.VMEM((per_row, window * layers, LANES), jnp.float32)
    staged = call(
        stage_kernel, (own_field,) * (4 + 5 * ITERS + HALO), [in_smem] * 3 + [in_vmem] * (3 + groups),
        [pltpu.VMEM(own_field.shape, jnp.float32)] + [pltpu.VMEM((span, breadth), jnp.float32)] * 3,
        4,
    )(ks_table, alpha_table, store_table, land_mask, diag, rhs, *received)
    head_shape = jax.ShapeDtypeStruct((held, span, breadth), jnp.float32)
    flow_scratch = (
        [field] * 12
        + [pltpu.VMEM((window, breadth), jnp.float32)]
        + [pltpu.VMEM((window * per_row, LANES), jnp.float32)] * 2
        + [pltpu.VMEM((window, breadth), jnp.float32)] * 3
    )
    known = diag, rhs, *staged
    near_side = call(
        functools.partial(flow_kernel, False), own_field, [in_smem] * 3 + [in_vmem] * (2 + len(known)), flow_scratch, 2,
    )(ks_table, alpha_table, store_table, land_mask, near_halo, *known)
    *heads, top = call(
        functools.partial(flow_kernel, True),
        (head_shape,) * groups + (jax.ShapeDtypeStruct((span, breadth), jnp.float32),),
        [in_smem] * 3 + [in_vmem] * (3 + len(known)),
        [pltpu.VMEM(own_field.shape, jnp.float32)] + flow_scratch, 2,
    )(ks_table, alpha_table, store_table, land_mask, far_halo, *known, near_side)
    tops = exchange([top] * groups)
    backs = exchange(heads)

    fold = reach_rows // groups
    packed = pltpu.VMEM((slots // groups, LANES), jnp.float32)
    partial = call(
        functools.partial(inflow_kernel, reach_rows, stride),
        jax.ShapeDtypeStruct((tiles * fold, node_count), jnp.float32),
        [in_vmem] * (4 + groups),
        [packed] * 3 + [pltpu.VMEM((across * per_row, LANES), jnp.float32)],
        3,
    )(cells, bed, slot_section, reach, *tops)
    partial, *backs[:-1] = lax.optimization_barrier((partial, *backs[:-1]))
    terms = lax.all_to_all(partial.reshape(tiles, fold, node_count), "tile", 0, 0)
    head = call(
        head_kernel, jax.ShapeDtypeStruct(head_start.shape, jnp.float32), [in_vmem] * groups,
        [pltpu.SemaphoreType.DMA((groups,))], 0.7, out_specs=in_hbm,
    )(*backs)
    inflow_shape = jax.ShapeDtypeStruct((reach_rows, node_count // groups), jnp.float32)
    return head, call(sum_kernel, inflow_shape, [in_vmem], [], 0.1)(terms)


def solution(mesh):
    placed = (
        P("layer", "tile", None),
        P("layer", "tile", None),
        P("tile", None),
        P(),
        P(),
        P(),
        P("tile", None),
        P("tile", None),
        P("tile", None),
        P("tile", None, None),
        P("tile", None, None),
    )
    return jax.shard_map(
        on_device,
        mesh=mesh,
        in_specs=placed,
        out_specs=(P("layer", "tile", None), P("tile", "layer")),
        check_vma=False,
    )
```

```python
import functools

import jax
import jax.numpy as jnp
from jax import lax
from jax.experimental import pallas as pl
from jax.experimental.pallas import tpu as pltpu
from jax.sharding import PartitionSpec as P

ITERS = 2
SWEEPS = 3

LATERAL = 1.0
VERTICAL = 2.0
GRAVITY = 1.0

HALO = ITERS * SWEEPS
BLOCK = 64
LANES = 128
VMEM_LIMIT = 32 * 1024 * 1024
VMEM_MOST = 60 * 1024 * 1024
FLAT = ("tile", "layer")

in_vmem = pl.BlockSpec(memory_space=pltpu.VMEM)
in_hbm = pl.BlockSpec(memory_space=pltpu.HBM)
in_smem = pl.BlockSpec(memory_space=pltpu.SMEM)


def bf16_pieces(value, count):
    pieces = []
    for _ in range(count):
        piece = value.astype(jnp.bfloat16)
        pieces.append(piece)
        value = value - piece.astype(jnp.float32)
    return pieces


def reciprocal(value):
    guess = pl.reciprocal(value, approx=True)
    return guess * (2.0 - value * guess)


def names_of(size):
    index = lax.broadcasted_iota(jnp.int32, (16, LANES), 0)
    return [(index + start).astype(jnp.float32).astype(jnp.bfloat16) for start in range(0, size, 16)]


def one_hot(row, names):
    one = jnp.ones((16, LANES), jnp.bfloat16)
    zero = jnp.zeros((16, LANES), jnp.bfloat16)
    return [jnp.maximum(one - jnp.abs(row - name), zero) for name in names]


def row_copies(ref, first, place):
    rows = ref[pl.ds(pl.multiple_of(first + place // 8 * 8, 8), 8), :]
    return jnp.broadcast_to(rows[place % 8:place % 8 + 1, :], (16, LANES)).astype(jnp.bfloat16)


def position():
    tile, layer = lax.axis_index("tile"), lax.axis_index("layer")
    groups = lax.axis_size("layer")
    flip = lax.rem(tile, 2)
    return layer, flip, jnp.where(flip == 1, groups - 1 - layer, layer)


def own_land(land_ref, span):
    _, _, number = position()
    return land_ref[pl.ds(pl.multiple_of(number * span, span), span), :].astype(jnp.float32)


def span_at(flip, groups, layer):
    return jnp.where(flip == 1, groups - 1 - layer, layer)


def split_cells(cells, first_row, breadth, width):
    local = cells - first_row * breadth
    shift = width.bit_length() - 1
    block = jnp.where(cells < 0, -1, local >> shift)
    return block.astype(jnp.float32), (local & (width - 1)).astype(jnp.float32)


GROUP = 128


def scatter_sum(group, blocks, block_ref, spot_ref, value_refs):
    block_names, spot_names = names_of(blocks), names_of(BLOCK)
    total = None
    for start in range(0, GROUP, GROUP // 2):
        left, right = [], []
        for place in range(start, start + GROUP // 2):
            left.append(jnp.concatenate(one_hot(row_copies(block_ref, group * GROUP, place), block_names), axis=0))
            hot = one_hot(row_copies(spot_ref, group * GROUP, place), spot_names)
            values = [row_copies(ref, group * GROUP, place) for ref in value_refs]
            right.append(jnp.concatenate([tile * value for value in values for tile in hot], axis=0))
        part = lax.dot_general(
            jnp.concatenate(left, axis=1),
            jnp.concatenate(right, axis=1),
            (((1,), (1,)), ((), ())),
            preferred_element_type=jnp.float32,
        )
        total = part if total is None else total + part
    return total


def scatter_range(first, last, blocks, block_ref, spot_ref, value_refs):
    def step(group, total):
        return total + scatter_sum(group, blocks, block_ref, spot_ref, value_refs)

    return lax.fori_loop(first, last, step, jnp.zeros((blocks, BLOCK * len(value_refs)), jnp.float32))


def early_kernel(breadth, span, cells_ref, bed_ref, block_ref, spot_ref, diag_ref, high_ref, low_ref, sum_sc):
    _, _, number = position()
    block_ref[...], spot_ref[...] = split_cells(cells_ref[...], number * span, breadth, BLOCK)
    high, low = bf16_pieces(bed_ref[...], 2)
    high_ref[...] = high.astype(jnp.float32)
    low_ref[...] = low.astype(jnp.float32)
    put_sums(diag_ref, sum_sc, block_ref, spot_ref, (high_ref, low_ref))


def put_sums(out_ref, sum_sc, block_ref, spot_ref, piece_refs):
    share = LANES // BLOCK
    blocks = share * out_ref.shape[0]
    part = scatter_range(0, block_ref.shape[0] // GROUP, blocks, block_ref, spot_ref, piece_refs)
    sum_sc[...] = part + pltpu.roll(part, BLOCK, 1)
    low_half = lax.broadcasted_iota(jnp.int32, out_ref.shape, 1) < BLOCK
    out_ref[...] = jnp.where(
        low_half, sum_sc[pl.ds(0, blocks // share, stride=share), :], sum_sc[pl.ds(1, blocks // share, stride=share), :]
    )


def river_kernel(
    stride, bed_ref, section_ref, block_ref, spot_ref, rhs_ref, slot_section_ref, reach_ref, rhigh_sc, rlow_sc, sum_sc,
):
    rows = section_ref.shape[0]
    slots = reach_ref.shape[1]
    first = (lax.axis_index("tile") + 1) * stride - 8
    own_rows = section_ref[pl.ds(pl.multiple_of(first, 8), 8), :]
    reach = jnp.concatenate([own_rows[k:k + 1, :] for k in range(slots // LANES)], axis=1)
    reach_ref[...] = reach
    index = lax.broadcasted_iota(jnp.int32, (rows, slots), 0).astype(jnp.float32)
    pick = jnp.where(index == reach, 1.0, 0.0).astype(jnp.bfloat16)
    picked = jnp.zeros(slot_section_ref.shape, jnp.float32)
    for piece in bf16_pieces(section_ref[...], 3):
        picked = picked + lax.dot_general(
            pick, piece, (((0,), (0,)), ((), ())), preferred_element_type=jnp.float32
        )
    slot_section_ref[...] = picked
    high, low = bf16_pieces(bed_ref[...] * picked, 2)
    rhigh_sc[...] = high.astype(jnp.float32)
    rlow_sc[...] = low.astype(jnp.float32)

    put_sums(rhs_ref, sum_sc, block_ref, spot_ref, (rhigh_sc, rlow_sc))


def edge_kernel(land_ref, diag_ref, rhs_ref, *refs):
    block_refs, (near_ref, far_ref) = refs[:-2], refs[-2:]
    _, held, span, breadth = block_refs[0].shape
    _, _, number = position()
    odd = lax.rem(number, 2) == 1
    per_row = breadth // LANES

    def put_edges(entry, top, bottom, lanes=slice(None)):
        near_ref[pl.ds(entry * HALO, HALO), lanes] = jnp.where(odd, top, bottom)
        far_ref[pl.ds(entry * HALO, HALO), lanes] = jnp.where(odd, bottom, top)

    entry = 0
    for kind in range(2):
        for block_ref in block_refs:
            for held_layer in range(held):
                put_edges(entry, block_ref[kind, held_layer, :HALO, :], block_ref[kind, held_layer, span - HALO:, :])
                entry += 1
    land = own_land(land_ref, span)
    put_edges(entry, land[:HALO], land[span - HALO:])
    for ref in (diag_ref, rhs_ref):
        entry += 1
        for part in range(per_row):
            top = ref[pl.ds(part, HALO, stride=per_row), :]
            bottom = ref[pl.ds((span - HALO) * per_row + part, HALO, stride=per_row), :]
            put_edges(entry, top, bottom, slice(part * LANES, (part + 1) * LANES))
    rest = near_ref.shape[0] - (entry + 1) * HALO
    for ref in (near_ref, far_ref):
        ref[pl.ds((entry + 1) * HALO, rest), :] = jnp.zeros((rest, breadth), jnp.float32)


def spread_kernel(section_hbm, owner_hbm, local_hbm, spread_ref, section_ref, owner_ref, local_ref, sems):
    pairs = ((section_hbm, section_ref), (owner_hbm, owner_ref), (local_hbm, local_ref))
    copies = [pltpu.make_async_copy(here, there, sems.at[k]) for k, (here, there) in enumerate(pairs)]
    for copy in copies:
        copy.start()
    for copy in copies:
        copy.wait()
    tiles, stride, _ = spread_ref.shape
    reach_rows = section_ref.shape[0]
    reach = (owner_ref[...] * stride + local_ref[...]).astype(jnp.float32)
    parts = [reach[:, start:start + LANES] for start in range(0, reach.shape[1], LANES)]
    parts.append(jnp.zeros((stride - reach_rows - len(parts), LANES), jnp.float32))
    payload = jnp.concatenate([section_ref[...], *parts], axis=0)
    for tile in range(tiles):
        spread_ref[tile] = payload


def prepare_kernel(head_ref, soil_ref, after_ref, *refs):
    del after_ref
    groups = len(refs)
    held, across, _ = head_ref.shape
    span = across // groups
    own, flip, _ = position()

    def rows_of(target):
        return pl.ds(pl.multiple_of(span_at(flip, groups, target) * span, span), span)

    for step, block_ref in enumerate(refs):
        rows = rows_of(own ^ step)
        for layer in range(held):
            block_ref[0, layer] = head_ref[layer, rows, :]
            block_ref[1, layer] = soil_ref[layer, rows, :].astype(jnp.float32)


class Rows:
    def __init__(self, layers, breadth):
        self.layers, self.breadth, self.per_row = layers, breadth, breadth // LANES

    def get(self, ref, row):
        spot = pl.ds(row * self.layers, self.layers)
        return jnp.concatenate([ref[part, spot, :] for part in range(self.per_row)], axis=1)

    def put(self, ref, row, value):
        spot = pl.ds(row * self.layers, self.layers)
        for part in range(self.per_row):
            ref[part, spot, :] = value[:, part * LANES:(part + 1) * LANES]

    def put_layer(self, ref, layer, row, value):
        for part in range(self.per_row):
            spot = pl.ds(row * self.layers + layer, value.shape[0], stride=self.layers)
            ref[part, spot, :] = value[:, part * LANES:(part + 1) * LANES]

    def east(self, field):
        return pltpu.roll(field, self.breadth - 1, 1)

    def west(self, field):
        return pltpu.roll(field, 1, 1)

    def below(self, field):
        return pltpu.roll(field, self.layers - 1, 0)

    def above(self, field):
        return pltpu.roll(field, 1, 0)


class Joined:
    def __init__(self, rows, own, full, first, last):
        self.rows, self.own, self.full, self.first, self.last = rows, own, full, first, last

    def holds(self, row):
        return self.first <= row < self.last

    def get(self, row):
        if self.holds(row):
            return self.rows.get(self.own, row - HALO)
        return self.rows.get(self.full, row)

    def put(self, row, value):
        self.rows.put(self.full, row, value)


def relax_row(rows, row, head, weights, wx_before, base, inverse):
    before, here, after = head
    wx, wy, wz = [field.get(row) for field in weights]
    total = base.get(row) + wx_before * before + wx * after
    total = total + wy * rows.east(here) + rows.west(wy * here)
    total = total + wz * rows.below(here) + rows.above(wz * here)
    return total * inverse.get(row), wx


def river_row(rows, ref, row, top):
    parts = [
        jnp.broadcast_to(ref[pl.ds(row * rows.per_row + part, 1), :], (rows.layers, LANES))
        for part in range(rows.per_row)
    ]
    return jnp.where(top, jnp.concatenate(parts, axis=1), 0.0)


class Faces:
    def __init__(self, rows, land, lands):
        self.rows, self.lands = rows, lands
        lx_ref, ly_ref, lz_ref = lands
        count = land.shape[0]
        level = lax.broadcasted_iota(jnp.int32, (rows.layers, rows.breadth), 0)
        self.not_bottom = level < rows.layers - 1
        not_last = lax.broadcasted_iota(jnp.int32, land.shape, 1) < rows.breadth - 1
        lx_ref[pl.ds(0, count - 1), :] = 2.0 * LATERAL * land[:count - 1] * land[1:]
        ly_ref[...] = jnp.where(not_last, 2.0 * LATERAL * land * rows.east(land), 0.0)
        lz_ref[...] = 2.0 * VERTICAL * land * land

    def conduct(self, ks, alpha, head):
        return ks * jnp.exp(alpha * jnp.minimum(head, 0.0))

    def face(self, land, here, there):
        return land * (here * there) * reciprocal(here + there)

    def between_rows(self, row, here, there):
        return self.face(self.lands[0][pl.ds(row, 1), :], here, there)

    def in_row(self, row, here):
        rows = self.rows
        wy = self.face(self.lands[1][pl.ds(row, 1), :], here, rows.east(here))
        wz = self.face(self.lands[2][pl.ds(row, 1), :], here, rows.below(here))
        wz = jnp.where(self.not_bottom, wz, 0.0)
        wz_above = rows.above(wz)
        return wy, wz, wy + rows.west(wy) + wz + wz_above, GRAVITY * (wz_above - wz)


def lane_tables(refs, layers):
    lane = lax.broadcasted_iota(jnp.int32, (layers, LANES), 1)
    tables = []
    for ref in refs:
        table = jnp.zeros((layers, LANES), jnp.float32)
        for kind in range(ref.shape[0]):
            table = jnp.where(lane == kind, ref[kind], table)
        tables.append(table)
    return tables


def look_up(rows, table, soil):
    parts = [
        jnp.take_along_axis(table, soil[:, part * LANES:(part + 1) * LANES], axis=1, mode="promise_in_bounds")
        for part in range(rows.per_row)
    ]
    return jnp.concatenate(parts, axis=1)


def stage_kernel(ks_ref, alpha_ref, store_ref, land_ref, diag_ref, rhs_ref, *refs):
    groups = lax.axis_size("layer")
    own, _, _ = position()
    block_refs, refs = refs[:groups], refs[groups:]
    first_out, ks_out, alpha_out, store_out = refs[:4]
    fields = [refs[4 + 5 * picard:9 + 5 * picard] for picard in range(ITERS)]
    head_outs = refs[4 + 5 * ITERS:4 + 5 * ITERS + HALO]
    soil_sc, *lands = refs[4 + 5 * ITERS + HALO:]
    _, held, span, breadth = block_refs[0].shape
    layers = groups * held
    rows = Rows(layers, breadth)
    faces = Faces(rows, own_land(land_ref, span), lands)
    top = lax.broadcasted_iota(jnp.int32, (layers, breadth), 0) == 0

    for step, block_ref in enumerate(block_refs):
        for held_layer in range(held):
            layer = (own ^ step) * held + held_layer
            rows.put_layer(first_out, layer, 0, block_ref[0, held_layer])
            rows.put_layer(soil_sc, layer, 0, block_ref[1, held_layer])
    tables = lane_tables((ks_ref, alpha_ref, store_ref), layers)
    for row in range(span):
        soil = rows.get(soil_sc, row).astype(jnp.int32)
        for table, out in zip(tables, (ks_out, alpha_out, store_out)):
            rows.put(out, row, look_up(rows, table, soil))

    now, begin, stop, done = first_out, 0, span, 0
    for wx_out, wy_out, wz_out, inv_out, base_out in fields:
        before = None
        for row in range(begin, stop):
            here = faces.conduct(rows.get(ks_out, row), rows.get(alpha_out, row), rows.get(now, row))
            wy, wz, diagonal, gravity = faces.in_row(row, here)
            rows.put(wy_out, row, wy)
            rows.put(wz_out, row, wz)
            store = rows.get(store_out, row)
            sums = store + diagonal, store * rows.get(first_out, row) + gravity
            if row > begin:
                wx = faces.between_rows(row - 1, before[0], here)
                rows.put(wx_out, row - 1, wx)
                diagonal, base = before[1]
                if row - 1 > begin:
                    diagonal = reciprocal(diagonal + before[2] + wx + river_row(rows, diag_ref, row - 1, top))
                    base = base + river_row(rows, rhs_ref, row - 1, top)
                rows.put(inv_out, row - 1, diagonal)
                rows.put(base_out, row - 1, base)
            else:
                wx = None
            before = here, sums, wx
        rows.put(inv_out, stop - 1, before[1][0])
        rows.put(base_out, stop - 1, before[1][1])
        weights = [Joined(rows, None, ref, HALO, HALO) for ref in (wx_out, wy_out, wz_out)]
        base, inverse = [Joined(rows, None, ref, HALO, HALO) for ref in (base_out, inv_out)]
        for _ in range(SWEEPS):
            begin, stop = begin + 1, stop - 1
            head = rows.get(now, begin - 1), rows.get(now, begin)
            wx_before = rows.get(wx_out, begin - 1)
            for row in range(begin, stop):
                head = *head[-2:], rows.get(now, row + 1)
                value, wx_before = relax_row(rows, row, head, weights, wx_before, base, inverse)
                rows.put(head_outs[done], row, value)
            now = head_outs[done]
            done += 1


def flow_kernel(is_far, kst_ref, alphat_ref, storet_ref, land_ref, halo_ref, diag_ref, rhs_ref, *refs):
    groups = lax.axis_size("layer")
    own, _, number = position()
    end = (number == 0) | (number == groups - 1)
    far_partner = jnp.where(end, own, own ^ (groups - 1))
    tile, tiles = lax.axis_index("tile"), lax.axis_size("tile")
    outside = ((tile == 0) & (number == 0)) | ((tile == tiles - 1) & (number == groups - 1))
    partner, water = (far_partner, outside) if is_far else (own ^ 1, False)
    first_ref, ks_ref, alpha_ref, store_ref = refs[:4]
    fields = [refs[4 + 5 * picard:9 + 5 * picard] for picard in range(ITERS)]
    staged_refs = refs[4 + 5 * ITERS:4 + 5 * ITERS + HALO]
    refs = refs[4 + 5 * ITERS + HALO:]
    if is_far:
        near_ref, refs = refs[0], refs[1:]
        head_refs, top_ref, result_ref, refs = refs[:groups], refs[groups], refs[groups + 1], refs[groups + 2:]
        held = head_refs[0].shape[0]
    else:
        result_ref, refs = refs[0], refs[1:]
    (
        first_sc, soil_sc, ks_sc, alpha_sc, store_sc, wx_sc, wy_sc, wz_sc, base_sc, inv_sc, ping_sc, pong_sc,
        land_sc, dtop_sc, rtop_sc, *lands,
    ) = refs
    breadth = land_ref.shape[1]
    span = land_ref.shape[0] // groups
    layers = first_ref.shape[1] // span
    held = layers // groups
    window = span + 2 * HALO
    last_own = HALO + span
    rows = Rows(layers, breadth)
    side = HALO * rows.per_row

    land_sc[...] = jnp.zeros_like(land_sc)
    land_sc[pl.ds(HALO, span), :] = own_land(land_ref, span)
    dtop_sc[pl.ds(side, span * rows.per_row), :] = diag_ref[...]
    rtop_sc[pl.ds(side, span * rows.per_row), :] = rhs_ref[...]
    top = lax.broadcasted_iota(jnp.int32, (layers, breadth), 0) == 0

    def put_halo(row):
        def entry(number):
            return halo_ref[pl.ds(number * HALO, HALO), :]

        for count in range(layers):
            layer = (partner ^ (count // held)) * held + count % held
            rows.put_layer(first_sc, layer, row, entry(count))
            rows.put_layer(soil_sc, layer, row, entry(layers + count))
        land_sc[pl.ds(row, HALO), :] = jnp.where(water, 0.0, entry(2 * layers))
        for count, top_sc in ((2 * layers + 1, dtop_sc), (2 * layers + 2, rtop_sc)):
            value = entry(count)
            for part in range(rows.per_row):
                spot = pl.ds(row * rows.per_row + part, HALO, stride=rows.per_row)
                top_sc[spot, :] = value[:, part * LANES:(part + 1) * LANES]

    def one_side(above):
        halo = 0 if above else last_own
        put_halo(halo)
        faces = Faces(rows, land_sc[...], lands)
        tables = lane_tables((kst_ref, alphat_ref, storet_ref), layers)
        for row in range(halo, halo + HALO):
            soil = rows.get(soil_sc, row).astype(jnp.int32)
            for table, ref in zip(tables, (ks_sc, alpha_sc, store_sc)):
                rows.put(ref, row, look_up(rows, table, soil))
        first, ks, alpha, store = [
            Joined(rows, held_ref, full, HALO, last_own)
            for held_ref, full in ((first_ref, first_sc), (ks_ref, ks_sc), (alpha_ref, alpha_sc), (store_ref, store_sc))
        ]
        now, begin, stop, done = first, 0, window, 0
        for wx_ref, wy_ref, wz_ref, inv_ref, base_ref in fields:
            low, high = HALO + done, last_own - done
            wx_of = Joined(rows, wx_ref, wx_sc, low, high - 1)
            wy_of, wz_of = Joined(rows, wy_ref, wy_sc, low, high), Joined(rows, wz_ref, wz_sc, low, high)
            inverse, base = [
                Joined(rows, held_ref, full, low + 1, high - 1) for held_ref, full in ((inv_ref, inv_sc), (base_ref, base_sc))
            ]
            start, finish, last_staged = (begin, low + 2, low) if above else (high - 2, stop, high - 1)
            here_before, wx_before, sums_before = None, None, None
            for row in range(start, finish):
                here, sums = None, None
                if row == last_staged or not wy_of.holds(row):
                    here = faces.conduct(ks.get(row), alpha.get(row), now.get(row))
                if row == last_staged:
                    sums = rows.get(inv_ref, row - HALO), rows.get(base_ref, row - HALO)
                elif not wy_of.holds(row) and begin < row < stop - 1:
                    wy, wz, diagonal, gravity = faces.in_row(row, here)
                    wy_of.put(row, wy)
                    wz_of.put(row, wz)
                    sums = store.get(row) + diagonal, store.get(row) * first.get(row) + gravity
                if row > start:
                    if wx_of.holds(row - 1):
                        wx = wx_of.get(row - 1)
                    else:
                        wx = faces.between_rows(row - 1, here_before, here)
                        wx_of.put(row - 1, wx)
                    if sums_before is not None:
                        diagonal = sums_before[0] + wx_before + wx + river_row(rows, dtop_sc, row - 1, top)
                        inverse.put(row - 1, reciprocal(diagonal))
                        base.put(row - 1, sums_before[1] + river_row(rows, rtop_sc, row - 1, top))
                    wx_before = wx
                here_before, sums_before = here, sums
            for _ in range(SWEEPS):
                begin, stop = begin + 1, stop - 1
                later = Joined(
                    rows, staged_refs[done], (ping_sc, pong_sc)[done % 2], HALO + done + 1, last_own - done - 1
                )
                done += 1
                for row in range(begin, later.first) if above else range(later.last, stop):
                    head = now.get(row - 1), now.get(row), now.get(row + 1)
                    value, _ = relax_row(rows, row, head, (wx_of, wy_of, wz_of), wx_of.get(row - 1), base, inverse)
                    later.put(row, value)
                now = later
        mine = range(HALO, now.first) if above else range(now.last, last_own)
        for row in mine:
            rows.put(result_ref, row - HALO, now.get(row))
        if is_far:
            for row in range(HALO, last_own):
                if row not in mine:
                    other = staged_refs[-1] if now.holds(row) else near_ref
                    rows.put(result_ref, row - HALO, rows.get(other, row - HALO))

    odd = lax.rem(number, 2)
    for above in (True, False):
        @pl.when(odd == (1 if above != is_far else 0))
        def _(above=above):
            one_side(above)

    if is_far:
        for part in range(rows.per_row):
            lanes = pl.ds(part * LANES, LANES)
            top_ref[:, lanes] = result_ref[part, pl.ds(0, span, stride=layers), :]
            for step, head_ref in enumerate(head_refs):
                for held_layer in range(held):
                    layer = (own ^ step) * held + held_layer
                    head_ref[held_layer, :, lanes] = result_ref[part, pl.ds(layer, span, stride=layers), :]


def inflow_kernel(reach_rows, stride, cells_ref, bed_ref, slot_section_ref, reach_ref, *refs):
    groups = lax.axis_size("layer")
    own_layer, flip, _ = position()
    top_refs = refs[:groups]
    out_ref, block_sc, lane_sc, found_sc, turned_sc = refs[groups:]
    span, breadth = top_refs[0].shape
    per_row = breadth // LANES
    blocks = groups * span * per_row
    slots = cells_ref.shape[0]
    quarter = LANES // groups
    packed = slots // groups
    for step, top_ref in enumerate(top_refs):
        number = span_at(flip, groups, own_layer ^ step)
        for part in range(per_row):
            spot = pl.ds(number * span * per_row + part, span, stride=per_row)
            turned_sc[spot, :] = top_ref[:, part * LANES:(part + 1) * LANES]

    own = lax.broadcasted_iota(jnp.int32, (packed, LANES), 1) // quarter

    def pack(ref):
        result = None
        for number in range(groups):
            shift = lax.rem((number + groups - own_layer) * quarter, LANES)
            moved = pltpu.roll(ref[pl.ds(number * packed, packed), :], shift, 1)
            result = moved if result is None else jnp.where(own == number, moved, result)
        return result

    cells = pack(cells_ref)
    block, lane = split_cells(cells, 0, breadth, LANES)
    block_sc[...] = block
    lane_sc[...] = lane
    table = jnp.concatenate(bf16_pieces(turned_sc[...].T, 2), axis=0)
    names = names_of(blocks)
    index = lax.broadcasted_iota(jnp.int32, (8, LANES), 0).astype(jnp.float32)
    for pair in range(0, packed, 2):
        hots = jnp.concatenate(
            [jnp.concatenate(one_hot(row_copies(block_sc, 0, row), names), axis=0) for row in (pair, pair + 1)], axis=1
        )
        found = lax.dot_general(
            table, hots, (((1,), (0,)), ((), ())), preferred_element_type=jnp.float32
        )
        found = found[:LANES] + found[LANES:]
        for row in (pair, pair + 1):
            lanes = jnp.broadcast_to(lane_sc[pl.ds(row, 1), :], (8, LANES))
            mine = found[:, (row - pair) * LANES:(row - pair + 1) * LANES]
            total = jnp.zeros((8, LANES), jnp.float32)
            for start in range(0, LANES, 8):
                total = total + jnp.where(lanes == index + float(start), mine[start:start + 8], 0.0)
            found_sc[pl.ds(row, 1), :] = jnp.sum(total, axis=0, keepdims=True)
    slot_in = jnp.where(cells >= 0, pack(bed_ref) * (found_sc[...] - pack(slot_section_ref)), 0.0)
    spread = jnp.concatenate(
        [slot_in if number == 0 else pltpu.roll(slot_in, LANES - number * quarter, 1) for number in range(groups)],
        axis=0,
    )
    in_quarter = lax.broadcasted_iota(jnp.int32, spread.shape, 1) < quarter
    pieces = bf16_pieces(jnp.where(in_quarter, spread, 0.0), 3)
    fold = reach_rows // groups
    index = lax.broadcasted_iota(jnp.int32, (out_ref.shape[0], slots), 0)
    index = index // fold * stride + lax.rem(index, fold)
    result = None
    for number in range(groups):
        name = (index + number * fold).astype(jnp.float32)
        put = jnp.where(name == reach_ref[...], 1.0, 0.0).astype(jnp.bfloat16)
        total = jnp.zeros(out_ref.shape, jnp.float32)
        for piece in pieces:
            total = total + lax.dot_general(
                put, piece, (((1,), (0,)), ((), ())), preferred_element_type=jnp.float32
            )
        result = total if result is None else result + pltpu.roll(total, number * quarter, 1)
    out_ref[...] = result


def sum_kernel(terms_ref, inflow_ref):
    total = terms_ref[0]
    for tile in range(1, terms_ref.shape[0]):
        total = total + terms_ref[tile]
    fold, quarter = total.shape[0], inflow_ref.shape[1]
    for number in range(inflow_ref.shape[0] // fold):
        lanes = slice(number * quarter, (number + 1) * quarter)
        inflow_ref[pl.ds(number * fold, fold), :] = total[:, lanes]


def head_kernel(*refs):
    groups = lax.axis_size("layer")
    back_refs, (head_hbm, sems) = refs[:groups], refs[groups:]
    _, span, _ = back_refs[0].shape
    own, flip, _ = position()
    copies = []
    for step, back_ref in enumerate(back_refs):
        rows = pl.ds(pl.multiple_of(span_at(flip, groups, own ^ step) * span, span), span)
        copies.append(pltpu.make_async_copy(back_ref, head_hbm.at[:, rows, :], sems.at[step]))
        copies[-1].start()
    for copy in copies:
        copy.wait()


def call(kernel, out_shape, in_specs, scratch, micros, vmem=VMEM_LIMIT, out_specs=None):
    single = not isinstance(out_shape, (tuple, list))
    return pl.pallas_call(
        kernel,
        out_shape=out_shape,
        in_specs=in_specs,
        out_specs=out_specs or (in_vmem if single else tuple(in_vmem for _ in out_shape)),
        scratch_shapes=scratch,
        compiler_params=pltpu.CompilerParams(vmem_limit_bytes=vmem),
        cost_estimate=pl.CostEstimate(flops=int(micros * 1.15e9), bytes_accessed=0, transcendentals=0),
    )


def on_device(
    head_start,
    soil_class,
    land_mask,
    ks_table,
    alpha_table,
    store_table,
    section,
    cross_owner,
    cross_local,
    node_cell,
    bed_cond,
):
    held, across, breadth = head_start.shape
    reach_rows, node_count = section.shape
    tiles = lax.axis_size("tile")
    groups = lax.axis_size("layer")
    layers = held * groups
    span = across // groups
    per_row = breadth // LANES
    blocks = span * per_row
    near = [(i, i ^ 1) for i in range(groups)]
    far = []
    for upper in range(tiles):
        far += [(upper * groups + i, upper * groups + (i ^ (groups - 1))) for i in range(1, groups - 1)]
        if upper + 1 < tiles:
            index = groups - 1 if upper % 2 == 0 else 0
            one, two = upper * groups + index, (upper + 1) * groups + index
            far += [(one, two), (two, one)]
    far += [(0, 0)]
    last = tiles * groups - (1 if tiles % 2 == 1 else groups)
    far += [(last, last)]

    cells = node_cell[0]
    bed = bed_cond[0]
    slots = cells.shape[0]

    def exchange(parts):
        received = [parts[0]]
        for step in range(1, groups):
            received.append(lax.ppermute(parts[step], "layer", [(i, i ^ step) for i in range(groups)]))
        return received

    stride = reach_rows + 8
    spread = call(
        spread_kernel, jax.ShapeDtypeStruct((tiles, stride, node_count), jnp.float32), [in_hbm] * 3,
        [
            pltpu.VMEM(section.shape, jnp.float32),
            pltpu.VMEM(cross_owner.shape, jnp.int32),
            pltpu.VMEM(cross_owner.shape, jnp.int32),
            pltpu.SemaphoreType.DMA((3,)),
        ],
        1, VMEM_MOST,
    )(section, cross_owner, cross_local)
    whole_section = lax.all_to_all(spread, "tile", 0, 0).reshape(tiles * stride, node_count)
    own_blocks = call(
        prepare_kernel,
        (jax.ShapeDtypeStruct((2, held, span, breadth), jnp.float32),) * groups,
        [in_vmem] * 2 + [in_hbm], [], 0.5,
    )(head_start, soil_class, spread)
    received = exchange(own_blocks)

    node_scratch = pltpu.VMEM((slots, LANES), jnp.float32)
    riv_shape = jax.ShapeDtypeStruct((blocks, LANES), jnp.float32)
    node_field = jax.ShapeDtypeStruct((slots, LANES), jnp.float32)
    groups_of_cells = span * breadth // BLOCK
    sums = pltpu.VMEM((groups_of_cells, LANES), jnp.float32)
    block_number, spot, diag = call(
        functools.partial(early_kernel, breadth, span), (node_field, node_field, riv_shape), [in_vmem] * 2,
        [node_scratch] * 2 + [sums], 3,
    )(cells, bed)
    rhs, slot_section, reach = call(
        functools.partial(river_kernel, stride),
        (riv_shape, node_field, jax.ShapeDtypeStruct((1, slots), jnp.float32)),
        [in_vmem] * 4, [node_scratch] * 2 + [sums], 5,
    )(bed, whole_section, block_number, spot)
    edges = jax.ShapeDtypeStruct((-(-(2 * layers + 3) * HALO // 8) * 8, breadth), jnp.float32)
    near_edge, far_edge = call(
        edge_kernel, (edges, edges), [in_vmem] * (3 + groups), [], 0.1,
    )(land_mask, diag, rhs, *received)
    far_halo = lax.ppermute(far_edge, FLAT, far)
    near_halo = lax.ppermute(near_edge, "layer", near)

    window = span + 2 * HALO
    own_field = jax.ShapeDtypeStruct((per_row, span * layers, LANES), jnp.float32)
    field = pltpu.VMEM((per_row, window * layers, LANES), jnp.float32)
    staged = call(
        stage_kernel, (own_field,) * (4 + 5 * ITERS + HALO), [in_smem] * 3 + [in_vmem] * (3 + groups),
        [pltpu.VMEM(own_field.shape, jnp.float32)] + [pltpu.VMEM((span, breadth), jnp.float32)] * 3,
        4,
    )(ks_table, alpha_table, store_table, land_mask, diag, rhs, *received)
    head_shape = jax.ShapeDtypeStruct((held, span, breadth), jnp.float32)
    flow_scratch = (
        [field] * 12
        + [pltpu.VMEM((window, breadth), jnp.float32)]
        + [pltpu.VMEM((window * per_row, LANES), jnp.float32)] * 2
        + [pltpu.VMEM((window, breadth), jnp.float32)] * 3
    )
    known = diag, rhs, *staged
    near_side = call(
        functools.partial(flow_kernel, False), own_field, [in_smem] * 3 + [in_vmem] * (2 + len(known)), flow_scratch, 2,
    )(ks_table, alpha_table, store_table, land_mask, near_halo, *known)
    *heads, top = call(
        functools.partial(flow_kernel, True),
        (head_shape,) * groups + (jax.ShapeDtypeStruct((span, breadth), jnp.float32),),
        [in_smem] * 3 + [in_vmem] * (3 + len(known)),
        [pltpu.VMEM(own_field.shape, jnp.float32)] + flow_scratch, 2,
    )(ks_table, alpha_table, store_table, land_mask, far_halo, *known, near_side)
    tops = exchange([top] * groups)
    backs = exchange(heads)

    fold = reach_rows // groups
    packed = pltpu.VMEM((slots // groups, LANES), jnp.float32)
    partial = call(
        functools.partial(inflow_kernel, reach_rows, stride),
        jax.ShapeDtypeStruct((tiles * fold, node_count), jnp.float32),
        [in_vmem] * (4 + groups),
        [packed] * 3 + [pltpu.VMEM((across * per_row, LANES), jnp.float32)],
        3,
    )(cells, bed, slot_section, reach, *tops)
    partial, *backs[:-1] = lax.optimization_barrier((partial, *backs[:-1]))
    terms = lax.all_to_all(partial.reshape(tiles, fold, node_count), "tile", 0, 0)
    head = call(
        head_kernel, jax.ShapeDtypeStruct(head_start.shape, jnp.float32), [in_vmem] * groups,
        [pltpu.SemaphoreType.DMA((groups,))], 0.7, out_specs=in_hbm,
    )(*backs)
    inflow_shape = jax.ShapeDtypeStruct((reach_rows, node_count // groups), jnp.float32)
    return head, call(sum_kernel, inflow_shape, [in_vmem], [], 0.1)(terms)


def solution(mesh):
    placed = (
        P("layer", "tile", None),
        P("layer", "tile", None),
        P("tile", None),
        P(),
        P(),
        P(),
        P("tile", None),
        P("tile", None),
        P("tile", None),
        P("tile", None, None),
        P("tile", None, None),
    )
    return jax.shard_map(
        on_device,
        mesh=mesh,
        in_specs=placed,
        out_specs=(P("layer", "tile", None), P("tile", "layer")),
        check_vma=False,
    )
```
